32 devices in a mesh: section: 2 (over x), lon: 4 (over z), lat: 4 (over y, core).
Axes of the slice: x: 2, y: 2, z: 4, core: 2. Of those that a mesh axis runs over, the one named last changes fastest.
Arguments:
- inputs: bfloat16 [2, 2, 24, 48, 512], P('section', None, 'lat', 'lon'), may hold values from -6 to 6
- cotangent: bfloat16 [2, 2, 24, 48, 512], P('section', None, 'lat', 'lon'), may hold values from -6 to 6
- land_sea: int32 [24, 48], P('lat', 'lon'), may hold values 0 or 1
- gains: float32 [2, 512], P('section'), may hold values from 0.5 to 1.5
- qkv_weight: bfloat16 [2, 512, 1536], P('section'), may hold values from -0.25 to 0.25
- out_weight: bfloat16 [2, 512, 512], P('section'), may hold values from -0.25 to 0.25
- land_bias: float32 [2, 16], P('section'), may hold values from -2 to 2
Outputs:
- input_grads: float32 [2, 2, 24, 48, 512], P('section', None, 'lat', 'lon')
- qkv_grad: float32 [2, 512, 1536], P('section')
- out_grad: float32 [2, 512, 512], P('section')
- gain_grad: float32 [2, 512], P('section')
- bias_grad: float32 [2, 16], P('section')
The draws below stay inside these ranges and needn't reach their ends.
All inputs are finite; a program needn't handle non-finite values. No bound on the sum of `land_sea` on one device may be relied on, other than what follows from the above.
Results may differ from the reference program's by a relative error of at most 0.011.
Values may be sent and summed in bfloat16 or wider, within the bound.
No kernel may reach another device: no remote copies, remote signals or barrier semaphores. Data moves between devices by JAX's collectives and lax.ppermute only.
A program may use at most 64 MiB of HBM per device.

```python
import jax
import jax.numpy as jnp
from jax import lax

C = 512
HEADS = 16
LEV = 2
WLAT = 6
WLON = 12
SHIFT = 6
LD = 12
NLAT = 24
NLON = 48


def set_ends(values, rng, low, top_value):
    place = [jax.random.randint(jax.random.fold_in(rng, axis), (), 0, length) for axis, length in enumerate(values.shape)]
    widest = values.shape.index(max(values.shape))
    beside = place[:widest] + [(place[widest] + 1) % values.shape[widest]] + place[widest + 1:]
    return values.at[tuple(place)].set(low).at[tuple(beside)].set(top_value)


def block_levels(own_key, shape, cuts, least, top_value):
    loudness = 1.0
    for dim, parts in cuts:
        heights = jax.random.uniform(jax.random.fold_in(jax.random.fold_in(own_key, 6), dim), (parts,), jnp.float32, least / len(cuts), top_value / len(cuts))
        loudness = loudness * jnp.repeat(jnp.exp(heights), shape[dim] // parts).reshape((-1,) + (1,) * (len(shape) - 1 - dim))
    return loudness


def scatter_about(key, dims, deviation, reach, split=(), held_as=jnp.bfloat16):
    drawn = jax.random.normal(key, dims, jnp.float32) * deviation
    if len(split) > 0:
        drawn = block_levels(key, dims, split, -0.22, 0.18) * drawn
    return jnp.clip(drawn, min=-reach, max=reach).astype(held_as)


def setup_inputs(seed: int = 0) -> dict:
    seeds = jax.random.split(jax.random.key(seed), 8)
    return {
        "inputs": scatter_about(seeds[0], (2, LEV, NLAT, NLON, C), 1.0, 6.0, ((0, 2), (2, 4), (3, 4))),
        "cotangent": scatter_about(seeds[1], (2, LEV, NLAT, NLON, C), 1.0, 6.0, ((0, 2), (2, 4), (3, 4))),
        "land_sea": set_ends((jax.random.randint(seeds[2], (NLAT, NLON), 0, 3) < 1).astype(jnp.int32), jax.random.fold_in(seeds[2], 1), 0, 1),
        "gains": jnp.clip(1.0 + 0.1 * jax.random.normal(seeds[3], (2, C), jnp.float32), 0.5, 1.5),
        "qkv_weight": scatter_about(seeds[4], (2, C, 3 * C), C ** -0.5, 0.25, ((0, 2),)),
        "out_weight": scatter_about(seeds[5], (2, C, C), C ** -0.5, 0.25, ((0, 2),)),
        "land_bias": jnp.clip(jax.random.uniform(seeds[6], (2, HEADS), jnp.float32, -2.0, 2.0) * block_levels(seeds[6], (2, HEADS), ((0, 2),), -0.4, 0.0), -2.0, 2.0),
    }


EPSILON = 1e-05

def contract_last(left, right):
    return lax.dot_general(left, right, (((1,), (1,)), ((), ())), preferred_element_type=jnp.float32)

def contract_first(left, right):
    return lax.dot_general(left, right, (((0,), (0,)), ((), ())), preferred_element_type=jnp.float32)

def to_windows(grid, lat_span, lon_span):
    levels, rows, cols, width = grid.shape
    blocks = grid.reshape(levels, rows // lat_span, lat_span, cols // lon_span, lon_span, width)
    blocks = blocks.transpose(1, 3, 0, 2, 4, 5)
    return blocks.reshape(-1, levels * lat_span * lon_span, width)

def from_windows(windows, levels, rows, cols, lat_span, lon_span):
    width = windows.shape[-1]
    blocks = windows.reshape(rows // lat_span, cols // lon_span, levels, lat_span, lon_span, width)
    return blocks.transpose(2, 0, 3, 1, 4, 5).reshape(levels, rows, cols, width)

def land_windows(land, levels, lat_span, lon_span):
    rows, cols = land.shape
    blocks = land.reshape(rows // lat_span, lat_span, cols // lon_span, lon_span).transpose(0, 2, 1, 3)
    return jnp.tile(blocks.reshape(-1, lat_span * lon_span), (1, levels))

def window_forward(tokens_win, land_win, gain, qkv_weight, land_bias):
    batch, count, width = tokens_win.shape
    heads = land_bias.shape[0]
    head_size = width // heads
    values32 = tokens_win.astype(jnp.float32)
    centred = values32 - lax.optimization_barrier(jnp.mean(values32, axis=-1, keepdims=True))
    inverse = lax.rsqrt(lax.optimization_barrier(jnp.mean(centred * centred, axis=-1, keepdims=True)) + EPSILON)
    normed = centred * inverse
    normed_b = (normed * gain).astype(jnp.bfloat16).reshape(batch * count, width)
    projected = jnp.dot(normed_b, qkv_weight, preferred_element_type=jnp.float32).astype(jnp.bfloat16)
    projected = projected.reshape(batch, count, 3, heads, head_size)
    queries = projected[:, :, 0]
    keys_win = projected[:, :, 1]
    values_win = projected[:, :, 2]
    scale = head_size ** (-0.5)
    scores = jnp.einsum('bihd,bjhd->bhij', queries, keys_win, preferred_element_type=jnp.float32) * scale
    scores = scores + land_bias[None, :, None, None] * land_win[:, None, None, :]
    weights = jax.nn.softmax(scores, axis=-1)
    weights_b = weights.astype(jnp.bfloat16)
    attended = jnp.einsum('bhij,bjhd->bihd', weights_b, values_win, preferred_element_type=jnp.float32)
    attended = attended.astype(jnp.bfloat16).reshape(batch * count, width)
    return (normed.reshape(batch * count, width), inverse.reshape(batch * count, 1), normed_b, queries, keys_win, values_win, weights, weights_b, attended)

def window_backward(cache, grad_out, land_win, gain, qkv_weight, out_weight, want_weights):
    normed, inverse, normed_b, queries, keys_win, values_win, weights, weights_b, attended = cache
    batch, count, heads, head_size = queries.shape
    width = heads * head_size
    scale = head_size ** (-0.5)
    grad_att = contract_last(grad_out, out_weight).astype(jnp.bfloat16).reshape(batch, count, heads, head_size)
    grad_weights = jnp.einsum('bihd,bjhd->bhij', grad_att, values_win, preferred_element_type=jnp.float32)
    grad_values = jnp.einsum('bhij,bihd->bjhd', weights_b, grad_att, preferred_element_type=jnp.float32)
    inner = lax.optimization_barrier(jnp.sum(weights * grad_weights, axis=-1, keepdims=True))
    grad_scores = weights * (grad_weights - inner)
    scaled_b = (grad_scores * scale).astype(jnp.bfloat16)
    grad_queries = jnp.einsum('bhij,bjhd->bihd', scaled_b, keys_win, preferred_element_type=jnp.float32)
    grad_keys = jnp.einsum('bhij,bihd->bjhd', scaled_b, queries, preferred_element_type=jnp.float32)
    grad_proj = jnp.stack([grad_queries, grad_keys, grad_values], axis=2).astype(jnp.bfloat16)
    grad_proj = grad_proj.reshape(batch * count, 3 * width)
    grad_normed = contract_last(grad_proj, qkv_weight)
    scaled = grad_normed * gain
    grad_tokens = inverse * (scaled - lax.optimization_barrier(jnp.mean(scaled, axis=-1, keepdims=True)) - normed * lax.optimization_barrier(jnp.mean(scaled * normed, axis=-1, keepdims=True)))
    if want_weights:
        grad_bias = lax.optimization_barrier(jnp.sum(grad_scores * land_win[:, None, None, :], axis=(0, 2, 3)))
        grad_gain = lax.optimization_barrier(jnp.sum(grad_normed * normed, axis=0))
        grad_qkv = contract_first(normed_b, grad_proj)
        grad_outw = contract_first(attended, grad_out)
        return (grad_tokens, (grad_qkv, grad_outw, grad_gain, grad_bias))
    return (grad_tokens, None)

def section_grads(tokens, grad_out, land, gain, qkv_weight, out_weight, land_bias):
    levels, rows, cols, width = tokens.shape
    heads = land_bias.shape[0]
    shifted = jnp.roll(tokens, -SHIFT, axis=2)
    grad_shift = jnp.roll(grad_out, -SHIFT, axis=2)
    land_shift = jnp.roll(land, -SHIFT, axis=1).astype(jnp.float32)
    token_win = to_windows(shifted, WLAT, WLON)
    grad_win = to_windows(grad_shift, WLAT, WLON)
    land_win = land_windows(land_shift, levels, WLAT, WLON)
    group = LD // WLON
    count = token_win.shape[1]
    token_win = token_win.reshape(-1, group, count, width)
    grad_win = grad_win.reshape(-1, group, count, width)
    land_win = land_win.reshape(-1, group, count)

    def step(carry, pieces):
        token_piece, grad_piece, land_piece = pieces
        cache = window_forward(token_piece, land_piece, gain, qkv_weight, land_bias)
        grad_tokens, sums = window_backward(cache, grad_piece.reshape(-1, width), land_piece, gain, qkv_weight, out_weight, True)
        carry = tuple((old + new for old, new in zip(carry, sums)))
        return (carry, grad_tokens.reshape(group, count, width))
    start = (jnp.zeros((width, 3 * width), jnp.float32), jnp.zeros((width, width), jnp.float32), jnp.zeros((width,), jnp.float32), jnp.zeros((heads,), jnp.float32))
    totals, grad_pieces = lax.scan(step, start, (token_win, grad_win, land_win))
    grid = from_windows(grad_pieces.reshape(-1, count, width), levels, rows, cols, WLAT, WLON)
    return (jnp.roll(grid, SHIFT, axis=2) + grad_out.astype(jnp.float32), totals)

def reference(inputs, cotangent, land_sea, gains, qkv_weight, out_weight, land_bias):
    decoder_grad, decoder_sums = section_grads(inputs[1], cotangent[1], land_sea, gains[1], qkv_weight[1], out_weight[1], land_bias[1])
    encoder_cot = (cotangent[0].astype(jnp.float32) + decoder_grad).astype(jnp.bfloat16)
    encoder_grad, encoder_sums = section_grads(inputs[0], encoder_cot, land_sea, gains[0], qkv_weight[0], out_weight[0], land_bias[0])
    square = jnp.float32(0.0)
    for piece in encoder_sums + decoder_sums:
        square = square + jnp.sum(piece * piece)
    entries = 2 * (4 * C * C + C + HEADS)
    factor = jnp.minimum(1.0, lax.rsqrt(square / entries + 1e-06))
    stacked = [jnp.stack([first, second]) * factor for first, second in zip(encoder_sums, decoder_sums)]
    return (jnp.stack([encoder_grad, decoder_grad]), stacked[0], stacked[1], stacked[2], stacked[3])
```

```python
import jax
import jax.numpy as jnp
from jax import lax
from jax.sharding import PartitionSpec as P

WLAT = 6
WLON = 12
SHIFT = 6


EPSILON = 1e-05


def from_behind(value, axis, by):
    count = lax.axis_size(axis)
    return lax.ppermute(value, axis, [(i, (i + by) % count) for i in range(count)])


def passed_along(block, axis, distance):
    devices = range(lax.axis_size(axis))
    route = [(i - distance, i) for i in devices if i - distance in devices]
    return lax.ppermute(block, axis, route)


def contract_last(left, right):
    return lax.dot_general(
        left, right, (((1,), (1,)), ((), ())), preferred_element_type=jnp.float32
    )


def contract_first(left, right):
    return lax.dot_general(
        left, right, (((0,), (0,)), ((), ())), preferred_element_type=jnp.float32
    )


def to_windows(grid, lat_span, lon_span):
    levels, rows, cols, width = grid.shape
    blocks = grid.reshape(levels, rows // lat_span, lat_span, cols // lon_span, lon_span, width)
    blocks = blocks.transpose(1, 3, 0, 2, 4, 5)
    return blocks.reshape(-1, levels * lat_span * lon_span, width)


def from_windows(windows, levels, rows, cols, lat_span, lon_span):
    width = windows.shape[-1]
    blocks = windows.reshape(rows // lat_span, cols // lon_span, levels, lat_span, lon_span, width)
    return blocks.transpose(2, 0, 3, 1, 4, 5).reshape(levels, rows, cols, width)


def land_windows(land, levels, lat_span, lon_span):
    rows, cols = land.shape
    blocks = land.reshape(rows // lat_span, lat_span, cols // lon_span, lon_span).transpose(
        0, 2, 1, 3
    )
    return jnp.tile(blocks.reshape(-1, lat_span * lon_span), (1, levels))


def window_forward(tokens_win, land_win, gain, qkv_weight, land_bias):
    batch, count, width = tokens_win.shape
    heads = land_bias.shape[0]
    head_size = width // heads
    values32 = tokens_win.astype(jnp.float32)
    centred = values32 - jnp.mean(values32, axis=-1, keepdims=True)
    inverse = lax.rsqrt(jnp.mean(centred * centred, axis=-1, keepdims=True) + EPSILON)
    normed = centred * inverse
    normed_b = (normed * gain).astype(jnp.bfloat16).reshape(batch * count, width)
    projected = jnp.dot(normed_b, qkv_weight, preferred_element_type=jnp.float32).astype(
        jnp.bfloat16
    )
    projected = projected.reshape(batch, count, 3, heads, head_size)
    queries = projected[:, :, 0]
    keys_win = projected[:, :, 1]
    values_win = projected[:, :, 2]
    scale = head_size ** (-0.5)
    scores = (
        jnp.einsum("bihd,bjhd->bhij", queries, keys_win, preferred_element_type=jnp.float32) * scale
    )
    scores = scores + land_bias[None, :, None, None] * land_win[:, None, None, :]
    weights = jax.nn.softmax(scores, axis=-1)
    weights_b = weights.astype(jnp.bfloat16)
    attended = jnp.einsum(
        "bhij,bjhd->bihd", weights_b, values_win, preferred_element_type=jnp.float32
    )
    attended = attended.astype(jnp.bfloat16).reshape(batch * count, width)
    return (
        normed.reshape(batch * count, width),
        inverse.reshape(batch * count, 1),
        normed_b,
        queries,
        keys_win,
        values_win,
        weights,
        weights_b,
        attended,
    )


def window_backward(cache, grad_out, land_win, gain, qkv_weight, out_weight, want_weights):
    normed, inverse, normed_b, queries, keys_win, values_win, weights, weights_b, attended = cache
    batch, count, heads, head_size = queries.shape
    width = heads * head_size
    scale = head_size ** (-0.5)
    grad_att = (
        contract_last(grad_out, out_weight)
        .astype(jnp.bfloat16)
        .reshape(batch, count, heads, head_size)
    )
    grad_weights = jnp.einsum(
        "bihd,bjhd->bhij", grad_att, values_win, preferred_element_type=jnp.float32
    )
    grad_values = jnp.einsum(
        "bhij,bihd->bjhd", weights_b, grad_att, preferred_element_type=jnp.float32
    )
    inner = jnp.sum(weights * grad_weights, axis=-1, keepdims=True)
    grad_scores = weights * (grad_weights - inner)
    scaled_b = (grad_scores * scale).astype(jnp.bfloat16)
    grad_queries = jnp.einsum(
        "bhij,bjhd->bihd", scaled_b, keys_win, preferred_element_type=jnp.float32
    )
    grad_keys = jnp.einsum("bhij,bihd->bjhd", scaled_b, queries, preferred_element_type=jnp.float32)
    grad_proj = jnp.stack([grad_queries, grad_keys, grad_values], axis=2).astype(jnp.bfloat16)
    grad_proj = grad_proj.reshape(batch * count, 3 * width)
    grad_normed = contract_last(grad_proj, qkv_weight)
    scaled = grad_normed * gain
    grad_tokens = inverse * (
        scaled
        - jnp.mean(scaled, axis=-1, keepdims=True)
        - normed * jnp.mean(scaled * normed, axis=-1, keepdims=True)
    )
    if want_weights:
        grad_bias = jnp.sum(grad_scores * land_win[:, None, None, :], axis=(0, 2, 3))
        grad_gain = jnp.sum(grad_normed * normed, axis=0)
        grad_qkv = contract_first(normed_b, grad_proj)
        grad_outw = contract_first(attended, grad_out)
        return (grad_tokens, (grad_qkv, grad_outw, grad_gain, grad_bias))
    return (grad_tokens, None)


def swapped(value, axis, bit):
    count = lax.axis_size(axis)
    return lax.ppermute(value, axis, [(i, i ^ bit) for i in range(count)])


def halved(block, axis, bit):
    mine = (lax.axis_index(axis) // bit) % 2
    pair = block.reshape(2, block.shape[0] // 2, -1)
    give = lax.dynamic_index_in_dim(pair, 1 - mine, 0, keepdims=False).astype(jnp.bfloat16)
    keep = lax.dynamic_index_in_dim(pair, mine, 0, keepdims=False)
    return keep + swapped(give, axis, bit).astype(jnp.float32)


def scattered(block, axis):
    count = lax.axis_size(axis)
    mine = lax.axis_index(axis)
    pieces = block.reshape(count, block.shape[0] // count, -1)
    total = lax.dynamic_index_in_dim(pieces, mine, 0, keepdims=False)
    for by in range(1, count):
        give = lax.dynamic_index_in_dim(pieces, (mine + by) % count, 0, keepdims=False)
        total = total + from_behind(give.astype(jnp.bfloat16), axis, by).astype(jnp.float32)
    return total


def doubled(block, axis, bit):
    mine = (lax.axis_index(axis) // bit) % 2
    other = swapped(block, axis, bit)
    low = jnp.where(mine == 0, block, other)
    high = jnp.where(mine == 0, other, block)
    return jnp.concatenate([low, high], axis=0)


def gathered(block, axis):
    count = lax.axis_size(axis)
    mine = lax.axis_index(axis)
    whole = jnp.zeros((count,) + block.shape, block.dtype)
    whole = lax.dynamic_update_index_in_dim(whole, block, mine, 0)
    for by in range(1, count):
        whole = lax.dynamic_update_index_in_dim(
            whole, from_behind(block, axis, by), (mine - by) % count, 0
        )
    return whole.reshape(count * block.shape[0], -1)


def small_sum(value, axes):
    for axis in axes:
        bit = 1
        while bit < lax.axis_size(axis):
            value = value + swapped(value, axis, bit)
            bit *= 2
    return value


def body(inputs, cotangent, land_sea, gains, qkv_weight, out_weight, land_bias):
    tokens = inputs[0]
    own_cot = cotangent[0]
    gain = gains[0]
    weight_qkv = qkv_weight[0]
    weight_out = out_weight[0]
    bias = land_bias[0]
    levels, rows, cols, width = tokens.shape
    heads = bias.shape[0]
    land_b = land_sea.astype(jnp.bfloat16)
    rim_tokens, rim_land = from_behind((tokens[:, :, :SHIFT], land_b[:, :SHIFT]), "lon", -1)
    rim_cot = from_behind(own_cot[:, :, :SHIFT], "lon", -1)
    shifted = jnp.concatenate([tokens[:, :, SHIFT:], rim_tokens], axis=2)
    cot_shift = jnp.concatenate([own_cot[:, :, SHIFT:], rim_cot], axis=2)
    land_shift = jnp.concatenate([land_b[:, SHIFT:], rim_land], axis=1).astype(jnp.float32)
    land_win = land_windows(land_shift, levels, WLAT, WLON)
    cache = window_forward(to_windows(shifted, WLAT, WLON), land_win, gain, weight_qkv, bias)
    normed_b, attended = cache[2], cache[8]
    count = levels * WLAT * WLON
    cot_win = to_windows(cot_shift, WLAT, WLON).reshape(-1, width)

    first, unused = window_backward(
        cache, cot_win, land_win, gain, weight_qkv, weight_out, False
    )
    skip = (first + cot_win.astype(jnp.float32)).astype(jnp.bfloat16)
    skip = passed_along(skip, "section", -1)
    total_cot = (cot_win.astype(jnp.float32) + skip.astype(jnp.float32)).astype(jnp.bfloat16)
    second, sums = window_backward(
        cache, total_cot, land_win, gain, weight_qkv, weight_out, True
    )
    final = (second + total_cot.astype(jnp.float32)).reshape(-1, count, width)
    grid = from_windows(final, levels, rows, cols, WLAT, WLON)
    rim_back = from_behind(grid[:, :, cols - SHIFT :].astype(jnp.bfloat16), "lon", 1)
    final_grad = jnp.concatenate(
        [rim_back.astype(jnp.float32), grid[:, :, : cols - SHIFT]], axis=2
    )

    grad_qkv, grad_outw, unused, grad_bias = sums
    grad_bias = small_sum(grad_bias, ("lat", "lon"))
    part_out = halved(scattered(halved(grad_outw, "lat", 1), "lon"), "lat", 2)
    part_qkv = scattered(halved(halved(grad_qkv, "lat", 1), "lat", 2), "lon")
    lat, lon = lax.axis_index("lat"), lax.axis_index("lon")
    piece = part_qkv.shape[0]
    start = ((lat % 2) * 2 + lat // 2) * (width // 4) + lon * piece
    weight_rows = lax.dynamic_slice_in_dim(weight_qkv, start, piece, 0).astype(jnp.float32)
    gain_rows = lax.dynamic_slice_in_dim(gain, start, piece, 0)
    part_gain = jnp.sum(part_qkv * weight_rows, axis=1) / gain_rows
    square = jnp.sum(part_qkv * part_qkv) + jnp.sum(part_out * part_out)
    square = square + jnp.sum(part_gain * part_gain)
    square = small_sum(square.reshape(1), ("section", "lat", "lon"))[0]
    both_bias = jnp.sum(grad_bias * grad_bias).reshape(1)
    square = square + small_sum(both_bias, ("section",))[0]
    entries = 2 * (4 * width * width + width + heads)
    factor = jnp.minimum(1.0, lax.rsqrt(square / entries + 1e-06))

    part_out = part_out.astype(jnp.bfloat16)
    part_qkv = part_qkv.astype(jnp.bfloat16)
    all_out = doubled(gathered(doubled(part_out, "lat", 2), "lon"), "lat", 1)
    all_qkv = doubled(doubled(gathered(part_qkv, "lon"), "lat", 2), "lat", 1)
    all_out = all_out.astype(jnp.float32) * factor
    all_qkv = all_qkv.astype(jnp.float32)
    grad_gain = jnp.sum(all_qkv * weight_qkv.astype(jnp.float32), axis=1) / gain * factor
    all_qkv = all_qkv * factor
    grad_bias = grad_bias * factor
    return (final_grad[None], all_qkv[None], all_out[None], grad_gain[None], grad_bias[None])


def solution(mesh):
    placed = (
        P("section", None, "lat", "lon", None),
        P("section", None, "lat", "lon", None),
        P("lat", "lon"),
        P("section", None),
        P("section", None, None),
        P("section", None, None),
        P("section", None),
    )
    return jax.shard_map(
        body,
        mesh=mesh,
        in_specs=placed,
        out_specs=(
            P("section", None, "lat", "lon", None),
            P("section", None, None),
            P("section", None, None),
            P("section", None),
            P("section", None),
        ),
        check_vma=False,
    )
```

```python
import functools

import jax
import jax.numpy as jnp
from jax import lax
from jax.experimental import pallas as pl
from jax.experimental.pallas import tpu as pltpu
from jax.sharding import PartitionSpec as P

SHIFT = 6
GROUP = 128
EPSILON = 1e-05
F32 = jnp.float32
BF16 = jnp.bfloat16


def from_behind(value, axis, by):
    count = lax.axis_size(axis)
    return lax.ppermute(value, axis, [(i, (i + by) % count) for i in range(count)])


def passed_along(block, axis, distance):
    devices = range(lax.axis_size(axis))
    route = [(i - distance, i) for i in devices if i - distance in devices]
    return lax.ppermute(block, axis, route)


def swapped(value, axis, bit):
    count = lax.axis_size(axis)
    return lax.ppermute(value, axis, [(i, i ^ bit) for i in range(count)])


def dot(left, right):
    return jnp.dot(left, right, preferred_element_type=F32)


def dot_last(left, right):
    return lax.dot_general(left, right, (((1,), (1,)), ((), ())), preferred_element_type=F32)


def call(kernel, outs, scratch=(), smem=(), operands=(), flops=10**8):
    moved = sum(o.size * o.dtype.itemsize for o in list(outs) + list(operands))
    return pl.pallas_call(
        kernel,
        out_shape=list(outs),
        in_specs=[
            pl.BlockSpec(memory_space=pltpu.SMEM if i in smem else pltpu.VMEM)
            for i in range(len(operands))
        ],
        out_specs=[pl.BlockSpec(memory_space=pltpu.VMEM) for _ in outs],
        scratch_shapes=list(scratch),
        compiler_params=pltpu.CompilerParams(vmem_limit_bytes=40 * 2**20),
        cost_estimate=pl.CostEstimate(flops=flops, bytes_accessed=moved, transcendentals=0),
    )(*operands)


def shape(dims, dtype):
    return jax.ShapeDtypeStruct(dims, dtype)


def pack_kernel(tokens, cot, land, own, rim, own32, rim32):
    levels, lats, cols, width = tokens.shape
    half = levels * lats * SHIFT
    rim32[2 * half :, :] = jnp.zeros((rim32.shape[0] - 2 * half, width), F32)
    for which, ref in enumerate((tokens, cot)):
        for level in range(levels):
            for lat in range(lats):
                base = which * half + (level * lats + lat) * SHIFT
                line = ref[level, lat].astype(F32)
                rim32[base : base + SHIFT, :] = line[:SHIFT]
                own32[base : base + SHIFT, :] = line[SHIFT:]
    rim32[2 * half : 2 * half + lats, :cols] = land[...].astype(F32)
    own[...] = own32[...].astype(BF16)
    rim[...] = rim32[...].astype(BF16)


def unpack_kernel(own, back, grid):
    levels, lats, cols, width = grid.shape
    came = back[...].astype(F32)
    for level in range(levels):
        for lat in range(lats):
            base = (level * lats + lat) * SHIFT
            grid[level, lat, :SHIFT, :] = came[base : base + SHIFT]
            grid[level, lat, SHIFT:, :] = own[base : base + SHIFT, :]


def land_column(land, rows, first):
    lats, cols = land.shape
    row = lax.broadcasted_iota(jnp.int32, (rows, lats), 0)
    lat = lax.rem(lax.div(row, SHIFT), lats)
    pick = (lat == lax.broadcasted_iota(jnp.int32, (rows, lats), 1)).astype(F32)
    lines = dot(pick.astype(BF16), land.astype(BF16))
    row = lax.broadcasted_iota(jnp.int32, (rows, cols), 0)
    column = lax.broadcasted_iota(jnp.int32, (rows, cols), 1)
    here = column == lax.rem(row, SHIFT) + first
    return jnp.sum(jnp.where(here, lines, 0.0), axis=1, keepdims=True)


def head_masks(dtype, size):
    lane = lax.broadcasted_iota(jnp.int32, (1, GROUP), 1)
    return [
        (lax.div(lane, size) == part).astype(F32).astype(dtype) for part in range(GROUP // size)
    ]


def stacked(block, masks):
    return jnp.concatenate([block * mask for mask in masks], axis=0)


def folded(block, masks):
    rows = block.shape[0] // len(masks)
    return sum(block[i * rows : (i + 1) * rows] * mask for i, mask in enumerate(masks))


def back_through(grad_out, probs, qkv, keys_t, weight_out, grad_proj, size, land):
    count, width = grad_out.shape
    per = GROUP // size
    scale = size ** (-0.5)
    masks_b, masks = head_masks(BF16, size), head_masks(F32, size)
    att_t = dot_last(weight_out[...], grad_out)
    grad_att = att_t.T.astype(BF16)
    att_t = att_t.astype(BF16)
    lane = lax.broadcasted_iota(jnp.int32, (1, GROUP), 1)
    bias_row = jnp.zeros((1, GROUP), F32)
    for group in range(width // GROUP):
        at = group * GROUP
        values = qkv[:, 2 * width + at : 2 * width + at + GROUP]
        grad_probs = dot(stacked(values, masks_b), att_t[at : at + GROUP, :])
        scores_b, probs_b, queries_t = [], [], []
        for part in range(per):
            head = group * per + part
            weights = probs[head * count : (head + 1) * count, :]
            grad_weights = grad_probs[part * count : (part + 1) * count]
            inner = jnp.sum(weights * grad_weights, axis=0, keepdims=True)
            grad_scores = weights * (grad_weights - inner)
            if land is not None:
                on_land = jnp.sum(grad_scores * land, axis=0, keepdims=True)
                on_land = jnp.sum(on_land, axis=1, keepdims=True)
                bias_row = bias_row + jnp.where(lane == head, on_land, 0.0)
            scaled_b = (grad_scores * scale).astype(BF16)
            scores_b.append(scaled_b)
            probs_b.append(weights.astype(BF16))
            queries_t.append(dot(keys_t[head * size : (head + 1) * size, :], scaled_b))
        queries = qkv[:, at : at + GROUP]
        grad_keys = dot(jnp.concatenate(scores_b, axis=0), queries)
        grad_values = dot(jnp.concatenate(probs_b, axis=0), grad_att[:, at : at + GROUP])
        grad_proj[:, at : at + GROUP] = jnp.concatenate(queries_t, axis=0).T.astype(BF16)
        grad_proj[:, width + at : width + at + GROUP] = folded(grad_keys, masks).astype(BF16)
        grad_proj[:, 2 * width + at : 2 * width + at + GROUP] = folded(grad_values, masks).astype(
            BF16
        )
    return bias_row


def through_norm(grad_proj, weight_qkv, gain, normed, inverse):
    scaled = dot_last(grad_proj, weight_qkv[...]) * gain[...]
    mean = jnp.mean(scaled, axis=-1, keepdims=True)
    along = jnp.mean(scaled * normed, axis=-1, keepdims=True)
    return inverse * (scaled - mean - normed * along)


def forward_kernel(
    bias, own, rim, land_own, gain, weight_qkv, weight_out,
    skip, cot, normed_out, inverse_out, normed_t, qkv, keys_t, probs, attended_t, land_out,
    grad_proj, values_t,
):
    width = gain.shape[1]
    heads = bias.shape[1]
    size = width // heads
    half = own.shape[0] // 2
    count = 2 * half
    per = GROUP // size
    scale = size ** (-0.5)
    masks_b = head_masks(BF16, size)
    mine = own[...].astype(F32)
    came = rim[...].astype(F32)
    lats, cols = land_own.shape
    land = jnp.concatenate(
        [
            land_column(land_own[...].astype(F32), half, SHIFT),
            land_column(came[2 * half : 2 * half + lats, :cols], half, 0),
        ],
        axis=0,
    )
    land_out[...] = jnp.broadcast_to(land, land_out.shape)
    values = jnp.concatenate([mine[:half], came[:half]], axis=0)
    centred = values - jnp.mean(values, axis=-1, keepdims=True)
    inverse = lax.rsqrt(jnp.mean(centred * centred, axis=-1, keepdims=True) + EPSILON)
    normed = centred * inverse
    normed_out[...] = normed
    inverse_out[...] = jnp.broadcast_to(inverse, inverse_out.shape)
    normed_b = (normed * gain[...]).astype(BF16)
    normed_t[...] = normed_b.T
    qkv[...] = dot(normed_b, weight_qkv[...]).astype(BF16)
    queries_t = qkv[:, :width].T
    keys_t[...] = qkv[:, width : 2 * width].T
    values_t[...] = qkv[:, 2 * width :].T
    for group in range(width // GROUP):
        at = group * GROUP
        keys = qkv[:, width + at : width + at + GROUP]
        scores = dot(stacked(keys, masks_b), queries_t[at : at + GROUP, :])
        for part in range(per):
            head = group * per + part
            block = scores[part * count : (part + 1) * count] * scale + bias[0, head] * land
            block = jnp.exp(block - jnp.max(block, axis=0, keepdims=True))
            weights = block * (1.0 / jnp.sum(block, axis=0, keepdims=True))
            probs[head * count : (head + 1) * count, :] = weights
            out = dot(values_t[head * size : (head + 1) * size, :], weights.astype(BF16))
            attended_t[head * size : (head + 1) * size, :] = out.astype(BF16)
    grad_out = jnp.concatenate([mine[half:], came[half : 2 * half]], axis=0)
    cot[...] = grad_out.astype(BF16)
    back_through(cot[...], probs, qkv, keys_t, weight_out, grad_proj, size, None)
    skip[...] = (
        through_norm(grad_proj[...], weight_qkv, gain, normed, inverse) + grad_out
    ).astype(BF16)


def backward_kernel(
    core, skip, cot, qkv, keys_t, probs, land, weight_out, normed_t, attended_t,
    total_out, grad_proj, bias_out, give_p, give_q,
    *, heads,
):
    count, width = cot.shape
    total_out[...] = (cot[...].astype(F32) + skip[...].astype(F32)).astype(BF16)
    bias_row = back_through(
        total_out[...], probs, qkv, keys_t, weight_out, grad_proj, width // heads, land[:, :1]
    )
    bias_out[...] = jnp.broadcast_to(bias_row, bias_out.shape)
    half = width // 2
    rows = pl.ds(pl.multiple_of((1 - core[0]) * half, half), half)
    weight_rows(rows, normed_t, attended_t, grad_proj, total_out, bias_row, give_p, give_q)


def weight_rows(rows, normed_t, attended_t, grad_proj, total, bias_row, out_p, out_q):
    width = normed_t.shape[0]
    tokens = normed_t[rows, :]
    out_p[:, : 2 * width] = dot(tokens, grad_proj[:, : 2 * width]).astype(out_p.dtype)
    out_p[:, 2 * width :] = jnp.broadcast_to(bias_row, (out_p.shape[0], GROUP)).astype(out_p.dtype)
    out_q[:, :width] = dot(tokens, grad_proj[:, 2 * width :]).astype(out_q.dtype)
    out_q[:, width:] = dot(attended_t[rows, :], total[...]).astype(out_q.dtype)


def finish_kernel(
    core, total, grad_proj, bias_row, normed_t, attended_t, normed, inverse, weight_qkv, gain,
    keep_p, keep_q, own, back,
):
    count, width = total.shape
    half = width // 2
    rows = pl.ds(pl.multiple_of(core[0] * half, half), half)
    bias_b = bias_row[:1, :].astype(BF16).astype(F32)
    weight_rows(rows, normed_t, attended_t, grad_proj, total, bias_b, keep_p, keep_q)
    final = through_norm(grad_proj[...], weight_qkv, gain, normed[...], inverse[:, :1])
    final = final + total[...].astype(F32)
    own[...] = final[: count // 2]
    back[...] = final[count // 2 :].astype(BF16)


def split_two(block, axis, bit):
    mine = (lax.axis_index(axis) // bit) % 2
    pair = block.reshape(2, block.shape[0] // 2, -1)
    give = lax.dynamic_index_in_dim(pair, 1 - mine, 0, keepdims=False).astype(BF16)
    return give, lax.dynamic_index_in_dim(pair, mine, 0, keepdims=False)


def halved(block, axis, bit):
    give, keep = split_two(block, axis, bit)
    return keep + swapped(give, axis, bit).astype(F32)


def scattered(block, axis):
    count = lax.axis_size(axis)
    mine = lax.axis_index(axis)
    pieces = block.reshape(count, block.shape[0] // count, -1)
    total = lax.dynamic_index_in_dim(pieces, mine, 0, keepdims=False)
    others = []
    for by in range(1, count):
        give = lax.dynamic_index_in_dim(pieces, (mine + by) % count, 0, keepdims=False)
        others.append(from_behind(give.astype(BF16), axis, by))
    for other in others:
        total = total + other.astype(F32)
    return total, others


def doubled(block, axis, bit):
    mine = (lax.axis_index(axis) // bit) % 2
    other = swapped(block, axis, bit)
    low = jnp.where(mine == 0, block, other)
    high = jnp.where(mine == 0, other, block)
    return jnp.concatenate([low, high], axis=0)


def gathered(block, axis):
    count = lax.axis_size(axis)
    mine = lax.axis_index(axis)
    whole = jnp.zeros((count,) + block.shape, block.dtype)
    whole = lax.dynamic_update_index_in_dim(whole, block, mine, 0)
    for by in range(1, count):
        whole = lax.dynamic_update_index_in_dim(
            whole, from_behind(block, axis, by), (mine - by) % count, 0
        )
    return whole.reshape(count * block.shape[0], -1)


def sum_squares(block):
    wide = block.astype(F32)
    return jnp.sum(wide * wide)


def body(inputs, cotangent, land_sea, gains, qkv_weight, out_weight, land_bias):
    tokens, own_cot = inputs[0], cotangent[0]
    weight_qkv, weight_out = qkv_weight[0], out_weight[0]
    levels, lats, cols, width = tokens.shape
    heads = land_bias.shape[1]
    half = levels * lats * SHIFT
    count = 2 * half
    packed = half * 2 + 16

    own, rim = call(
        pack_kernel,
        [shape((2 * half, width), BF16), shape((packed, width), BF16)],
        scratch=[pltpu.VMEM((2 * half, width), F32), pltpu.VMEM((packed, width), F32)],
        operands=(tokens, own_cot, land_sea),
    )
    rim = from_behind(rim, "lon", -1)
    skip, cot, normed, inverse, normed_t, qkv, keys_t, probs, attended_t, land = call(
        forward_kernel,
        [
            shape((count, width), BF16),
            shape((count, width), BF16),
            shape((count, width), F32),
            shape((count, GROUP), F32),
            shape((width, count), BF16),
            shape((count, 3 * width), BF16),
            shape((width, count), BF16),
            shape((heads * count, count), F32),
            shape((width, count), BF16),
            shape((count, GROUP), F32),
        ],
        scratch=[pltpu.VMEM((count, 3 * width), BF16), pltpu.VMEM((width, count), BF16)],
        smem=(0,),
        operands=(land_bias, own, rim, land_sea, gains, weight_qkv, weight_out),
        flops=10**9,
    )
    skip = passed_along(skip, "section", -1)
    lat, lon = lax.axis_index("lat"), lax.axis_index("lon")
    core = (lat % 2).astype(jnp.int32).reshape(1)
    total, grad_proj, bias_row, give_p, give_q = call(
        functools.partial(backward_kernel, heads=heads),
        [
            shape((count, width), BF16),
            shape((count, 3 * width), BF16),
            shape((8, GROUP), F32),
            shape((width // 2, 2 * width + GROUP), BF16),
            shape((width // 2, 2 * width), BF16),
        ],
        smem=(0,),
        operands=(core, skip, cot, qkv, keys_t, probs, land, weight_out, normed_t, attended_t),
        flops=10**9,
    )
    came_p = swapped(give_p, "lat", 1)
    came_q = swapped(give_q, "lat", 1)
    keep_p, keep_q, own_grad, back = call(
        finish_kernel,
        [
            shape((width // 2, 2 * width + GROUP), F32),
            shape((width // 2, 2 * width), F32),
            shape((half, width), F32),
            shape((half, width), BF16),
        ],
        smem=(0,),
        operands=(
            core, total, grad_proj, bias_row, normed_t, attended_t, normed, inverse,
            weight_qkv, gains,
        ),
        flops=5 * 10**8,
    )
    back = from_behind(back, "lon", 1)
    (final_grad,) = call(
        unpack_kernel, [shape(tokens.shape, F32)], operands=(own_grad, back)
    )

    part_p = keep_p + came_p.astype(F32)
    part_q = keep_q + came_q.astype(F32)
    give, keep = split_two(part_p, "lat", 2)
    came = swapped(give, "lat", 2).astype(F32)
    is_bias = lax.broadcasted_iota(jnp.int32, keep.shape, 1) >= 2 * width
    part_p = jnp.where(is_bias, lax.reduce_precision(keep, 8, 7), keep) + came
    bias_part = lax.reduce_precision(part_p[:1, 2 * width :], 8, 7)
    part_p, others = scattered(part_p, "lon")
    bias_parts = [bias_part] + [other[:1, 2 * width :].astype(F32) for other in others]
    bias_parts = jnp.concatenate(bias_parts[:1] + bias_parts[:0:-1], axis=0)
    grad_bias = jnp.sum(jnp.roll(bias_parts, lon, axis=0), axis=0)[:heads]
    part_q = halved(scattered(part_q, "lon")[0], "lat", 2)
    part_p = part_p[:, : 2 * width].astype(BF16)
    part_q = part_q.astype(BF16)
    half_p = doubled(gathered(part_p, "lon"), "lat", 2)
    half_q = gathered(doubled(part_q, "lat", 2), "lon")

    mine = lat % 2
    weight_half = lax.dynamic_slice_in_dim(weight_qkv, mine * (width // 2), width // 2, 0)
    gain_half = lax.dynamic_slice_in_dim(gains[0], mine * (width // 2), width // 2, 0)
    weight_half = weight_half.astype(F32)
    gain_half = (
        jnp.sum(half_p.astype(F32) * weight_half[:, : 2 * width], axis=1)
        + jnp.sum(half_q[:, :width].astype(F32) * weight_half[:, 2 * width :], axis=1)
    ) / gain_half
    square = sum_squares(half_p) + sum_squares(half_q) + sum_squares(gain_half)
    square = square + 0.5 * sum_squares(grad_bias)
    row = jnp.concatenate([gain_half, square.reshape(1), jnp.zeros((127,), F32)])
    row = row.reshape(1, -1)
    sections, lats_on = lax.axis_size("section"), lax.axis_size("lat")
    pairs = [
        (s * lats_on + i, (sections - 1 - s) * lats_on + (i ^ 1))
        for s in range(sections) for i in range(lats_on)
    ]
    row_other = swapped(row, "lat", 1)
    square = square + row_other[0, width // 2]
    square = square + (
        swapped(row[:, width // 2 :], "section", 1)[0, 0]
        + lax.ppermute(row[:, width // 2 :], ("section", "lat"), pairs)[0, 0]
    )
    entries = 2 * (4 * width * width + width + heads)
    factor = jnp.minimum(1.0, lax.rsqrt(square / entries + 1e-06))
    gain_other = row_other[0, : width // 2]
    grad_gain = jnp.concatenate(
        [
            jnp.where(mine == 0, gain_half, gain_other),
            jnp.where(mine == 0, gain_other, gain_half),
        ]
    )
    all_p = doubled(half_p, "lat", 1).astype(F32) * factor
    all_q = doubled(half_q, "lat", 1).astype(F32) * factor
    grad_qkv = jnp.concatenate([all_p, all_q[:, :width]], axis=1)
    grad_out = all_q[:, width:]
    return (
        final_grad[None],
        grad_qkv[None],
        grad_out[None],
        (grad_gain * factor)[None],
        (grad_bias * factor)[None],
    )


def solution(mesh):
    placed = (
        P("section", None, "lat", "lon", None),
        P("section", None, "lat", "lon", None),
        P("lat", "lon"),
        P("section", None),
        P("section", None, None),
        P("section", None, None),
        P("section", None),
    )
    return jax.shard_map(
        body,
        mesh=mesh,
        in_specs=placed,
        out_specs=(
            P("section", None, "lat", "lon", None),
            P("section", None, None),
            P("section", None, None),
            P("section", None),
            P("section", None),
        ),
        check_vma=False,
    )
```

```python
import functools

import jax
import jax.numpy as jnp
from jax import lax
from jax.experimental import pallas as pl
from jax.experimental.pallas import tpu as pltpu
from jax.sharding import PartitionSpec as P

SHIFT = 6
GROUP = 128
CUT = 1280
EPSILON = 1e-05
F32 = jnp.float32
BF16 = jnp.bfloat16


def from_behind(value, axis, by):
    count = lax.axis_size(axis)
    return lax.ppermute(value, axis, [(i, (i + by) % count) for i in range(count)])


def passed_along(block, axis, distance):
    devices = range(lax.axis_size(axis))
    route = [(i - distance, i) for i in devices if i - distance in devices]
    return lax.ppermute(block, axis, route)


def swapped(value, axis, bit):
    count = lax.axis_size(axis)
    return lax.ppermute(value, axis, [(i, i ^ bit) for i in range(count)])


def dot(left, right):
    return jnp.dot(left, right, preferred_element_type=F32)


def dot_last(left, right):
    return lax.dot_general(left, right, (((1,), (1,)), ((), ())), preferred_element_type=F32)


def call(kernel, outs, scratch=(), smem=(), operands=(), flops=10**8, limit=12):
    moved = sum(o.size * o.dtype.itemsize for o in list(outs) + list(operands))
    return pl.pallas_call(
        kernel,
        out_shape=list(outs),
        in_specs=[
            pl.BlockSpec(memory_space=pltpu.SMEM if i in smem else pltpu.VMEM)
            for i in range(len(operands))
        ],
        out_specs=[pl.BlockSpec(memory_space=pltpu.VMEM) for _ in outs],
        scratch_shapes=list(scratch),
        compiler_params=pltpu.CompilerParams(vmem_limit_bytes=limit * 2**20),
        cost_estimate=pl.CostEstimate(flops=flops, bytes_accessed=moved, transcendentals=0),
    )(*operands)


def shape(dims, dtype):
    return jax.ShapeDtypeStruct(dims, dtype)


def aligned(start, size):
    return pl.ds(pl.multiple_of(start, size), size)


def pack_kernel(tokens, cot, land, own, rim, own32, rim32):
    levels, lats, cols, width = tokens.shape[1:]
    half = levels * lats * SHIFT
    rim32[2 * half :, :] = jnp.zeros((rim32.shape[0] - 2 * half, width), F32)
    for which, ref in enumerate((tokens, cot)):
        for level in range(levels):
            for lat in range(lats):
                base = which * half + (level * lats + lat) * SHIFT
                line = ref[0, level, lat].astype(F32)
                rim32[base : base + SHIFT, :] = line[:SHIFT]
                own32[base : base + SHIFT, :] = line[SHIFT:]
    rim32[2 * half : 2 * half + lats, :cols] = land[...].astype(F32)
    own[...] = own32[...].astype(BF16)
    rim[...] = rim32[...].astype(BF16)


def unpack_kernel(own, back, grid):
    levels, lats, cols, width = grid.shape[1:]
    came = back[...].astype(F32)
    for level in range(levels):
        for lat in range(lats):
            base = (level * lats + lat) * SHIFT
            grid[0, level, lat, :SHIFT, :] = came[base : base + SHIFT]
            grid[0, level, lat, SHIFT:, :] = own[base : base + SHIFT, :]


def land_column(land, rows, first):
    lats, cols = land.shape
    row = lax.broadcasted_iota(jnp.int32, (rows, lats), 0)
    lat = lax.rem(lax.div(row, SHIFT), lats)
    pick = (lat == lax.broadcasted_iota(jnp.int32, (rows, lats), 1)).astype(F32)
    lines = dot(pick.astype(BF16), land.astype(BF16))
    row = lax.broadcasted_iota(jnp.int32, (rows, cols), 0)
    column = lax.broadcasted_iota(jnp.int32, (rows, cols), 1)
    here = column == lax.rem(row, SHIFT) + first
    return jnp.sum(jnp.where(here, lines, 0.0), axis=1, keepdims=True)


def head_masks(dtype, size):
    lane = lax.broadcasted_iota(jnp.int32, (1, GROUP), 1)
    return [
        (lax.div(lane, size) == part).astype(F32).astype(dtype) for part in range(GROUP // size)
    ]


def stacked(block, masks):
    return jnp.concatenate([block * mask for mask in masks], axis=0)


def folded(block, masks):
    rows = block.shape[0] // len(masks)
    return sum(block[i * rows : (i + 1) * rows] * mask for i, mask in enumerate(masks))


def back_through(grad_out, probs, qkv, keys_t, weight_out, grad_proj, size, land):
    count, width = grad_out.shape
    per = GROUP // size
    scale = size ** (-0.5)
    masks_b, masks = head_masks(BF16, size), head_masks(F32, size)
    att_t = dot_last(weight_out[...], grad_out)
    grad_att = att_t.T.astype(BF16)
    att_t = att_t.astype(BF16)
    lane = lax.broadcasted_iota(jnp.int32, (1, GROUP), 1)
    bias_row = jnp.zeros((1, GROUP), F32)
    for group in range(width // GROUP):
        at = group * GROUP
        values = qkv[:, 2 * width + at : 2 * width + at + GROUP]
        grad_probs = dot(stacked(values, masks_b), att_t[at : at + GROUP, :])
        scores_b, probs_b, queries_t = [], [], []
        for part in range(per):
            head = group * per + part
            weights = probs[head * count : (head + 1) * count, :]
            grad_weights = grad_probs[part * count : (part + 1) * count]
            inner = jnp.sum(weights * grad_weights, axis=0, keepdims=True)
            grad_scores = weights * (grad_weights - inner)
            if land is not None:
                on_land = jnp.sum(grad_scores * land, axis=0, keepdims=True)
                on_land = jnp.sum(on_land, axis=1, keepdims=True)
                bias_row = bias_row + jnp.where(lane == head, on_land, 0.0)
            scaled_b = (grad_scores * scale).astype(BF16)
            scores_b.append(scaled_b)
            probs_b.append(weights.astype(BF16))
            queries_t.append(dot(keys_t[head * size : (head + 1) * size, :], scaled_b))
        queries = qkv[:, at : at + GROUP]
        grad_keys = dot(jnp.concatenate(scores_b, axis=0), queries)
        grad_values = dot(jnp.concatenate(probs_b, axis=0), grad_att[:, at : at + GROUP])
        grad_proj[:, at : at + GROUP] = jnp.concatenate(queries_t, axis=0).T.astype(BF16)
        grad_proj[:, width + at : width + at + GROUP] = folded(grad_keys, masks).astype(BF16)
        grad_proj[:, 2 * width + at : 2 * width + at + GROUP] = folded(grad_values, masks).astype(
            BF16
        )
    return bias_row


def through_norm(grad_proj, weight_qkv, gain, normed, inverse):
    scaled = dot_last(grad_proj, weight_qkv[...]) * gain[...]
    mean = jnp.mean(scaled, axis=-1, keepdims=True)
    along = jnp.mean(scaled * normed, axis=-1, keepdims=True)
    return inverse * (scaled - mean - normed * along)


def forward_kernel(
    bias, own, rim, land_own, gain, weight_qkv, weight_out,
    skip, cot, normed_out, inverse_out, normed_t, qkv, keys_t, probs, attended_t, land_out,
    grad_proj, values_t,
):
    width = gain.shape[1]
    heads = bias.shape[1]
    size = width // heads
    half = own.shape[0] // 2
    count = 2 * half
    per = GROUP // size
    scale = size ** (-0.5)
    masks_b = head_masks(BF16, size)
    mine = own[...].astype(F32)
    came = rim[...].astype(F32)
    lats, cols = land_own.shape
    land = jnp.concatenate(
        [
            land_column(land_own[...].astype(F32), half, SHIFT),
            land_column(came[2 * half : 2 * half + lats, :cols], half, 0),
        ],
        axis=0,
    )
    land_out[...] = jnp.broadcast_to(land, land_out.shape)
    values = jnp.concatenate([mine[:half], came[:half]], axis=0)
    centred = values - jnp.mean(values, axis=-1, keepdims=True)
    inverse = lax.rsqrt(jnp.mean(centred * centred, axis=-1, keepdims=True) + EPSILON)
    normed = centred * inverse
    normed_out[...] = normed
    inverse_out[...] = jnp.broadcast_to(inverse, inverse_out.shape)
    normed_b = (normed * gain[...]).astype(BF16)
    normed_t[...] = normed_b.T
    qkv[...] = dot(normed_b, weight_qkv[...]).astype(BF16)
    queries_t = qkv[:, :width].T
    keys_t[...] = qkv[:, width : 2 * width].T
    values_t[...] = qkv[:, 2 * width :].T
    for group in range(width // GROUP):
        at = group * GROUP
        keys = qkv[:, width + at : width + at + GROUP]
        scores = dot(stacked(keys, masks_b), queries_t[at : at + GROUP, :])
        for part in range(per):
            head = group * per + part
            block = scores[part * count : (part + 1) * count] * scale + bias[0, head] * land
            block = jnp.exp(block - jnp.max(block, axis=0, keepdims=True))
            weights = block * (1.0 / jnp.sum(block, axis=0, keepdims=True))
            probs[head * count : (head + 1) * count, :] = weights
            out = dot(values_t[head * size : (head + 1) * size, :], weights.astype(BF16))
            attended_t[head * size : (head + 1) * size, :] = out.astype(BF16)
    grad_out = jnp.concatenate([mine[half:], came[half : 2 * half]], axis=0)
    cot[...] = grad_out.astype(BF16)
    back_through(cot[...], probs, qkv, keys_t, weight_out, grad_proj, size, None)
    skip[...] = (
        through_norm(grad_proj[...], weight_qkv, gain, normed, inverse) + grad_out
    ).astype(BF16)


def backward_kernel(
    core, skip, cot, qkv, keys_t, probs, land, weight_out, normed_t, attended_t,
    total_out, grad_proj, bias_out, give,
    *, heads,
):
    count, width = cot.shape
    total_out[...] = (cot[...].astype(F32) + skip[...].astype(F32)).astype(BF16)
    bias_row = back_through(
        total_out[...], probs, qkv, keys_t, weight_out, grad_proj, width // heads, land[:, :1]
    )
    bias_out[...] = jnp.broadcast_to(bias_row, bias_out.shape)
    half = width // 2
    rows = aligned((1 - core[0]) * half, half)
    weight_rows(rows, normed_t, attended_t, grad_proj, total_out, bias_row, give)


def weight_rows(rows, normed_t, attended_t, grad_proj, total, bias_row, out):
    tokens = normed_t[rows, :]
    three = grad_proj.shape[1]
    out[:, :CUT] = dot(tokens, grad_proj[:, :CUT]).astype(out.dtype)
    out[:, CUT : CUT + GROUP] = jnp.broadcast_to(bias_row, (out.shape[0], GROUP)).astype(out.dtype)
    out[:, CUT + GROUP : three + GROUP] = dot(tokens, grad_proj[:, CUT:]).astype(out.dtype)
    out[:, three + GROUP :] = dot(attended_t[rows, :], total[...]).astype(out.dtype)


def finish_kernel(
    core, total, grad_proj, bias_row, normed_t, attended_t, normed, inverse, weight_qkv, gain,
    keep, own, back,
):
    count, width = total.shape
    half = width // 2
    rows = aligned(core[0] * half, half)
    bias_b = bias_row[:1, :].astype(BF16).astype(F32)
    weight_rows(rows, normed_t, attended_t, grad_proj, total, bias_b, keep)
    final = through_norm(grad_proj[...], weight_qkv, gain, normed[...], inverse[:, :1])
    final = final + total[...].astype(F32)
    own[...] = final[: count // 2]
    back[...] = final[count // 2 :].astype(BF16)


def first_kernel(place, keep, came, give_p, kept_p, kept_q, *rest):
    *give_q, total = rest
    wide_p = give_p.shape[1]
    half = keep.shape[0] // 2
    total[...] = keep[...] + came[...].astype(F32)
    give_p[...] = total[aligned((1 - place[1]) * half, half), :wide_p].astype(BF16)
    mine = aligned(place[1] * half, half)
    kept_p[:, :CUT] = total[mine, :CUT]
    kept_p[:, CUT:] = total[mine, CUT:wide_p].astype(BF16).astype(F32)
    piece, count = kept_q.shape[0], len(give_q) + 1
    kept_q[...] = total[aligned(place[2] * piece, piece), wide_p:]
    for by, give in enumerate(give_q, 1):
        owner = lax.rem(place[2] + by, count)
        give[...] = total[aligned(owner * piece, piece), wide_p:].astype(BF16)


def second_kernel(place, kept_p, came_p, kept_q, *rest):
    count = (len(rest) - 5) // 2 + 1
    came_q, (give_q, left_q, left_p), rest = rest[: count - 1], rest[count - 1 : count + 2], rest[count + 2 :]
    *give_p, total_p, total_q = rest
    total_p[...] = kept_p[...] + came_p[...].astype(F32)
    piece = left_p.shape[0]
    mine = aligned(place[2] * piece, piece)
    left_p[:, :CUT] = total_p[mine, :CUT]
    left_p[:, CUT:] = total_p[mine, CUT:].astype(BF16).astype(F32)
    for by, give in enumerate(give_p, 1):
        owner = lax.rem(place[2] + by, count)
        give[...] = total_p[aligned(owner * piece, piece), :].astype(BF16)
    total = kept_q[...]
    for came in came_q:
        total = total + came[...].astype(F32)
    total_q[...] = total
    half = give_q.shape[0]
    give_q[...] = total_q[aligned((1 - place[1]) * half, half), :].astype(BF16)
    left_q[...] = total_q[aligned(place[1] * half, half), :]


def third_kernel(place, left_p, left_q, came_q, *rest):
    *came_p, piece_p, piece_q, bias = rest
    count = len(came_p) + 1
    total = left_p[:, :CUT]
    for came in came_p:
        total = total + came[:, :CUT].astype(F32)
    piece_p[...] = total.astype(BF16)
    piece_q[...] = (left_q[...] + came_q[...].astype(F32)).astype(BF16)
    terms = [left_p[:8, CUT:]] + [came[...].astype(F32)[:8, CUT:] for came in came_p]
    total = jnp.zeros_like(terms[0])
    for source in range(count):
        for by, term in enumerate(terms):
            here = lax.rem(place[2] - by + count, count) == source
            total = total + jnp.where(here, term, 0.0)
    bias[...] = total


def fourth_kernel(place, piece_p, piece_q, other_q, *rest):
    *others_p, block_p, block_q = rest
    count = len(others_p) + 1
    piece = piece_p.shape[0]
    for by, part in enumerate((piece_p, *others_p)):
        source = lax.rem(place[2] - by + count, count)
        block_p[aligned(source * piece, piece), :] = part[...]
    piece = piece_q.shape[0]
    block_q[aligned(place[1] * piece, piece), :] = piece_q[...]
    block_q[aligned((1 - place[1]) * piece, piece), :] = other_q[...]


def fifth_kernel(place, weight_qkv, gain, bias, block_p, other_p, block_q, *rest):
    *others_q, half, row = rest
    count = len(others_q) + 1
    rows, width = half.shape[0], weight_qkv.shape[0]
    piece = block_p.shape[0]
    half[aligned(place[1] * piece, piece), :CUT] = block_p[...]
    half[aligned((1 - place[1]) * piece, piece), :CUT] = other_p[...]
    piece = block_q.shape[0]
    for by, part in enumerate((block_q, *others_q)):
        source = lax.rem(place[2] - by + count, count)
        half[aligned(source * piece, piece), CUT:] = part[...]
    three = weight_qkv.shape[1]
    wide = half[:, :three].astype(F32)
    mine = aligned(place[0] * rows, rows)
    gain_half = jnp.sum(wide * weight_qkv[mine, :].astype(F32), axis=1, keepdims=True)
    gain_half = jnp.broadcast_to(gain_half, (rows, GROUP)).T[:8]
    core = place[0].astype(F32)
    own_gain = gain[:, :rows] * (1.0 - core) + gain[:, rows:] * core
    gain_half = gain_half / own_gain
    out = half[:, three:].astype(F32)
    square = jnp.sum(jnp.sum(wide * wide, axis=0, keepdims=True), axis=1, keepdims=True)
    square = square + jnp.sum(jnp.sum(out * out, axis=0, keepdims=True), axis=1, keepdims=True)
    square = square + jnp.sum(gain_half[:1] * gain_half[:1], axis=1, keepdims=True)
    square = square + 0.5 * jnp.sum(bias[:1, :] * bias[:1, :], axis=1, keepdims=True)
    row[:, :rows] = gain_half
    row[:, rows:] = jnp.broadcast_to(square, (8, GROUP))


def last_kernel(
    place, half, other, row, row_core, row_section, row_both, bias,
    grad_qkv, grad_out, grad_gain, grad_bias,
    *, entries,
):
    rows, three = half.shape[0], grad_qkv.shape[1]
    square = row[:1, rows : rows + 1] + row_core[:1, rows : rows + 1]
    square = square + (row_section[:1, rows : rows + 1] + row_both[:1, rows : rows + 1])
    factor = jnp.minimum(1.0, lax.rsqrt(square / entries + 1e-06))
    step = pl.program_id(0)
    piece = grad_qkv.shape[0]
    per = rows // piece
    at = aligned(lax.rem(step, per) * piece, piece)
    own = lax.div(step, per) == place[0]

    @pl.when(own)
    def _():
        grad_qkv[...] = half[at, :three].astype(F32) * factor
        grad_out[...] = half[at, three:].astype(F32) * factor

    @pl.when(jnp.logical_not(own))
    def _():
        grad_qkv[...] = other[at, :three].astype(F32) * factor
        grad_out[...] = other[at, three:].astype(F32) * factor

    core = place[0].astype(F32)
    mine, its = row[:1, :rows] * factor, row_core[:1, :rows] * factor
    grad_gain[:, :rows] = mine * (1.0 - core) + its * core
    grad_gain[:, rows:] = mine * core + its * (1.0 - core)
    grad_bias[...] = bias[:1, : grad_bias.shape[1]] * factor


def pieces_sent(pieces, axis):
    return [from_behind(piece, axis, by) for by, piece in enumerate(pieces, 1)]


def body(inputs, cotangent, land_sea, gains, qkv_weight, out_weight, land_bias):
    weight_qkv, weight_out = qkv_weight[0], out_weight[0]
    levels, lats, cols, width = inputs.shape[1:]
    heads = land_bias.shape[1]
    half = levels * lats * SHIFT
    count = 2 * half
    packed = half * 2 + 16
    lons = lax.axis_size("lon")
    lat, lon = lax.axis_index("lat"), lax.axis_index("lon")
    place = jnp.stack([lat % 2, lat // 2, lon]).astype(jnp.int32)

    own, rim = call(
        pack_kernel,
        [shape((2 * half, width), BF16), shape((packed, width), BF16)],
        scratch=[pltpu.VMEM((2 * half, width), F32), pltpu.VMEM((packed, width), F32)],
        operands=(inputs, cotangent, land_sea),
    )
    rim = from_behind(rim, "lon", -1)
    skip, cot, normed, inverse, normed_t, qkv, keys_t, probs, attended_t, land = call(
        forward_kernel,
        [
            shape((count, width), BF16),
            shape((count, width), BF16),
            shape((count, width), F32),
            shape((count, GROUP), F32),
            shape((width, count), BF16),
            shape((count, 3 * width), BF16),
            shape((width, count), BF16),
            shape((heads * count, count), F32),
            shape((width, count), BF16),
            shape((count, GROUP), F32),
        ],
        scratch=[pltpu.VMEM((count, 3 * width), BF16), pltpu.VMEM((width, count), BF16)],
        smem=(0,),
        operands=(land_bias, own, rim, land_sea, gains, weight_qkv, weight_out),
        flops=10**9,
    )
    skip = passed_along(skip, "section", -1)
    rows, wide = width // 2, 4 * width + GROUP
    total, grad_proj, bias_row, give = call(
        functools.partial(backward_kernel, heads=heads),
        [
            shape((count, width), BF16),
            shape((count, 3 * width), BF16),
            shape((8, GROUP), F32),
            shape((rows, wide), BF16),
        ],
        smem=(0,),
        operands=(place, skip, cot, qkv, keys_t, probs, land, weight_out, normed_t, attended_t),
        flops=10**9,
    )
    came = swapped(give, "lat", 1)
    keep, own_grad, back = call(
        finish_kernel,
        [
            shape((rows, wide), F32),
            shape((half, width), F32),
            shape((half, width), BF16),
        ],
        smem=(0,),
        operands=(
            place, total, grad_proj, bias_row, normed_t, attended_t, normed, inverse,
            weight_qkv, gains,
        ),
        flops=5 * 10**8,
    )
    back = from_behind(back, "lon", 1)
    entries = 2 * (4 * width * width + width + heads)
    if rows // 2 // lons % 16 == 0:
        grads, mark = staged(place, keep, came, weight_qkv, gains, lons, heads, entries)
    else:
        grads, mark = plain(keep, came, weight_qkv, gains, heads, entries)
    own_grad, back, _ = lax.optimization_barrier((own_grad, back, mark))
    (final_grad,) = call(
        unpack_kernel, [shape(inputs.shape, F32)], operands=(own_grad, back)
    )
    return (final_grad, *(grad[None] for grad in grads))


def staged(place, keep, came, weight_qkv, gains, lons, heads, entries):
    rows, wide = keep.shape
    width = 2 * rows
    wide_p = CUT + GROUP
    wide_q = wide - wide_p
    some = range(lons - 1)
    give_p, kept_p, kept_q, *give_q = call(
        first_kernel,
        [
            shape((rows // 2, wide_p), BF16),
            shape((rows // 2, wide_p), F32),
            shape((rows // lons, wide_q), F32),
            *(shape((rows // lons, wide_q), BF16) for _ in some),
        ],
        scratch=[pltpu.VMEM((rows, wide), F32)],
        smem=(0,),
        operands=(place, keep, came),
    )
    came_p = swapped(give_p, "lat", 2)
    came_q = pieces_sent(give_q, "lon")
    piece = rows // 2 // lons
    give_q, left_q, left_p, *give_p = call(
        second_kernel,
        [
            shape((piece, wide_q), BF16),
            shape((piece, wide_q), F32),
            shape((piece, wide_p), F32),
            *(shape((piece, wide_p), BF16) for _ in some),
        ],
        scratch=[pltpu.VMEM((rows // 2, wide_p), F32), pltpu.VMEM((rows // lons, wide_q), F32)],
        smem=(0,),
        operands=(place, kept_p, came_p, kept_q, *came_q),
    )
    came_p = pieces_sent(give_p, "lon")
    came_q = swapped(give_q, "lat", 2)
    piece_p, piece_q, bias = call(
        third_kernel,
        [
            shape((piece, CUT), BF16),
            shape((piece, wide_q), BF16),
            shape((8, GROUP), F32),
        ],
        smem=(0,),
        operands=(place, left_p, left_q, came_q, *came_p),
    )
    others_p = pieces_sent([piece_p for _ in some], "lon")
    other_q = swapped(piece_q, "lat", 2)
    block_p, block_q = call(
        fourth_kernel,
        [shape((rows // 2, CUT), BF16), shape((rows // lons, wide_q), BF16)],
        smem=(0,),
        operands=(place, piece_p, piece_q, other_q, *others_p),
    )
    other_p = swapped(block_p, "lat", 2)
    others_q = pieces_sent([block_q for _ in some], "lon")
    half, row = call(
        fifth_kernel,
        [shape((rows, 4 * width), BF16), shape((8, rows + GROUP), F32)],
        smem=(0,),
        operands=(place, weight_qkv, gains, bias, block_p, other_p, block_q, *others_q),
    )
    row_section = swapped(row, "section", 1)
    row_both = lax.ppermute(row, ("section", "lat"), across())
    row_core = swapped(row, "lat", 1)
    other = swapped(half, "lat", 1)
    steps = 8
    vmem = pl.BlockSpec(memory_space=pltpu.VMEM)
    grads = pl.pallas_call(
        functools.partial(last_kernel, entries=entries),
        grid=(steps,),
        out_shape=[
            shape((width, 3 * width), F32),
            shape((width, width), F32),
            shape((1, width), F32),
            shape((1, heads), F32),
        ],
        in_specs=[pl.BlockSpec(memory_space=pltpu.SMEM)] + [vmem] * 7,
        out_specs=[
            pl.BlockSpec((width // steps, 3 * width), lambda i: (i, 0)),
            pl.BlockSpec((width // steps, width), lambda i: (i, 0)),
            pl.BlockSpec((1, width), lambda i: (0, 0)),
            pl.BlockSpec((1, heads), lambda i: (0, 0)),
        ],
        compiler_params=pltpu.CompilerParams(vmem_limit_bytes=12 * 2**20),
    )(place, half, other, row, row_core, row_section, row_both, bias)
    return (grads[0], grads[1], grads[2][0], grads[3][0]), bias


def across():
    sections, lats = lax.axis_size("section"), lax.axis_size("lat")
    return [
        (s * lats + i, (sections - 1 - s) * lats + (i ^ 1))
        for s in range(sections)
        for i in range(lats)
    ]


def split_two(block, axis, bit):
    mine = (lax.axis_index(axis) // bit) % 2
    pair = block.reshape(2, block.shape[0] // 2, -1)
    give = lax.dynamic_index_in_dim(pair, 1 - mine, 0, keepdims=False).astype(BF16)
    return give, lax.dynamic_index_in_dim(pair, mine, 0, keepdims=False)


def doubled(block, axis, bit):
    mine = (lax.axis_index(axis) // bit) % 2
    other = swapped(block, axis, bit)
    low = jnp.where(mine == 0, block, other)
    high = jnp.where(mine == 0, other, block)
    return jnp.concatenate([low, high], axis=0)


def scattered(block, axis):
    count = lax.axis_size(axis)
    mine = lax.axis_index(axis)
    pieces = block.reshape(count, block.shape[0] // count, -1)
    total = lax.dynamic_index_in_dim(pieces, mine, 0, keepdims=False)
    others = []
    for by in range(1, count):
        give = lax.dynamic_index_in_dim(pieces, (mine + by) % count, 0, keepdims=False)
        others.append(from_behind(give.astype(BF16), axis, by))
    for other in others:
        total = total + other.astype(F32)
    return total, others


def gathered(block, axis):
    count = lax.axis_size(axis)
    mine = lax.axis_index(axis)
    whole = jnp.zeros((count,) + block.shape, block.dtype)
    whole = lax.dynamic_update_index_in_dim(whole, block, mine, 0)
    for by in range(1, count):
        whole = lax.dynamic_update_index_in_dim(
            whole, from_behind(block, axis, by), (mine - by) % count, 0
        )
    return whole.reshape(count * block.shape[0], -1)


def sum_squares(block):
    wide = block.astype(F32)
    return jnp.sum(wide * wide)


def plain(keep, came, weight_qkv, gains, heads, entries):
    width = gains.shape[1]
    lat, lon = lax.axis_index("lat"), lax.axis_index("lon")
    part = keep + came.astype(F32)
    give, keep = split_two(part, "lat", 2)
    came = swapped(give, "lat", 2).astype(F32)
    column = lax.broadcasted_iota(jnp.int32, keep.shape, 1)
    is_bias = (column >= CUT) & (column < CUT + GROUP)
    part = jnp.where(is_bias, lax.reduce_precision(keep, 8, 7), keep) + came
    bias_part = lax.reduce_precision(part[:1, CUT : CUT + GROUP], 8, 7)
    part, others = scattered(part, "lon")
    terms = [bias_part] + [other[:1, CUT : CUT + GROUP].astype(F32) for other in others]
    terms = jnp.concatenate(terms[:1] + terms[:0:-1], axis=0)
    bias = jnp.sum(jnp.roll(terms, lon, axis=0), axis=0)[:heads]
    part = jnp.concatenate([part[:, :CUT], part[:, CUT + GROUP :]], axis=1).astype(BF16)
    half = doubled(gathered(part, "lon"), "lat", 2)
    mine = lat % 2
    weight_half = lax.dynamic_slice_in_dim(weight_qkv, mine * (width // 2), width // 2, 0)
    gain_half = lax.dynamic_slice_in_dim(gains[0], mine * (width // 2), width // 2, 0)
    weighed = half[:, : 3 * width].astype(F32) * weight_half.astype(F32)
    gain_half = jnp.sum(weighed, axis=1) / gain_half
    square = sum_squares(half) + sum_squares(gain_half) + 0.5 * sum_squares(bias)
    square = square.reshape(1)
    square = square + swapped(square, "lat", 1)
    square = square + swapped(square, "section", 1)
    factor = jnp.minimum(1.0, lax.rsqrt(square[0] / entries + 1e-06))
    grads = doubled(half, "lat", 1).astype(F32) * factor
    gain = doubled(gain_half.reshape(-1, 1), "lat", 1)[:, 0] * factor
    return (grads[:, : 3 * width], grads[:, 3 * width :], gain, bias * factor), bias


def solution(mesh):
    placed = (
        P("section", None, "lat", "lon", None),
        P("section", None, "lat", "lon", None),
        P("lat", "lon"),
        P("section", None),
        P("section", None, None),
        P("section", None, None),
        P("section", None),
    )
    return jax.shard_map(
        body,
        mesh=mesh,
        in_specs=placed,
        out_specs=(
            P("section", None, "lat", "lon", None),
            P("section", None, None),
            P("section", None, None),
            P("section", None),
            P("section", None),
        ),
        check_vma=False,
    )
```

```python
import functools

import jax
import jax.numpy as jnp
from jax import lax
from jax.experimental import pallas as pl
from jax.experimental.pallas import tpu as pltpu
from jax.sharding import PartitionSpec as P

SHIFT = 6
GROUP = 128
CUT = 1280
EPSILON = 1e-05
F32 = jnp.float32
BF16 = jnp.bfloat16


def from_behind(value, axis, by):
    count = lax.axis_size(axis)
    return lax.ppermute(value, axis, [(i, (i + by) % count) for i in range(count)])


def passed_along(block, axis, distance):
    devices = range(lax.axis_size(axis))
    route = [(i - distance, i) for i in devices if i - distance in devices]
    return lax.ppermute(block, axis, route)


def swapped(value, axis, bit):
    count = lax.axis_size(axis)
    return lax.ppermute(value, axis, [(i, i ^ bit) for i in range(count)])


def dot(left, right):
    return jnp.dot(left, right, preferred_element_type=F32)


def dot_last(left, right):
    return lax.dot_general(left, right, (((1,), (1,)), ((), ())), preferred_element_type=F32)


def call(kernel, outs, scratch=(), places="", out_places="", operands=(), flops=10**8, limit=12):
    spaces = {"v": pltpu.VMEM, "s": pltpu.SMEM, "a": pl.ANY}
    places = places or "v" * len(operands)
    out_places = out_places or "v" * len(outs)
    moved = sum(o.size * o.dtype.itemsize for o in list(outs) + list(operands))
    return pl.pallas_call(
        kernel,
        out_shape=list(outs),
        in_specs=[pl.BlockSpec(memory_space=spaces[letter]) for letter in places],
        out_specs=[pl.BlockSpec(memory_space=spaces[letter]) for letter in out_places],
        scratch_shapes=list(scratch),
        compiler_params=pltpu.CompilerParams(vmem_limit_bytes=limit * 2**20),
        cost_estimate=pl.CostEstimate(flops=flops, bytes_accessed=moved, transcendentals=0),
    )(*operands)


def started(source, target, semaphores, index):
    copy = pltpu.make_async_copy(source, target, semaphores.at[index])
    copy.start()
    return copy


def shape(dims, dtype):
    return jax.ShapeDtypeStruct(dims, dtype)


def aligned(start, size):
    return pl.ds(pl.multiple_of(start, size), size)


def pack_kernel(tokens, cot, land, own, rim, tokens_v, cot_v, land_v, own32, rim32, sems):
    arrays = ((tokens, tokens_v), (cot, cot_v), (land, land_v))
    copies = [started(source, target, sems, i) for i, (source, target) in enumerate(arrays)]
    levels, lats, cols, width = tokens.shape[1:]
    half = levels * lats * SHIFT
    rim32[2 * half :, :] = jnp.zeros((rim32.shape[0] - 2 * half, width), F32)
    for which, ref in enumerate((tokens_v, cot_v)):
        copies[which].wait()
        for level in range(levels):
            for lat in range(lats):
                base = which * half + (level * lats + lat) * SHIFT
                line = ref[0, level, lat].astype(F32)
                rim32[base : base + SHIFT, :] = line[:SHIFT]
                own32[base : base + SHIFT, :] = line[SHIFT:]
    copies[2].wait()
    rim32[2 * half : 2 * half + lats, :cols] = land_v[...].astype(F32)
    own[...] = own32[...].astype(BF16)
    rim[...] = rim32[...].astype(BF16)


def unpack_kernel(own, back, grid, grid_v, sems):
    levels, lats, cols, width = grid.shape[1:]
    came = back[...].astype(F32)
    for level in range(levels):
        for lat in range(lats):
            base = (level * lats + lat) * SHIFT
            grid_v[0, level, lat, :SHIFT, :] = came[base : base + SHIFT]
            grid_v[0, level, lat, SHIFT:, :] = own[base : base + SHIFT, :]
    started(grid_v, grid, sems, 0).wait()


def land_column(land, rows, first):
    lats, cols = land.shape
    row = lax.broadcasted_iota(jnp.int32, (rows, lats), 0)
    lat = lax.rem(lax.div(row, SHIFT), lats)
    pick = (lat == lax.broadcasted_iota(jnp.int32, (rows, lats), 1)).astype(F32)
    lines = dot(pick.astype(BF16), land.astype(BF16))
    row = lax.broadcasted_iota(jnp.int32, (rows, cols), 0)
    column = lax.broadcasted_iota(jnp.int32, (rows, cols), 1)
    here = column == lax.rem(row, SHIFT) + first
    return jnp.sum(jnp.where(here, lines, 0.0), axis=1, keepdims=True)


def head_masks(dtype, size):
    lane = lax.broadcasted_iota(jnp.int32, (1, GROUP), 1)
    return [
        (lax.div(lane, size) == part).astype(F32).astype(dtype) for part in range(GROUP // size)
    ]


def stacked(block, masks):
    return jnp.concatenate([block * mask for mask in masks], axis=0)


def folded(block, masks):
    rows = block.shape[0] // len(masks)
    return sum(block[i * rows : (i + 1) * rows] * mask for i, mask in enumerate(masks))


def back_through(grad_out, probs, qkv, keys_t, weight_out, grad_proj, size, land, ready=None):
    count, width = grad_out.shape
    per = GROUP // size
    scale = size ** (-0.5)
    masks_b, masks = head_masks(BF16, size), head_masks(F32, size)
    att_t = dot_last(weight_out[...], grad_out)
    grad_att = att_t.T.astype(BF16)
    att_t = att_t.astype(BF16)
    lane = lax.broadcasted_iota(jnp.int32, (1, GROUP), 1)
    bias_row = jnp.zeros((1, GROUP), F32)
    for group in range(width // GROUP):
        at = group * GROUP
        if ready is not None:
            ready[group].wait()
        values = qkv[:, 2 * width + at : 2 * width + at + GROUP]
        grad_probs = dot(stacked(values, masks_b), att_t[at : at + GROUP, :])
        scores_b, probs_b, queries_t = [], [], []
        for part in range(per):
            head = group * per + part
            weights = probs[head * count : (head + 1) * count, :]
            grad_weights = grad_probs[part * count : (part + 1) * count]
            inner = jnp.sum(weights * grad_weights, axis=0, keepdims=True)
            grad_scores = weights * (grad_weights - inner)
            if land is not None:
                on_land = jnp.sum(grad_scores * land, axis=0, keepdims=True)
                on_land = jnp.sum(on_land, axis=1, keepdims=True)
                bias_row = bias_row + jnp.where(lane == head, on_land, 0.0)
            scaled_b = (grad_scores * scale).astype(BF16)
            scores_b.append(scaled_b)
            probs_b.append(weights.astype(BF16))
            queries_t.append(dot(keys_t[head * size : (head + 1) * size, :], scaled_b))
        queries = qkv[:, at : at + GROUP]
        grad_keys = dot(jnp.concatenate(scores_b, axis=0), queries)
        grad_values = dot(jnp.concatenate(probs_b, axis=0), grad_att[:, at : at + GROUP])
        grad_proj[:, at : at + GROUP] = jnp.concatenate(queries_t, axis=0).T.astype(BF16)
        grad_proj[:, width + at : width + at + GROUP] = folded(grad_keys, masks).astype(BF16)
        grad_proj[:, 2 * width + at : 2 * width + at + GROUP] = folded(grad_values, masks).astype(
            BF16
        )
    return bias_row


def through_norm(grad_proj, weight_qkv, gain, normed, inverse):
    scaled = dot_last(grad_proj, weight_qkv[...]) * gain[...]
    mean = jnp.mean(scaled, axis=-1, keepdims=True)
    along = jnp.mean(scaled * normed, axis=-1, keepdims=True)
    return inverse * (scaled - mean - normed * along)


def forward_kernel(
    bias, own, rim, land_own, gain, weight_qkv, weight_out,
    skip, cot, normed_out, normed_t_out, qkv_out, probs_out, attended_t_out, extra_out,
    bias_v, land_v, gain_v, qkv_v, out_v,
    normed_v, normed_t, qkv, probs, attended_t, extra, queries_t, keys_t, values_t, grad_proj,
    sems_in, sems_out,
):
    width = gain.shape[1]
    heads = bias.shape[1]
    size = width // heads
    half = own.shape[0] // 2
    count = 2 * half
    per = GROUP // size
    scale = size ** (-0.5)
    got = [
        started(source, target, sems_in, i)
        for i, (source, target) in enumerate(
            [
                (gain, gain_v),
                (land_own, land_v),
                (bias, bias_v),
                (weight_qkv.at[:, :width], qkv_v.at[:, :width]),
                (weight_qkv.at[:, width : 2 * width], qkv_v.at[:, width : 2 * width]),
                (weight_qkv.at[:, 2 * width :], qkv_v.at[:, 2 * width :]),
                (weight_out, out_v),
            ]
        )
    ]
    sent = []
    masks_b = head_masks(BF16, size)
    mine = own[...].astype(F32)
    came = rim[...].astype(F32)
    lats, cols = land_own.shape
    values = jnp.concatenate([mine[:half], came[:half]], axis=0)
    centred = values - jnp.mean(values, axis=-1, keepdims=True)
    inverse = lax.rsqrt(jnp.mean(centred * centred, axis=-1, keepdims=True) + EPSILON)
    normed = centred * inverse
    normed_v[...] = normed
    sent.append(started(normed_v, normed_out, sems_out, 0))
    for copy in got[:3]:
        copy.wait()
    normed_b = (normed * gain_v[...]).astype(BF16)
    normed_t[...] = normed_b.T
    sent.append(started(normed_t, normed_t_out, sems_out, 1))
    land = jnp.concatenate(
        [
            land_column(land_v[...].astype(F32), half, SHIFT),
            land_column(came[2 * half : 2 * half + lats, :cols], half, 0),
        ],
        axis=0,
    )
    extra[:, :GROUP] = jnp.broadcast_to(land, (count, GROUP))
    extra[:, GROUP:] = jnp.broadcast_to(inverse, (count, GROUP))
    sent.append(started(extra, extra_out, sems_out, 2))
    for part, turned in enumerate((queries_t, keys_t, values_t)):
        got[3 + part].wait()
        columns = slice(part * width, (part + 1) * width)
        qkv[:, columns] = dot(normed_b, qkv_v[:, columns]).astype(BF16)
        turned[...] = qkv[:, columns].T
    sent.append(started(qkv, qkv_out, sems_out, 3))
    for group in range(width // GROUP):
        at = group * GROUP
        keys = qkv[:, width + at : width + at + GROUP]
        scores = dot(stacked(keys, masks_b), queries_t[at : at + GROUP, :])
        for part in range(per):
            head = group * per + part
            block = scores[part * count : (part + 1) * count] * scale
            block = block + bias_v[:, head : head + 1] * land
            block = jnp.exp(block - jnp.max(block, axis=0, keepdims=True))
            weights = block * (1.0 / jnp.sum(block, axis=0, keepdims=True))
            probs[head * count : (head + 1) * count, :] = weights
            out = dot(values_t[head * size : (head + 1) * size, :], weights.astype(BF16))
            attended_t[head * size : (head + 1) * size, :] = out.astype(BF16)
        rows = pl.ds(group * per * count, per * count)
        sent.append(started(probs.at[rows, :], probs_out.at[rows, :], sems_out, 4 + group))
    sent.append(started(attended_t, attended_t_out, sems_out, 4 + width // GROUP))
    grad_out = jnp.concatenate([mine[half:], came[half : 2 * half]], axis=0)
    cot[...] = grad_out.astype(BF16)
    got[6].wait()
    back_through(cot[...], probs, qkv, keys_t, out_v, grad_proj, size, None)
    skip[...] = (
        through_norm(grad_proj[...], qkv_v, gain_v, normed, inverse) + grad_out
    ).astype(BF16)
    for copy in sent:
        copy.wait()


def backward_kernel(
    place, skip, cot, qkv_in, probs_in, weight_out, extra_in, normed_t_in, attended_t_in,
    total_out, grad_proj, bias_out, give,
    qkv, probs, out_v, extra, normed_t, attended_t, keys_t, sems,
    *, heads,
):
    count, width = cot.shape
    per = probs.shape[0] * GROUP // width
    got = [
        started(source, target, sems, i)
        for i, (source, target) in enumerate(
            [
                (weight_out, out_v),
                (qkv_in, qkv),
                (extra_in, extra),
                (normed_t_in, normed_t),
                (attended_t_in, attended_t),
            ]
        )
    ]
    groups = []
    for group in range(width // GROUP):
        rows = pl.ds(group * per, per)
        groups.append(started(probs_in.at[rows, :], probs.at[rows, :], sems, len(got) + group))
    total_out[...] = (cot[...].astype(F32) + skip[...].astype(F32)).astype(BF16)
    got[1].wait()
    keys_t[...] = qkv[:, width : 2 * width].T
    got[2].wait()
    got[0].wait()
    bias_row = back_through(
        total_out[...], probs, qkv, keys_t, out_v, grad_proj, width // heads, extra[:, :1], groups
    )
    bias_out[...] = jnp.broadcast_to(bias_row, bias_out.shape)
    half = width // 2
    got[3].wait()
    got[4].wait()
    rows = aligned((1 - place[0]) * half, half)
    weight_rows(rows, normed_t, attended_t, grad_proj, total_out, bias_row, give)


def weight_rows(rows, normed_t, attended_t, grad_proj, total, bias_row, out):
    tokens = normed_t[rows, :]
    three = grad_proj.shape[1]
    out[:, :CUT] = dot(tokens, grad_proj[:, :CUT]).astype(out.dtype)
    out[:, CUT : CUT + GROUP] = jnp.broadcast_to(bias_row, (out.shape[0], GROUP)).astype(out.dtype)
    out[:, CUT + GROUP : three + GROUP] = dot(tokens, grad_proj[:, CUT:]).astype(out.dtype)
    out[:, three + GROUP :] = dot(attended_t[rows, :], total[...]).astype(out.dtype)


def finish_kernel(
    place, total, grad_proj, bias_row, normed_t_in, attended_t_in, normed_in, extra_in,
    weight_qkv, gain,
    keep, own, back,
    normed_t, attended_t, normed, extra, qkv_v, gain_v, sems,
):
    count, width = total.shape
    half = width // 2
    got = [
        started(source, target, sems, i)
        for i, (source, target) in enumerate(
            [
                (normed_t_in, normed_t),
                (attended_t_in, attended_t),
                (weight_qkv.at[:half, :], qkv_v.at[:half, :]),
                (weight_qkv.at[half:, :], qkv_v.at[half:, :]),
                (normed_in, normed),
                (extra_in, extra),
                (gain, gain_v),
            ]
        )
    ]
    got[0].wait()
    got[1].wait()
    rows = aligned(place[0] * half, half)
    bias_b = bias_row[:1, :].astype(BF16).astype(F32)
    weight_rows(rows, normed_t, attended_t, grad_proj, total, bias_b, keep)
    for copy in got[2:]:
        copy.wait()
    final = through_norm(grad_proj[...], qkv_v, gain_v, normed[...], extra[:, GROUP : GROUP + 1])
    final = final + total[...].astype(F32)
    own[...] = final[: count // 2]
    back[...] = final[count // 2 :].astype(BF16)


def first_kernel(place, keep, came, give_p, kept_p, give_q, total):
    wide_p = give_p.shape[1]
    half = keep.shape[0] // 2
    total[...] = keep[...] + came[...].astype(F32)
    give_p[...] = total[aligned((1 - place[1]) * half, half), :wide_p].astype(BF16)
    mine = aligned(place[1] * half, half)
    kept_p[:, :CUT] = total[mine, :CUT]
    kept_p[:, CUT:] = total[mine, CUT:wide_p].astype(BF16).astype(F32)
    give_q[...] = total[:, wide_p:].astype(BF16).reshape(give_q.shape)


def added(pieces):
    total = pieces[0].astype(F32)
    for other in range(1, pieces.shape[0]):
        total = total + pieces[other].astype(F32)
    return total


def second_kernel(place, kept_p, came_p, came_q, give_q, left_q, give_p, total_q):
    give_p[...] = (kept_p[...] + came_p[...].astype(F32)).astype(BF16).reshape(give_p.shape)
    total_q[...] = added(came_q)
    half = give_q.shape[0]
    give_q[...] = total_q[aligned((1 - place[1]) * half, half), :].astype(BF16)
    left_q[...] = total_q[aligned(place[1] * half, half), :]


def third_kernel(left_q, came_q, came_p, pieces_p, piece_q, bias):
    total = added(came_p)
    piece = total[:, :CUT].astype(BF16)
    for other in range(pieces_p.shape[0]):
        pieces_p[other] = piece
    piece_q[...] = (left_q[...] + came_q[...].astype(F32)).astype(BF16)
    bias[...] = total[:8, CUT:]


def fourth_kernel(place, pieces_p, piece_q, other_q, block_p, blocks_q):
    block_p[...] = pieces_p[...].reshape(block_p.shape)
    piece = piece_q.shape[0]
    for other in range(blocks_q.shape[0]):
        blocks_q[other, aligned(place[1] * piece, piece), :] = piece_q[...]
        blocks_q[other, aligned((1 - place[1]) * piece, piece), :] = other_q[...]


def fifth_kernel(place, weight_qkv, gain, bias, block_p, other_p, blocks_q, half, row):
    rows, width = half.shape[0], weight_qkv.shape[0]
    piece = block_p.shape[0]
    half[aligned(place[1] * piece, piece), :CUT] = block_p[...]
    half[aligned((1 - place[1]) * piece, piece), :CUT] = other_p[...]
    half[:, CUT:] = blocks_q[...].reshape(rows, half.shape[1] - CUT)
    three = weight_qkv.shape[1]
    wide = half[:, :three].astype(F32)
    mine = aligned(place[0] * rows, rows)
    gain_half = jnp.sum(wide * weight_qkv[mine, :].astype(F32), axis=1, keepdims=True)
    gain_half = jnp.broadcast_to(gain_half, (rows, GROUP)).T[:8]
    core = place[0].astype(F32)
    own_gain = gain[:, :rows] * (1.0 - core) + gain[:, rows:] * core
    gain_half = gain_half / own_gain
    out = half[:, three:].astype(F32)
    square = jnp.sum(jnp.sum(wide * wide, axis=0, keepdims=True), axis=1, keepdims=True)
    square = square + jnp.sum(jnp.sum(out * out, axis=0, keepdims=True), axis=1, keepdims=True)
    square = square + jnp.sum(gain_half[:1] * gain_half[:1], axis=1, keepdims=True)
    square = square + 0.5 * jnp.sum(bias[:1, :] * bias[:1, :], axis=1, keepdims=True)
    row[:, :rows] = gain_half
    row[:, rows:] = jnp.broadcast_to(square, (8, GROUP))


def last_kernel(
    place, half, other, row, row_core, row_section, row_both, bias,
    grad_qkv, grad_out, grad_gain, grad_bias,
    qkv_v, out_v, gain_v, bias_v, sems,
    *, entries,
):
    rows, three = half.shape[0], grad_qkv.shape[1]
    square = row[:1, rows : rows + 1] + row_core[:1, rows : rows + 1]
    square = square + (row_section[:1, rows : rows + 1] + row_both[:1, rows : rows + 1])
    factor = jnp.minimum(1.0, lax.rsqrt(square / entries + 1e-06))
    sent = []
    piece = 64
    for which, ref in enumerate((half, other)):
        base = place[0] * rows if which == 0 else (1 - place[0]) * rows
        for part in range(rows // piece):
            here = slice(part * piece, (part + 1) * piece)
            at = aligned(base + part * piece, piece)
            slot = slice(which * rows + part * piece, which * rows + (part + 1) * piece)
            qkv_v[slot, :] = ref[here, :three].astype(F32) * factor
            sent.append(started(qkv_v.at[slot, :], grad_qkv.at[at, :], sems, len(sent)))
            out_v[slot, :] = ref[here, three:].astype(F32) * factor
            sent.append(started(out_v.at[slot, :], grad_out.at[at, :], sems, len(sent)))
    core = place[0].astype(F32)
    mine, its = row[:1, :rows] * factor, row_core[:1, :rows] * factor
    gain_v[:, :rows] = mine * (1.0 - core) + its * core
    gain_v[:, rows:] = mine * core + its * (1.0 - core)
    bias_v[...] = bias[:1, : bias_v.shape[1]] * factor
    sent.append(started(gain_v, grad_gain, sems, len(sent)))
    sent.append(started(bias_v, grad_bias, sems, len(sent)))
    for copy in sent:
        copy.wait()


def exchanged(pieces, axis):
    return lax.all_to_all(pieces, axis, 0, 0, tiled=True)


def vmem(dims, dtype):
    return pltpu.VMEM(dims, dtype)


def copies(number):
    return pltpu.SemaphoreType.DMA((number,))


def body(inputs, cotangent, land_sea, gains, qkv_weight, out_weight, land_bias):
    weight_qkv, weight_out = qkv_weight[0], out_weight[0]
    levels, lats, cols, width = inputs.shape[1:]
    heads = land_bias.shape[1]
    half = levels * lats * SHIFT
    count = 2 * half
    packed = half * 2 + 16
    lons = lax.axis_size("lon")
    lat, lon = lax.axis_index("lat"), lax.axis_index("lon")
    place = jnp.stack([lat % 2, lat // 2, lon]).astype(jnp.int32)

    own, rim = call(
        pack_kernel,
        [shape((2 * half, width), BF16), shape((packed, width), BF16)],
        scratch=[
            vmem(inputs.shape, BF16),
            vmem(inputs.shape, BF16),
            vmem(land_sea.shape, jnp.int32),
            vmem((2 * half, width), F32),
            vmem((packed, width), F32),
            copies(3),
        ],
        places="aaa",
        operands=(inputs, cotangent, land_sea),
    )
    rim = from_behind(rim, "lon", -1)
    groups = width // GROUP
    state = [
        shape((count, width), F32),
        shape((width, count), BF16),
        shape((count, 3 * width), BF16),
        shape((heads * count, count), F32),
        shape((width, count), BF16),
        shape((count, 2 * GROUP), F32),
    ]
    skip, cot, normed, normed_t, qkv, probs, attended_t, extra = call(
        forward_kernel,
        [shape((count, width), BF16), shape((count, width), BF16), *state],
        scratch=[
            vmem(land_bias.shape, F32),
            vmem(land_sea.shape, jnp.int32),
            vmem(gains.shape, F32),
            vmem(weight_qkv.shape, BF16),
            vmem(weight_out.shape, BF16),
            *(vmem(kept.shape, kept.dtype) for kept in state),
            vmem((width, count), BF16),
            vmem((width, count), BF16),
            vmem((width, count), BF16),
            vmem((count, 3 * width), BF16),
            copies(7),
            copies(5 + groups),
        ],
        places="avvaaaa",
        out_places="vvaaaaaa",
        operands=(land_bias, own, rim, land_sea, gains, weight_qkv, weight_out),
        flops=10**9,
        limit=20,
    )
    skip = passed_along(skip, "section", -1)
    rows, wide = width // 2, 4 * width + GROUP
    total, grad_proj, bias_row, give = call(
        functools.partial(backward_kernel, heads=heads),
        [
            shape((count, width), BF16),
            shape((count, 3 * width), BF16),
            shape((8, GROUP), F32),
            shape((rows, wide), BF16),
        ],
        scratch=[
            vmem(qkv.shape, BF16),
            vmem(probs.shape, F32),
            vmem(weight_out.shape, BF16),
            vmem(extra.shape, F32),
            vmem(normed_t.shape, BF16),
            vmem(attended_t.shape, BF16),
            vmem((width, count), BF16),
            copies(5 + groups),
        ],
        places="svvaaaaaa",
        operands=(place, skip, cot, qkv, probs, weight_out, extra, normed_t, attended_t),
        flops=10**9,
        limit=20,
    )
    came = swapped(give, "lat", 1)
    keep, own_grad, back = call(
        finish_kernel,
        [
            shape((rows, wide), F32),
            shape((half, width), F32),
            shape((half, width), BF16),
        ],
        scratch=[
            vmem(normed_t.shape, BF16),
            vmem(attended_t.shape, BF16),
            vmem(normed.shape, F32),
            vmem(extra.shape, F32),
            vmem(weight_qkv.shape, BF16),
            vmem(gains.shape, F32),
            copies(7),
        ],
        places="svvvaaaaaa",
        operands=(
            place, total, grad_proj, bias_row, normed_t, attended_t, normed, extra,
            weight_qkv, gains,
        ),
        flops=5 * 10**8,
    )
    back = from_behind(back, "lon", 1)
    entries = 2 * (4 * width * width + width + heads)
    if rows // 2 // lons % 16 == 0:
        grads, mark = staged(place, keep, came, weight_qkv, gains, lons, heads, entries)
    else:
        grads, mark = plain(keep, came, weight_qkv, gains, heads, entries)
    own_grad, back, _ = lax.optimization_barrier((own_grad, back, mark))
    (final_grad,) = call(
        unpack_kernel,
        [shape(inputs.shape, F32)],
        scratch=[vmem(inputs.shape, F32), copies(1)],
        out_places="a",
        operands=(own_grad, back),
    )
    return (final_grad, *(grad[None] for grad in grads))


def staged(place, keep, came, weight_qkv, gains, lons, heads, entries):
    rows, wide = keep.shape
    width = 2 * rows
    wide_p = CUT + GROUP
    wide_q = wide - wide_p
    give_p, kept_p, give_q = call(
        first_kernel,
        [
            shape((rows // 2, wide_p), BF16),
            shape((rows // 2, wide_p), F32),
            shape((lons, rows // lons, wide_q), BF16),
        ],
        scratch=[vmem((rows, wide), F32)],
        places="svv",
        operands=(place, keep, came),
    )
    came_p = swapped(give_p, "lat", 2)
    came_q = exchanged(give_q, "lon")
    piece = rows // 2 // lons
    give_q, left_q, give_p = call(
        second_kernel,
        [
            shape((piece, wide_q), BF16),
            shape((piece, wide_q), F32),
            shape((lons, piece, wide_p), BF16),
        ],
        scratch=[vmem((rows // lons, wide_q), F32)],
        places="svvv",
        operands=(place, kept_p, came_p, came_q),
    )
    came_q = swapped(give_q, "lat", 2)
    came_p = exchanged(give_p, "lon")
    pieces_p, piece_q, bias = call(
        third_kernel,
        [
            shape((lons, piece, CUT), BF16),
            shape((piece, wide_q), BF16),
            shape((8, GROUP), F32),
        ],
        operands=(left_q, came_q, came_p),
    )
    other_q = swapped(piece_q, "lat", 2)
    pieces_p = exchanged(pieces_p, "lon")
    block_p, blocks_q = call(
        fourth_kernel,
        [shape((rows // 2, CUT), BF16), shape((lons, rows // lons, wide_q), BF16)],
        places="svvv",
        operands=(place, pieces_p, piece_q, other_q),
    )
    other_p = swapped(block_p, "lat", 2)
    blocks_q = exchanged(blocks_q, "lon")
    half, row = call(
        fifth_kernel,
        [shape((rows, 4 * width), BF16), shape((8, rows + GROUP), F32)],
        places="svvvvvv",
        operands=(place, weight_qkv, gains, bias, block_p, other_p, blocks_q),
    )
    row_section = swapped(row, "section", 1)
    row_both = lax.ppermute(row, ("section", "lat"), across())
    row_core = swapped(row, "lat", 1)
    other = swapped(half, "lat", 1)
    grads = call(
        functools.partial(last_kernel, entries=entries),
        [
            shape((width, 3 * width), F32),
            shape((width, width), F32),
            shape((1, width), F32),
            shape((1, heads), F32),
        ],
        scratch=[
            vmem((width, 3 * width), F32),
            vmem((width, width), F32),
            vmem((1, width), F32),
            vmem((1, heads), F32),
            copies(4 * rows // 64 + 2),
        ],
        places="svvvvvvv",
        out_places="aaaa",
        operands=(place, half, other, row, row_core, row_section, row_both, bias),
    )
    return (grads[0], grads[1], grads[2][0], grads[3][0]), left_q


def across():
    sections, lats = lax.axis_size("section"), lax.axis_size("lat")
    return [
        (s * lats + i, (sections - 1 - s) * lats + (i ^ 1))
        for s in range(sections)
        for i in range(lats)
    ]


def split_two(block, axis, bit):
    mine = (lax.axis_index(axis) // bit) % 2
    pair = block.reshape(2, block.shape[0] // 2, -1)
    give = lax.dynamic_index_in_dim(pair, 1 - mine, 0, keepdims=False).astype(BF16)
    return give, lax.dynamic_index_in_dim(pair, mine, 0, keepdims=False)


def doubled(block, axis, bit):
    mine = (lax.axis_index(axis) // bit) % 2
    other = swapped(block, axis, bit)
    low = jnp.where(mine == 0, block, other)
    high = jnp.where(mine == 0, other, block)
    return jnp.concatenate([low, high], axis=0)


def scattered(block, axis):
    count = lax.axis_size(axis)
    mine = lax.axis_index(axis)
    pieces = block.reshape(count, block.shape[0] // count, -1)
    total = lax.dynamic_index_in_dim(pieces, mine, 0, keepdims=False)
    others = []
    for by in range(1, count):
        give = lax.dynamic_index_in_dim(pieces, (mine + by) % count, 0, keepdims=False)
        others.append(from_behind(give.astype(BF16), axis, by))
    for other in others:
        total = total + other.astype(F32)
    return total, others


def gathered(block, axis):
    count = lax.axis_size(axis)
    mine = lax.axis_index(axis)
    whole = jnp.zeros((count,) + block.shape, block.dtype)
    whole = lax.dynamic_update_index_in_dim(whole, block, mine, 0)
    for by in range(1, count):
        whole = lax.dynamic_update_index_in_dim(
            whole, from_behind(block, axis, by), (mine - by) % count, 0
        )
    return whole.reshape(count * block.shape[0], -1)


def sum_squares(block):
    wide = block.astype(F32)
    return jnp.sum(wide * wide)


def plain(keep, came, weight_qkv, gains, heads, entries):
    width = gains.shape[1]
    lat, lon = lax.axis_index("lat"), lax.axis_index("lon")
    part = keep + came.astype(F32)
    give, keep = split_two(part, "lat", 2)
    came = swapped(give, "lat", 2).astype(F32)
    column = lax.broadcasted_iota(jnp.int32, keep.shape, 1)
    is_bias = (column >= CUT) & (column < CUT + GROUP)
    part = jnp.where(is_bias, lax.reduce_precision(keep, 8, 7), keep) + came
    bias_part = lax.reduce_precision(part[:1, CUT : CUT + GROUP], 8, 7)
    part, others = scattered(part, "lon")
    terms = [bias_part] + [other[:1, CUT : CUT + GROUP].astype(F32) for other in others]
    terms = jnp.concatenate(terms[:1] + terms[:0:-1], axis=0)
    bias = jnp.sum(jnp.roll(terms, lon, axis=0), axis=0)[:heads]
    part = jnp.concatenate([part[:, :CUT], part[:, CUT + GROUP :]], axis=1).astype(BF16)
    half = doubled(gathered(part, "lon"), "lat", 2)
    mine = lat % 2
    weight_half = lax.dynamic_slice_in_dim(weight_qkv, mine * (width // 2), width // 2, 0)
    gain_half = lax.dynamic_slice_in_dim(gains[0], mine * (width // 2), width // 2, 0)
    weighed = half[:, : 3 * width].astype(F32) * weight_half.astype(F32)
    gain_half = jnp.sum(weighed, axis=1) / gain_half
    square = sum_squares(half) + sum_squares(gain_half) + 0.5 * sum_squares(bias)
    square = square.reshape(1)
    square = square + swapped(square, "lat", 1)
    square = square + swapped(square, "section", 1)
    factor = jnp.minimum(1.0, lax.rsqrt(square[0] / entries + 1e-06))
    grads = doubled(half, "lat", 1).astype(F32) * factor
    gain = doubled(gain_half.reshape(-1, 1), "lat", 1)[:, 0] * factor
    return (grads[:, : 3 * width], grads[:, 3 * width :], gain, bias * factor), bias


def solution(mesh):
    placed = (
        P("section", None, "lat", "lon", None),
        P("section", None, "lat", "lon", None),
        P("lat", "lon"),
        P("section", None),
        P("section", None, None),
        P("section", None, None),
        P("section", None),
    )
    return jax.shard_map(
        body,
        mesh=mesh,
        in_specs=placed,
        out_specs=(
            P("section", None, "lat", "lon", None),
            P("section", None, None),
            P("section", None, None),
            P("section", None),
            P("section", None),
        ),
        check_vma=False,
    )
```

```python
import functools

import jax
import jax.numpy as jnp
from jax import lax
from jax.experimental import pallas as pl
from jax.experimental.pallas import tpu as pltpu
from jax.sharding import PartitionSpec as P

SHIFT = 6
GROUP = 128
CUT = 1152
EPSILON = 1e-05
F32 = jnp.float32
BF16 = jnp.bfloat16


def from_behind(value, axis, by):
    count = lax.axis_size(axis)
    return lax.ppermute(value, axis, [(i, (i + by) % count) for i in range(count)])


def passed_along(block, axis, distance):
    devices = range(lax.axis_size(axis))
    route = [(i - distance, i) for i in devices if i - distance in devices]
    return lax.ppermute(block, axis, route)


def swapped(value, axis, bit):
    count = lax.axis_size(axis)
    return lax.ppermute(value, axis, [(i, i ^ bit) for i in range(count)])


def dot(left, right):
    return jnp.dot(left, right, preferred_element_type=F32)


def dot_last(left, right):
    return lax.dot_general(left, right, (((1,), (1,)), ((), ())), preferred_element_type=F32)


def call(kernel, outs, scratch=(), places="", out_places="", operands=(), flops=10**8, limit=8):
    spaces = {"v": pltpu.VMEM, "s": pltpu.SMEM, "a": pl.ANY, "h": pltpu.HBM}
    places = places or "v" * len(operands)
    out_places = out_places or "v" * len(outs)
    moved = sum(o.size * o.dtype.itemsize for o in list(outs) + list(operands))
    return pl.pallas_call(
        kernel,
        out_shape=list(outs),
        in_specs=[pl.BlockSpec(memory_space=spaces[letter]) for letter in places],
        out_specs=[pl.BlockSpec(memory_space=spaces[letter]) for letter in out_places],
        scratch_shapes=list(scratch),
        compiler_params=pltpu.CompilerParams(vmem_limit_bytes=limit * 2**20),
        cost_estimate=pl.CostEstimate(flops=flops, bytes_accessed=moved, transcendentals=0),
    )(*operands)


def started(source, target, semaphores, index):
    copy = pltpu.make_async_copy(source, target, semaphores.at[index])
    copy.start()
    return copy


def shape(dims, dtype):
    return jax.ShapeDtypeStruct(dims, dtype)


def aligned(start, size):
    return pl.ds(pl.multiple_of(start, size), size)


def pack_kernel(tokens, cot, land, own, rim, tokens_v, cot_v, land_v, own32, rim32, sems):
    arrays = ((tokens, tokens_v), (cot, cot_v), (land, land_v))
    copies = [started(source, target, sems, i) for i, (source, target) in enumerate(arrays)]
    lats, cols, levels, width = tokens.shape[1:]
    half = levels * lats * SHIFT
    rim32[2 * half :, :] = jnp.zeros((rim32.shape[0] - 2 * half, width), F32)
    for which, ref in enumerate((tokens_v, cot_v)):
        copies[which].wait()
        for lat in range(lats):
            for col in range(cols):
                row = which * half + (lat * SHIFT + col % SHIFT) * levels
                part = rim32 if col < SHIFT else own32
                part[row : row + levels, :] = ref[0, lat, col].astype(F32)
    copies[2].wait()
    rim32[2 * half : 2 * half + lats, :cols] = land_v[...].astype(F32)
    own[...] = own32[...].astype(BF16)
    rim[...] = rim32[...].astype(BF16)


def unpack_kernel(own, back, after, grid, grid_v, sems):
    lats, cols, levels, width = grid.shape[1:]
    came = back[...].astype(F32)
    for lat in range(lats):
        for col in range(cols):
            row = (lat * SHIFT + col % SHIFT) * levels
            if col < SHIFT:
                grid_v[0, lat, col] = came[row : row + levels]
            else:
                grid_v[0, lat, col] = own[row : row + levels, :]
    started(grid_v, grid, sems, 0).wait()


def land_column(land, rows, first):
    lats, cols = land.shape
    row = lax.broadcasted_iota(jnp.int32, (rows, lats), 0)
    lat = lax.div(row, rows // lats)
    pick = (lat == lax.broadcasted_iota(jnp.int32, (rows, lats), 1)).astype(F32)
    lines = dot(pick.astype(BF16), land.astype(BF16))
    row = lax.broadcasted_iota(jnp.int32, (rows, cols), 0)
    column = lax.broadcasted_iota(jnp.int32, (rows, cols), 1)
    levels = rows // (lats * SHIFT)
    here = column == lax.rem(lax.div(row, levels), SHIFT) + first
    return jnp.sum(jnp.where(here, lines, 0.0), axis=1, keepdims=True)


def head_masks(dtype, size):
    lane = lax.broadcasted_iota(jnp.int32, (1, GROUP), 1)
    return [
        (lax.div(lane, size) == part).astype(F32).astype(dtype) for part in range(GROUP // size)
    ]


def stacked(block, masks):
    return jnp.concatenate([block * mask for mask in masks], axis=0)


def folded(block, masks):
    rows = block.shape[0] // len(masks)
    return sum(block[i * rows : (i + 1) * rows] * mask for i, mask in enumerate(masks))


def back_through(grad_out, probs, qkv, keys_t, weight_out, grad_proj, size, land):
    count, width = grad_out.shape
    per = GROUP // size
    scale = size ** (-0.5)
    masks_b, masks = head_masks(BF16, size), head_masks(F32, size)
    att_t = dot_last(weight_out[...], grad_out)
    grad_att = att_t.T.astype(BF16)
    att_t = att_t.astype(BF16)
    lane = lax.broadcasted_iota(jnp.int32, (1, GROUP), 1)
    bias_row = jnp.zeros((1, GROUP), F32)
    for group in range(width // GROUP):
        at = group * GROUP
        values = qkv[:, 2 * width + at : 2 * width + at + GROUP]
        grad_probs = dot(stacked(values, masks_b), att_t[at : at + GROUP, :])
        scores_b, probs_b, queries_t = [], [], []
        for part in range(per):
            head = group * per + part
            weights = probs[head * count : (head + 1) * count, :]
            grad_weights = grad_probs[part * count : (part + 1) * count]
            inner = jnp.sum(weights * grad_weights, axis=0, keepdims=True)
            grad_scores = weights * (grad_weights - inner)
            if land is not None:
                on_land = jnp.sum(grad_scores * land, axis=0, keepdims=True)
                on_land = jnp.sum(on_land, axis=1, keepdims=True)
                bias_row = bias_row + jnp.where(lane == head, on_land, 0.0)
            scaled_b = (grad_scores * scale).astype(BF16)
            scores_b.append(scaled_b)
            probs_b.append(weights.astype(BF16))
            queries_t.append(dot(keys_t[head * size : (head + 1) * size, :], scaled_b))
        queries = qkv[:, at : at + GROUP]
        grad_keys = dot(jnp.concatenate(scores_b, axis=0), queries)
        grad_values = dot(jnp.concatenate(probs_b, axis=0), grad_att[:, at : at + GROUP])
        grad_proj[:, at : at + GROUP] = jnp.concatenate(queries_t, axis=0).T.astype(BF16)
        grad_proj[:, width + at : width + at + GROUP] = folded(grad_keys, masks).astype(BF16)
        grad_proj[:, 2 * width + at : 2 * width + at + GROUP] = folded(grad_values, masks).astype(
            BF16
        )
    return bias_row


def through_norm(grad_proj, weight_qkv, gain, normed, inverse):
    scaled = dot_last(grad_proj, weight_qkv[...]) * gain[...]
    mean = jnp.mean(scaled, axis=-1, keepdims=True)
    along = jnp.mean(scaled * normed, axis=-1, keepdims=True)
    return inverse * (scaled - mean - normed * along)


def forward_kernel(
    bias, own, rim, land_own, gain, weight_qkv, weight_out,
    skip, cot, normed_t, qkv, probs, attended_t, land_out, normed_out, inverse_out,
    bias_v, land_v, gain_v, qkv_v, out_v,
    normed_v, inverse_v, queries_t, keys_t, values_t, grad_proj, sems_in, sems_out,
):
    width = gain.shape[1]
    heads = bias.shape[1]
    size = width // heads
    half = own.shape[0] // 2
    count = 2 * half
    per = GROUP // size
    scale = size ** (-0.5)
    got = [
        started(source, target, sems_in, i)
        for i, (source, target) in enumerate(
            [
                (gain, gain_v),
                (land_own, land_v),
                (bias, bias_v),
                (weight_qkv.at[:, :width], qkv_v.at[:, :width]),
                (weight_qkv.at[:, width : 2 * width], qkv_v.at[:, width : 2 * width]),
                (weight_qkv.at[:, 2 * width :], qkv_v.at[:, 2 * width :]),
                (weight_out, out_v),
            ]
        )
    ]
    sent = []
    masks_b = head_masks(BF16, size)
    mine = own[...].astype(F32)
    came = rim[...].astype(F32)
    lats, cols = land_own.shape
    values = jnp.concatenate([mine[:half], came[:half]], axis=0)
    centred = values - jnp.mean(values, axis=-1, keepdims=True)
    inverse = lax.rsqrt(jnp.mean(centred * centred, axis=-1, keepdims=True) + EPSILON)
    normed = centred * inverse
    normed_v[...] = normed
    sent.append(started(normed_v, normed_out, sems_out, 0))
    for copy in got[:3]:
        copy.wait()
    normed_b = (normed * gain_v[...]).astype(BF16)
    normed_t[...] = normed_b.T
    land = jnp.concatenate(
        [
            land_column(land_v[...].astype(F32), half, SHIFT),
            land_column(came[2 * half : 2 * half + lats, :cols], half, 0),
        ],
        axis=0,
    )
    land_out[...] = jnp.broadcast_to(land, (count, GROUP))
    inverse_v[...] = jnp.broadcast_to(inverse, (count, GROUP))
    sent.append(started(inverse_v, inverse_out, sems_out, 1))
    for part, turned in enumerate((queries_t, keys_t, values_t)):
        got[3 + part].wait()
        columns = slice(part * width, (part + 1) * width)
        qkv[:, columns] = dot(normed_b, qkv_v[:, columns]).astype(BF16)
        turned[...] = qkv[:, columns].T
    for group in range(width // GROUP):
        at = group * GROUP
        keys = qkv[:, width + at : width + at + GROUP]
        scores = dot(stacked(keys, masks_b), queries_t[at : at + GROUP, :])
        for part in range(per):
            head = group * per + part
            block = scores[part * count : (part + 1) * count] * scale
            block = block + bias_v[:, head : head + 1] * land
            block = jnp.exp(block - jnp.max(block, axis=0, keepdims=True))
            weights = block * (1.0 / jnp.sum(block, axis=0, keepdims=True))
            probs[head * count : (head + 1) * count, :] = weights
            out = dot(values_t[head * size : (head + 1) * size, :], weights.astype(BF16))
            attended_t[head * size : (head + 1) * size, :] = out.astype(BF16)
    grad_out = jnp.concatenate([mine[half:], came[half : 2 * half]], axis=0)
    cot[...] = grad_out.astype(BF16)
    got[6].wait()
    back_through(cot[...], probs, qkv, keys_t, out_v, grad_proj, size, None)
    skip[...] = (
        through_norm(grad_proj[...], qkv_v, gain_v, normed, inverse) + grad_out
    ).astype(BF16)
    for copy in sent:
        copy.wait()


def backward_kernel(
    place, skip, cot, qkv, probs, land, normed_t, attended_t, weight_out,
    total_out, grad_proj, bias_out, give,
    out_v, keys_t, sems,
    *, heads,
):
    count, width = cot.shape
    got = started(weight_out, out_v, sems, 0)
    total_out[...] = (cot[...].astype(F32) + skip[...].astype(F32)).astype(BF16)
    keys_t[...] = qkv[:, width : 2 * width].T
    got.wait()
    bias_row = back_through(
        total_out[...], probs, qkv, keys_t, out_v, grad_proj, width // heads, land[:, :1]
    )
    bias_out[...] = jnp.broadcast_to(bias_row, bias_out.shape)
    half = width // 2
    rows = aligned((1 - place[0]) * half, half)
    weight_rows(rows, normed_t, attended_t, grad_proj, total_out, bias_row, give)


def weight_rows(rows, normed_t, attended_t, grad_proj, total, bias_row, out):
    tokens = normed_t[rows, :]
    three = grad_proj.shape[1]
    out[:, :CUT] = dot(tokens, grad_proj[:, :CUT]).astype(out.dtype)
    out[:, CUT : CUT + GROUP] = jnp.broadcast_to(bias_row, (out.shape[0], GROUP)).astype(out.dtype)
    out[:, CUT + GROUP : three + GROUP] = dot(tokens, grad_proj[:, CUT:]).astype(out.dtype)
    out[:, three + GROUP :] = dot(attended_t[rows, :], total[...]).astype(out.dtype)


def finish_kernel(
    place, total, grad_proj, bias_row, normed_t, attended_t, normed_in, inverse_in,
    weight_qkv, gain,
    keep, own, back,
    normed, inverse, qkv_v, gain_v, sems,
):
    count, width = total.shape
    half = width // 2
    got = [
        started(source, target, sems, i)
        for i, (source, target) in enumerate(
            [
                (weight_qkv.at[:half, :], qkv_v.at[:half, :]),
                (weight_qkv.at[half:, :], qkv_v.at[half:, :]),
                (normed_in, normed),
                (inverse_in, inverse),
                (gain, gain_v),
            ]
        )
    ]
    rows = aligned(place[0] * half, half)
    bias_b = bias_row[:1, :].astype(BF16).astype(F32)
    weight_rows(rows, normed_t, attended_t, grad_proj, total, bias_b, keep)
    for copy in got:
        copy.wait()
    final = through_norm(grad_proj[...], qkv_v, gain_v, normed[...], inverse[:, :1])
    final = final + total[...].astype(F32)
    own[...] = final[: count // 2]
    back[...] = final[count // 2 :].astype(BF16)


def first_p_kernel(place, keep, came, give, kept, total):
    wide = give.shape[1]
    half = give.shape[0]
    total[...] = keep[:, :wide] + came[:, :wide].astype(F32)
    give[...] = total[aligned((1 - place[1]) * half, half), :].astype(BF16)
    mine = aligned(place[1] * half, half)
    kept[:, :CUT] = total[mine, :CUT]
    kept[:, CUT:] = total[mine, CUT:].astype(BF16).astype(F32)


def first_q_kernel(place, keep, came, after, kept, *rest):
    *give, total = rest
    piece, wide = kept.shape
    total[...] = keep[:, -wide:] + came[:, -wide:].astype(F32)
    kept[...] = total[aligned(place[2] * piece, piece), :]
    for other, ref in enumerate(give, 1):
        ref[...] = total[aligned((place[2] ^ other) * piece, piece), :].astype(BF16)


def second_p_kernel(place, kept, came, left, *rest):
    *give, total = rest
    piece = left.shape[0]
    total[...] = kept[...] + came[...].astype(F32)
    mine = aligned(place[2] * piece, piece)
    left[:, :CUT] = total[mine, :CUT]
    left[:, CUT:] = total[mine, CUT:].astype(BF16).astype(F32)
    for other, ref in enumerate(give, 1):
        ref[...] = total[aligned((place[2] ^ other) * piece, piece), :].astype(BF16)


def second_q_kernel(place, after, kept, *rest):
    *came, give, left, sums = rest
    total = kept[...]
    for ref in came:
        total = total + ref[...].astype(F32)
    sums[...] = total
    half = give.shape[0]
    give[...] = sums[aligned((1 - place[1]) * half, half), :].astype(BF16)
    left[...] = sums[aligned(place[1] * half, half), :]


def third_q_kernel(left, came, piece):
    piece[...] = (left[...] + came[...].astype(F32)).astype(BF16)


def third_p_kernel(place, after, left, *rest):
    *came, piece, bias = rest
    total = left[:, :CUT]
    for ref in came:
        total = total + ref[:, :CUT].astype(F32)
    piece[...] = total.astype(BF16)
    terms = [left[:8, CUT:]] + [ref[...].astype(F32)[:8, CUT:] for ref in came]
    total = jnp.zeros_like(terms[0])
    for source in range(len(terms)):
        for other, term in enumerate(terms):
            total = total + jnp.where((place[2] ^ other) == source, term, 0.0)
    bias[...] = total


def fourth_q_kernel(place, after, own, came, block):
    piece = own.shape[0]
    block[aligned(place[1] * piece, piece), :] = own[...]
    block[aligned((1 - place[1]) * piece, piece), :] = came[...]


def fourth_p_kernel(place, after, *rest):
    *parts, block = rest
    piece = parts[0].shape[0]
    for other, part in enumerate(parts):
        block[aligned((place[2] ^ other) * piece, piece), :] = part[...]


def fifth_kernel(place, weight_qkv, gain, bias, block_p, other_p, *rest):
    *parts_q, half, row, weight_v, gain_v, sems = rest
    rows = half.shape[0]
    mine = aligned(place[0] * rows, rows)
    got = [
        started(weight_qkv.at[mine, :], weight_v, sems, 0),
        started(gain, gain_v, sems, 1),
    ]
    piece = block_p.shape[0]
    half[aligned(place[1] * piece, piece), :CUT] = block_p[...]
    half[aligned((1 - place[1]) * piece, piece), :CUT] = other_p[...]
    piece = parts_q[0].shape[0]
    for other, part in enumerate(parts_q):
        half[aligned((place[2] ^ other) * piece, piece), CUT:] = part[...]
    three = weight_v.shape[1]
    wide = half[:, :three].astype(F32)
    for copy in got:
        copy.wait()
    gain_half = jnp.sum(wide * weight_v[...].astype(F32), axis=1, keepdims=True)
    gain_half = jnp.broadcast_to(gain_half, (rows, GROUP)).T[:8]
    core = place[0].astype(F32)
    own_gain = gain_v[:, :rows] * (1.0 - core) + gain_v[:, rows:] * core
    gain_half = gain_half / own_gain
    out = half[:, three:].astype(F32)
    square = jnp.sum(jnp.sum(wide * wide, axis=0, keepdims=True), axis=1, keepdims=True)
    square = square + jnp.sum(jnp.sum(out * out, axis=0, keepdims=True), axis=1, keepdims=True)
    square = square + jnp.sum(gain_half[:1] * gain_half[:1], axis=1, keepdims=True)
    square = square + 0.5 * jnp.sum(bias[:1, :] * bias[:1, :], axis=1, keepdims=True)
    row[:, :rows] = gain_half
    row[:, rows:] = jnp.broadcast_to(square, (8, GROUP))


def last_kernel(
    place, half, other, row, row_core, row_section, row_both, bias,
    grad_qkv, grad_out, grad_gain, grad_bias,
    qkv_v, out_v, gain_v, bias_v, sems,
    *, entries,
):
    rows, three = half.shape[0], grad_qkv.shape[1]
    square = row[:1, rows : rows + 1] + row_core[:1, rows : rows + 1]
    square = square + (row_section[:1, rows : rows + 1] + row_both[:1, rows : rows + 1])
    factor = jnp.minimum(1.0, lax.rsqrt(square / entries + 1e-06))
    sent = []
    piece = 64
    for which, ref in enumerate((half, other)):
        base = place[0] * rows if which == 0 else (1 - place[0]) * rows
        for part in range(rows // piece):
            here = slice(part * piece, (part + 1) * piece)
            at = aligned(base + part * piece, piece)
            slot = slice(which * rows + part * piece, which * rows + (part + 1) * piece)
            qkv_v[slot, :] = ref[here, :three].astype(F32) * factor
            sent.append(started(qkv_v.at[slot, :], grad_qkv.at[at, :], sems, len(sent)))
            out_v[slot, :] = ref[here, three:].astype(F32) * factor
            sent.append(started(out_v.at[slot, :], grad_out.at[at, :], sems, len(sent)))
    core = place[0].astype(F32)
    mine, its = row[:1, :rows] * factor, row_core[:1, :rows] * factor
    gain_v[:, :rows] = mine * (1.0 - core) + its * core
    gain_v[:, rows:] = mine * core + its * (1.0 - core)
    bias_v[...] = bias[:1, : bias_v.shape[1]] * factor
    sent.append(started(gain_v, grad_gain, sems, len(sent)))
    sent.append(started(bias_v, grad_bias, sems, len(sent)))
    for copy in sent:
        copy.wait()


def sent_round(pieces, axis):
    return [swapped(piece, axis, other) for other, piece in enumerate(pieces, 1)]


def vmem(dims, dtype):
    return pltpu.VMEM(dims, dtype)


def copies(number):
    return pltpu.SemaphoreType.DMA((number,))


def body(inputs, cotangent, land_sea, gains, qkv_weight, out_weight, land_bias):
    weight_qkv, weight_out = qkv_weight[0], out_weight[0]
    levels, lats, cols, width = inputs.shape[1:]
    heads = land_bias.shape[1]
    half = levels * lats * SHIFT
    count = 2 * half
    packed = half * 2 + 16
    lons = lax.axis_size("lon")
    lat, lon = lax.axis_index("lat"), lax.axis_index("lon")
    place = jnp.stack([lat % 2, lat // 2, lon]).astype(jnp.int32)

    tokens = inputs.transpose(0, 2, 3, 1, 4)
    own_cot = cotangent.transpose(0, 2, 3, 1, 4)

    own, rim = call(
        pack_kernel,
        [shape((2 * half, width), BF16), shape((packed, width), BF16)],
        scratch=[
            vmem(tokens.shape, BF16),
            vmem(tokens.shape, BF16),
            vmem(land_sea.shape, jnp.int32),
            vmem((2 * half, width), F32),
            vmem((packed, width), F32),
            copies(3),
        ],
        places="hhh",
        operands=(tokens, own_cot, land_sea),
    )
    rim = from_behind(rim, "lon", -1)
    skip, cot, normed_t, qkv, probs, attended_t, land, normed, inverse = call(
        forward_kernel,
        [
            shape((count, width), BF16),
            shape((count, width), BF16),
            shape((width, count), BF16),
            shape((count, 3 * width), BF16),
            shape((heads * count, count), F32),
            shape((width, count), BF16),
            shape((count, GROUP), F32),
            shape((count, width), F32),
            shape((count, GROUP), F32),
        ],
        scratch=[
            vmem(land_bias.shape, F32),
            vmem(land_sea.shape, jnp.int32),
            vmem(gains.shape, F32),
            vmem(weight_qkv.shape, BF16),
            vmem(weight_out.shape, BF16),
            vmem((count, width), F32),
            vmem((count, GROUP), F32),
            vmem((width, count), BF16),
            vmem((width, count), BF16),
            vmem((width, count), BF16),
            vmem((count, 3 * width), BF16),
            copies(7),
            copies(2),
        ],
        places="hvvhhhh",
        out_places="vvvvvvvhh",
        operands=(land_bias, own, rim, land_sea, gains, weight_qkv, weight_out),
        flops=10**9,
        limit=16,
    )
    skip = passed_along(skip, "section", -1)
    rows, wide = width // 2, 4 * width + GROUP
    total, grad_proj, bias_row, give = call(
        functools.partial(backward_kernel, heads=heads),
        [
            shape((count, width), BF16),
            shape((count, 3 * width), BF16),
            shape((8, GROUP), F32),
            shape((rows, wide), BF16),
        ],
        scratch=[vmem(weight_out.shape, BF16), vmem((width, count), BF16), copies(1)],
        places="svvvvvvvh",
        operands=(place, skip, cot, qkv, probs, land, normed_t, attended_t, weight_out),
        flops=10**9,
    )
    came = swapped(give, "lat", 1)
    keep, own_grad, back = call(
        finish_kernel,
        [
            shape((rows, wide), F32),
            shape((half, width), F32),
            shape((half, width), BF16),
        ],
        scratch=[
            vmem(normed.shape, F32),
            vmem(inverse.shape, F32),
            vmem(weight_qkv.shape, BF16),
            vmem(gains.shape, F32),
            copies(5),
        ],
        places="svvvvvhhhh",
        operands=(
            place, total, grad_proj, bias_row, normed_t, attended_t, normed, inverse,
            weight_qkv, gains,
        ),
        flops=5 * 10**8,
    )
    back = from_behind(back, "lon", 1)
    entries = 2 * (4 * width * width + width + heads)
    if rows // 2 // lons % 16 == 0 and lons & (lons - 1) == 0:
        grads, mark = staged(place, keep, came, weight_qkv, gains, lons, heads, entries)
    else:
        grads, mark = plain(keep, came, weight_qkv, gains, heads, entries)
    (final_grad,) = call(
        unpack_kernel,
        [shape(tokens.shape, F32)],
        scratch=[vmem(tokens.shape, F32), copies(1)],
        places="vva",
        out_places="h",
        operands=(own_grad, back, mark),
    )
    final_grad = final_grad.transpose(0, 3, 1, 2, 4)
    return (final_grad, *(grad[None] for grad in grads))


def staged(place, keep, came, weight_qkv, gains, lons, heads, entries):
    rows, wide = keep.shape
    width = 2 * rows
    wide_p = CUT + GROUP
    wide_q = wide - wide_p
    some = range(lons - 1)
    piece = rows // 2 // lons
    give_p, kept_p = call(
        first_p_kernel,
        [shape((rows // 2, wide_p), BF16), shape((rows // 2, wide_p), F32)],
        scratch=[vmem((rows, wide_p), F32)],
        places="svv",
        operands=(place, keep, came),
    )
    came_p = swapped(give_p, "lat", 2)
    kept_q, *give_q = call(
        first_q_kernel,
        [
            shape((rows // lons, wide_q), F32),
            *(shape((rows // lons, wide_q), BF16) for _ in some),
        ],
        scratch=[vmem((rows, wide_q), F32)],
        places="svva",
        operands=(place, keep, came, kept_p),
    )
    came_q = sent_round(give_q, "lon")
    left_p, *give_p = call(
        second_p_kernel,
        [shape((piece, wide_p), F32), *(shape((piece, wide_p), BF16) for _ in some)],
        scratch=[vmem((rows // 2, wide_p), F32)],
        places="svv",
        operands=(place, kept_p, came_p),
    )
    came_p = sent_round(give_p, "lon")
    give_q, left_q = call(
        second_q_kernel,
        [shape((piece, wide_q), BF16), shape((piece, wide_q), F32)],
        scratch=[vmem((rows // lons, wide_q), F32)],
        places="sav" + "v" * len(some),
        operands=(place, left_p, kept_q, *came_q),
    )
    came_q = swapped(give_q, "lat", 2)
    (piece_q,) = call(third_q_kernel, [shape((piece, wide_q), BF16)], operands=(left_q, came_q))
    other_q = swapped(piece_q, "lat", 2)
    piece_p, bias = call(
        third_p_kernel,
        [shape((piece, CUT), BF16), shape((8, GROUP), F32)],
        places="sav" + "v" * len(some),
        operands=(place, piece_q, left_p, *came_p),
    )
    others_p = sent_round([piece_p for _ in some], "lon")
    (block_q,) = call(
        fourth_q_kernel,
        [shape((rows // lons, wide_q), BF16)],
        places="savv",
        operands=(place, piece_p, piece_q, other_q),
    )
    others_q = sent_round([block_q for _ in some], "lon")
    (block_p,) = call(
        fourth_p_kernel,
        [shape((rows // 2, CUT), BF16)],
        places="sav" + "v" * len(some),
        operands=(place, block_q, piece_p, *others_p),
    )
    other_p = swapped(block_p, "lat", 2)
    half, row = call(
        fifth_kernel,
        [shape((rows, 4 * width), BF16), shape((8, rows + GROUP), F32)],
        scratch=[vmem((rows, 3 * width), BF16), vmem((1, width), F32), copies(2)],
        places="shhvvvv" + "v" * len(some),
        operands=(place, weight_qkv, gains, bias, block_p, other_p, block_q, *others_q),
    )
    row_section = swapped(row, "section", 1)
    row_both = lax.ppermute(row, ("section", "lat"), across())
    row_core = swapped(row, "lat", 1)
    other = swapped(half, "lat", 1)
    grads = call(
        functools.partial(last_kernel, entries=entries),
        [
            shape((width, 3 * width), F32),
            shape((width, width), F32),
            shape((1, width), F32),
            shape((1, heads), F32),
        ],
        scratch=[
            vmem((width, 3 * width), F32),
            vmem((width, width), F32),
            vmem((1, width), F32),
            vmem((1, heads), F32),
            copies(4 * rows // 64 + 2),
        ],
        places="svvvvvvv",
        out_places="hhhh",
        operands=(place, half, other, row, row_core, row_section, row_both, bias),
    )
    return (grads[0], grads[1], grads[2][0], grads[3][0]), left_q


def across():
    sections, lats = lax.axis_size("section"), lax.axis_size("lat")
    return [
        (s * lats + i, (sections - 1 - s) * lats + (i ^ 1))
        for s in range(sections)
        for i in range(lats)
    ]


def split_two(block, axis, bit):
    mine = (lax.axis_index(axis) // bit) % 2
    pair = block.reshape(2, block.shape[0] // 2, -1)
    give = lax.dynamic_index_in_dim(pair, 1 - mine, 0, keepdims=False).astype(BF16)
    return give, lax.dynamic_index_in_dim(pair, mine, 0, keepdims=False)


def doubled(block, axis, bit):
    mine = (lax.axis_index(axis) // bit) % 2
    other = swapped(block, axis, bit)
    low = jnp.where(mine == 0, block, other)
    high = jnp.where(mine == 0, other, block)
    return jnp.concatenate([low, high], axis=0)


def scattered(block, axis):
    count = lax.axis_size(axis)
    mine = lax.axis_index(axis)
    pieces = block.reshape(count, block.shape[0] // count, -1)
    total = lax.dynamic_index_in_dim(pieces, mine, 0, keepdims=False)
    others = []
    for by in range(1, count):
        give = lax.dynamic_index_in_dim(pieces, (mine + by) % count, 0, keepdims=False)
        others.append(from_behind(give.astype(BF16), axis, by))
    for other in others:
        total = total + other.astype(F32)
    return total, others


def gathered(block, axis):
    count = lax.axis_size(axis)
    mine = lax.axis_index(axis)
    whole = jnp.zeros((count,) + block.shape, block.dtype)
    whole = lax.dynamic_update_index_in_dim(whole, block, mine, 0)
    for by in range(1, count):
        whole = lax.dynamic_update_index_in_dim(
            whole, from_behind(block, axis, by), (mine - by) % count, 0
        )
    return whole.reshape(count * block.shape[0], -1)


def sum_squares(block):
    wide = block.astype(F32)
    return jnp.sum(wide * wide)


def plain(keep, came, weight_qkv, gains, heads, entries):
    width = gains.shape[1]
    lat, lon = lax.axis_index("lat"), lax.axis_index("lon")
    part = keep + came.astype(F32)
    give, keep = split_two(part, "lat", 2)
    came = swapped(give, "lat", 2).astype(F32)
    column = lax.broadcasted_iota(jnp.int32, keep.shape, 1)
    is_bias = (column >= CUT) & (column < CUT + GROUP)
    part = jnp.where(is_bias, lax.reduce_precision(keep, 8, 7), keep) + came
    bias_part = lax.reduce_precision(part[:1, CUT : CUT + GROUP], 8, 7)
    part, others = scattered(part, "lon")
    terms = [bias_part] + [other[:1, CUT : CUT + GROUP].astype(F32) for other in others]
    terms = jnp.concatenate(terms[:1] + terms[:0:-1], axis=0)
    bias = jnp.sum(jnp.roll(terms, lon, axis=0), axis=0)[:heads]
    part = jnp.concatenate([part[:, :CUT], part[:, CUT + GROUP :]], axis=1).astype(BF16)
    half = doubled(gathered(part, "lon"), "lat", 2)
    mine = lat % 2
    weight_half = lax.dynamic_slice_in_dim(weight_qkv, mine * (width // 2), width // 2, 0)
    gain_half = lax.dynamic_slice_in_dim(gains[0], mine * (width // 2), width // 2, 0)
    weighed = half[:, : 3 * width].astype(F32) * weight_half.astype(F32)
    gain_half = jnp.sum(weighed, axis=1) / gain_half
    square = sum_squares(half) + sum_squares(gain_half) + 0.5 * sum_squares(bias)
    square = square.reshape(1)
    square = square + swapped(square, "lat", 1)
    square = square + swapped(square, "section", 1)
    factor = jnp.minimum(1.0, lax.rsqrt(square[0] / entries + 1e-06))
    grads = doubled(half, "lat", 1).astype(F32) * factor
    gain = doubled(gain_half.reshape(-1, 1), "lat", 1)[:, 0] * factor
    return (grads[:, : 3 * width], grads[:, 3 * width :], gain, bias * factor), bias


def solution(mesh):
    placed = (
        P("section", None, "lat", "lon", None),
        P("section", None, "lat", "lon", None),
        P("lat", "lon"),
        P("section", None),
        P("section", None, None),
        P("section", None, None),
        P("section", None),
    )
    return jax.shard_map(
        body,
        mesh=mesh,
        in_specs=placed,
        out_specs=(
            P("section", None, "lat", "lon", None),
            P("section", None, None),
            P("section", None, None),
            P("section", None),
            P("section", None),
        ),
        check_vma=False,
    )
```

```python
import functools

import jax
import jax.numpy as jnp
from jax import lax
from jax.experimental import pallas as pl
from jax.experimental.pallas import tpu as pltpu
from jax.sharding import PartitionSpec as P

SHIFT = 6
GROUP = 128
CUT = 1280
EPSILON = 1e-05
F32 = jnp.float32
BF16 = jnp.bfloat16


def from_behind(value, axis, by):
    count = lax.axis_size(axis)
    return lax.ppermute(value, axis, [(i, (i + by) % count) for i in range(count)])


def passed_along(block, axis, distance):
    devices = range(lax.axis_size(axis))
    route = [(i - distance, i) for i in devices if i - distance in devices]
    return lax.ppermute(block, axis, route)


def swapped(value, axis, bit):
    count = lax.axis_size(axis)
    return lax.ppermute(value, axis, [(i, i ^ bit) for i in range(count)])


def dot(left, right):
    return jnp.dot(left, right, preferred_element_type=F32)


def dot_last(left, right):
    return lax.dot_general(left, right, (((1,), (1,)), ((), ())), preferred_element_type=F32)


def call(kernel, outs, scratch=(), places="", out_places="", operands=(), flops=10**8, limit=8):
    spaces = {"v": pltpu.VMEM, "s": pltpu.SMEM, "a": pl.ANY, "h": pltpu.HBM}
    places = places or "v" * len(operands)
    out_places = out_places or "v" * len(outs)
    moved = sum(o.size * o.dtype.itemsize for o in list(outs) + list(operands))
    return pl.pallas_call(
        kernel,
        out_shape=list(outs),
        in_specs=[pl.BlockSpec(memory_space=spaces[letter]) for letter in places],
        out_specs=[pl.BlockSpec(memory_space=spaces[letter]) for letter in out_places],
        scratch_shapes=list(scratch),
        compiler_params=pltpu.CompilerParams(vmem_limit_bytes=limit * 2**20),
        cost_estimate=pl.CostEstimate(flops=flops, bytes_accessed=moved, transcendentals=0),
    )(*operands)


def started(source, target, semaphores, index):
    copy = pltpu.make_async_copy(source, target, semaphores.at[index])
    copy.start()
    return copy


def shape(dims, dtype):
    return jax.ShapeDtypeStruct(dims, dtype)


def aligned(start, size):
    return pl.ds(pl.multiple_of(start, size), size)


def position():
    lat, lon = lax.axis_index("lat"), lax.axis_index("lon")
    return lax.rem(lat, 2), lax.div(lat, 2), lon


def pack_kernel(tokens, cot, land, own, rim, tokens_v, cot_v, land_v, own32, rim32, sems):
    arrays = ((tokens, tokens_v), (cot, cot_v), (land, land_v))
    copies = [started(source, target, sems, i) for i, (source, target) in enumerate(arrays)]
    lats, cols, levels, width = tokens.shape[1:]
    half = levels * lats * SHIFT
    rim32[2 * half :, :] = jnp.zeros((rim32.shape[0] - 2 * half, width), F32)
    for which, ref in enumerate((tokens_v, cot_v)):
        copies[which].wait()
        for lat in range(lats):
            for col in range(cols):
                row = which * half + (lat * SHIFT + col % SHIFT) * levels
                part = rim32 if col < SHIFT else own32
                part[row : row + levels, :] = ref[0, lat, col].astype(F32)
    copies[2].wait()
    rim32[2 * half : 2 * half + lats, :cols] = land_v[...].astype(F32)
    own[...] = own32[...].astype(BF16)
    rim[...] = rim32[...].astype(BF16)


def unpack_kernel(own, back, grid, grid_v, sems):
    lats, cols, levels, width = grid.shape[1:]
    came = back[...].astype(F32)
    for lat in range(lats):
        for col in range(cols):
            row = (lat * SHIFT + col % SHIFT) * levels
            if col < SHIFT:
                grid_v[0, lat, col] = came[row : row + levels]
            else:
                grid_v[0, lat, col] = own[row : row + levels, :]
    started(grid_v, grid, sems, 0).wait()


def land_column(land, rows, first):
    lats, cols = land.shape
    row = lax.broadcasted_iota(jnp.int32, (rows, lats), 0)
    lat = lax.div(row, rows // lats)
    pick = (lat == lax.broadcasted_iota(jnp.int32, (rows, lats), 1)).astype(F32)
    lines = dot(pick.astype(BF16), land.astype(BF16))
    row = lax.broadcasted_iota(jnp.int32, (rows, cols), 0)
    column = lax.broadcasted_iota(jnp.int32, (rows, cols), 1)
    levels = rows // (lats * SHIFT)
    here = column == lax.rem(lax.div(row, levels), SHIFT) + first
    return jnp.sum(jnp.where(here, lines, 0.0), axis=1, keepdims=True)


def head_masks(dtype, size):
    lane = lax.broadcasted_iota(jnp.int32, (1, GROUP), 1)
    return [
        (lax.div(lane, size) == part).astype(F32).astype(dtype) for part in range(GROUP // size)
    ]


def stacked(block, masks):
    return jnp.concatenate([block * mask for mask in masks], axis=0)


def folded(block, masks):
    rows = block.shape[0] // len(masks)
    return sum(block[i * rows : (i + 1) * rows] * mask for i, mask in enumerate(masks))


def back_through(grad_out, probs, probs_b, qkv, keys_t, weight_out, grad_proj, size, land):
    count, width = grad_out.shape
    per = GROUP // size
    scale = size ** (-0.5)
    masks_b, masks = head_masks(BF16, size), head_masks(F32, size)
    att_t = dot_last(weight_out[...], grad_out)
    grad_att = att_t.T.astype(BF16)
    att_t = att_t.astype(BF16)
    lane = lax.broadcasted_iota(jnp.int32, (1, GROUP), 1)
    bias_row = jnp.zeros((1, GROUP), F32)
    for group in range(width // GROUP):
        at = group * GROUP
        values = qkv[:, 2 * width + at : 2 * width + at + GROUP]
        grad_probs = dot(stacked(values, masks_b), att_t[at : at + GROUP, :])
        scores_b, queries_t = [], []
        for part in range(per):
            head = group * per + part
            weights = probs[head * count : (head + 1) * count, :].astype(F32)
            grad_weights = grad_probs[part * count : (part + 1) * count]
            inner = jnp.sum(weights * grad_weights, axis=0, keepdims=True)
            grad_scores = weights * (grad_weights - inner)
            if land is not None:
                on_land = jnp.sum(grad_scores * land, axis=0, keepdims=True)
                on_land = jnp.sum(on_land, axis=1, keepdims=True)
                bias_row = bias_row + jnp.where(lane == head, on_land, 0.0)
            scaled_b = (grad_scores * scale).astype(BF16)
            scores_b.append(scaled_b)
            queries_t.append(dot(keys_t[head * size : (head + 1) * size, :], scaled_b))
        queries = qkv[:, at : at + GROUP]
        grad_keys = dot(jnp.concatenate(scores_b, axis=0), queries)
        mixed = probs_b[group * per * count : (group + 1) * per * count, :]
        grad_values = dot(mixed, grad_att[:, at : at + GROUP])
        grad_proj[:, at : at + GROUP] = jnp.concatenate(queries_t, axis=0).T.astype(BF16)
        grad_proj[:, width + at : width + at + GROUP] = folded(grad_keys, masks).astype(BF16)
        grad_proj[:, 2 * width + at : 2 * width + at + GROUP] = folded(grad_values, masks).astype(
            BF16
        )
    return bias_row


def through_norm(grad_proj, weight_t, gain, normed, inverse):
    scaled = dot(grad_proj, weight_t[...]) * gain
    mean = jnp.mean(scaled, axis=-1, keepdims=True)
    along = jnp.mean(scaled * normed, axis=-1, keepdims=True)
    return inverse * (scaled - mean - normed * along)


def ready_kernel(
    own_in, weight_qkv, weight_out, gain, land, bias,
    own, qkv_v, qkv_t, out_v, params,
    gain_v, land_v, bias_v, sems,
):
    arrays = (
        (weight_qkv, qkv_v), (weight_out, out_v), (gain, gain_v), (land, land_v), (bias, bias_v),
        (own_in, own),
    )
    copies = [started(source, target, sems, i) for i, (source, target) in enumerate(arrays)]
    for copy in copies[1:]:
        copy.wait()
    lats, cols = land.shape
    params[...] = jnp.zeros(params.shape, F32)
    params[0:1, :] = gain_v[...]
    params[1:2, : bias.shape[1]] = bias_v[...]
    params[8 : 8 + lats, :cols] = land_v[...].astype(F32)
    copies[0].wait()
    width = weight_qkv.shape[0]
    for part in range(weight_qkv.shape[1] // width):
        rows = slice(part * width, (part + 1) * width)
        qkv_t[rows, :] = qkv_v[:, rows].T


def forward_kernel(
    own, rim, weight_qkv, weight_t, weight_out, params,
    skip, cot, normed_t, qkv, probs_b, attended_t, extra, normed_out,
    probs, queries_t, keys_t, values_t, grad_proj,
    *, heads, lats, cols,
):
    width = params.shape[1]
    size = width // heads
    half = own.shape[0] // 2
    count = 2 * half
    per = GROUP // size
    scale = size ** (-0.5)
    masks_b = head_masks(BF16, size)
    mine = own[...].astype(F32)
    came = rim[...].astype(F32)
    gain = params[0:1, :]
    values = jnp.concatenate([mine[:half], came[:half]], axis=0)
    centred = values - jnp.mean(values, axis=-1, keepdims=True)
    inverse = lax.rsqrt(jnp.mean(centred * centred, axis=-1, keepdims=True) + EPSILON)
    normed = centred * inverse
    normed_out[...] = normed
    normed_b = (normed * gain).astype(BF16)
    normed_t[...] = normed_b.T
    land = jnp.concatenate(
        [
            land_column(params[8 : 8 + lats, :cols], half, SHIFT),
            land_column(came[2 * half : 2 * half + lats, :cols], half, 0),
        ],
        axis=0,
    )
    extra[:, :GROUP] = jnp.broadcast_to(land, (count, GROUP))
    extra[:, GROUP:] = jnp.broadcast_to(inverse, (count, GROUP))
    for part, turned in enumerate((queries_t, keys_t, values_t)):
        columns = slice(part * width, (part + 1) * width)
        qkv[:, columns] = dot(normed_b, weight_qkv[:, columns]).astype(BF16)
        turned[...] = qkv[:, columns].T
    for group in range(width // GROUP):
        at = group * GROUP
        keys = qkv[:, width + at : width + at + GROUP]
        scores = dot(stacked(keys, masks_b), queries_t[at : at + GROUP, :])
        for part in range(per):
            head = group * per + part
            block = scores[part * count : (part + 1) * count] * scale
            block = block + params[1:2, head : head + 1] * land
            block = jnp.exp(block - jnp.max(block, axis=0, keepdims=True))
            weights = block * (1.0 / jnp.sum(block, axis=0, keepdims=True))
            probs[head * count : (head + 1) * count, :] = weights
            weights_b = weights.astype(BF16)
            probs_b[head * count : (head + 1) * count, :] = weights_b
            out = dot(values_t[head * size : (head + 1) * size, :], weights_b)
            attended_t[head * size : (head + 1) * size, :] = out.astype(BF16)
    grad_out = jnp.concatenate([mine[half:], came[half : 2 * half]], axis=0)
    cot[...] = grad_out.astype(BF16)
    back_through(cot[...], probs, probs_b, qkv, keys_t, weight_out, grad_proj, size, None)
    skip[...] = (
        through_norm(grad_proj[...], weight_t, gain, normed, inverse) + grad_out
    ).astype(BF16)


def backward_kernel(
    skip, cot, qkv, probs, weight_out, extra, normed_t, attended_t,
    total_out, grad_proj, bias_out, give,
    keys_t,
    *, heads,
):
    count, width = cot.shape
    core, _, _ = position()
    total_out[...] = (cot[...].astype(F32) + skip[...].astype(F32)).astype(BF16)
    keys_t[...] = qkv[:, width : 2 * width].T
    bias_row = back_through(
        total_out[...], probs, probs, qkv, keys_t, weight_out, grad_proj, width // heads,
        extra[:, :1],
    )
    bias_out[...] = jnp.broadcast_to(bias_row, bias_out.shape)
    half = width // 2
    rows = aligned((1 - core) * half, half)
    weight_rows(rows, normed_t, attended_t, grad_proj, total_out, bias_row, give)


def weight_rows(rows, normed_t, attended_t, grad_proj, total, bias_row, out):
    tokens = normed_t[rows, :]
    three = grad_proj.shape[1]
    out[:, :CUT] = dot(tokens, grad_proj[:, :CUT]).astype(out.dtype)
    out[:, CUT : CUT + GROUP] = jnp.broadcast_to(bias_row, (out.shape[0], GROUP)).astype(out.dtype)
    out[:, CUT + GROUP : three + GROUP] = dot(tokens, grad_proj[:, CUT:]).astype(out.dtype)
    out[:, three + GROUP :] = dot(attended_t[rows, :], total[...]).astype(out.dtype)


def finish_kernel(
    total, grad_proj, bias_row, normed_t, attended_t, normed, extra, weight_t, params,
    keep, own, back,
):
    count, width = total.shape
    half = width // 2
    core, _, _ = position()
    rows = aligned(core * half, half)
    bias_b = bias_row[:1, :].astype(BF16).astype(F32)
    weight_rows(rows, normed_t, attended_t, grad_proj, total, bias_b, keep)
    inverse = extra[:, GROUP : GROUP + 1]
    final = through_norm(grad_proj[...], weight_t, params[0:1, :], normed[...], inverse)
    final = final + total[...].astype(F32)
    own[...] = final[: count // 2]
    back[...] = final[count // 2 :].astype(BF16)


def first_kernel(keep, came, give_p, kept_p, kept_q, *rest):
    _, y, z = position()
    *give_q, total = rest
    wide_p = give_p.shape[1]
    half = keep.shape[0] // 2
    total[...] = keep[...] + came[...].astype(F32)
    give_p[...] = total[aligned((1 - y) * half, half), :wide_p].astype(BF16)
    mine = aligned(y * half, half)
    kept_p[:, :CUT] = total[mine, :CUT]
    kept_p[:, CUT:] = total[mine, CUT:wide_p].astype(BF16).astype(F32)
    piece = kept_q.shape[0]
    kept_q[...] = total[aligned(z * piece, piece), wide_p:]
    for other, ref in enumerate(give_q, 1):
        ref[...] = total[aligned((z ^ other) * piece, piece), wide_p:].astype(BF16)


def second_kernel(after, kept_p, came_p, kept_q, *rest):
    _, y, z = position()
    count = (len(rest) - 5) // 2
    came_q, (give_q, left_q, left_p) = rest[:count], rest[count : count + 3]
    *give_p, total_p, total_q = rest[count + 3 :]
    total_p[...] = kept_p[...] + came_p[...].astype(F32)
    piece = left_p.shape[0]
    mine = aligned(z * piece, piece)
    left_p[:, :CUT] = total_p[mine, :CUT]
    left_p[:, CUT:] = total_p[mine, CUT:].astype(BF16).astype(F32)
    for other, ref in enumerate(give_p, 1):
        ref[...] = total_p[aligned((z ^ other) * piece, piece), :].astype(BF16)
    total = kept_q[...]
    for ref in came_q:
        total = total + ref[...].astype(F32)
    total_q[...] = total
    half = give_q.shape[0]
    give_q[...] = total_q[aligned((1 - y) * half, half), :].astype(BF16)
    left_q[...] = total_q[aligned(y * half, half), :]


def third_kernel(left_p, left_q, came_q, *rest):
    _, _, z = position()
    *came_p, piece_p, piece_q, bias = rest
    total = left_p[:, :CUT]
    for ref in came_p:
        total = total + ref[:, :CUT].astype(F32)
    piece_p[...] = total.astype(BF16)
    piece_q[...] = (left_q[...] + came_q[...].astype(F32)).astype(BF16)
    terms = [left_p[:8, CUT:]] + [ref[...].astype(F32)[:8, CUT:] for ref in came_p]
    total = jnp.zeros_like(terms[0])
    for source in range(len(terms)):
        for other, term in enumerate(terms):
            total = total + jnp.where((z ^ other) == source, term, 0.0)
    bias[...] = total


def fourth_kernel(piece_q, other_q, *rest):
    _, y, z = position()
    *parts_p, block_p, block_q = rest
    piece = parts_p[0].shape[0]
    for other, part in enumerate(parts_p):
        block_p[aligned((z ^ other) * piece, piece), :] = part[...]
    piece = piece_q.shape[0]
    block_q[aligned(y * piece, piece), :] = piece_q[...]
    block_q[aligned((1 - y) * piece, piece), :] = other_q[...]


def fifth_kernel(weight_qkv, params, bias, block_p, other_p, *rest):
    *parts_q, half, row = rest
    core, y, z = position()
    rows = half.shape[0]
    mine = aligned(core * rows, rows)
    piece = block_p.shape[0]
    half[aligned(y * piece, piece), :CUT] = block_p[...]
    half[aligned((1 - y) * piece, piece), :CUT] = other_p[...]
    piece = parts_q[0].shape[0]
    for other, part in enumerate(parts_q):
        half[aligned((z ^ other) * piece, piece), CUT:] = part[...]
    three = weight_qkv.shape[1]
    wide = half[:, :three].astype(F32)
    gain_half = jnp.sum(wide * weight_qkv[mine, :].astype(F32), axis=1, keepdims=True)
    gain_half = jnp.broadcast_to(gain_half, (rows, GROUP)).T[:8]
    own_gain = jnp.where(core == 0, params[0:1, :rows], params[0:1, rows:])
    gain_half = gain_half / own_gain
    out = half[:, three:].astype(F32)
    square = jnp.sum(jnp.sum(wide * wide, axis=0, keepdims=True), axis=1, keepdims=True)
    square = square + jnp.sum(jnp.sum(out * out, axis=0, keepdims=True), axis=1, keepdims=True)
    square = square + jnp.sum(gain_half[:1] * gain_half[:1], axis=1, keepdims=True)
    square = square + 0.5 * jnp.sum(bias[:1, :] * bias[:1, :], axis=1, keepdims=True)
    row[:, :rows] = gain_half
    row[:, rows:] = jnp.broadcast_to(square, (8, GROUP))


def last_kernel(
    half, other, row, row_core, row_section, row_both, bias,
    grad_qkv, grad_out, grad_gain, grad_bias,
    qkv_v, out_v, gain_v, bias_v, sems,
    *, entries,
):
    core, _, _ = position()
    rows, three = half.shape[0], grad_qkv.shape[1]
    square = row[:1, rows : rows + 1] + row_core[:1, rows : rows + 1]
    square = square + (row_section[:1, rows : rows + 1] + row_both[:1, rows : rows + 1])
    factor = jnp.minimum(1.0, lax.rsqrt(square / entries + 1e-06))
    sent = []
    piece = 64
    for which, ref in enumerate((half, other)):
        base = core * rows if which == 0 else (1 - core) * rows
        for part in range(rows // piece):
            here = slice(part * piece, (part + 1) * piece)
            at = aligned(base + part * piece, piece)
            slot = slice(which * rows + part * piece, which * rows + (part + 1) * piece)
            qkv_v[slot, :] = ref[here, :three].astype(F32) * factor
            sent.append(started(qkv_v.at[slot, :], grad_qkv.at[at, :], sems, len(sent)))
            out_v[slot, :] = ref[here, three:].astype(F32) * factor
            sent.append(started(out_v.at[slot, :], grad_out.at[at, :], sems, len(sent)))
    mine, its = row[:1, :rows] * factor, row_core[:1, :rows] * factor
    gain_v[:, :rows] = jnp.where(core == 0, mine, its)
    gain_v[:, rows:] = jnp.where(core == 0, its, mine)
    bias_v[...] = bias[:1, : bias_v.shape[1]] * factor
    sent.append(started(gain_v, grad_gain, sems, len(sent)))
    sent.append(started(bias_v, grad_bias, sems, len(sent)))
    for copy in sent:
        copy.wait()


def sent_round(pieces, axis):
    return [swapped(piece, axis, other) for other, piece in enumerate(pieces, 1)]


def vmem(dims, dtype):
    return pltpu.VMEM(dims, dtype)


def copies(number):
    return pltpu.SemaphoreType.DMA((number,))


def body(inputs, cotangent, land_sea, gains, qkv_weight, out_weight, land_bias):
    weight_qkv, weight_out = qkv_weight[0], out_weight[0]
    levels, lats, cols, width = inputs.shape[1:]
    heads = land_bias.shape[1]
    half = levels * lats * SHIFT
    count = 2 * half
    packed = half * 2 + 16
    lons = lax.axis_size("lon")

    tokens = inputs.transpose(0, 2, 3, 1, 4)
    own_cot = cotangent.transpose(0, 2, 3, 1, 4)

    own, rim = call(
        pack_kernel,
        [shape((2 * half, width), BF16), shape((packed, width), BF16)],
        scratch=[
            vmem(tokens.shape, BF16),
            vmem(tokens.shape, BF16),
            vmem(land_sea.shape, jnp.int32),
            vmem((2 * half, width), F32),
            vmem((packed, width), F32),
            copies(3),
        ],
        places="hhh",
        operands=(tokens, own_cot, land_sea),
        limit=60,
    )
    rim = from_behind(rim, "lon", -1)
    own, qkv_v, qkv_t, out_v, params = call(
        ready_kernel,
        [
            shape(own.shape, BF16),
            shape(weight_qkv.shape, BF16),
            shape(weight_qkv.shape[::-1], BF16),
            shape(weight_out.shape, BF16),
            shape((16, width), F32),
        ],
        scratch=[
            vmem(gains.shape, F32),
            vmem(land_sea.shape, jnp.int32),
            vmem(land_bias.shape, F32),
            copies(6),
        ],
        places="hhhhhh",
        operands=(own, weight_qkv, weight_out, gains, land_sea, land_bias),
        limit=48,
    )
    skip, cot, normed_t, qkv, probs, attended_t, extra, normed = call(
        functools.partial(forward_kernel, heads=heads, lats=lats, cols=cols),
        [
            shape((count, width), BF16),
            shape((count, width), BF16),
            shape((width, count), BF16),
            shape((count, 3 * width), BF16),
            shape((heads * count, count), BF16),
            shape((width, count), BF16),
            shape((count, 2 * GROUP), F32),
            shape((count, width), F32),
        ],
        scratch=[
            vmem((heads * count, count), F32),
            vmem((width, count), BF16),
            vmem((width, count), BF16),
            vmem((width, count), BF16),
            vmem((count, 3 * width), BF16),
        ],
        operands=(own, rim, qkv_v, qkv_t, out_v, params),
        flops=10**9,
        limit=16,
    )
    skip = passed_along(skip, "section", -1)
    rows, wide = width // 2, 4 * width + GROUP
    total, grad_proj, bias_row, give = call(
        functools.partial(backward_kernel, heads=heads),
        [
            shape((count, width), BF16),
            shape((count, 3 * width), BF16),
            shape((8, GROUP), F32),
            shape((rows, wide), BF16),
        ],
        scratch=[vmem((width, count), BF16)],
        operands=(skip, cot, qkv, probs, out_v, extra, normed_t, attended_t),
        flops=10**9,
    )
    came = swapped(give, "lat", 1)
    keep, own_grad, back = call(
        finish_kernel,
        [
            shape((rows, wide), F32),
            shape((half, width), F32),
            shape((half, width), BF16),
        ],
        operands=(
            total, grad_proj, bias_row, normed_t, attended_t, normed, extra, qkv_t, params,
        ),
        flops=5 * 10**8,
    )
    back = from_behind(back, "lon", 1)
    entries = 2 * (4 * width * width + width + heads)
    if rows // 2 // lons % 16 == 0 and lons & (lons - 1) == 0:
        grads = staged(keep, came, back, qkv_v, params, lons, heads, entries)
    else:
        grads = plain(keep, came, weight_qkv, gains, heads, entries)
    (final_grad,) = call(
        unpack_kernel,
        [shape(tokens.shape, F32)],
        scratch=[vmem(tokens.shape, F32), copies(1)],
        out_places="h",
        operands=(own_grad, back),
    )
    final_grad = final_grad.transpose(0, 3, 1, 2, 4)
    return (final_grad, *(grad[None] for grad in grads))


def staged(keep, came, after, weight_qkv, params, lons, heads, entries):
    rows, wide = keep.shape
    width = 2 * rows
    wide_p = CUT + GROUP
    wide_q = wide - wide_p
    some = range(lons - 1)
    several = "v" * len(some)
    give_p, kept_p, kept_q, *give_q = call(
        first_kernel,
        [
            shape((rows // 2, wide_p), BF16),
            shape((rows // 2, wide_p), F32),
            shape((rows // lons, wide_q), F32),
            *(shape((rows // lons, wide_q), BF16) for _ in some),
        ],
        scratch=[vmem((rows, wide), F32)],
        operands=(keep, came),
    )
    came_p = swapped(give_p, "lat", 2)
    came_q = sent_round(give_q, "lon")
    piece = rows // 2 // lons
    give_q, left_q, left_p, *give_p = call(
        second_kernel,
        [
            shape((piece, wide_q), BF16),
            shape((piece, wide_q), F32),
            shape((piece, wide_p), F32),
            *(shape((piece, wide_p), BF16) for _ in some),
        ],
        scratch=[vmem((rows // 2, wide_p), F32), vmem((rows // lons, wide_q), F32)],
        places="avvv" + several,
        operands=(after, kept_p, came_p, kept_q, *came_q),
    )
    came_p = sent_round(give_p, "lon")
    came_q = swapped(give_q, "lat", 2)
    piece_p, piece_q, bias = call(
        third_kernel,
        [
            shape((piece, CUT), BF16),
            shape((piece, wide_q), BF16),
            shape((8, GROUP), F32),
        ],
        operands=(left_p, left_q, came_q, *came_p),
    )
    others_p = sent_round([piece_p for _ in some], "lon")
    other_q = swapped(piece_q, "lat", 2)
    block_p, block_q = call(
        fourth_kernel,
        [shape((rows // 2, CUT), BF16), shape((rows // lons, wide_q), BF16)],
        operands=(piece_q, other_q, piece_p, *others_p),
    )
    other_p = swapped(block_p, "lat", 2)
    others_q = sent_round([block_q for _ in some], "lon")
    half, row = call(
        fifth_kernel,
        [shape((rows, 4 * width), BF16), shape((8, rows + GROUP), F32)],
        operands=(weight_qkv, params, bias, block_p, other_p, block_q, *others_q),
    )
    row_section = swapped(row, "section", 1)
    row_both = lax.ppermute(row, ("section", "lat"), across())
    row_core = swapped(row, "lat", 1)
    other = swapped(half, "lat", 1)
    grads = call(
        functools.partial(last_kernel, entries=entries),
        [
            shape((width, 3 * width), F32),
            shape((width, width), F32),
            shape((1, width), F32),
            shape((1, heads), F32),
        ],
        scratch=[
            vmem((width, 3 * width), F32),
            vmem((width, width), F32),
            vmem((1, width), F32),
            vmem((1, heads), F32),
            copies(4 * rows // 64 + 2),
        ],
        out_places="hhhh",
        operands=(half, other, row, row_core, row_section, row_both, bias),
    )
    return grads[0], grads[1], grads[2][0], grads[3][0]


def across():
    sections, lats = lax.axis_size("section"), lax.axis_size("lat")
    return [
        (s * lats + i, (sections - 1 - s) * lats + (i ^ 1))
        for s in range(sections)
        for i in range(lats)
    ]


def split_two(block, axis, bit):
    mine = (lax.axis_index(axis) // bit) % 2
    pair = block.reshape(2, block.shape[0] // 2, -1)
    give = lax.dynamic_index_in_dim(pair, 1 - mine, 0, keepdims=False).astype(BF16)
    return give, lax.dynamic_index_in_dim(pair, mine, 0, keepdims=False)


def doubled(block, axis, bit):
    mine = (lax.axis_index(axis) // bit) % 2
    other = swapped(block, axis, bit)
    low = jnp.where(mine == 0, block, other)
    high = jnp.where(mine == 0, other, block)
    return jnp.concatenate([low, high], axis=0)


def scattered(block, axis):
    count = lax.axis_size(axis)
    mine = lax.axis_index(axis)
    pieces = block.reshape(count, block.shape[0] // count, -1)
    total = lax.dynamic_index_in_dim(pieces, mine, 0, keepdims=False)
    others = []
    for by in range(1, count):
        give = lax.dynamic_index_in_dim(pieces, (mine + by) % count, 0, keepdims=False)
        others.append(from_behind(give.astype(BF16), axis, by))
    for other in others:
        total = total + other.astype(F32)
    return total, others


def gathered(block, axis):
    count = lax.axis_size(axis)
    mine = lax.axis_index(axis)
    whole = jnp.zeros((count,) + block.shape, block.dtype)
    whole = lax.dynamic_update_index_in_dim(whole, block, mine, 0)
    for by in range(1, count):
        whole = lax.dynamic_update_index_in_dim(
            whole, from_behind(block, axis, by), (mine - by) % count, 0
        )
    return whole.reshape(count * block.shape[0], -1)


def sum_squares(block):
    wide = block.astype(F32)
    return jnp.sum(wide * wide)


def plain(keep, came, weight_qkv, gains, heads, entries):
    width = gains.shape[1]
    lat, lon = lax.axis_index("lat"), lax.axis_index("lon")
    part = keep + came.astype(F32)
    give, keep = split_two(part, "lat", 2)
    came = swapped(give, "lat", 2).astype(F32)
    column = lax.broadcasted_iota(jnp.int32, keep.shape, 1)
    is_bias = (column >= CUT) & (column < CUT + GROUP)
    part = jnp.where(is_bias, lax.reduce_precision(keep, 8, 7), keep) + came
    bias_part = lax.reduce_precision(part[:1, CUT : CUT + GROUP], 8, 7)
    part, others = scattered(part, "lon")
    terms = [bias_part] + [other[:1, CUT : CUT + GROUP].astype(F32) for other in others]
    terms = jnp.concatenate(terms[:1] + terms[:0:-1], axis=0)
    bias = jnp.sum(jnp.roll(terms, lon, axis=0), axis=0)[:heads]
    part = jnp.concatenate([part[:, :CUT], part[:, CUT + GROUP :]], axis=1).astype(BF16)
    half = doubled(gathered(part, "lon"), "lat", 2)
    mine = lat % 2
    weight_half = lax.dynamic_slice_in_dim(weight_qkv, mine * (width // 2), width // 2, 0)
    gain_half = lax.dynamic_slice_in_dim(gains[0], mine * (width // 2), width // 2, 0)
    weighed = half[:, : 3 * width].astype(F32) * weight_half.astype(F32)
    gain_half = jnp.sum(weighed, axis=1) / gain_half
    square = sum_squares(half) + sum_squares(gain_half) + 0.5 * sum_squares(bias)
    square = square.reshape(1)
    square = square + swapped(square, "lat", 1)
    square = square + swapped(square, "section", 1)
    factor = jnp.minimum(1.0, lax.rsqrt(square[0] / entries + 1e-06))
    grads = doubled(half, "lat", 1).astype(F32) * factor
    gain = doubled(gain_half.reshape(-1, 1), "lat", 1)[:, 0] * factor
    return grads[:, : 3 * width], grads[:, 3 * width :], gain, bias * factor


def solution(mesh):
    placed = (
        P("section", None, "lat", "lon", None),
        P("section", None, "lat", "lon", None),
        P("lat", "lon"),
        P("section", None),
        P("section", None, None),
        P("section", None, None),
        P("section", None),
    )
    return jax.shard_map(
        body,
        mesh=mesh,
        in_specs=placed,
        out_specs=(
            P("section", None, "lat", "lon", None),
            P("section", None, None),
            P("section", None, None),
            P("section", None),
            P("section", None),
        ),
        check_vma=False,
    )
```

```python
import functools

import jax
import jax.numpy as jnp
from jax import lax
from jax.experimental import pallas as pl
from jax.experimental.pallas import tpu as pltpu
from jax.sharding import PartitionSpec as P

SHIFT = 6
GROUP = 128
CUT = 1408
EPSILON = 1e-05
F32 = jnp.float32
BF16 = jnp.bfloat16


def from_behind(value, axis, by):
    count = lax.axis_size(axis)
    return lax.ppermute(value, axis, [(i, (i + by) % count) for i in range(count)])


def passed_along(block, axis, distance):
    devices = range(lax.axis_size(axis))
    route = [(i - distance, i) for i in devices if i - distance in devices]
    return lax.ppermute(block, axis, route)


def swapped(value, axis, bit):
    count = lax.axis_size(axis)
    return lax.ppermute(value, axis, [(i, i ^ bit) for i in range(count)])


def dot(left, right):
    return jnp.dot(left, right, preferred_element_type=F32)


def dot_last(left, right):
    return lax.dot_general(left, right, (((1,), (1,)), ((), ())), preferred_element_type=F32)


def call(kernel, outs, scratch=(), places="", out_places="", operands=(), flops=10**8, limit=8):
    spaces = {"v": pltpu.VMEM, "s": pltpu.SMEM, "a": pl.ANY, "h": pltpu.HBM}
    places = places or "v" * len(operands)
    out_places = out_places or "v" * len(outs)
    moved = sum(o.size * o.dtype.itemsize for o in list(outs) + list(operands))
    return pl.pallas_call(
        kernel,
        out_shape=list(outs),
        in_specs=[pl.BlockSpec(memory_space=spaces[letter]) for letter in places],
        out_specs=[pl.BlockSpec(memory_space=spaces[letter]) for letter in out_places],
        scratch_shapes=list(scratch),
        compiler_params=pltpu.CompilerParams(vmem_limit_bytes=limit * 2**20),
        cost_estimate=pl.CostEstimate(flops=flops, bytes_accessed=moved, transcendentals=0),
    )(*operands)


def started(source, target, semaphores, index):
    copy = pltpu.make_async_copy(source, target, semaphores.at[index])
    copy.start()
    return copy


def shape(dims, dtype):
    return jax.ShapeDtypeStruct(dims, dtype)


def aligned(start, size):
    return pl.ds(pl.multiple_of(start, size), size)


def position():
    lat, lon = lax.axis_index("lat"), lax.axis_index("lon")
    return lax.rem(lat, 2), lax.div(lat, 2), lon


def pack_kernel(
    tokens, cot, land, gain, bias, own, rim,
    tokens_v, cot_v, land_v, gain_v, bias_v, rim32, sems,
):
    arrays = ((tokens, tokens_v), (cot, cot_v), (land, land_v), (gain, gain_v), (bias, bias_v))
    copies = [started(source, target, sems, i) for i, (source, target) in enumerate(arrays)]
    lats, cols, levels, width = tokens.shape[1:]
    half = levels * lats * SHIFT
    rim32[2 * half :, :] = jnp.zeros((rim32.shape[0] - 2 * half, width), F32)
    own[2 * half :, :] = jnp.zeros((own.shape[0] - 2 * half, width), F32)
    for which, ref in enumerate((tokens_v, cot_v)):
        copies[which].wait()
        for lat in range(lats):
            for col in range(cols):
                row = which * half + (lat * SHIFT + col % SHIFT) * levels
                part = rim32 if col < SHIFT else own
                part[row : row + levels, :] = ref[0, lat, col].astype(F32)
    for copy in copies[2:]:
        copy.wait()
    rim32[2 * half : 2 * half + lats, :cols] = land_v[...].astype(F32)
    own[2 * half : 2 * half + 1, :] = gain_v[...]
    own[2 * half + 1 : 2 * half + 2, : bias.shape[1]] = bias_v[...]
    own[2 * half + 8 : 2 * half + 8 + lats, :cols] = land_v[...].astype(F32)
    rim[...] = rim32[...].astype(BF16)


def unpack_kernel(own, back, grid, grid_v, sems):
    lats, cols, levels, width = grid.shape[1:]
    came = back[...].astype(F32)
    for lat in range(lats):
        for col in range(cols):
            row = (lat * SHIFT + col % SHIFT) * levels
            if col < SHIFT:
                grid_v[0, lat, col] = came[row : row + levels]
            else:
                grid_v[0, lat, col] = own[row : row + levels, :]
    started(grid_v, grid, sems, 0).wait()


def land_column(land, rows, first):
    lats, cols = land.shape
    row = lax.broadcasted_iota(jnp.int32, (rows, lats), 0)
    lat = lax.div(row, rows // lats)
    pick = (lat == lax.broadcasted_iota(jnp.int32, (rows, lats), 1)).astype(F32)
    lines = dot(pick.astype(BF16), land.astype(BF16))
    row = lax.broadcasted_iota(jnp.int32, (rows, cols), 0)
    column = lax.broadcasted_iota(jnp.int32, (rows, cols), 1)
    levels = rows // (lats * SHIFT)
    here = column == lax.rem(lax.div(row, levels), SHIFT) + first
    return jnp.sum(jnp.where(here, lines, 0.0), axis=1, keepdims=True)


def head_masks(dtype, size):
    lane = lax.broadcasted_iota(jnp.int32, (1, GROUP), 1)
    return [
        (lax.div(lane, size) == part).astype(F32).astype(dtype) for part in range(GROUP // size)
    ]


def stacked(block, masks):
    return jnp.concatenate([block * mask for mask in masks], axis=0)


def folded(block, masks):
    rows = block.shape[0] // len(masks)
    return sum(block[i * rows : (i + 1) * rows] * mask for i, mask in enumerate(masks))


def back_through(grad_out, probs, probs_b, qkv, keys_t, weight_out, grad_proj, size, land):
    count, width = grad_out.shape
    per = GROUP // size
    scale = size ** (-0.5)
    masks_b, masks = head_masks(BF16, size), head_masks(F32, size)
    att_t = dot_last(weight_out[...], grad_out)
    grad_att = att_t.T.astype(BF16)
    att_t = att_t.astype(BF16)
    lane = lax.broadcasted_iota(jnp.int32, (1, GROUP), 1)
    bias_row = jnp.zeros((1, GROUP), F32)
    for group in range(width // GROUP):
        at = group * GROUP
        values = qkv[:, 2 * width + at : 2 * width + at + GROUP]
        grad_probs = dot(stacked(values, masks_b), att_t[at : at + GROUP, :])
        scores_b, queries_t = [], []
        for part in range(per):
            head = group * per + part
            weights = probs[head * count : (head + 1) * count, :].astype(F32)
            grad_weights = grad_probs[part * count : (part + 1) * count]
            inner = jnp.sum(weights * grad_weights, axis=0, keepdims=True)
            grad_scores = weights * (grad_weights - inner)
            if land is not None:
                on_land = jnp.sum(grad_scores * land, axis=0, keepdims=True)
                on_land = jnp.sum(on_land, axis=1, keepdims=True)
                bias_row = bias_row + jnp.where(lane == head, on_land, 0.0)
            scaled_b = (grad_scores * scale).astype(BF16)
            scores_b.append(scaled_b)
            queries_t.append(dot(keys_t[head * size : (head + 1) * size, :], scaled_b))
        queries = qkv[:, at : at + GROUP]
        grad_keys = dot(jnp.concatenate(scores_b, axis=0), queries)
        mixed = probs_b[group * per * count : (group + 1) * per * count, :]
        grad_values = dot(mixed, grad_att[:, at : at + GROUP])
        grad_proj[:, at : at + GROUP] = jnp.concatenate(queries_t, axis=0).T.astype(BF16)
        grad_proj[:, width + at : width + at + GROUP] = folded(grad_keys, masks).astype(BF16)
        grad_proj[:, 2 * width + at : 2 * width + at + GROUP] = folded(grad_values, masks).astype(
            BF16
        )
    return bias_row


def through_norm(grad_proj, weight_t, gain, normed, inverse):
    scaled = dot(grad_proj, weight_t[...]) * gain
    mean = jnp.mean(scaled, axis=-1, keepdims=True)
    along = jnp.mean(scaled * normed, axis=-1, keepdims=True)
    return inverse * (scaled - mean - normed * along)


def ready_kernel(after, weight_qkv, weight_out, qkv_v, qkv_t, out_v, sems):
    copies = [
        started(weight_qkv, qkv_v, sems, 0),
        started(weight_out, out_v, sems, 1),
    ]
    copies[0].wait()
    width = weight_qkv.shape[0]
    for part in range(weight_qkv.shape[1] // width):
        rows = slice(part * width, (part + 1) * width)
        qkv_t[rows, :] = qkv_v[:, rows].T
    copies[1].wait()


def forward_kernel(
    own, rim, weight_qkv, weight_t, weight_out,
    skip, cot, normed_t, qkv, probs_b, attended_t, extra, normed_out,
    probs, queries_t, keys_t, values_t, grad_proj,
    *, heads, lats, cols,
):
    width = own.shape[1]
    size = width // heads
    half = cot.shape[0] // 2
    count = 2 * half
    per = GROUP // size
    scale = size ** (-0.5)
    masks_b = head_masks(BF16, size)
    mine = own[: 2 * half, :]
    params = own[2 * half :, :]
    came = rim[...].astype(F32)
    gain = params[0:1, :]
    values = jnp.concatenate([mine[:half], came[:half]], axis=0)
    centred = values - jnp.mean(values, axis=-1, keepdims=True)
    inverse = lax.rsqrt(jnp.mean(centred * centred, axis=-1, keepdims=True) + EPSILON)
    normed = centred * inverse
    normed_out[...] = normed
    normed_b = (normed * gain).astype(BF16)
    normed_t[...] = normed_b.T
    land = jnp.concatenate(
        [
            land_column(params[8 : 8 + lats, :cols], half, SHIFT),
            land_column(came[2 * half : 2 * half + lats, :cols], half, 0),
        ],
        axis=0,
    )
    extra[:, :GROUP] = jnp.broadcast_to(land, (count, GROUP))
    extra[:, GROUP:] = jnp.broadcast_to(inverse, (count, GROUP))
    for part, turned in enumerate((queries_t, keys_t, values_t)):
        columns = slice(part * width, (part + 1) * width)
        qkv[:, columns] = dot(normed_b, weight_qkv[:, columns]).astype(BF16)
        turned[...] = qkv[:, columns].T
    for group in range(width // GROUP):
        at = group * GROUP
        keys = qkv[:, width + at : width + at + GROUP]
        scores = dot(stacked(keys, masks_b), queries_t[at : at + GROUP, :])
        for part in range(per):
            head = group * per + part
            block = scores[part * count : (part + 1) * count] * scale
            block = block + params[1:2, head : head + 1] * land
            block = jnp.exp(block - jnp.max(block, axis=0, keepdims=True))
            weights = block * (1.0 / jnp.sum(block, axis=0, keepdims=True))
            probs[head * count : (head + 1) * count, :] = weights
            weights_b = weights.astype(BF16)
            probs_b[head * count : (head + 1) * count, :] = weights_b
            out = dot(values_t[head * size : (head + 1) * size, :], weights_b)
            attended_t[head * size : (head + 1) * size, :] = out.astype(BF16)
    grad_out = jnp.concatenate([mine[half:], came[half : 2 * half]], axis=0)
    cot[...] = grad_out.astype(BF16)
    back_through(cot[...], probs, probs_b, qkv, keys_t, weight_out, grad_proj, size, None)
    skip[...] = (
        through_norm(grad_proj[...], weight_t, gain, normed, inverse) + grad_out
    ).astype(BF16)


def backward_kernel(
    skip, cot, qkv, probs, weight_out, extra, normed_t, attended_t,
    total_out, grad_proj, bias_out, give,
    keys_t,
    *, heads,
):
    count, width = cot.shape
    core, _, _ = position()
    total_out[...] = (cot[...].astype(F32) + skip[...].astype(F32)).astype(BF16)
    keys_t[...] = qkv[:, width : 2 * width].T
    bias_row = back_through(
        total_out[...], probs, probs, qkv, keys_t, weight_out, grad_proj, width // heads,
        extra[:, :1],
    )
    bias_out[...] = jnp.broadcast_to(bias_row, bias_out.shape)
    half = width // 2
    rows = aligned((1 - core) * half, half)
    weight_rows(rows, normed_t, attended_t, grad_proj, total_out, bias_row, give)


def weight_rows(rows, normed_t, attended_t, grad_proj, total, bias_row, out):
    tokens = normed_t[rows, :]
    three = grad_proj.shape[1]
    out[:, :CUT] = dot(tokens, grad_proj[:, :CUT]).astype(out.dtype)
    out[:, CUT : CUT + GROUP] = jnp.broadcast_to(bias_row, (out.shape[0], GROUP)).astype(out.dtype)
    out[:, CUT + GROUP : three + GROUP] = dot(tokens, grad_proj[:, CUT:]).astype(out.dtype)
    out[:, three + GROUP :] = dot(attended_t[rows, :], total[...]).astype(out.dtype)


def finish_kernel(
    total, grad_proj, bias_row, normed_t, attended_t, normed, extra, weight_t, params,
    keep, own, back,
):
    count, width = total.shape
    half = width // 2
    core, _, _ = position()
    rows = aligned(core * half, half)
    bias_b = bias_row[:1, :].astype(BF16).astype(F32)
    weight_rows(rows, normed_t, attended_t, grad_proj, total, bias_b, keep)
    inverse = extra[:, GROUP : GROUP + 1]
    final = through_norm(grad_proj[...], weight_t, params[count : count + 1, :], normed[...], inverse)
    final = final + total[...].astype(F32)
    own[...] = final[: count // 2]
    back[...] = final[count // 2 :].astype(BF16)


def first_kernel(keep, came, give_p, kept_p, kept_q, *rest):
    _, y, z = position()
    *give_q, total = rest
    wide_p = give_p.shape[1]
    half = keep.shape[0] // 2
    total[...] = keep[...] + came[...].astype(F32)
    give_p[...] = total[aligned((1 - y) * half, half), :wide_p].astype(BF16)
    mine = aligned(y * half, half)
    kept_p[:, :CUT] = total[mine, :CUT]
    kept_p[:, CUT:] = total[mine, CUT:wide_p].astype(BF16).astype(F32)
    piece = kept_q.shape[0]
    kept_q[...] = total[aligned(z * piece, piece), wide_p:]
    for other, ref in zip(range(len(give_q), 0, -1), give_q):
        ref[...] = total[aligned((z ^ other) * piece, piece), wide_p:].astype(BF16)


def second_kernel(after, kept_p, came_p, kept_q, *rest):
    _, y, z = position()
    count = (len(rest) - 5) // 2
    came_q, (give_q, left_q, left_p) = rest[:count], rest[count : count + 3]
    *give_p, total_p, total_q = rest[count + 3 :]
    total_p[...] = kept_p[...] + came_p[...].astype(F32)
    piece = left_p.shape[0]
    mine = aligned(z * piece, piece)
    left_p[:, :CUT] = total_p[mine, :CUT]
    left_p[:, CUT:] = total_p[mine, CUT:].astype(BF16).astype(F32)
    for other, ref in zip(range(len(give_p), 0, -1), give_p):
        ref[...] = total_p[aligned((z ^ other) * piece, piece), :].astype(BF16)
    total = kept_q[...]
    for ref in came_q:
        total = total + ref[...].astype(F32)
    total_q[...] = total
    half = give_q.shape[0]
    give_q[...] = total_q[aligned((1 - y) * half, half), :].astype(BF16)
    left_q[...] = total_q[aligned(y * half, half), :]


def third_kernel(left_p, left_q, came_q, *rest):
    _, _, z = position()
    *came_p, piece_p, piece_q, bias = rest
    total = left_p[:, :CUT]
    for ref in came_p:
        total = total + ref[:, :CUT].astype(F32)
    piece_p[...] = total.astype(BF16)
    piece_q[...] = (left_q[...] + came_q[...].astype(F32)).astype(BF16)
    terms = [left_p[:8, CUT:]] + [ref[...].astype(F32)[:8, CUT:] for ref in came_p[::-1]]
    total = jnp.zeros_like(terms[0])
    for source in range(len(terms)):
        for other, term in enumerate(terms):
            total = total + jnp.where((z ^ other) == source, term, 0.0)
    bias[...] = total


def fourth_kernel(piece_q, other_q, *rest):
    _, y, z = position()
    *parts_p, block_p, block_q = rest
    piece = parts_p[0].shape[0]
    for other, part in enumerate(parts_p):
        block_p[aligned((z ^ other) * piece, piece), :] = part[...]
    piece = piece_q.shape[0]
    block_q[aligned(y * piece, piece), :] = piece_q[...]
    block_q[aligned((1 - y) * piece, piece), :] = other_q[...]


def fifth_kernel(weight_qkv, gain, bias, block_p, other_p, *rest):
    *parts_q, half, row = rest
    core, y, z = position()
    rows = half.shape[0]
    mine = aligned(core * rows, rows)
    piece = block_p.shape[0]
    half[aligned(y * piece, piece), :CUT] = block_p[...]
    half[aligned((1 - y) * piece, piece), :CUT] = other_p[...]
    piece = parts_q[0].shape[0]
    for other, part in enumerate(parts_q):
        half[aligned((z ^ other) * piece, piece), CUT:] = part[...]
    three = weight_qkv.shape[1]
    wide = half[:, :three].astype(F32)
    gain_half = jnp.sum(wide * weight_qkv[mine, :].astype(F32), axis=1, keepdims=True)
    gain_half = jnp.broadcast_to(gain_half, (rows, GROUP)).T[:8]
    own_gain = jnp.where(core == 0, gain[:, :rows], gain[:, rows:])
    gain_half = gain_half / own_gain
    out = half[:, three:].astype(F32)
    square = jnp.sum(jnp.sum(wide * wide, axis=0, keepdims=True), axis=1, keepdims=True)
    square = square + jnp.sum(jnp.sum(out * out, axis=0, keepdims=True), axis=1, keepdims=True)
    square = square + jnp.sum(gain_half[:1] * gain_half[:1], axis=1, keepdims=True)
    square = square + 0.5 * jnp.sum(bias[:1, :] * bias[:1, :], axis=1, keepdims=True)
    row[:, :rows] = gain_half
    row[:, rows:] = jnp.broadcast_to(square, (8, GROUP))


def last_kernel(
    half, other, row, row_core, row_section, row_both, bias,
    grad_qkv, grad_out, grad_gain, grad_bias,
    qkv_v, out_v, gain_v, bias_v, sems,
    *, entries,
):
    core, _, _ = position()
    rows, three = half.shape[0], grad_qkv.shape[1]
    square = row[:1, rows : rows + 1] + row_core[:1, rows : rows + 1]
    square = square + (row_section[:1, rows : rows + 1] + row_both[:1, rows : rows + 1])
    factor = jnp.minimum(1.0, lax.rsqrt(square / entries + 1e-06))
    sent = []
    piece = 64
    for which, ref in enumerate((half, other)):
        base = core * rows if which == 0 else (1 - core) * rows
        for part in range(rows // piece):
            here = slice(part * piece, (part + 1) * piece)
            at = aligned(base + part * piece, piece)
            slot = slice(which * rows + part * piece, which * rows + (part + 1) * piece)
            qkv_v[slot, :] = ref[here, :three].astype(F32) * factor
            sent.append(started(qkv_v.at[slot, :], grad_qkv.at[at, :], sems, len(sent)))
            out_v[slot, :] = ref[here, three:].astype(F32) * factor
            sent.append(started(out_v.at[slot, :], grad_out.at[at, :], sems, len(sent)))
    mine, its = row[:1, :rows] * factor, row_core[:1, :rows] * factor
    gain_v[:, :rows] = jnp.where(core == 0, mine, its)
    gain_v[:, rows:] = jnp.where(core == 0, its, mine)
    bias_v[...] = bias[:1, : bias_v.shape[1]] * factor
    sent.append(started(gain_v, grad_gain, sems, len(sent)))
    sent.append(started(bias_v, grad_bias, sems, len(sent)))
    for copy in sent:
        copy.wait()


def far_first(pieces, axis):
    others = range(len(pieces), 0, -1)
    return [swapped(piece, axis, other) for other, piece in zip(others, pieces)]


def to_all(piece, axis):
    return [swapped(piece, axis, other) for other in range(1, lax.axis_size(axis))]


def vmem(dims, dtype):
    return pltpu.VMEM(dims, dtype)


def copies(number):
    return pltpu.SemaphoreType.DMA((number,))


def body(inputs, cotangent, land_sea, gains, qkv_weight, out_weight, land_bias):
    weight_qkv, weight_out = qkv_weight[0], out_weight[0]
    levels, lats, cols, width = inputs.shape[1:]
    heads = land_bias.shape[1]
    half = levels * lats * SHIFT
    count = 2 * half
    packed = half * 2 + 16
    lons = lax.axis_size("lon")

    tokens = inputs.transpose(0, 2, 3, 1, 4)
    own_cot = cotangent.transpose(0, 2, 3, 1, 4)

    own, rim = call(
        pack_kernel,
        [shape((packed, width), F32), shape((packed, width), BF16)],
        scratch=[
            vmem(tokens.shape, BF16),
            vmem(tokens.shape, BF16),
            vmem(land_sea.shape, jnp.int32),
            vmem(gains.shape, F32),
            vmem(land_bias.shape, F32),
            vmem((packed, width), F32),
            copies(5),
        ],
        places="hhhhh",
        operands=(tokens, own_cot, land_sea, gains, land_bias),
        limit=60,
    )
    rim = from_behind(rim, "lon", -1)
    qkv_v, qkv_t, out_v = call(
        ready_kernel,
        [
            shape(weight_qkv.shape, BF16),
            shape(weight_qkv.shape[::-1], BF16),
            shape(weight_out.shape, BF16),
        ],
        scratch=[copies(2)],
        places="ahh",
        operands=(own, weight_qkv, weight_out),
        limit=48,
    )
    skip, cot, normed_t, qkv, probs, attended_t, extra, normed = call(
        functools.partial(forward_kernel, heads=heads, lats=lats, cols=cols),
        [
            shape((count, width), BF16),
            shape((count, width), BF16),
            shape((width, count), BF16),
            shape((count, 3 * width), BF16),
            shape((heads * count, count), BF16),
            shape((width, count), BF16),
            shape((count, 2 * GROUP), F32),
            shape((count, width), F32),
        ],
        scratch=[
            vmem((heads * count, count), F32),
            vmem((width, count), BF16),
            vmem((width, count), BF16),
            vmem((width, count), BF16),
            vmem((count, 3 * width), BF16),
        ],
        operands=(own, rim, qkv_v, qkv_t, out_v),
        flops=10**9,
        limit=16,
    )
    skip = passed_along(skip, "section", -1)
    rows, wide = width // 2, 4 * width + GROUP
    total, grad_proj, bias_row, give = call(
        functools.partial(backward_kernel, heads=heads),
        [
            shape((count, width), BF16),
            shape((count, 3 * width), BF16),
            shape((8, GROUP), F32),
            shape((rows, wide), BF16),
        ],
        scratch=[vmem((width, count), BF16)],
        operands=(skip, cot, qkv, probs, out_v, extra, normed_t, attended_t),
        flops=10**9,
    )
    came = swapped(give, "lat", 1)
    keep, own_grad, back = call(
        finish_kernel,
        [
            shape((rows, wide), F32),
            shape((half, width), F32),
            shape((half, width), BF16),
        ],
        operands=(
            total, grad_proj, bias_row, normed_t, attended_t, normed, extra, qkv_t, own,
        ),
        flops=5 * 10**8,
    )
    back = from_behind(back, "lon", 1)
    entries = 2 * (4 * width * width + width + heads)
    if rows // 2 // lons % 16 == 0 and lons & (lons - 1) == 0:
        grads = staged(keep, came, back, qkv_v, gains, lons, heads, entries)
    else:
        grads = plain(keep, came, weight_qkv, gains, heads, entries)
    (final_grad,) = call(
        unpack_kernel,
        [shape(tokens.shape, F32)],
        scratch=[vmem(tokens.shape, F32), copies(1)],
        out_places="h",
        operands=(own_grad, back),
    )
    final_grad = final_grad.transpose(0, 3, 1, 2, 4)
    return (final_grad, *(grad[None] for grad in grads))


def staged(keep, came, after, weight_qkv, gains, lons, heads, entries):
    rows, wide = keep.shape
    width = 2 * rows
    wide_p = CUT + GROUP
    wide_q = wide - wide_p
    some = range(lons - 1)
    several = "v" * len(some)
    give_p, kept_p, kept_q, *give_q = call(
        first_kernel,
        [
            shape((rows // 2, wide_p), BF16),
            shape((rows // 2, wide_p), F32),
            shape((rows // lons, wide_q), F32),
            *(shape((rows // lons, wide_q), BF16) for _ in some),
        ],
        scratch=[vmem((rows, wide), F32)],
        operands=(keep, came),
    )
    came_p = swapped(give_p, "lat", 2)
    came_q = far_first(give_q, "lon")
    piece = rows // 2 // lons
    give_q, left_q, left_p, *give_p = call(
        second_kernel,
        [
            shape((piece, wide_q), BF16),
            shape((piece, wide_q), F32),
            shape((piece, wide_p), F32),
            *(shape((piece, wide_p), BF16) for _ in some),
        ],
        scratch=[vmem((rows // 2, wide_p), F32), vmem((rows // lons, wide_q), F32)],
        places="avvv" + several,
        operands=(after, kept_p, came_p, kept_q, *came_q),
    )
    came_p = far_first(give_p, "lon")
    came_q = swapped(give_q, "lat", 2)
    piece_p, piece_q, bias = call(
        third_kernel,
        [
            shape((piece, CUT), BF16),
            shape((piece, wide_q), BF16),
            shape((8, GROUP), F32),
        ],
        operands=(left_p, left_q, came_q, *came_p),
    )
    others_p = to_all(piece_p, "lon")
    other_q = swapped(piece_q, "lat", 2)
    block_p, block_q = call(
        fourth_kernel,
        [shape((rows // 2, CUT), BF16), shape((rows // lons, wide_q), BF16)],
        operands=(piece_q, other_q, piece_p, *others_p),
    )
    other_p = swapped(block_p, "lat", 2)
    others_q = to_all(block_q, "lon")
    half, row = call(
        fifth_kernel,
        [shape((rows, 4 * width), BF16), shape((8, rows + GROUP), F32)],
        operands=(weight_qkv, gains, bias, block_p, other_p, block_q, *others_q),
    )
    row_section = swapped(row, "section", 1)
    row_both = lax.ppermute(row, ("section", "lat"), across())
    row_core = swapped(row, "lat", 1)
    other = swapped(half, "lat", 1)
    grads = call(
        functools.partial(last_kernel, entries=entries),
        [
            shape((width, 3 * width), F32),
            shape((width, width), F32),
            shape((1, width), F32),
            shape((1, heads), F32),
        ],
        scratch=[
            vmem((width, 3 * width), F32),
            vmem((width, width), F32),
            vmem((1, width), F32),
            vmem((1, heads), F32),
            copies(4 * rows // 64 + 2),
        ],
        out_places="hhhh",
        operands=(half, other, row, row_core, row_section, row_both, bias),
    )
    return grads[0], grads[1], grads[2][0], grads[3][0]


def across():
    sections, lats = lax.axis_size("section"), lax.axis_size("lat")
    return [
        (s * lats + i, (sections - 1 - s) * lats + (i ^ 1))
        for s in range(sections)
        for i in range(lats)
    ]


def split_two(block, axis, bit):
    mine = (lax.axis_index(axis) // bit) % 2
    pair = block.reshape(2, block.shape[0] // 2, -1)
    give = lax.dynamic_index_in_dim(pair, 1 - mine, 0, keepdims=False).astype(BF16)
    return give, lax.dynamic_index_in_dim(pair, mine, 0, keepdims=False)


def doubled(block, axis, bit):
    mine = (lax.axis_index(axis) // bit) % 2
    other = swapped(block, axis, bit)
    low = jnp.where(mine == 0, block, other)
    high = jnp.where(mine == 0, other, block)
    return jnp.concatenate([low, high], axis=0)


def scattered(block, axis):
    count = lax.axis_size(axis)
    mine = lax.axis_index(axis)
    pieces = block.reshape(count, block.shape[0] // count, -1)
    total = lax.dynamic_index_in_dim(pieces, mine, 0, keepdims=False)
    others = []
    for by in range(1, count):
        give = lax.dynamic_index_in_dim(pieces, (mine + by) % count, 0, keepdims=False)
        others.append(from_behind(give.astype(BF16), axis, by))
    for other in others:
        total = total + other.astype(F32)
    return total, others


def gathered(block, axis):
    count = lax.axis_size(axis)
    mine = lax.axis_index(axis)
    whole = jnp.zeros((count,) + block.shape, block.dtype)
    whole = lax.dynamic_update_index_in_dim(whole, block, mine, 0)
    for by in range(1, count):
        whole = lax.dynamic_update_index_in_dim(
            whole, from_behind(block, axis, by), (mine - by) % count, 0
        )
    return whole.reshape(count * block.shape[0], -1)


def sum_squares(block):
    wide = block.astype(F32)
    return jnp.sum(wide * wide)


def plain(keep, came, weight_qkv, gains, heads, entries):
    width = gains.shape[1]
    lat, lon = lax.axis_index("lat"), lax.axis_index("lon")
    part = keep + came.astype(F32)
    give, keep = split_two(part, "lat", 2)
    came = swapped(give, "lat", 2).astype(F32)
    column = lax.broadcasted_iota(jnp.int32, keep.shape, 1)
    is_bias = (column >= CUT) & (column < CUT + GROUP)
    part = jnp.where(is_bias, lax.reduce_precision(keep, 8, 7), keep) + came
    bias_part = lax.reduce_precision(part[:1, CUT : CUT + GROUP], 8, 7)
    part, others = scattered(part, "lon")
    terms = [bias_part] + [other[:1, CUT : CUT + GROUP].astype(F32) for other in others]
    terms = jnp.concatenate(terms[:1] + terms[:0:-1], axis=0)
    bias = jnp.sum(jnp.roll(terms, lon, axis=0), axis=0)[:heads]
    part = jnp.concatenate([part[:, :CUT], part[:, CUT + GROUP :]], axis=1).astype(BF16)
    half = doubled(gathered(part, "lon"), "lat", 2)
    mine = lat % 2
    weight_half = lax.dynamic_slice_in_dim(weight_qkv, mine * (width // 2), width // 2, 0)
    gain_half = lax.dynamic_slice_in_dim(gains[0], mine * (width // 2), width // 2, 0)
    weighed = half[:, : 3 * width].astype(F32) * weight_half.astype(F32)
    gain_half = jnp.sum(weighed, axis=1) / gain_half
    square = sum_squares(half) + sum_squares(gain_half) + 0.5 * sum_squares(bias)
    square = square.reshape(1)
    square = square + swapped(square, "lat", 1)
    square = square + swapped(square, "section", 1)
    factor = jnp.minimum(1.0, lax.rsqrt(square[0] / entries + 1e-06))
    grads = doubled(half, "lat", 1).astype(F32) * factor
    gain = doubled(gain_half.reshape(-1, 1), "lat", 1)[:, 0] * factor
    return grads[:, : 3 * width], grads[:, 3 * width :], gain, bias * factor


def solution(mesh):
    placed = (
        P("section", None, "lat", "lon", None),
        P("section", None, "lat", "lon", None),
        P("lat", "lon"),
        P("section", None),
        P("section", None, None),
        P("section", None, None),
        P("section", None),
    )
    return jax.shard_map(
        body,
        mesh=mesh,
        in_specs=placed,
        out_specs=(
            P("section", None, "lat", "lon", None),
            P("section", None, None),
            P("section", None, None),
            P("section", None),
            P("section", None),
        ),
        check_vma=False,
    )
```

```python
import functools

import jax
import jax.numpy as jnp
from jax import lax
from jax.experimental import pallas as pl
from jax.experimental.pallas import tpu as pltpu
from jax.sharding import PartitionSpec as P

SHIFT = 6
GROUP = 128
CUT = 1280
EPSILON = 1e-05
F32 = jnp.float32
BF16 = jnp.bfloat16


def from_behind(value, axis, by):
    count = lax.axis_size(axis)
    return lax.ppermute(value, axis, [(i, (i + by) % count) for i in range(count)])


def passed_along(block, axis, distance):
    devices = range(lax.axis_size(axis))
    route = [(i - distance, i) for i in devices if i - distance in devices]
    return lax.ppermute(block, axis, route)


def swapped(value, axis, bit):
    count = lax.axis_size(axis)
    return lax.ppermute(value, axis, [(i, i ^ bit) for i in range(count)])


def dot(left, right):
    return jnp.dot(left, right, preferred_element_type=F32)


def dot_last(left, right):
    return lax.dot_general(left, right, (((1,), (1,)), ((), ())), preferred_element_type=F32)


def call(kernel, outs, scratch=(), places="", out_places="", operands=(), flops=10**8, limit=8):
    spaces = {"v": pltpu.VMEM, "s": pltpu.SMEM, "a": pl.ANY, "h": pltpu.HBM}
    places = places or "v" * len(operands)
    out_places = out_places or "v" * len(outs)
    moved = sum(o.size * o.dtype.itemsize for o in list(outs) + list(operands))
    return pl.pallas_call(
        kernel,
        out_shape=list(outs),
        in_specs=[pl.BlockSpec(memory_space=spaces[letter]) for letter in places],
        out_specs=[pl.BlockSpec(memory_space=spaces[letter]) for letter in out_places],
        scratch_shapes=list(scratch),
        compiler_params=pltpu.CompilerParams(vmem_limit_bytes=limit * 2**20),
        cost_estimate=pl.CostEstimate(flops=flops, bytes_accessed=moved, transcendentals=0),
    )(*operands)


def started(source, target, semaphores, index):
    copy = pltpu.make_async_copy(source, target, semaphores.at[index])
    copy.start()
    return copy


def shape(dims, dtype):
    return jax.ShapeDtypeStruct(dims, dtype)


def aligned(start, size):
    return pl.ds(pl.multiple_of(start, size), size)


def position():
    lat, lon = lax.axis_index("lat"), lax.axis_index("lon")
    return lax.rem(lat, 2), lax.div(lat, 2), lon


def pack_rim_kernel(tokens, land, rim, tokens_v, land_v, rim32, sems):
    copies = [started(tokens, tokens_v, sems, 0), started(land, land_v, sems, 1)]
    lats, cols, levels, width = tokens.shape[1:]
    half = levels * lats * SHIFT
    rim32[half:, :] = jnp.zeros((rim32.shape[0] - half, width), F32)
    copies[0].wait()
    for lat in range(lats):
        for col in range(SHIFT):
            row = (lat * SHIFT + col) * levels
            rim32[row : row + levels, :] = tokens_v[0, lat, col].astype(F32)
    copies[1].wait()
    rim32[half : half + lats, :cols] = land_v[...].astype(F32)
    rim[...] = rim32[...].astype(BF16)


def pack_kernel(
    after, tokens, cot, land, gain, bias, own, rim,
    tokens_v, cot_v, land_v, gain_v, bias_v, rim32, sems,
):
    arrays = ((cot, cot_v), (tokens, tokens_v), (land, land_v), (gain, gain_v), (bias, bias_v))
    copies = [started(source, target, sems, i) for i, (source, target) in enumerate(arrays)]
    lats, cols, levels, width = tokens.shape[1:]
    half = levels * lats * SHIFT
    rim32[half:, :] = jnp.zeros((rim32.shape[0] - half, width), F32)
    own[2 * half :, :] = jnp.zeros((own.shape[0] - 2 * half, width), F32)
    copies[0].wait()
    copies[1].wait()
    for lat in range(lats):
        for col in range(SHIFT):
            row = (lat * SHIFT + col) * levels
            rim32[row : row + levels, :] = cot_v[0, lat, col].astype(F32)
            own[row : row + levels, :] = tokens_v[0, lat, SHIFT + col].astype(F32)
            own[half + row : half + row + levels, :] = cot_v[0, lat, SHIFT + col].astype(F32)
    for copy in copies[2:]:
        copy.wait()
    own[2 * half : 2 * half + 1, :] = gain_v[...]
    own[2 * half + 1 : 2 * half + 2, : bias.shape[1]] = bias_v[...]
    own[2 * half + 8 : 2 * half + 8 + lats, :cols] = land_v[...].astype(F32)
    rim[...] = rim32[...].astype(BF16)


def unpack_kernel(own, back, grid, grid_v, sems):
    lats, cols, levels, width = grid.shape[1:]
    came = back[...].astype(F32)
    for lat in range(lats):
        for col in range(cols):
            row = (lat * SHIFT + col % SHIFT) * levels
            if col < SHIFT:
                grid_v[0, lat, col] = came[row : row + levels]
            else:
                grid_v[0, lat, col] = own[row : row + levels, :]
    started(grid_v, grid, sems, 0).wait()


def land_column(land, rows, first):
    lats, cols = land.shape
    row = lax.broadcasted_iota(jnp.int32, (rows, lats), 0)
    lat = lax.div(row, rows // lats)
    pick = (lat == lax.broadcasted_iota(jnp.int32, (rows, lats), 1)).astype(F32)
    lines = dot(pick.astype(BF16), land.astype(BF16))
    row = lax.broadcasted_iota(jnp.int32, (rows, cols), 0)
    column = lax.broadcasted_iota(jnp.int32, (rows, cols), 1)
    levels = rows // (lats * SHIFT)
    here = column == lax.rem(lax.div(row, levels), SHIFT) + first
    return jnp.sum(jnp.where(here, lines, 0.0), axis=1, keepdims=True)


def head_masks(dtype, size):
    lane = lax.broadcasted_iota(jnp.int32, (1, GROUP), 1)
    return [
        (lax.div(lane, size) == part).astype(F32).astype(dtype) for part in range(GROUP // size)
    ]


def stacked(block, masks):
    return jnp.concatenate([block * mask for mask in masks], axis=0)


def folded(block, masks):
    rows = block.shape[0] // len(masks)
    return sum(block[i * rows : (i + 1) * rows] * mask for i, mask in enumerate(masks))


def back_through(grad_out, probs, qkv, keys_t, weight_out, grad_proj, size, land):
    count, width = grad_out.shape
    per = GROUP // size
    scale = size ** (-0.5)
    masks_b, masks = head_masks(BF16, size), head_masks(F32, size)
    att_t = dot_last(weight_out[...], grad_out)
    grad_att = att_t.T.astype(BF16)
    att_t = att_t.astype(BF16)
    lane = lax.broadcasted_iota(jnp.int32, (1, GROUP), 1)
    bias_row = jnp.zeros((1, GROUP), F32)
    for group in range(width // GROUP):
        at = group * GROUP
        values = qkv[:, 2 * width + at : 2 * width + at + GROUP]
        grad_probs = dot(stacked(values, masks_b), att_t[at : at + GROUP, :])
        scores_b, queries_t = [], []
        for part in range(per):
            head = group * per + part
            weights = probs[head * count : (head + 1) * count, :].astype(F32)
            grad_weights = grad_probs[part * count : (part + 1) * count]
            inner = jnp.sum(weights * grad_weights, axis=0, keepdims=True)
            grad_scores = weights * (grad_weights - inner)
            if land is not None:
                on_land = jnp.sum(grad_scores * land, axis=0, keepdims=True)
                on_land = jnp.sum(on_land, axis=1, keepdims=True)
                bias_row = bias_row + jnp.where(lane == head, on_land, 0.0)
            scaled_b = (grad_scores * scale).astype(BF16)
            scores_b.append(scaled_b)
            queries_t.append(dot(keys_t[head * size : (head + 1) * size, :], scaled_b))
        queries = qkv[:, at : at + GROUP]
        grad_keys = dot(jnp.concatenate(scores_b, axis=0), queries)
        mixed = probs[group * per * count : (group + 1) * per * count, :]
        grad_values = dot(mixed, grad_att[:, at : at + GROUP])
        grad_proj[:, at : at + GROUP] = jnp.concatenate(queries_t, axis=0).T.astype(BF16)
        grad_proj[:, width + at : width + at + GROUP] = folded(grad_keys, masks).astype(BF16)
        grad_proj[:, 2 * width + at : 2 * width + at + GROUP] = folded(grad_values, masks).astype(
            BF16
        )
    return bias_row


def through_norm(grad_proj, weight_t, gain, normed, inverse):
    scaled = dot(grad_proj, weight_t[...]) * gain
    mean = jnp.mean(scaled, axis=-1, keepdims=True)
    along = jnp.mean(scaled * normed, axis=-1, keepdims=True)
    return inverse * (scaled - mean - normed * along)


def ready_kernel(after, weight_qkv, weight_out, qkv_v, qkv_t, out_v, sems):
    copies = [
        started(weight_qkv, qkv_v, sems, 0),
        started(weight_out, out_v, sems, 1),
    ]
    copies[0].wait()
    width = weight_qkv.shape[0]
    for part in range(weight_qkv.shape[1] // width):
        rows = slice(part * width, (part + 1) * width)
        qkv_t[rows, :] = qkv_v[:, rows].T
    copies[1].wait()


def forward_kernel(
    own, rim, weight_qkv,
    normed_t, qkv, probs, attended_t, extra, normed_out,
    queries_t, values_t,
    *, heads, lats, cols,
):
    width = own.shape[1]
    size = width // heads
    count = qkv.shape[0]
    half = count // 2
    per = GROUP // size
    scale = size ** (-0.5)
    masks_b = head_masks(BF16, size)
    params = own[count:, :]
    came = rim[...].astype(F32)
    gain = params[0:1, :]
    values = jnp.concatenate([own[:half, :], came[:half]], axis=0)
    centred = values - jnp.mean(values, axis=-1, keepdims=True)
    inverse = lax.rsqrt(jnp.mean(centred * centred, axis=-1, keepdims=True) + EPSILON)
    normed = centred * inverse
    normed_out[...] = normed
    normed_b = (normed * gain).astype(BF16)
    normed_t[...] = normed_b.T
    land = jnp.concatenate(
        [
            land_column(params[8 : 8 + lats, :cols], half, SHIFT),
            land_column(came[half : half + lats, :cols], half, 0),
        ],
        axis=0,
    )
    extra[:, :GROUP] = jnp.broadcast_to(land, (count, GROUP))
    extra[:, GROUP:] = jnp.broadcast_to(inverse, (count, GROUP))
    for part, turned in enumerate((queries_t, None, values_t)):
        columns = slice(part * width, (part + 1) * width)
        qkv[:, columns] = dot(normed_b, weight_qkv[:, columns]).astype(BF16)
        if turned is not None:
            turned[...] = qkv[:, columns].T
    for group in range(width // GROUP):
        at = group * GROUP
        keys = qkv[:, width + at : width + at + GROUP]
        scores = dot(stacked(keys, masks_b), queries_t[at : at + GROUP, :])
        for part in range(per):
            head = group * per + part
            block = scores[part * count : (part + 1) * count] * scale
            block = block + params[1:2, head : head + 1] * land
            block = jnp.exp(block - jnp.max(block, axis=0, keepdims=True))
            weights = block * (1.0 / jnp.sum(block, axis=0, keepdims=True))
            weights_b = weights.astype(BF16)
            probs[head * count : (head + 1) * count, :] = weights_b
            out = dot(values_t[head * size : (head + 1) * size, :], weights_b)
            attended_t[head * size : (head + 1) * size, :] = out.astype(BF16)


def first_backward_kernel(
    own, rim, qkv, probs, weight_out, weight_t, extra, normed,
    skip, cot,
    keys_t, grad_proj,
    *, heads,
):
    count, width = cot.shape
    half = count // 2
    came = rim[...].astype(F32)
    grad_out = jnp.concatenate([own[half:count, :], came[:half]], axis=0)
    cot[...] = grad_out.astype(BF16)
    keys_t[...] = qkv[:, width : 2 * width].T
    back_through(cot[...], probs, qkv, keys_t, weight_out, grad_proj, width // heads, None)
    gain, inverse = own[count : count + 1, :], extra[:, GROUP : GROUP + 1]
    skip[...] = (
        through_norm(grad_proj[...], weight_t, gain, normed[...], inverse) + grad_out
    ).astype(BF16)


def backward_kernel(
    skip, cot, qkv, probs, weight_out, extra, normed_t, attended_t,
    total_out, grad_proj, bias_out, give,
    keys_t,
    *, heads,
):
    count, width = cot.shape
    core, _, _ = position()
    total_out[...] = (cot[...].astype(F32) + skip[...].astype(F32)).astype(BF16)
    keys_t[...] = qkv[:, width : 2 * width].T
    bias_row = back_through(
        total_out[...], probs, qkv, keys_t, weight_out, grad_proj, width // heads,
        extra[:, :1],
    )
    bias_out[...] = jnp.broadcast_to(bias_row, bias_out.shape)
    half = width // 2
    rows = aligned((1 - core) * half, half)
    weight_rows(rows, normed_t, attended_t, grad_proj, total_out, bias_row, give)


def weight_rows(rows, normed_t, attended_t, grad_proj, total, bias_row, out):
    tokens = normed_t[rows, :]
    three = grad_proj.shape[1]
    out[:, :CUT] = dot(tokens, grad_proj[:, :CUT]).astype(out.dtype)
    out[:, CUT : CUT + GROUP] = jnp.broadcast_to(bias_row, (out.shape[0], GROUP)).astype(out.dtype)
    out[:, CUT + GROUP : three + GROUP] = dot(tokens, grad_proj[:, CUT:]).astype(out.dtype)
    out[:, three + GROUP :] = dot(attended_t[rows, :], total[...]).astype(out.dtype)


def finish_kernel(
    total, grad_proj, bias_row, normed_t, attended_t, normed, extra, weight_t, params,
    keep, own, back,
):
    count, width = total.shape
    half = width // 2
    core, _, _ = position()
    rows = aligned(core * half, half)
    bias_b = bias_row[:1, :].astype(BF16).astype(F32)
    weight_rows(rows, normed_t, attended_t, grad_proj, total, bias_b, keep)
    inverse = extra[:, GROUP : GROUP + 1]
    final = through_norm(grad_proj[...], weight_t, params[count : count + 1, :], normed[...], inverse)
    final = final + total[...].astype(F32)
    own[...] = final[: count // 2]
    back[...] = final[count // 2 :].astype(BF16)


def first_kernel(keep, came, give_p, kept_p, kept_q, *rest):
    _, y, z = position()
    *give_q, total = rest
    wide_p = give_p.shape[1]
    half = keep.shape[0] // 2
    total[...] = keep[...] + came[...].astype(F32)
    give_p[...] = total[aligned((1 - y) * half, half), :wide_p].astype(BF16)
    mine = aligned(y * half, half)
    kept_p[:, :CUT] = total[mine, :CUT]
    kept_p[:, CUT:] = total[mine, CUT:wide_p].astype(BF16).astype(F32)
    piece = kept_q.shape[0]
    kept_q[...] = total[aligned(z * piece, piece), wide_p:]
    for other, ref in zip(range(len(give_q), 0, -1), give_q):
        ref[...] = total[aligned((z ^ other) * piece, piece), wide_p:].astype(BF16)


def second_kernel(kept_p, came_p, kept_q, *rest):
    _, y, z = position()
    count = (len(rest) - 5) // 2
    came_q, (give_q, left_q, left_p) = rest[:count], rest[count : count + 3]
    *give_p, total_p, total_q = rest[count + 3 :]
    total_p[...] = kept_p[...] + came_p[...].astype(F32)
    piece = left_p.shape[0]
    mine = aligned(z * piece, piece)
    left_p[:, :CUT] = total_p[mine, :CUT]
    left_p[:, CUT:] = total_p[mine, CUT:].astype(BF16).astype(F32)
    for other, ref in zip(range(len(give_p), 0, -1), give_p):
        ref[...] = total_p[aligned((z ^ other) * piece, piece), :].astype(BF16)
    total = kept_q[...]
    for ref in came_q:
        total = total + ref[...].astype(F32)
    total_q[...] = total
    half = give_q.shape[0]
    give_q[...] = total_q[aligned((1 - y) * half, half), :].astype(BF16)
    left_q[...] = total_q[aligned(y * half, half), :]


def third_kernel(after, left_p, left_q, came_q, *rest):
    _, _, z = position()
    *came_p, piece_p, piece_q, bias = rest
    total = left_p[:, :CUT]
    for ref in came_p:
        total = total + ref[:, :CUT].astype(F32)
    piece_p[...] = total.astype(BF16)
    piece_q[...] = (left_q[...] + came_q[...].astype(F32)).astype(BF16)
    terms = [left_p[:8, CUT:]] + [ref[...].astype(F32)[:8, CUT:] for ref in came_p[::-1]]
    total = jnp.zeros_like(terms[0])
    for source in range(len(terms)):
        for other, term in enumerate(terms):
            total = total + jnp.where((z ^ other) == source, term, 0.0)
    bias[...] = total


def fourth_kernel(piece_q, other_q, *rest):
    _, y, z = position()
    *parts_p, block_p, block_q = rest
    piece = parts_p[0].shape[0]
    for other, part in enumerate(parts_p):
        block_p[aligned((z ^ other) * piece, piece), :] = part[...]
    piece = piece_q.shape[0]
    block_q[aligned(y * piece, piece), :] = piece_q[...]
    block_q[aligned((1 - y) * piece, piece), :] = other_q[...]


def fifth_kernel(weight_qkv, gain, bias, block_p, other_p, *rest):
    *parts_q, half, row = rest
    core, y, z = position()
    rows = half.shape[0]
    mine = aligned(core * rows, rows)
    piece = block_p.shape[0]
    half[aligned(y * piece, piece), :CUT] = block_p[...]
    half[aligned((1 - y) * piece, piece), :CUT] = other_p[...]
    piece = parts_q[0].shape[0]
    for other, part in enumerate(parts_q):
        half[aligned((z ^ other) * piece, piece), CUT:] = part[...]
    three = weight_qkv.shape[1]
    wide = half[:, :three].astype(F32)
    gain_half = jnp.sum(wide * weight_qkv[mine, :].astype(F32), axis=1, keepdims=True)
    gain_half = jnp.broadcast_to(gain_half, (rows, GROUP)).T[:8]
    own_gain = jnp.where(core == 0, gain[:, :rows], gain[:, rows:])
    gain_half = gain_half / own_gain
    out = half[:, three:].astype(F32)
    square = jnp.sum(jnp.sum(wide * wide, axis=0, keepdims=True), axis=1, keepdims=True)
    square = square + jnp.sum(jnp.sum(out * out, axis=0, keepdims=True), axis=1, keepdims=True)
    square = square + jnp.sum(gain_half[:1] * gain_half[:1], axis=1, keepdims=True)
    square = square + 0.5 * jnp.sum(bias[:1, :] * bias[:1, :], axis=1, keepdims=True)
    row[:, :rows] = gain_half
    row[:, rows:] = jnp.broadcast_to(square, (8, GROUP))


def last_kernel(
    half, other, row, row_core, row_section, row_both, bias,
    grad_qkv, grad_out, grad_gain, grad_bias,
    qkv_v, out_v, gain_v, bias_v, sems,
    *, entries,
):
    core, _, _ = position()
    rows, three = half.shape[0], grad_qkv.shape[1]
    square = row[:1, rows : rows + 1] + row_core[:1, rows : rows + 1]
    square = square + (row_section[:1, rows : rows + 1] + row_both[:1, rows : rows + 1])
    factor = jnp.minimum(1.0, lax.rsqrt(square / entries + 1e-06))
    sent = []
    piece = 64
    for which, ref in enumerate((half, other)):
        base = core * rows if which == 0 else (1 - core) * rows
        for part in range(rows // piece):
            here = slice(part * piece, (part + 1) * piece)
            at = aligned(base + part * piece, piece)
            slot = slice(which * rows + part * piece, which * rows + (part + 1) * piece)
            qkv_v[slot, :] = ref[here, :three].astype(F32) * factor
            sent.append(started(qkv_v.at[slot, :], grad_qkv.at[at, :], sems, len(sent)))
            out_v[slot, :] = ref[here, three:].astype(F32) * factor
            sent.append(started(out_v.at[slot, :], grad_out.at[at, :], sems, len(sent)))
    mine, its = row[:1, :rows] * factor, row_core[:1, :rows] * factor
    gain_v[:, :rows] = jnp.where(core == 0, mine, its)
    gain_v[:, rows:] = jnp.where(core == 0, its, mine)
    bias_v[...] = bias[:1, : bias_v.shape[1]] * factor
    sent.append(started(gain_v, grad_gain, sems, len(sent)))
    sent.append(started(bias_v, grad_bias, sems, len(sent)))
    for copy in sent:
        copy.wait()


def far_first(pieces, axis):
    others = range(len(pieces), 0, -1)
    return [swapped(piece, axis, other) for other, piece in zip(others, pieces)]


def to_all(piece, axis):
    return [swapped(piece, axis, other) for other in range(1, lax.axis_size(axis))]


def vmem(dims, dtype):
    return pltpu.VMEM(dims, dtype)


def copies(number):
    return pltpu.SemaphoreType.DMA((number,))


def body(inputs, cotangent, land_sea, gains, qkv_weight, out_weight, land_bias):
    weight_qkv, weight_out = qkv_weight[0], out_weight[0]
    levels, lats, cols, width = inputs.shape[1:]
    heads = land_bias.shape[1]
    half = levels * lats * SHIFT
    count = 2 * half
    packed = half * 2 + 16
    lons = lax.axis_size("lon")

    tokens = inputs.transpose(0, 2, 3, 1, 4)
    own_cot = cotangent.transpose(0, 2, 3, 1, 4)

    (rim,) = call(
        pack_rim_kernel,
        [shape((half + 8, width), BF16)],
        scratch=[
            vmem(tokens.shape, BF16),
            vmem(land_sea.shape, jnp.int32),
            vmem((half + 8, width), F32),
            copies(2),
        ],
        places="hh",
        operands=(tokens, land_sea),
        limit=60,
    )
    own, rim_cot = call(
        pack_kernel,
        [shape((packed, width), F32), shape((half + 8, width), BF16)],
        scratch=[
            vmem(tokens.shape, BF16),
            vmem(tokens.shape, BF16),
            vmem(land_sea.shape, jnp.int32),
            vmem(gains.shape, F32),
            vmem(land_bias.shape, F32),
            vmem((half + 8, width), F32),
            copies(5),
        ],
        places="ahhhhh",
        operands=(rim, tokens, own_cot, land_sea, gains, land_bias),
        limit=60,
    )
    rim = from_behind(rim, "lon", -1)
    rim_cot = from_behind(rim_cot, "lon", -1)
    qkv_v, qkv_t, out_v = call(
        ready_kernel,
        [
            shape(weight_qkv.shape, BF16),
            shape(weight_qkv.shape[::-1], BF16),
            shape(weight_out.shape, BF16),
        ],
        scratch=[copies(2)],
        places="ahh",
        operands=(own, weight_qkv, weight_out),
        limit=48,
    )
    normed_t, qkv, probs, attended_t, extra, normed = call(
        functools.partial(forward_kernel, heads=heads, lats=lats, cols=cols),
        [
            shape((width, count), BF16),
            shape((count, 3 * width), BF16),
            shape((heads * count, count), BF16),
            shape((width, count), BF16),
            shape((count, 2 * GROUP), F32),
            shape((count, width), F32),
        ],
        scratch=[vmem((width, count), BF16), vmem((width, count), BF16)],
        operands=(own, rim, qkv_v),
        flops=10**9,
    )
    skip, cot = call(
        functools.partial(first_backward_kernel, heads=heads),
        [shape((count, width), BF16), shape((count, width), BF16)],
        scratch=[vmem((width, count), BF16), vmem((count, 3 * width), BF16)],
        operands=(own, rim_cot, qkv, probs, out_v, qkv_t, extra, normed),
        flops=10**9,
    )
    skip = passed_along(skip, "section", -1)
    rows, wide = width // 2, 4 * width + GROUP
    total, grad_proj, bias_row, give = call(
        functools.partial(backward_kernel, heads=heads),
        [
            shape((count, width), BF16),
            shape((count, 3 * width), BF16),
            shape((8, GROUP), F32),
            shape((rows, wide), BF16),
        ],
        scratch=[vmem((width, count), BF16)],
        operands=(skip, cot, qkv, probs, out_v, extra, normed_t, attended_t),
        flops=10**9,
    )
    came = swapped(give, "lat", 1)
    keep, own_grad, back = call(
        finish_kernel,
        [
            shape((rows, wide), F32),
            shape((half, width), F32),
            shape((half, width), BF16),
        ],
        operands=(
            total, grad_proj, bias_row, normed_t, attended_t, normed, extra, qkv_t, own,
        ),
        flops=5 * 10**8,
    )
    back = from_behind(back, "lon", 1)
    entries = 2 * (4 * width * width + width + heads)
    if rows // 2 // lons % 16 == 0 and lons & (lons - 1) == 0:
        grads = staged(keep, came, back, qkv_v, gains, lons, heads, entries)
    else:
        grads = plain(keep, came, weight_qkv, gains, heads, entries)
    (final_grad,) = call(
        unpack_kernel,
        [shape(tokens.shape, F32)],
        scratch=[vmem(tokens.shape, F32), copies(1)],
        out_places="h",
        operands=(own_grad, back),
    )
    final_grad = final_grad.transpose(0, 3, 1, 2, 4)
    return (final_grad, *(grad[None] for grad in grads))


def staged(keep, came, after, weight_qkv, gains, lons, heads, entries):
    rows, wide = keep.shape
    width = 2 * rows
    wide_p = CUT + GROUP
    wide_q = wide - wide_p
    some = range(lons - 1)
    several = "v" * len(some)
    give_p, kept_p, kept_q, *give_q = call(
        first_kernel,
        [
            shape((rows // 2, wide_p), BF16),
            shape((rows // 2, wide_p), F32),
            shape((rows // lons, wide_q), F32),
            *(shape((rows // lons, wide_q), BF16) for _ in some),
        ],
        scratch=[vmem((rows, wide), F32)],
        operands=(keep, came),
    )
    came_p = swapped(give_p, "lat", 2)
    came_q = far_first(give_q, "lon")
    piece = rows // 2 // lons
    give_q, left_q, left_p, *give_p = call(
        second_kernel,
        [
            shape((piece, wide_q), BF16),
            shape((piece, wide_q), F32),
            shape((piece, wide_p), F32),
            *(shape((piece, wide_p), BF16) for _ in some),
        ],
        scratch=[vmem((rows // 2, wide_p), F32), vmem((rows // lons, wide_q), F32)],
        operands=(kept_p, came_p, kept_q, *came_q),
    )
    came_p = far_first(give_p, "lon")
    came_q = swapped(give_q, "lat", 2)
    piece_p, piece_q, bias = call(
        third_kernel,
        [
            shape((piece, CUT), BF16),
            shape((piece, wide_q), BF16),
            shape((8, GROUP), F32),
        ],
        places="avvv" + several,
        operands=(after, left_p, left_q, came_q, *came_p),
    )
    others_p = to_all(piece_p, "lon")
    other_q = swapped(piece_q, "lat", 2)
    block_p, block_q = call(
        fourth_kernel,
        [shape((rows // 2, CUT), BF16), shape((rows // lons, wide_q), BF16)],
        operands=(piece_q, other_q, piece_p, *others_p),
    )
    other_p = swapped(block_p, "lat", 2)
    others_q = to_all(block_q, "lon")
    half, row = call(
        fifth_kernel,
        [shape((rows, 4 * width), BF16), shape((8, rows + GROUP), F32)],
        operands=(weight_qkv, gains, bias, block_p, other_p, block_q, *others_q),
    )
    row_section = swapped(row, "section", 1)
    row_both = lax.ppermute(row, ("section", "lat"), across())
    row_core = swapped(row, "lat", 1)
    other = swapped(half, "lat", 1)
    grads = call(
        functools.partial(last_kernel, entries=entries),
        [
            shape((width, 3 * width), F32),
            shape((width, width), F32),
            shape((1, width), F32),
            shape((1, heads), F32),
        ],
        scratch=[
            vmem((width, 3 * width), F32),
            vmem((width, width), F32),
            vmem((1, width), F32),
            vmem((1, heads), F32),
            copies(4 * rows // 64 + 2),
        ],
        out_places="hhhh",
        operands=(half, other, row, row_core, row_section, row_both, bias),
    )
    return grads[0], grads[1], grads[2][0], grads[3][0]


def across():
    sections, lats = lax.axis_size("section"), lax.axis_size("lat")
    return [
        (s * lats + i, (sections - 1 - s) * lats + (i ^ 1))
        for s in range(sections)
        for i in range(lats)
    ]


def split_two(block, axis, bit):
    mine = (lax.axis_index(axis) // bit) % 2
    pair = block.reshape(2, block.shape[0] // 2, -1)
    give = lax.dynamic_index_in_dim(pair, 1 - mine, 0, keepdims=False).astype(BF16)
    return give, lax.dynamic_index_in_dim(pair, mine, 0, keepdims=False)


def doubled(block, axis, bit):
    mine = (lax.axis_index(axis) // bit) % 2
    other = swapped(block, axis, bit)
    low = jnp.where(mine == 0, block, other)
    high = jnp.where(mine == 0, other, block)
    return jnp.concatenate([low, high], axis=0)


def scattered(block, axis):
    count = lax.axis_size(axis)
    mine = lax.axis_index(axis)
    pieces = block.reshape(count, block.shape[0] // count, -1)
    total = lax.dynamic_index_in_dim(pieces, mine, 0, keepdims=False)
    others = []
    for by in range(1, count):
        give = lax.dynamic_index_in_dim(pieces, (mine + by) % count, 0, keepdims=False)
        others.append(from_behind(give.astype(BF16), axis, by))
    for other in others:
        total = total + other.astype(F32)
    return total, others


def gathered(block, axis):
    count = lax.axis_size(axis)
    mine = lax.axis_index(axis)
    whole = jnp.zeros((count,) + block.shape, block.dtype)
    whole = lax.dynamic_update_index_in_dim(whole, block, mine, 0)
    for by in range(1, count):
        whole = lax.dynamic_update_index_in_dim(
            whole, from_behind(block, axis, by), (mine - by) % count, 0
        )
    return whole.reshape(count * block.shape[0], -1)


def sum_squares(block):
    wide = block.astype(F32)
    return jnp.sum(wide * wide)


def plain(keep, came, weight_qkv, gains, heads, entries):
    width = gains.shape[1]
    lat, lon = lax.axis_index("lat"), lax.axis_index("lon")
    part = keep + came.astype(F32)
    give, keep = split_two(part, "lat", 2)
    came = swapped(give, "lat", 2).astype(F32)
    column = lax.broadcasted_iota(jnp.int32, keep.shape, 1)
    is_bias = (column >= CUT) & (column < CUT + GROUP)
    part = jnp.where(is_bias, lax.reduce_precision(keep, 8, 7), keep) + came
    bias_part = lax.reduce_precision(part[:1, CUT : CUT + GROUP], 8, 7)
    part, others = scattered(part, "lon")
    terms = [bias_part] + [other[:1, CUT : CUT + GROUP].astype(F32) for other in others]
    terms = jnp.concatenate(terms[:1] + terms[:0:-1], axis=0)
    bias = jnp.sum(jnp.roll(terms, lon, axis=0), axis=0)[:heads]
    part = jnp.concatenate([part[:, :CUT], part[:, CUT + GROUP :]], axis=1).astype(BF16)
    half = doubled(gathered(part, "lon"), "lat", 2)
    mine = lat % 2
    weight_half = lax.dynamic_slice_in_dim(weight_qkv, mine * (width // 2), width // 2, 0)
    gain_half = lax.dynamic_slice_in_dim(gains[0], mine * (width // 2), width // 2, 0)
    weighed = half[:, : 3 * width].astype(F32) * weight_half.astype(F32)
    gain_half = jnp.sum(weighed, axis=1) / gain_half
    square = sum_squares(half) + sum_squares(gain_half) + 0.5 * sum_squares(bias)
    square = square.reshape(1)
    square = square + swapped(square, "lat", 1)
    square = square + swapped(square, "section", 1)
    factor = jnp.minimum(1.0, lax.rsqrt(square[0] / entries + 1e-06))
    grads = doubled(half, "lat", 1).astype(F32) * factor
    gain = doubled(gain_half.reshape(-1, 1), "lat", 1)[:, 0] * factor
    return grads[:, : 3 * width], grads[:, 3 * width :], gain, bias * factor


def solution(mesh):
    placed = (
        P("section", None, "lat", "lon", None),
        P("section", None, "lat", "lon", None),
        P("lat", "lon"),
        P("section", None),
        P("section", None, None),
        P("section", None, None),
        P("section", None),
    )
    return jax.shard_map(
        body,
        mesh=mesh,
        in_specs=placed,
        out_specs=(
            P("section", None, "lat", "lon", None),
            P("section", None, None),
            P("section", None, None),
            P("section", None),
            P("section", None),
        ),
        check_vma=False,
    )
```

```python
import functools

import jax
import jax.numpy as jnp
from jax import lax
from jax.experimental import pallas as pl
from jax.experimental.pallas import tpu as pltpu
from jax.sharding import PartitionSpec as P

SHIFT = 6
GROUP = 128
CUT = 1280
EPSILON = 1e-05
F32 = jnp.float32
BF16 = jnp.bfloat16


def from_behind(value, axis, by):
    count = lax.axis_size(axis)
    return lax.ppermute(value, axis, [(i, (i + by) % count) for i in range(count)])


def passed_along(block, axis, distance):
    devices = range(lax.axis_size(axis))
    route = [(i - distance, i) for i in devices if i - distance in devices]
    return lax.ppermute(block, axis, route)


def swapped(value, axis, bit):
    count = lax.axis_size(axis)
    return lax.ppermute(value, axis, [(i, i ^ bit) for i in range(count)])


def dot(left, right):
    return jnp.dot(left, right, preferred_element_type=F32)


def dot_last(left, right):
    return lax.dot_general(left, right, (((1,), (1,)), ((), ())), preferred_element_type=F32)


def call(kernel, outs, scratch=(), places="", out_places="", operands=(), flops=10**8, limit=8):
    spaces = {"v": pltpu.VMEM, "s": pltpu.SMEM, "a": pl.ANY, "h": pltpu.HBM}
    places = places or "v" * len(operands)
    out_places = out_places or "v" * len(outs)
    moved = sum(o.size * o.dtype.itemsize for o in list(outs) + list(operands))
    return pl.pallas_call(
        kernel,
        out_shape=list(outs),
        in_specs=[pl.BlockSpec(memory_space=spaces[letter]) for letter in places],
        out_specs=[pl.BlockSpec(memory_space=spaces[letter]) for letter in out_places],
        scratch_shapes=list(scratch),
        compiler_params=pltpu.CompilerParams(vmem_limit_bytes=limit * 2**20),
        cost_estimate=pl.CostEstimate(flops=flops, bytes_accessed=moved, transcendentals=0),
    )(*operands)


def started(source, target, semaphores, index):
    copy = pltpu.make_async_copy(source, target, semaphores.at[index])
    copy.start()
    return copy


def shape(dims, dtype):
    return jax.ShapeDtypeStruct(dims, dtype)


def aligned(start, size):
    return pl.ds(pl.multiple_of(start, size), size)


def position():
    lat, lon = lax.axis_index("lat"), lax.axis_index("lon")
    return lax.rem(lat, 2), lax.div(lat, 2), lon


def pack_kernel(
    tokens, cot, land, gain, bias, own, rim, rim_cot,
    tokens_v, cot_v, land_v, gain_v, bias_v, rim32, rim_cot32, sems,
):
    arrays = ((tokens, tokens_v), (cot, cot_v), (land, land_v), (gain, gain_v), (bias, bias_v))
    copies = [started(source, target, sems, i) for i, (source, target) in enumerate(arrays)]
    lats, cols, levels, width = tokens.shape[1:]
    half = levels * lats * SHIFT
    rim32[half:, :] = jnp.zeros((rim32.shape[0] - half, width), F32)
    rim_cot32[half:, :] = jnp.zeros((rim32.shape[0] - half, width), F32)
    own[2 * half :, :] = jnp.zeros((own.shape[0] - 2 * half, width), F32)
    for which, (ref, part) in enumerate(((tokens_v, rim32), (cot_v, rim_cot32))):
        copies[which].wait()
        for lat in range(lats):
            for col in range(SHIFT):
                row = (lat * SHIFT + col) * levels
                part[row : row + levels, :] = ref[0, lat, col].astype(F32)
                row = row + which * half
                own[row : row + levels, :] = ref[0, lat, SHIFT + col].astype(F32)
    for copy in copies[2:]:
        copy.wait()
    rim32[half : half + lats, :cols] = land_v[...].astype(F32)
    own[2 * half : 2 * half + 1, :] = gain_v[...]
    own[2 * half + 1 : 2 * half + 2, : bias.shape[1]] = bias_v[...]
    own[2 * half + 8 : 2 * half + 8 + lats, :cols] = land_v[...].astype(F32)
    rim[...] = rim32[...].astype(BF16)
    rim_cot[...] = rim_cot32[...].astype(BF16)


def unpack_kernel(own, back, grid, grid_v, sems):
    lats, cols, levels, width = grid.shape[1:]
    came = back[...].astype(F32)
    for lat in range(lats):
        for col in range(cols):
            row = (lat * SHIFT + col % SHIFT) * levels
            if col < SHIFT:
                grid_v[0, lat, col] = came[row : row + levels]
            else:
                grid_v[0, lat, col] = own[row : row + levels, :]
    started(grid_v, grid, sems, 0).wait()


def land_column(land, rows, first):
    lats, cols = land.shape
    row = lax.broadcasted_iota(jnp.int32, (rows, lats), 0)
    lat = lax.div(row, rows // lats)
    pick = (lat == lax.broadcasted_iota(jnp.int32, (rows, lats), 1)).astype(F32)
    lines = dot(pick.astype(BF16), land.astype(BF16))
    row = lax.broadcasted_iota(jnp.int32, (rows, cols), 0)
    column = lax.broadcasted_iota(jnp.int32, (rows, cols), 1)
    levels = rows // (lats * SHIFT)
    here = column == lax.rem(lax.div(row, levels), SHIFT) + first
    return jnp.sum(jnp.where(here, lines, 0.0), axis=1, keepdims=True)


def head_masks(dtype, size):
    lane = lax.broadcasted_iota(jnp.int32, (1, GROUP), 1)
    return [
        (lax.div(lane, size) == part).astype(F32).astype(dtype) for part in range(GROUP // size)
    ]


def stacked(block, masks):
    return jnp.concatenate([block * mask for mask in masks], axis=0)


def folded(block, masks):
    rows = block.shape[0] // len(masks)
    return sum(block[i * rows : (i + 1) * rows] * mask for i, mask in enumerate(masks))


def back_through(grad_out, probs, qkv, keys_t, weight_out, grad_proj, size, land):
    count, width = grad_out.shape
    per = GROUP // size
    scale = size ** (-0.5)
    masks_b, masks = head_masks(BF16, size), head_masks(F32, size)
    att_t = dot_last(weight_out[...], grad_out)
    grad_att = att_t.T.astype(BF16)
    att_t = att_t.astype(BF16)
    lane = lax.broadcasted_iota(jnp.int32, (1, GROUP), 1)
    bias_row = jnp.zeros((1, GROUP), F32)
    for group in range(width // GROUP):
        at = group * GROUP
        values = qkv[:, 2 * width + at : 2 * width + at + GROUP]
        grad_probs = dot(stacked(values, masks_b), att_t[at : at + GROUP, :])
        scores_b, queries_t = [], []
        for part in range(per):
            head = group * per + part
            weights = probs[head * count : (head + 1) * count, :].astype(F32)
            grad_weights = grad_probs[part * count : (part + 1) * count]
            inner = jnp.sum(weights * grad_weights, axis=0, keepdims=True)
            grad_scores = weights * (grad_weights - inner)
            if land is not None:
                on_land = jnp.sum(grad_scores * land, axis=0, keepdims=True)
                on_land = jnp.sum(on_land, axis=1, keepdims=True)
                bias_row = bias_row + jnp.where(lane == head, on_land, 0.0)
            scaled_b = (grad_scores * scale).astype(BF16)
            scores_b.append(scaled_b)
            queries_t.append(dot(keys_t[head * size : (head + 1) * size, :], scaled_b))
        queries = qkv[:, at : at + GROUP]
        grad_keys = dot(jnp.concatenate(scores_b, axis=0), queries)
        mixed = probs[group * per * count : (group + 1) * per * count, :]
        grad_values = dot(mixed, grad_att[:, at : at + GROUP])
        grad_proj[:, at : at + GROUP] = jnp.concatenate(queries_t, axis=0).T.astype(BF16)
        grad_proj[:, width + at : width + at + GROUP] = folded(grad_keys, masks).astype(BF16)
        grad_proj[:, 2 * width + at : 2 * width + at + GROUP] = folded(grad_values, masks).astype(
            BF16
        )
    return bias_row


def through_norm(grad_proj, weight_t, gain, normed, inverse):
    scaled = dot(grad_proj, weight_t[...]) * gain
    mean = jnp.mean(scaled, axis=-1, keepdims=True)
    along = jnp.mean(scaled * normed, axis=-1, keepdims=True)
    return inverse * (scaled - mean - normed * along)


def ready_kernel(after, weight_qkv, weight_out, qkv_v, qkv_t, out_v, sems):
    copies = [
        started(weight_qkv, qkv_v, sems, 0),
        started(weight_out, out_v, sems, 1),
    ]
    copies[0].wait()
    width = weight_qkv.shape[0]
    for part in range(weight_qkv.shape[1] // width):
        rows = slice(part * width, (part + 1) * width)
        qkv_t[rows, :] = qkv_v[:, rows].T
    copies[1].wait()


def forward_kernel(
    own, rim, weight_qkv,
    normed_t, qkv, probs, attended_t, extra, normed_out,
    queries_t, values_t,
    *, heads, lats, cols,
):
    width = own.shape[1]
    size = width // heads
    count = qkv.shape[0]
    half = count // 2
    per = GROUP // size
    scale = size ** (-0.5)
    masks_b = head_masks(BF16, size)
    params = own[count:, :]
    came = rim[...].astype(F32)
    gain = params[0:1, :]
    values = jnp.concatenate([own[:half, :], came[:half]], axis=0)
    centred = values - jnp.mean(values, axis=-1, keepdims=True)
    inverse = lax.rsqrt(jnp.mean(centred * centred, axis=-1, keepdims=True) + EPSILON)
    normed = centred * inverse
    normed_out[...] = normed
    normed_b = (normed * gain).astype(BF16)
    normed_t[...] = normed_b.T
    land = jnp.concatenate(
        [
            land_column(params[8 : 8 + lats, :cols], half, SHIFT),
            land_column(came[half : half + lats, :cols], half, 0),
        ],
        axis=0,
    )
    extra[:, :GROUP] = jnp.broadcast_to(land, (count, GROUP))
    extra[:, GROUP:] = jnp.broadcast_to(inverse, (count, GROUP))
    for part, turned in enumerate((queries_t, None, values_t)):
        columns = slice(part * width, (part + 1) * width)
        qkv[:, columns] = dot(normed_b, weight_qkv[:, columns]).astype(BF16)
        if turned is not None:
            turned[...] = qkv[:, columns].T
    for group in range(width // GROUP):
        at = group * GROUP
        keys = qkv[:, width + at : width + at + GROUP]
        scores = dot(stacked(keys, masks_b), queries_t[at : at + GROUP, :])
        for part in range(per):
            head = group * per + part
            block = scores[part * count : (part + 1) * count] * scale
            block = block + params[1:2, head : head + 1] * land
            block = jnp.exp(block - jnp.max(block, axis=0, keepdims=True))
            weights = block * (1.0 / jnp.sum(block, axis=0, keepdims=True))
            weights_b = weights.astype(BF16)
            probs[head * count : (head + 1) * count, :] = weights_b
            out = dot(values_t[head * size : (head + 1) * size, :], weights_b)
            attended_t[head * size : (head + 1) * size, :] = out.astype(BF16)


def first_backward_kernel(
    own, rim, qkv, probs, weight_out, weight_t, extra, normed,
    skip, cot,
    keys_t, grad_proj,
    *, heads,
):
    count, width = cot.shape
    half = count // 2
    came = rim[...].astype(F32)
    grad_out = jnp.concatenate([own[half:count, :], came[:half]], axis=0)
    cot[...] = grad_out.astype(BF16)
    keys_t[...] = qkv[:, width : 2 * width].T
    back_through(cot[...], probs, qkv, keys_t, weight_out, grad_proj, width // heads, None)
    gain, inverse = own[count : count + 1, :], extra[:, GROUP : GROUP + 1]
    skip[...] = (
        through_norm(grad_proj[...], weight_t, gain, normed[...], inverse) + grad_out
    ).astype(BF16)


def backward_kernel(
    skip, cot, qkv, probs, weight_out, extra, normed_t, attended_t,
    total_out, grad_proj, bias_out, give,
    keys_t,
    *, heads,
):
    count, width = cot.shape
    core, _, _ = position()
    total_out[...] = (cot[...].astype(F32) + skip[...].astype(F32)).astype(BF16)
    keys_t[...] = qkv[:, width : 2 * width].T
    bias_row = back_through(
        total_out[...], probs, qkv, keys_t, weight_out, grad_proj, width // heads,
        extra[:, :1],
    )
    bias_out[...] = jnp.broadcast_to(bias_row, bias_out.shape)
    half = width // 2
    rows = aligned((1 - core) * half, half)
    weight_rows(rows, normed_t, attended_t, grad_proj, total_out, bias_row, give)


def weight_rows(rows, normed_t, attended_t, grad_proj, total, bias_row, out):
    tokens = normed_t[rows, :]
    three = grad_proj.shape[1]
    out[:, :CUT] = dot(tokens, grad_proj[:, :CUT]).astype(out.dtype)
    out[:, CUT : CUT + GROUP] = jnp.broadcast_to(bias_row, (out.shape[0], GROUP)).astype(out.dtype)
    out[:, CUT + GROUP : three + GROUP] = dot(tokens, grad_proj[:, CUT:]).astype(out.dtype)
    out[:, three + GROUP :] = dot(attended_t[rows, :], total[...]).astype(out.dtype)


def finish_kernel(
    total, grad_proj, bias_row, normed_t, attended_t, normed, extra, weight_t, params,
    keep, own, back,
):
    count, width = total.shape
    half = width // 2
    core, _, _ = position()
    rows = aligned(core * half, half)
    bias_b = bias_row[:1, :].astype(BF16).astype(F32)
    weight_rows(rows, normed_t, attended_t, grad_proj, total, bias_b, keep)
    inverse = extra[:, GROUP : GROUP + 1]
    final = through_norm(grad_proj[...], weight_t, params[count : count + 1, :], normed[...], inverse)
    final = final + total[...].astype(F32)
    own[...] = final[: count // 2]
    back[...] = final[count // 2 :].astype(BF16)


def first_kernel(keep, came, give_p, kept_p, kept_q, *rest):
    _, y, z = position()
    *give_q, total = rest
    wide_p = give_p.shape[1]
    half = keep.shape[0] // 2
    total[...] = keep[...] + came[...].astype(F32)
    give_p[...] = total[aligned((1 - y) * half, half), :wide_p].astype(BF16)
    mine = aligned(y * half, half)
    kept_p[:, :CUT] = total[mine, :CUT]
    kept_p[:, CUT:] = total[mine, CUT:wide_p].astype(BF16).astype(F32)
    piece = kept_q.shape[0]
    kept_q[...] = total[aligned(z * piece, piece), wide_p:]
    for other, ref in zip(range(len(give_q), 0, -1), give_q):
        ref[...] = total[aligned((z ^ other) * piece, piece), wide_p:].astype(BF16)


def second_kernel(after, kept_p, came_p, kept_q, *rest):
    _, y, z = position()
    count = (len(rest) - 5) // 2
    came_q, (give_q, left_q, left_p) = rest[:count], rest[count : count + 3]
    *give_p, total_p, total_q = rest[count + 3 :]
    total_p[...] = kept_p[...] + came_p[...].astype(F32)
    piece = left_p.shape[0]
    mine = aligned(z * piece, piece)
    left_p[:, :CUT] = total_p[mine, :CUT]
    left_p[:, CUT:] = total_p[mine, CUT:].astype(BF16).astype(F32)
    for other, ref in zip(range(len(give_p), 0, -1), give_p):
        ref[...] = total_p[aligned((z ^ other) * piece, piece), :].astype(BF16)
    total = kept_q[...]
    for ref in came_q:
        total = total + ref[...].astype(F32)
    total_q[...] = total
    half = give_q.shape[0]
    give_q[...] = total_q[aligned((1 - y) * half, half), :].astype(BF16)
    left_q[...] = total_q[aligned(y * half, half), :]


def third_kernel(left_p, left_q, came_q, *rest):
    _, _, z = position()
    *came_p, piece_p, piece_q, bias = rest
    total = left_p[:, :CUT]
    for ref in came_p:
        total = total + ref[:, :CUT].astype(F32)
    piece_p[...] = total.astype(BF16)
    piece_q[...] = (left_q[...] + came_q[...].astype(F32)).astype(BF16)
    terms = [left_p[:8, CUT:]] + [ref[...].astype(F32)[:8, CUT:] for ref in came_p[::-1]]
    total = jnp.zeros_like(terms[0])
    for source in range(len(terms)):
        for other, term in enumerate(terms):
            total = total + jnp.where((z ^ other) == source, term, 0.0)
    bias[...] = total


def fourth_kernel(piece_q, other_q, *rest):
    _, y, z = position()
    *parts_p, block_p, block_q = rest
    piece = parts_p[0].shape[0]
    for other, part in enumerate(parts_p):
        block_p[aligned((z ^ other) * piece, piece), :] = part[...]
    piece = piece_q.shape[0]
    block_q[aligned(y * piece, piece), :] = piece_q[...]
    block_q[aligned((1 - y) * piece, piece), :] = other_q[...]


def fifth_kernel(weight_qkv, gain, bias, block_p, other_p, *rest):
    *parts_q, half, row = rest
    core, y, z = position()
    rows = half.shape[0]
    mine = aligned(core * rows, rows)
    piece = block_p.shape[0]
    half[aligned(y * piece, piece), :CUT] = block_p[...]
    half[aligned((1 - y) * piece, piece), :CUT] = other_p[...]
    piece = parts_q[0].shape[0]
    for other, part in enumerate(parts_q):
        half[aligned((z ^ other) * piece, piece), CUT:] = part[...]
    three = weight_qkv.shape[1]
    wide = half[:, :three].astype(F32)
    gain_half = jnp.sum(wide * weight_qkv[mine, :].astype(F32), axis=1, keepdims=True)
    gain_half = jnp.broadcast_to(gain_half, (rows, GROUP)).T[:8]
    own_gain = jnp.where(core == 0, gain[:, :rows], gain[:, rows:])
    gain_half = gain_half / own_gain
    out = half[:, three:].astype(F32)
    square = jnp.sum(jnp.sum(wide * wide, axis=0, keepdims=True), axis=1, keepdims=True)
    square = square + jnp.sum(jnp.sum(out * out, axis=0, keepdims=True), axis=1, keepdims=True)
    square = square + jnp.sum(gain_half[:1] * gain_half[:1], axis=1, keepdims=True)
    square = square + 0.5 * jnp.sum(bias[:1, :] * bias[:1, :], axis=1, keepdims=True)
    row[:, :rows] = gain_half
    row[:, rows:] = jnp.broadcast_to(square, (8, GROUP))


def last_kernel(
    half, other, row, row_core, row_section, row_both, bias,
    grad_qkv, grad_out, grad_gain, grad_bias,
    qkv_v, out_v, gain_v, bias_v, sems,
    *, entries,
):
    core, _, _ = position()
    rows, three = half.shape[0], grad_qkv.shape[1]
    square = row[:1, rows : rows + 1] + row_core[:1, rows : rows + 1]
    square = square + (row_section[:1, rows : rows + 1] + row_both[:1, rows : rows + 1])
    factor = jnp.minimum(1.0, lax.rsqrt(square / entries + 1e-06))
    sent = []
    piece = 64
    for which, ref in enumerate((half, other)):
        base = core * rows if which == 0 else (1 - core) * rows
        for part in range(rows // piece):
            here = slice(part * piece, (part + 1) * piece)
            at = aligned(base + part * piece, piece)
            slot = slice(which * rows + part * piece, which * rows + (part + 1) * piece)
            qkv_v[slot, :] = ref[here, :three].astype(F32) * factor
            sent.append(started(qkv_v.at[slot, :], grad_qkv.at[at, :], sems, len(sent)))
            out_v[slot, :] = ref[here, three:].astype(F32) * factor
            sent.append(started(out_v.at[slot, :], grad_out.at[at, :], sems, len(sent)))
    mine, its = row[:1, :rows] * factor, row_core[:1, :rows] * factor
    gain_v[:, :rows] = jnp.where(core == 0, mine, its)
    gain_v[:, rows:] = jnp.where(core == 0, its, mine)
    bias_v[...] = bias[:1, : bias_v.shape[1]] * factor
    sent.append(started(gain_v, grad_gain, sems, len(sent)))
    sent.append(started(bias_v, grad_bias, sems, len(sent)))
    for copy in sent:
        copy.wait()


def far_first(pieces, axis):
    others = range(len(pieces), 0, -1)
    return [swapped(piece, axis, other) for other, piece in zip(others, pieces)]


def to_all(piece, axis):
    return [swapped(piece, axis, other) for other in range(1, lax.axis_size(axis))]


def vmem(dims, dtype):
    return pltpu.VMEM(dims, dtype)


def copies(number):
    return pltpu.SemaphoreType.DMA((number,))


def body(inputs, cotangent, land_sea, gains, qkv_weight, out_weight, land_bias):
    weight_qkv, weight_out = qkv_weight[0], out_weight[0]
    levels, lats, cols, width = inputs.shape[1:]
    heads = land_bias.shape[1]
    half = levels * lats * SHIFT
    count = 2 * half
    packed = half * 2 + 16
    lons = lax.axis_size("lon")

    tokens = inputs.transpose(0, 2, 3, 1, 4)
    own_cot = cotangent.transpose(0, 2, 3, 1, 4)

    own, rim, rim_cot = call(
        pack_kernel,
        [
            shape((packed, width), F32),
            shape((half + 8, width), BF16),
            shape((half + 8, width), BF16),
        ],
        scratch=[
            vmem(tokens.shape, BF16),
            vmem(tokens.shape, BF16),
            vmem(land_sea.shape, jnp.int32),
            vmem(gains.shape, F32),
            vmem(land_bias.shape, F32),
            vmem((half + 8, width), F32),
            vmem((half + 8, width), F32),
            copies(5),
        ],
        places="hhhhh",
        operands=(tokens, own_cot, land_sea, gains, land_bias),
        limit=60,
    )
    rim = from_behind(rim, "lon", -1)
    rim_cot = from_behind(rim_cot, "lon", -1)
    qkv_v, qkv_t, out_v = call(
        ready_kernel,
        [
            shape(weight_qkv.shape, BF16),
            shape(weight_qkv.shape[::-1], BF16),
            shape(weight_out.shape, BF16),
        ],
        scratch=[copies(2)],
        places="ahh",
        operands=(own, weight_qkv, weight_out),
        limit=48,
    )
    normed_t, qkv, probs, attended_t, extra, normed = call(
        functools.partial(forward_kernel, heads=heads, lats=lats, cols=cols),
        [
            shape((width, count), BF16),
            shape((count, 3 * width), BF16),
            shape((heads * count, count), BF16),
            shape((width, count), BF16),
            shape((count, 2 * GROUP), F32),
            shape((count, width), F32),
        ],
        scratch=[vmem((width, count), BF16), vmem((width, count), BF16)],
        operands=(own, rim, qkv_v),
        flops=10**9,
    )
    skip, cot = call(
        functools.partial(first_backward_kernel, heads=heads),
        [shape((count, width), BF16), shape((count, width), BF16)],
        scratch=[vmem((width, count), BF16), vmem((count, 3 * width), BF16)],
        operands=(own, rim_cot, qkv, probs, out_v, qkv_t, extra, normed),
        flops=10**9,
    )
    skip = passed_along(skip, "section", -1)
    rows, wide = width // 2, 4 * width + GROUP
    total, grad_proj, bias_row, give = call(
        functools.partial(backward_kernel, heads=heads),
        [
            shape((count, width), BF16),
            shape((count, 3 * width), BF16),
            shape((8, GROUP), F32),
            shape((rows, wide), BF16),
        ],
        scratch=[vmem((width, count), BF16)],
        operands=(skip, cot, qkv, probs, out_v, extra, normed_t, attended_t),
        flops=10**9,
    )
    came = swapped(give, "lat", 1)
    keep, own_grad, back = call(
        finish_kernel,
        [
            shape((rows, wide), F32),
            shape((half, width), F32),
            shape((half, width), BF16),
        ],
        operands=(
            total, grad_proj, bias_row, normed_t, attended_t, normed, extra, qkv_t, own,
        ),
        flops=5 * 10**8,
    )
    back = from_behind(back, "lon", 1)
    entries = 2 * (4 * width * width + width + heads)
    if rows // 2 // lons % 16 == 0 and lons & (lons - 1) == 0:
        grads = staged(keep, came, back, qkv_v, gains, lons, heads, entries)
    else:
        grads = plain(keep, came, weight_qkv, gains, heads, entries)
    (final_grad,) = call(
        unpack_kernel,
        [shape(tokens.shape, F32)],
        scratch=[vmem(tokens.shape, F32), copies(1)],
        out_places="h",
        operands=(own_grad, back),
    )
    final_grad = final_grad.transpose(0, 3, 1, 2, 4)
    return (final_grad, *(grad[None] for grad in grads))


def staged(keep, came, after, weight_qkv, gains, lons, heads, entries):
    rows, wide = keep.shape
    width = 2 * rows
    wide_p = CUT + GROUP
    wide_q = wide - wide_p
    some = range(lons - 1)
    several = "v" * len(some)
    give_p, kept_p, kept_q, *give_q = call(
        first_kernel,
        [
            shape((rows // 2, wide_p), BF16),
            shape((rows // 2, wide_p), F32),
            shape((rows // lons, wide_q), F32),
            *(shape((rows // lons, wide_q), BF16) for _ in some),
        ],
        scratch=[vmem((rows, wide), F32)],
        operands=(keep, came),
    )
    came_p = swapped(give_p, "lat", 2)
    came_q = far_first(give_q, "lon")
    piece = rows // 2 // lons
    give_q, left_q, left_p, *give_p = call(
        second_kernel,
        [
            shape((piece, wide_q), BF16),
            shape((piece, wide_q), F32),
            shape((piece, wide_p), F32),
            *(shape((piece, wide_p), BF16) for _ in some),
        ],
        scratch=[vmem((rows // 2, wide_p), F32), vmem((rows // lons, wide_q), F32)],
        places="avvv" + several,
        operands=(after, kept_p, came_p, kept_q, *came_q),
    )
    came_p = far_first(give_p, "lon")
    came_q = swapped(give_q, "lat", 2)
    piece_p, piece_q, bias = call(
        third_kernel,
        [
            shape((piece, CUT), BF16),
            shape((piece, wide_q), BF16),
            shape((8, GROUP), F32),
        ],
        operands=(left_p, left_q, came_q, *came_p),
    )
    others_p = to_all(piece_p, "lon")
    other_q = swapped(piece_q, "lat", 2)
    block_p, block_q = call(
        fourth_kernel,
        [shape((rows // 2, CUT), BF16), shape((rows // lons, wide_q), BF16)],
        operands=(piece_q, other_q, piece_p, *others_p),
    )
    other_p = swapped(block_p, "lat", 2)
    others_q = to_all(block_q, "lon")
    half, row = call(
        fifth_kernel,
        [shape((rows, 4 * width), BF16), shape((8, rows + GROUP), F32)],
        operands=(weight_qkv, gains, bias, block_p, other_p, block_q, *others_q),
    )
    row_section = swapped(row, "section", 1)
    row_both = lax.ppermute(row, ("section", "lat"), across())
    row_core = swapped(row, "lat", 1)
    other = swapped(half, "lat", 1)
    grads = call(
        functools.partial(last_kernel, entries=entries),
        [
            shape((width, 3 * width), F32),
            shape((width, width), F32),
            shape((1, width), F32),
            shape((1, heads), F32),
        ],
        scratch=[
            vmem((width, 3 * width), F32),
            vmem((width, width), F32),
            vmem((1, width), F32),
            vmem((1, heads), F32),
            copies(4 * rows // 64 + 2),
        ],
        out_places="hhhh",
        operands=(half, other, row, row_core, row_section, row_both, bias),
    )
    return grads[0], grads[1], grads[2][0], grads[3][0]


def across():
    sections, lats = lax.axis_size("section"), lax.axis_size("lat")
    return [
        (s * lats + i, (sections - 1 - s) * lats + (i ^ 1))
        for s in range(sections)
        for i in range(lats)
    ]


def split_two(block, axis, bit):
    mine = (lax.axis_index(axis) // bit) % 2
    pair = block.reshape(2, block.shape[0] // 2, -1)
    give = lax.dynamic_index_in_dim(pair, 1 - mine, 0, keepdims=False).astype(BF16)
    return give, lax.dynamic_index_in_dim(pair, mine, 0, keepdims=False)


def doubled(block, axis, bit):
    mine = (lax.axis_index(axis) // bit) % 2
    other = swapped(block, axis, bit)
    low = jnp.where(mine == 0, block, other)
    high = jnp.where(mine == 0, other, block)
    return jnp.concatenate([low, high], axis=0)


def scattered(block, axis):
    count = lax.axis_size(axis)
    mine = lax.axis_index(axis)
    pieces = block.reshape(count, block.shape[0] // count, -1)
    total = lax.dynamic_index_in_dim(pieces, mine, 0, keepdims=False)
    others = []
    for by in range(1, count):
        give = lax.dynamic_index_in_dim(pieces, (mine + by) % count, 0, keepdims=False)
        others.append(from_behind(give.astype(BF16), axis, by))
    for other in others:
        total = total + other.astype(F32)
    return total, others


def gathered(block, axis):
    count = lax.axis_size(axis)
    mine = lax.axis_index(axis)
    whole = jnp.zeros((count,) + block.shape, block.dtype)
    whole = lax.dynamic_update_index_in_dim(whole, block, mine, 0)
    for by in range(1, count):
        whole = lax.dynamic_update_index_in_dim(
            whole, from_behind(block, axis, by), (mine - by) % count, 0
        )
    return whole.reshape(count * block.shape[0], -1)


def sum_squares(block):
    wide = block.astype(F32)
    return jnp.sum(wide * wide)


def plain(keep, came, weight_qkv, gains, heads, entries):
    width = gains.shape[1]
    lat, lon = lax.axis_index("lat"), lax.axis_index("lon")
    part = keep + came.astype(F32)
    give, keep = split_two(part, "lat", 2)
    came = swapped(give, "lat", 2).astype(F32)
    column = lax.broadcasted_iota(jnp.int32, keep.shape, 1)
    is_bias = (column >= CUT) & (column < CUT + GROUP)
    part = jnp.where(is_bias, lax.reduce_precision(keep, 8, 7), keep) + came
    bias_part = lax.reduce_precision(part[:1, CUT : CUT + GROUP], 8, 7)
    part, others = scattered(part, "lon")
    terms = [bias_part] + [other[:1, CUT : CUT + GROUP].astype(F32) for other in others]
    terms = jnp.concatenate(terms[:1] + terms[:0:-1], axis=0)
    bias = jnp.sum(jnp.roll(terms, lon, axis=0), axis=0)[:heads]
    part = jnp.concatenate([part[:, :CUT], part[:, CUT + GROUP :]], axis=1).astype(BF16)
    half = doubled(gathered(part, "lon"), "lat", 2)
    mine = lat % 2
    weight_half = lax.dynamic_slice_in_dim(weight_qkv, mine * (width // 2), width // 2, 0)
    gain_half = lax.dynamic_slice_in_dim(gains[0], mine * (width // 2), width // 2, 0)
    weighed = half[:, : 3 * width].astype(F32) * weight_half.astype(F32)
    gain_half = jnp.sum(weighed, axis=1) / gain_half
    square = sum_squares(half) + sum_squares(gain_half) + 0.5 * sum_squares(bias)
    square = square.reshape(1)
    square = square + swapped(square, "lat", 1)
    square = square + swapped(square, "section", 1)
    factor = jnp.minimum(1.0, lax.rsqrt(square[0] / entries + 1e-06))
    grads = doubled(half, "lat", 1).astype(F32) * factor
    gain = doubled(gain_half.reshape(-1, 1), "lat", 1)[:, 0] * factor
    return grads[:, : 3 * width], grads[:, 3 * width :], gain, bias * factor


def solution(mesh):
    placed = (
        P("section", None, "lat", "lon", None),
        P("section", None, "lat", "lon", None),
        P("lat", "lon"),
        P("section", None),
        P("section", None, None),
        P("section", None, None),
        P("section", None),
    )
    return jax.shard_map(
        body,
        mesh=mesh,
        in_specs=placed,
        out_specs=(
            P("section", None, "lat", "lon", None),
            P("section", None, None),
            P("section", None, None),
            P("section", None),
            P("section", None),
        ),
        check_vma=False,
    )
```

```python
import functools

import jax
import jax.numpy as jnp
from jax import lax
from jax.experimental import pallas as pl
from jax.experimental.pallas import tpu as pltpu
from jax.sharding import PartitionSpec as P

SHIFT = 6
GROUP = 128
CUT = 1280
EPSILON = 1e-05
F32 = jnp.float32
BF16 = jnp.bfloat16


def from_behind(value, axis, by):
    count = lax.axis_size(axis)
    return lax.ppermute(value, axis, [(i, (i + by) % count) for i in range(count)])


def passed_along(block, axis, distance):
    devices = range(lax.axis_size(axis))
    route = [(i - distance, i) for i in devices if i - distance in devices]
    return lax.ppermute(block, axis, route)


def swapped(value, axis, bit):
    count = lax.axis_size(axis)
    return lax.ppermute(value, axis, [(i, i ^ bit) for i in range(count)])


def dot(left, right):
    return jnp.dot(left, right, preferred_element_type=F32)


def dot_last(left, right):
    return lax.dot_general(left, right, (((1,), (1,)), ((), ())), preferred_element_type=F32)


def call(kernel, outs, scratch=(), places="", out_places="", operands=(), flops=10**8, limit=8):
    spaces = {"v": pltpu.VMEM, "s": pltpu.SMEM, "a": pl.ANY, "h": pltpu.HBM}
    places = places or "v" * len(operands)
    out_places = out_places or "v" * len(outs)
    moved = sum(o.size * o.dtype.itemsize for o in list(outs) + list(operands))
    return pl.pallas_call(
        kernel,
        out_shape=list(outs),
        in_specs=[pl.BlockSpec(memory_space=spaces[letter]) for letter in places],
        out_specs=[pl.BlockSpec(memory_space=spaces[letter]) for letter in out_places],
        scratch_shapes=list(scratch),
        compiler_params=pltpu.CompilerParams(vmem_limit_bytes=limit * 2**20),
        cost_estimate=pl.CostEstimate(flops=flops, bytes_accessed=moved, transcendentals=0),
    )(*operands)


def started(source, target, semaphores, index):
    copy = pltpu.make_async_copy(source, target, semaphores.at[index])
    copy.start()
    return copy


def shape(dims, dtype):
    return jax.ShapeDtypeStruct(dims, dtype)


def aligned(start, size):
    return pl.ds(pl.multiple_of(start, size), size)


def position():
    lat, lon = lax.axis_index("lat"), lax.axis_index("lon")
    return lax.rem(lat, 2), lax.div(lat, 2), lon


def pack_kernel(
    tokens, cot, land, gain, bias, own, rim,
    tokens_v, cot_v, land_v, gain_v, bias_v, rim32, sems,
):
    arrays = ((tokens, tokens_v), (cot, cot_v), (land, land_v), (gain, gain_v), (bias, bias_v))
    copies = [started(source, target, sems, i) for i, (source, target) in enumerate(arrays)]
    lats, cols, levels, width = tokens.shape[1:]
    half = levels * lats * SHIFT
    rim32[2 * half :, :] = jnp.zeros((rim32.shape[0] - 2 * half, width), F32)
    own[2 * half :, :] = jnp.zeros((own.shape[0] - 2 * half, width), F32)
    for which, ref in enumerate((tokens_v, cot_v)):
        copies[which].wait()
        for lat in range(lats):
            for col in range(cols):
                row = which * half + (lat * SHIFT + col % SHIFT) * levels
                part = rim32 if col < SHIFT else own
                part[row : row + levels, :] = ref[0, lat, col].astype(F32)
    for copy in copies[2:]:
        copy.wait()
    rim32[2 * half : 2 * half + lats, :cols] = land_v[...].astype(F32)
    own[2 * half : 2 * half + 1, :] = gain_v[...]
    own[2 * half + 1 : 2 * half + 2, : bias.shape[1]] = bias_v[...]
    own[2 * half + 8 : 2 * half + 8 + lats, :cols] = land_v[...].astype(F32)
    rim[...] = rim32[...].astype(BF16)


def unpack_kernel(own, back, grid, grid_v, sems):
    lats, cols, levels, width = grid.shape[1:]
    came = back[...].astype(F32)
    for lat in range(lats):
        for col in range(cols):
            row = (lat * SHIFT + col % SHIFT) * levels
            if col < SHIFT:
                grid_v[0, lat, col] = came[row : row + levels]
            else:
                grid_v[0, lat, col] = own[row : row + levels, :]
    started(grid_v, grid, sems, 0).wait()


def land_column(land, rows, first):
    lats, cols = land.shape
    row = lax.broadcasted_iota(jnp.int32, (rows, lats), 0)
    lat = lax.div(row, rows // lats)
    pick = (lat == lax.broadcasted_iota(jnp.int32, (rows, lats), 1)).astype(F32)
    lines = dot(pick.astype(BF16), land.astype(BF16))
    row = lax.broadcasted_iota(jnp.int32, (rows, cols), 0)
    column = lax.broadcasted_iota(jnp.int32, (rows, cols), 1)
    levels = rows // (lats * SHIFT)
    here = column == lax.rem(lax.div(row, levels), SHIFT) + first
    return jnp.sum(jnp.where(here, lines, 0.0), axis=1, keepdims=True)


def head_masks(dtype, size):
    lane = lax.broadcasted_iota(jnp.int32, (1, GROUP), 1)
    return [
        (lax.div(lane, size) == part).astype(F32).astype(dtype) for part in range(GROUP // size)
    ]


def stacked(block, masks):
    return jnp.concatenate([block * mask for mask in masks], axis=0)


def folded(block, masks):
    rows = block.shape[0] // len(masks)
    return sum(block[i * rows : (i + 1) * rows] * mask for i, mask in enumerate(masks))


def back_through(grad_out, probs, probs_b, qkv, keys_t, weight_out, grad_proj, size, land):
    count, width = grad_out.shape
    per = GROUP // size
    scale = size ** (-0.5)
    masks_b, masks = head_masks(BF16, size), head_masks(F32, size)
    att_t = dot_last(weight_out[...], grad_out)
    grad_att = att_t.T.astype(BF16)
    att_t = att_t.astype(BF16)
    lane = lax.broadcasted_iota(jnp.int32, (1, GROUP), 1)
    bias_row = jnp.zeros((1, GROUP), F32)
    for group in range(width // GROUP):
        at = group * GROUP
        values = qkv[:, 2 * width + at : 2 * width + at + GROUP]
        grad_probs = dot(stacked(values, masks_b), att_t[at : at + GROUP, :])
        scores_b, queries_t = [], []
        for part in range(per):
            head = group * per + part
            weights = probs[head * count : (head + 1) * count, :].astype(F32)
            grad_weights = grad_probs[part * count : (part + 1) * count]
            inner = jnp.sum(weights * grad_weights, axis=0, keepdims=True)
            grad_scores = weights * (grad_weights - inner)
            if land is not None:
                on_land = jnp.sum(grad_scores * land, axis=0, keepdims=True)
                on_land = jnp.sum(on_land, axis=1, keepdims=True)
                bias_row = bias_row + jnp.where(lane == head, on_land, 0.0)
            scaled_b = (grad_scores * scale).astype(BF16)
            scores_b.append(scaled_b)
            queries_t.append(dot(keys_t[head * size : (head + 1) * size, :], scaled_b))
        queries = qkv[:, at : at + GROUP]
        grad_keys = dot(jnp.concatenate(scores_b, axis=0), queries)
        mixed = probs_b[group * per * count : (group + 1) * per * count, :]
        grad_values = dot(mixed, grad_att[:, at : at + GROUP])
        grad_proj[:, at : at + GROUP] = jnp.concatenate(queries_t, axis=0).T.astype(BF16)
        grad_proj[:, width + at : width + at + GROUP] = folded(grad_keys, masks).astype(BF16)
        grad_proj[:, 2 * width + at : 2 * width + at + GROUP] = folded(grad_values, masks).astype(
            BF16
        )
    return bias_row


def through_norm(grad_proj, weight_t, gain, normed, inverse):
    scaled = dot(grad_proj, weight_t[...]) * gain
    mean = jnp.mean(scaled, axis=-1, keepdims=True)
    along = jnp.mean(scaled * normed, axis=-1, keepdims=True)
    return inverse * (scaled - mean - normed * along)


def ready_kernel(after, weight_qkv, weight_out, qkv_v, qkv_t, out_v, sems):
    copies = [
        started(weight_qkv, qkv_v, sems, 0),
        started(weight_out, out_v, sems, 1),
    ]
    copies[0].wait()
    width = weight_qkv.shape[0]
    for part in range(weight_qkv.shape[1] // width):
        rows = slice(part * width, (part + 1) * width)
        qkv_t[rows, :] = qkv_v[:, rows].T
    copies[1].wait()


def forward_kernel(
    own, rim, weight_qkv, weight_t, weight_out,
    skip, cot, normed_t, qkv, probs_b, attended_t, extra, normed_out,
    probs, queries_t, keys_t, values_t, grad_proj,
    *, heads, lats, cols,
):
    width = own.shape[1]
    size = width // heads
    half = cot.shape[0] // 2
    count = 2 * half
    per = GROUP // size
    scale = size ** (-0.5)
    masks_b = head_masks(BF16, size)
    mine = own[: 2 * half, :]
    params = own[2 * half :, :]
    came = rim[...].astype(F32)
    gain = params[0:1, :]
    values = jnp.concatenate([mine[:half], came[:half]], axis=0)
    centred = values - jnp.mean(values, axis=-1, keepdims=True)
    inverse = lax.rsqrt(jnp.mean(centred * centred, axis=-1, keepdims=True) + EPSILON)
    normed = centred * inverse
    normed_out[...] = normed
    normed_b = (normed * gain).astype(BF16)
    normed_t[...] = normed_b.T
    land = jnp.concatenate(
        [
            land_column(params[8 : 8 + lats, :cols], half, SHIFT),
            land_column(came[2 * half : 2 * half + lats, :cols], half, 0),
        ],
        axis=0,
    )
    extra[:, :GROUP] = jnp.broadcast_to(land, (count, GROUP))
    extra[:, GROUP:] = jnp.broadcast_to(inverse, (count, GROUP))
    for part, turned in enumerate((queries_t, keys_t, values_t)):
        columns = slice(part * width, (part + 1) * width)
        qkv[:, columns] = dot(normed_b, weight_qkv[:, columns]).astype(BF16)
        turned[...] = qkv[:, columns].T
    for group in range(width // GROUP):
        at = group * GROUP
        keys = qkv[:, width + at : width + at + GROUP]
        scores = dot(stacked(keys, masks_b), queries_t[at : at + GROUP, :])
        for part in range(per):
            head = group * per + part
            block = scores[part * count : (part + 1) * count] * scale
            block = block + params[1:2, head : head + 1] * land
            block = jnp.exp(block - jnp.max(block, axis=0, keepdims=True))
            weights = block * (1.0 / jnp.sum(block, axis=0, keepdims=True))
            probs[head * count : (head + 1) * count, :] = weights
            weights_b = weights.astype(BF16)
            probs_b[head * count : (head + 1) * count, :] = weights_b
            out = dot(values_t[head * size : (head + 1) * size, :], weights_b)
            attended_t[head * size : (head + 1) * size, :] = out.astype(BF16)
    grad_out = jnp.concatenate([mine[half:], came[half : 2 * half]], axis=0)
    cot[...] = grad_out.astype(BF16)
    back_through(cot[...], probs, probs_b, qkv, keys_t, weight_out, grad_proj, size, None)
    skip[...] = (
        through_norm(grad_proj[...], weight_t, gain, normed, inverse) + grad_out
    ).astype(BF16)


def backward_kernel(
    skip, cot, qkv, probs, weight_out, extra, normed_t, attended_t,
    total_out, grad_proj, bias_out, give,
    keys_t,
    *, heads,
):
    count, width = cot.shape
    core, _, _ = position()
    total_out[...] = (cot[...].astype(F32) + skip[...].astype(F32)).astype(BF16)
    keys_t[...] = qkv[:, width : 2 * width].T
    bias_row = back_through(
        total_out[...], probs, probs, qkv, keys_t, weight_out, grad_proj, width // heads,
        extra[:, :1],
    )
    bias_out[...] = jnp.broadcast_to(bias_row, bias_out.shape)
    half = width // 2
    rows = aligned((1 - core) * half, half)
    weight_rows(rows, normed_t, attended_t, grad_proj, total_out, bias_row, give)


def weight_rows(rows, normed_t, attended_t, grad_proj, total, bias_row, out):
    tokens = normed_t[rows, :]
    three = grad_proj.shape[1]
    out[:, :CUT] = dot(tokens, grad_proj[:, :CUT]).astype(out.dtype)
    out[:, CUT : CUT + GROUP] = jnp.broadcast_to(bias_row, (out.shape[0], GROUP)).astype(out.dtype)
    out[:, CUT + GROUP : three + GROUP] = dot(tokens, grad_proj[:, CUT:]).astype(out.dtype)
    out[:, three + GROUP :] = dot(attended_t[rows, :], total[...]).astype(out.dtype)


def finish_kernel(
    total, grad_proj, bias_row, normed_t, attended_t, normed, extra, weight_t, params,
    keep, own, back,
):
    count, width = total.shape
    half = width // 2
    core, _, _ = position()
    rows = aligned(core * half, half)
    bias_b = bias_row[:1, :].astype(BF16).astype(F32)
    weight_rows(rows, normed_t, attended_t, grad_proj, total, bias_b, keep)
    inverse = extra[:, GROUP : GROUP + 1]
    final = through_norm(grad_proj[...], weight_t, params[count : count + 1, :], normed[...], inverse)
    final = final + total[...].astype(F32)
    own[...] = final[: count // 2]
    back[...] = final[count // 2 :].astype(BF16)


def first_kernel(keep, came, give_p, kept_p, kept_q, *rest):
    _, y, z = position()
    *give_q, total = rest
    wide_p = give_p.shape[1]
    half = keep.shape[0] // 2
    total[...] = keep[...] + came[...].astype(F32)
    give_p[...] = total[aligned((1 - y) * half, half), :wide_p].astype(BF16)
    mine = aligned(y * half, half)
    kept_p[:, :CUT] = total[mine, :CUT]
    kept_p[:, CUT:] = total[mine, CUT:wide_p].astype(BF16).astype(F32)
    piece = kept_q.shape[0]
    kept_q[...] = total[aligned(z * piece, piece), wide_p:]
    for other, ref in enumerate(give_q, 1):
        ref[...] = total[aligned((z ^ other) * piece, piece), wide_p:].astype(BF16)


def second_kernel(after, kept_p, came_p, kept_q, *rest):
    _, y, z = position()
    count = (len(rest) - 5) // 2
    came_q, (give_q, left_q, left_p) = rest[:count], rest[count : count + 3]
    *give_p, total_p, total_q = rest[count + 3 :]
    total_p[...] = kept_p[...] + came_p[...].astype(F32)
    piece = left_p.shape[0]
    mine = aligned(z * piece, piece)
    left_p[:, :CUT] = total_p[mine, :CUT]
    left_p[:, CUT:] = total_p[mine, CUT:].astype(BF16).astype(F32)
    for other, ref in enumerate(give_p, 1):
        ref[...] = total_p[aligned((z ^ other) * piece, piece), :].astype(BF16)
    total = kept_q[...]
    for ref in came_q:
        total = total + ref[...].astype(F32)
    total_q[...] = total
    half = give_q.shape[0]
    give_q[...] = total_q[aligned((1 - y) * half, half), :].astype(BF16)
    left_q[...] = total_q[aligned(y * half, half), :]


def third_kernel(left_p, left_q, came_q, *rest):
    _, _, z = position()
    *came_p, piece_p, piece_q, bias = rest
    total = left_p[:, :CUT]
    for ref in came_p:
        total = total + ref[:, :CUT].astype(F32)
    piece_p[...] = total.astype(BF16)
    piece_q[...] = (left_q[...] + came_q[...].astype(F32)).astype(BF16)
    terms = [left_p[:8, CUT:]] + [ref[...].astype(F32)[:8, CUT:] for ref in came_p]
    total = jnp.zeros_like(terms[0])
    for source in range(len(terms)):
        for other, term in enumerate(terms):
            total = total + jnp.where((z ^ other) == source, term, 0.0)
    bias[...] = total


def fourth_kernel(piece_q, other_q, *rest):
    _, y, z = position()
    *parts_p, block_p, block_q = rest
    piece = parts_p[0].shape[0]
    for other, part in enumerate(parts_p):
        block_p[aligned((z ^ other) * piece, piece), :] = part[...]
    piece = piece_q.shape[0]
    block_q[aligned(y * piece, piece), :] = piece_q[...]
    block_q[aligned((1 - y) * piece, piece), :] = other_q[...]


def fifth_kernel(weight_qkv, gain, bias, block_p, other_p, *rest):
    *parts_q, row, half = rest
    core, y, z = position()
    rows = half.shape[0]
    mine = aligned(core * rows, rows)
    piece = block_p.shape[0]
    half[aligned(y * piece, piece), :CUT] = block_p[...]
    half[aligned((1 - y) * piece, piece), :CUT] = other_p[...]
    piece = parts_q[0].shape[0]
    for other, part in enumerate(parts_q):
        half[aligned((z ^ other) * piece, piece), CUT:] = part[...]
    three = weight_qkv.shape[1]
    wide = half[:, :three].astype(F32)
    gain_half = jnp.sum(wide * weight_qkv[mine, :].astype(F32), axis=1, keepdims=True)
    gain_half = jnp.broadcast_to(gain_half, (rows, GROUP)).T[:8]
    own_gain = jnp.where(core == 0, gain[:, :rows], gain[:, rows:])
    gain_half = gain_half / own_gain
    out = half[:, three:].astype(F32)
    square = jnp.sum(jnp.sum(wide * wide, axis=0, keepdims=True), axis=1, keepdims=True)
    square = square + jnp.sum(jnp.sum(out * out, axis=0, keepdims=True), axis=1, keepdims=True)
    square = square + jnp.sum(gain_half[:1] * gain_half[:1], axis=1, keepdims=True)
    square = square + 0.5 * jnp.sum(bias[:1, :] * bias[:1, :], axis=1, keepdims=True)
    row[:, :rows] = gain_half
    row[:, rows:] = jnp.broadcast_to(square, (8, GROUP))


def last_kernel(
    half, other, row, row_core, row_section, row_both, bias,
    grad_qkv, grad_out, grad_gain, grad_bias,
    qkv_v, out_v, gain_v, bias_v, sems,
    *, entries,
):
    core, _, _ = position()
    rows, three = half.shape[0], grad_qkv.shape[1]
    square = row[:1, rows : rows + 1] + row_core[:1, rows : rows + 1]
    square = square + (row_section[:1, rows : rows + 1] + row_both[:1, rows : rows + 1])
    factor = jnp.minimum(1.0, lax.rsqrt(square / entries + 1e-06))
    sent = []
    piece = 64
    for which, ref in enumerate((half, other)):
        base = core * rows if which == 0 else (1 - core) * rows
        for part in range(rows // piece):
            here = slice(part * piece, (part + 1) * piece)
            at = aligned(base + part * piece, piece)
            slot = slice(which * rows + part * piece, which * rows + (part + 1) * piece)
            qkv_v[slot, :] = ref[here, :three].astype(F32) * factor
            sent.append(started(qkv_v.at[slot, :], grad_qkv.at[at, :], sems, len(sent)))
            out_v[slot, :] = ref[here, three:].astype(F32) * factor
            sent.append(started(out_v.at[slot, :], grad_out.at[at, :], sems, len(sent)))
    mine, its = row[:1, :rows] * factor, row_core[:1, :rows] * factor
    gain_v[:, :rows] = jnp.where(core == 0, mine, its)
    gain_v[:, rows:] = jnp.where(core == 0, its, mine)
    bias_v[...] = bias[:1, : bias_v.shape[1]] * factor
    sent.append(started(gain_v, grad_gain, sems, len(sent)))
    sent.append(started(bias_v, grad_bias, sems, len(sent)))
    for copy in sent:
        copy.wait()


def sent_round(pieces, axis):
    return [swapped(piece, axis, other) for other, piece in enumerate(pieces, 1)]


def vmem(dims, dtype):
    return pltpu.VMEM(dims, dtype)


def copies(number):
    return pltpu.SemaphoreType.DMA((number,))


def body(inputs, cotangent, land_sea, gains, qkv_weight, out_weight, land_bias):
    weight_qkv, weight_out = qkv_weight[0], out_weight[0]
    levels, lats, cols, width = inputs.shape[1:]
    heads = land_bias.shape[1]
    half = levels * lats * SHIFT
    count = 2 * half
    packed = half * 2 + 16
    lons = lax.axis_size("lon")

    tokens = inputs.transpose(0, 2, 3, 1, 4)
    own_cot = cotangent.transpose(0, 2, 3, 1, 4)

    own, rim = call(
        pack_kernel,
        [shape((packed, width), F32), shape((packed, width), BF16)],
        scratch=[
            vmem(tokens.shape, BF16),
            vmem(tokens.shape, BF16),
            vmem(land_sea.shape, jnp.int32),
            vmem(gains.shape, F32),
            vmem(land_bias.shape, F32),
            vmem((packed, width), F32),
            copies(5),
        ],
        places="hhhhh",
        operands=(tokens, own_cot, land_sea, gains, land_bias),
        limit=60,
    )
    rim = from_behind(rim, "lon", -1)
    qkv_v, qkv_t, out_v = call(
        ready_kernel,
        [
            shape(weight_qkv.shape, BF16),
            shape(weight_qkv.shape[::-1], BF16),
            shape(weight_out.shape, BF16),
        ],
        scratch=[copies(2)],
        places="ahh",
        operands=(own, weight_qkv, weight_out),
        limit=48,
    )
    skip, cot, normed_t, qkv, probs, attended_t, extra, normed = call(
        functools.partial(forward_kernel, heads=heads, lats=lats, cols=cols),
        [
            shape((count, width), BF16),
            shape((count, width), BF16),
            shape((width, count), BF16),
            shape((count, 3 * width), BF16),
            shape((heads * count, count), BF16),
            shape((width, count), BF16),
            shape((count, 2 * GROUP), F32),
            shape((count, width), F32),
        ],
        scratch=[
            vmem((heads * count, count), F32),
            vmem((width, count), BF16),
            vmem((width, count), BF16),
            vmem((width, count), BF16),
            vmem((count, 3 * width), BF16),
        ],
        operands=(own, rim, qkv_v, qkv_t, out_v),
        flops=10**9,
        limit=16,
    )
    skip = passed_along(skip, "section", -1)
    rows, wide = width // 2, 4 * width + GROUP
    total, grad_proj, bias_row, give = call(
        functools.partial(backward_kernel, heads=heads),
        [
            shape((count, width), BF16),
            shape((count, 3 * width), BF16),
            shape((8, GROUP), F32),
            shape((rows, wide), BF16),
        ],
        scratch=[vmem((width, count), BF16)],
        operands=(skip, cot, qkv, probs, out_v, extra, normed_t, attended_t),
        flops=10**9,
    )
    came = swapped(give, "lat", 1)
    keep, own_grad, back = call(
        finish_kernel,
        [
            shape((rows, wide), F32),
            shape((half, width), F32),
            shape((half, width), BF16),
        ],
        operands=(
            total, grad_proj, bias_row, normed_t, attended_t, normed, extra, qkv_t, own,
        ),
        flops=5 * 10**8,
    )
    back = from_behind(back, "lon", 1)
    entries = 2 * (4 * width * width + width + heads)
    if rows // 2 // lons % 16 == 0 and lons & (lons - 1) == 0:
        grads = staged(keep, came, back, qkv_v, gains, lons, heads, entries)
    else:
        grads = plain(keep, came, weight_qkv, gains, heads, entries)
    (final_grad,) = call(
        unpack_kernel,
        [shape(tokens.shape, F32)],
        scratch=[vmem(tokens.shape, F32), copies(1)],
        out_places="h",
        operands=(own_grad, back),
    )
    final_grad = final_grad.transpose(0, 3, 1, 2, 4)
    return (final_grad, *(grad[None] for grad in grads))


def staged(keep, came, after, weight_qkv, gains, lons, heads, entries):
    rows, wide = keep.shape
    width = 2 * rows
    wide_p = CUT + GROUP
    wide_q = wide - wide_p
    some = range(lons - 1)
    several = "v" * len(some)
    give_p, kept_p, kept_q, *give_q = call(
        first_kernel,
        [
            shape((rows // 2, wide_p), BF16),
            shape((rows // 2, wide_p), F32),
            shape((rows // lons, wide_q), F32),
            *(shape((rows // lons, wide_q), BF16) for _ in some),
        ],
        scratch=[vmem((rows, wide), F32)],
        operands=(keep, came),
    )
    came_p = swapped(give_p, "lat", 2)
    came_q = sent_round(give_q, "lon")
    piece = rows // 2 // lons
    give_q, left_q, left_p, *give_p = call(
        second_kernel,
        [
            shape((piece, wide_q), BF16),
            shape((piece, wide_q), F32),
            shape((piece, wide_p), F32),
            *(shape((piece, wide_p), BF16) for _ in some),
        ],
        scratch=[vmem((rows // 2, wide_p), F32), vmem((rows // lons, wide_q), F32)],
        places="avvv" + several,
        operands=(after, kept_p, came_p, kept_q, *came_q),
    )
    came_p = sent_round(give_p, "lon")
    came_q = swapped(give_q, "lat", 2)
    piece_p, piece_q, bias = call(
        third_kernel,
        [
            shape((piece, CUT), BF16),
            shape((piece, wide_q), BF16),
            shape((8, GROUP), F32),
        ],
        operands=(left_p, left_q, came_q, *came_p),
    )
    others_p = sent_round([piece_p for _ in some], "lon")
    other_q = swapped(piece_q, "lat", 2)
    block_p, block_q = call(
        fourth_kernel,
        [shape((rows // 2, CUT), BF16), shape((rows // lons, wide_q), BF16)],
        operands=(piece_q, other_q, piece_p, *others_p),
    )
    other_p = swapped(block_p, "lat", 2)
    others_q = sent_round([block_q for _ in some], "lon")
    row, half = call(
        fifth_kernel,
        [shape((8, rows + GROUP), F32), shape((rows, 4 * width), BF16)],
        operands=(weight_qkv, gains, bias, block_p, other_p, block_q, *others_q),
    )
    row_section = swapped(row, "section", 1)
    row_both = lax.ppermute(row, ("section", "lat"), across())
    row_core = swapped(row, "lat", 1)
    other = swapped(half, "lat", 1)
    grads = call(
        functools.partial(last_kernel, entries=entries),
        [
            shape((width, 3 * width), F32),
            shape((width, width), F32),
            shape((1, width), F32),
            shape((1, heads), F32),
        ],
        scratch=[
            vmem((width, 3 * width), F32),
            vmem((width, width), F32),
            vmem((1, width), F32),
            vmem((1, heads), F32),
            copies(4 * rows // 64 + 2),
        ],
        out_places="hhhh",
        operands=(half, other, row, row_core, row_section, row_both, bias),
    )
    return grads[0], grads[1], grads[2][0], grads[3][0]


def across():
    sections, lats = lax.axis_size("section"), lax.axis_size("lat")
    return [
        (s * lats + i, (sections - 1 - s) * lats + (i ^ 1))
        for s in range(sections)
        for i in range(lats)
    ]


def split_two(block, axis, bit):
    mine = (lax.axis_index(axis) // bit) % 2
    pair = block.reshape(2, block.shape[0] // 2, -1)
    give = lax.dynamic_index_in_dim(pair, 1 - mine, 0, keepdims=False).astype(BF16)
    return give, lax.dynamic_index_in_dim(pair, mine, 0, keepdims=False)


def doubled(block, axis, bit):
    mine = (lax.axis_index(axis) // bit) % 2
    other = swapped(block, axis, bit)
    low = jnp.where(mine == 0, block, other)
    high = jnp.where(mine == 0, other, block)
    return jnp.concatenate([low, high], axis=0)


def scattered(block, axis):
    count = lax.axis_size(axis)
    mine = lax.axis_index(axis)
    pieces = block.reshape(count, block.shape[0] // count, -1)
    total = lax.dynamic_index_in_dim(pieces, mine, 0, keepdims=False)
    others = []
    for by in range(1, count):
        give = lax.dynamic_index_in_dim(pieces, (mine + by) % count, 0, keepdims=False)
        others.append(from_behind(give.astype(BF16), axis, by))
    for other in others:
        total = total + other.astype(F32)
    return total, others


def gathered(block, axis):
    count = lax.axis_size(axis)
    mine = lax.axis_index(axis)
    whole = jnp.zeros((count,) + block.shape, block.dtype)
    whole = lax.dynamic_update_index_in_dim(whole, block, mine, 0)
    for by in range(1, count):
        whole = lax.dynamic_update_index_in_dim(
            whole, from_behind(block, axis, by), (mine - by) % count, 0
        )
    return whole.reshape(count * block.shape[0], -1)


def sum_squares(block):
    wide = block.astype(F32)
    return jnp.sum(wide * wide)


def plain(keep, came, weight_qkv, gains, heads, entries):
    width = gains.shape[1]
    lat, lon = lax.axis_index("lat"), lax.axis_index("lon")
    part = keep + came.astype(F32)
    give, keep = split_two(part, "lat", 2)
    came = swapped(give, "lat", 2).astype(F32)
    column = lax.broadcasted_iota(jnp.int32, keep.shape, 1)
    is_bias = (column >= CUT) & (column < CUT + GROUP)
    part = jnp.where(is_bias, lax.reduce_precision(keep, 8, 7), keep) + came
    bias_part = lax.reduce_precision(part[:1, CUT : CUT + GROUP], 8, 7)
    part, others = scattered(part, "lon")
    terms = [bias_part] + [other[:1, CUT : CUT + GROUP].astype(F32) for other in others]
    terms = jnp.concatenate(terms[:1] + terms[:0:-1], axis=0)
    bias = jnp.sum(jnp.roll(terms, lon, axis=0), axis=0)[:heads]
    part = jnp.concatenate([part[:, :CUT], part[:, CUT + GROUP :]], axis=1).astype(BF16)
    half = doubled(gathered(part, "lon"), "lat", 2)
    mine = lat % 2
    weight_half = lax.dynamic_slice_in_dim(weight_qkv, mine * (width // 2), width // 2, 0)
    gain_half = lax.dynamic_slice_in_dim(gains[0], mine * (width // 2), width // 2, 0)
    weighed = half[:, : 3 * width].astype(F32) * weight_half.astype(F32)
    gain_half = jnp.sum(weighed, axis=1) / gain_half
    square = sum_squares(half) + sum_squares(gain_half) + 0.5 * sum_squares(bias)
    square = square.reshape(1)
    square = square + swapped(square, "lat", 1)
    square = square + swapped(square, "section", 1)
    factor = jnp.minimum(1.0, lax.rsqrt(square[0] / entries + 1e-06))
    grads = doubled(half, "lat", 1).astype(F32) * factor
    gain = doubled(gain_half.reshape(-1, 1), "lat", 1)[:, 0] * factor
    return grads[:, : 3 * width], grads[:, 3 * width :], gain, bias * factor


def solution(mesh):
    placed = (
        P("section", None, "lat", "lon", None),
        P("section", None, "lat", "lon", None),
        P("lat", "lon"),
        P("section", None),
        P("section", None, None),
        P("section", None, None),
        P("section", None),
    )
    return jax.shard_map(
        body,
        mesh=mesh,
        in_specs=placed,
        out_specs=(
            P("section", None, "lat", "lon", None),
            P("section", None, None),
            P("section", None, None),
            P("section", None),
            P("section", None),
        ),
        check_vma=False,
    )
```

```python
import functools

import jax
import jax.numpy as jnp
from jax import lax
from jax.experimental import pallas as pl
from jax.experimental.pallas import tpu as pltpu
from jax.sharding import PartitionSpec as P

SHIFT = 6
GROUP = 128
CUT = 1536
EPSILON = 1e-05
F32 = jnp.float32
BF16 = jnp.bfloat16


def from_behind(value, axis, by):
    count = lax.axis_size(axis)
    return lax.ppermute(value, axis, [(i, (i + by) % count) for i in range(count)])


def passed_along(block, axis, distance):
    devices = range(lax.axis_size(axis))
    route = [(i - distance, i) for i in devices if i - distance in devices]
    return lax.ppermute(block, axis, route)


def swapped(value, axis, bit):
    count = lax.axis_size(axis)
    return lax.ppermute(value, axis, [(i, i ^ bit) for i in range(count)])


def dot(left, right):
    return jnp.dot(left, right, preferred_element_type=F32)


def dot_last(left, right):
    return lax.dot_general(left, right, (((1,), (1,)), ((), ())), preferred_element_type=F32)


def call(kernel, outs, scratch=(), places="", out_places="", operands=(), flops=10**8, limit=8):
    spaces = {"v": pltpu.VMEM, "s": pltpu.SMEM, "a": pl.ANY, "h": pltpu.HBM}
    places = places or "v" * len(operands)
    out_places = out_places or "v" * len(outs)
    moved = sum(o.size * o.dtype.itemsize for o in list(outs) + list(operands))
    return pl.pallas_call(
        kernel,
        out_shape=list(outs),
        in_specs=[pl.BlockSpec(memory_space=spaces[letter]) for letter in places],
        out_specs=[pl.BlockSpec(memory_space=spaces[letter]) for letter in out_places],
        scratch_shapes=list(scratch),
        compiler_params=pltpu.CompilerParams(vmem_limit_bytes=limit * 2**20),
        cost_estimate=pl.CostEstimate(flops=flops, bytes_accessed=moved, transcendentals=0),
    )(*operands)


def started(source, target, semaphores, index):
    copy = pltpu.make_async_copy(source, target, semaphores.at[index])
    copy.start()
    return copy


def shape(dims, dtype):
    return jax.ShapeDtypeStruct(dims, dtype)


def aligned(start, size):
    return pl.ds(pl.multiple_of(start, size), size)


def position():
    lat, lon = lax.axis_index("lat"), lax.axis_index("lon")
    return lax.rem(lat, 2), lax.div(lat, 2), lon


def pack_kernel(
    tokens, cot, land, gain, bias, own, rim,
    tokens_v, cot_v, land_v, gain_v, bias_v, rim32, sems,
):
    arrays = ((tokens, tokens_v), (cot, cot_v), (land, land_v), (gain, gain_v), (bias, bias_v))
    copies = [started(source, target, sems, i) for i, (source, target) in enumerate(arrays)]
    lats, cols, levels, width = tokens.shape[1:]
    half = levels * lats * SHIFT
    rim32[2 * half :, :] = jnp.zeros((rim32.shape[0] - 2 * half, width), F32)
    own[2 * half :, :] = jnp.zeros((own.shape[0] - 2 * half, width), F32)
    for which, ref in enumerate((tokens_v, cot_v)):
        copies[which].wait()
        for lat in range(lats):
            for col in range(cols):
                row = which * half + (lat * SHIFT + col % SHIFT) * levels
                part = rim32 if col < SHIFT else own
                part[row : row + levels, :] = ref[0, lat, col].astype(F32)
    for copy in copies[2:]:
        copy.wait()
    rim32[2 * half : 2 * half + lats, :cols] = land_v[...].astype(F32)
    own[2 * half : 2 * half + 1, :] = gain_v[...]
    own[2 * half + 1 : 2 * half + 2, : bias.shape[1]] = bias_v[...]
    own[2 * half + 8 : 2 * half + 8 + lats, :cols] = land_v[...].astype(F32)
    rim[...] = rim32[...].astype(BF16)


def unpack_kernel(own, back, grid, grid_v, sems):
    lats, cols, levels, width = grid.shape[1:]
    came = back[...].astype(F32)
    for lat in range(lats):
        for col in range(cols):
            row = (lat * SHIFT + col % SHIFT) * levels
            if col < SHIFT:
                grid_v[0, lat, col] = came[row : row + levels]
            else:
                grid_v[0, lat, col] = own[row : row + levels, :]
    started(grid_v, grid, sems, 0).wait()


def land_column(land, rows, first):
    lats, cols = land.shape
    row = lax.broadcasted_iota(jnp.int32, (rows, lats), 0)
    lat = lax.div(row, rows // lats)
    pick = (lat == lax.broadcasted_iota(jnp.int32, (rows, lats), 1)).astype(F32)
    lines = dot(pick.astype(BF16), land.astype(BF16))
    row = lax.broadcasted_iota(jnp.int32, (rows, cols), 0)
    column = lax.broadcasted_iota(jnp.int32, (rows, cols), 1)
    levels = rows // (lats * SHIFT)
    here = column == lax.rem(lax.div(row, levels), SHIFT) + first
    return jnp.sum(jnp.where(here, lines, 0.0), axis=1, keepdims=True)


def head_masks(dtype, size):
    lane = lax.broadcasted_iota(jnp.int32, (1, GROUP), 1)
    return [
        (lax.div(lane, size) == part).astype(F32).astype(dtype) for part in range(GROUP // size)
    ]


def stacked(block, masks):
    return jnp.concatenate([block * mask for mask in masks], axis=0)


def folded(block, masks):
    rows = block.shape[0] // len(masks)
    return sum(block[i * rows : (i + 1) * rows] * mask for i, mask in enumerate(masks))


def back_through(grad_out, probs, probs_b, qkv, keys_t, weight_out, grad_proj, size, land):
    count, width = grad_out.shape
    per = GROUP // size
    scale = size ** (-0.5)
    masks_b, masks = head_masks(BF16, size), head_masks(F32, size)
    att_t = dot_last(weight_out[...], grad_out)
    grad_att = att_t.T.astype(BF16)
    att_t = att_t.astype(BF16)
    lane = lax.broadcasted_iota(jnp.int32, (1, GROUP), 1)
    bias_row = jnp.zeros((1, GROUP), F32)
    for group in range(width // GROUP):
        at = group * GROUP
        values = qkv[:, 2 * width + at : 2 * width + at + GROUP]
        grad_probs = dot(stacked(values, masks_b), att_t[at : at + GROUP, :])
        scores_b, queries_t = [], []
        for part in range(per):
            head = group * per + part
            weights = probs[head * count : (head + 1) * count, :].astype(F32)
            grad_weights = grad_probs[part * count : (part + 1) * count]
            inner = jnp.sum(weights * grad_weights, axis=0, keepdims=True)
            grad_scores = weights * (grad_weights - inner)
            if land is not None:
                on_land = jnp.sum(grad_scores * land, axis=0, keepdims=True)
                on_land = jnp.sum(on_land, axis=1, keepdims=True)
                bias_row = bias_row + jnp.where(lane == head, on_land, 0.0)
            scaled_b = (grad_scores * scale).astype(BF16)
            scores_b.append(scaled_b)
            queries_t.append(dot(keys_t[head * size : (head + 1) * size, :], scaled_b))
        queries = qkv[:, at : at + GROUP]
        grad_keys = dot(jnp.concatenate(scores_b, axis=0), queries)
        mixed = probs_b[group * per * count : (group + 1) * per * count, :]
        grad_values = dot(mixed, grad_att[:, at : at + GROUP])
        grad_proj[:, at : at + GROUP] = jnp.concatenate(queries_t, axis=0).T.astype(BF16)
        grad_proj[:, width + at : width + at + GROUP] = folded(grad_keys, masks).astype(BF16)
        grad_proj[:, 2 * width + at : 2 * width + at + GROUP] = folded(grad_values, masks).astype(
            BF16
        )
    return bias_row


def through_norm(grad_proj, weight_t, gain, normed, inverse):
    scaled = dot(grad_proj, weight_t[...]) * gain
    mean = jnp.mean(scaled, axis=-1, keepdims=True)
    along = jnp.mean(scaled * normed, axis=-1, keepdims=True)
    return inverse * (scaled - mean - normed * along)


def ready_kernel(after, weight_qkv, weight_out, qkv_v, qkv_t, out_v, sems):
    copies = [
        started(weight_qkv, qkv_v, sems, 0),
        started(weight_out, out_v, sems, 1),
    ]
    copies[0].wait()
    width = weight_qkv.shape[0]
    for part in range(weight_qkv.shape[1] // width):
        rows = slice(part * width, (part + 1) * width)
        qkv_t[rows, :] = qkv_v[:, rows].T
    copies[1].wait()


def forward_kernel(
    own, rim, weight_qkv, weight_t, weight_out,
    skip, cot, normed_t, qkv, probs_b, attended_t, extra, normed_out,
    probs, queries_t, keys_t, values_t, grad_proj,
    *, heads, lats, cols,
):
    width = own.shape[1]
    size = width // heads
    half = cot.shape[0] // 2
    count = 2 * half
    per = GROUP // size
    scale = size ** (-0.5)
    masks_b = head_masks(BF16, size)
    mine = own[: 2 * half, :]
    params = own[2 * half :, :]
    came = rim[...].astype(F32)
    gain = params[0:1, :]
    values = jnp.concatenate([mine[:half], came[:half]], axis=0)
    centred = values - jnp.mean(values, axis=-1, keepdims=True)
    inverse = lax.rsqrt(jnp.mean(centred * centred, axis=-1, keepdims=True) + EPSILON)
    normed = centred * inverse
    normed_out[...] = normed
    normed_b = (normed * gain).astype(BF16)
    normed_t[...] = normed_b.T
    land = jnp.concatenate(
        [
            land_column(params[8 : 8 + lats, :cols], half, SHIFT),
            land_column(came[2 * half : 2 * half + lats, :cols], half, 0),
        ],
        axis=0,
    )
    extra[:, :GROUP] = jnp.broadcast_to(land, (count, GROUP))
    extra[:, GROUP:] = jnp.broadcast_to(inverse, (count, GROUP))
    for part, turned in enumerate((queries_t, keys_t, values_t)):
        columns = slice(part * width, (part + 1) * width)
        qkv[:, columns] = dot(normed_b, weight_qkv[:, columns]).astype(BF16)
        turned[...] = qkv[:, columns].T
    for group in range(width // GROUP):
        at = group * GROUP
        keys = qkv[:, width + at : width + at + GROUP]
        scores = dot(stacked(keys, masks_b), queries_t[at : at + GROUP, :])
        for part in range(per):
            head = group * per + part
            block = scores[part * count : (part + 1) * count] * scale
            block = block + params[1:2, head : head + 1] * land
            block = jnp.exp(block - jnp.max(block, axis=0, keepdims=True))
            weights = block * (1.0 / jnp.sum(block, axis=0, keepdims=True))
            probs[head * count : (head + 1) * count, :] = weights
            weights_b = weights.astype(BF16)
            probs_b[head * count : (head + 1) * count, :] = weights_b
            out = dot(values_t[head * size : (head + 1) * size, :], weights_b)
            attended_t[head * size : (head + 1) * size, :] = out.astype(BF16)
    grad_out = jnp.concatenate([mine[half:], came[half : 2 * half]], axis=0)
    cot[...] = grad_out.astype(BF16)
    back_through(cot[...], probs, probs_b, qkv, keys_t, weight_out, grad_proj, size, None)
    skip[...] = (
        through_norm(grad_proj[...], weight_t, gain, normed, inverse) + grad_out
    ).astype(BF16)


def backward_kernel(
    skip, cot, qkv, probs, weight_out, extra, normed_t, attended_t,
    total_out, grad_proj, bias_out, give,
    keys_t,
    *, heads,
):
    count, width = cot.shape
    core, _, _ = position()
    total_out[...] = (cot[...].astype(F32) + skip[...].astype(F32)).astype(BF16)
    keys_t[...] = qkv[:, width : 2 * width].T
    bias_row = back_through(
        total_out[...], probs, probs, qkv, keys_t, weight_out, grad_proj, width // heads,
        extra[:, :1],
    )
    bias_out[...] = jnp.broadcast_to(bias_row, bias_out.shape)
    half = width // 2
    rows = aligned((1 - core) * half, half)
    weight_rows(rows, normed_t, attended_t, grad_proj, total_out, bias_row, give)


def weight_rows(rows, normed_t, attended_t, grad_proj, total, bias_row, out):
    tokens = normed_t[rows, :]
    three = grad_proj.shape[1]
    out[:, :CUT] = dot(tokens, grad_proj[:, :CUT]).astype(out.dtype)
    out[:, CUT : CUT + GROUP] = jnp.broadcast_to(bias_row, (out.shape[0], GROUP)).astype(out.dtype)
    if CUT < three:
        out[:, CUT + GROUP : three + GROUP] = dot(tokens, grad_proj[:, CUT:]).astype(out.dtype)
    out[:, three + GROUP :] = dot(attended_t[rows, :], total[...]).astype(out.dtype)


def finish_kernel(
    total, grad_proj, bias_row, normed_t, attended_t, normed, extra, weight_t, params,
    keep, own, back,
):
    count, width = total.shape
    half = width // 2
    core, _, _ = position()
    rows = aligned(core * half, half)
    bias_b = bias_row[:1, :].astype(BF16).astype(F32)
    weight_rows(rows, normed_t, attended_t, grad_proj, total, bias_b, keep)
    inverse = extra[:, GROUP : GROUP + 1]
    final = through_norm(grad_proj[...], weight_t, params[count : count + 1, :], normed[...], inverse)
    final = final + total[...].astype(F32)
    own[...] = final[: count // 2]
    back[...] = final[count // 2 :].astype(BF16)


def first_kernel(keep, came, give_p, kept_p, kept_q, *rest):
    _, y, z = position()
    *give_q, total = rest
    wide_p = give_p.shape[1]
    half = keep.shape[0] // 2
    total[...] = keep[...] + came[...].astype(F32)
    give_p[...] = total[aligned((1 - y) * half, half), :wide_p].astype(BF16)
    mine = aligned(y * half, half)
    kept_p[:, :CUT] = total[mine, :CUT]
    kept_p[:, CUT:] = total[mine, CUT:wide_p].astype(BF16).astype(F32)
    piece = kept_q.shape[0]
    kept_q[...] = total[aligned(z * piece, piece), wide_p:]
    for other, ref in zip(range(len(give_q), 0, -1), give_q):
        ref[...] = total[aligned((z ^ other) * piece, piece), wide_p:].astype(BF16)


def second_kernel(after, kept_p, came_p, kept_q, *rest):
    _, y, z = position()
    count = (len(rest) - 5) // 2
    came_q, (give_q, left_q, left_p) = rest[:count], rest[count : count + 3]
    *give_p, total_p, total_q = rest[count + 3 :]
    total_p[...] = kept_p[...] + came_p[...].astype(F32)
    piece = left_p.shape[0]
    mine = aligned(z * piece, piece)
    left_p[:, :CUT] = total_p[mine, :CUT]
    left_p[:, CUT:] = total_p[mine, CUT:].astype(BF16).astype(F32)
    for other, ref in zip(range(len(give_p), 0, -1), give_p):
        ref[...] = total_p[aligned((z ^ other) * piece, piece), :].astype(BF16)
    total = kept_q[...]
    for ref in came_q:
        total = total + ref[...].astype(F32)
    total_q[...] = total
    half = give_q.shape[0]
    give_q[...] = total_q[aligned((1 - y) * half, half), :].astype(BF16)
    left_q[...] = total_q[aligned(y * half, half), :]


def third_kernel(left_p, left_q, came_q, *rest):
    _, _, z = position()
    *came_p, piece_p, piece_q, bias = rest
    total = left_p[:, :CUT]
    for ref in came_p:
        total = total + ref[:, :CUT].astype(F32)
    piece_p[...] = total.astype(BF16)
    piece_q[...] = (left_q[...] + came_q[...].astype(F32)).astype(BF16)
    terms = [left_p[:8, CUT:]] + [ref[...].astype(F32)[:8, CUT:] for ref in came_p[::-1]]
    total = jnp.zeros_like(terms[0])
    for source in range(len(terms)):
        for other, term in enumerate(terms):
            total = total + jnp.where((z ^ other) == source, term, 0.0)
    bias[...] = total


def fourth_kernel(piece_q, other_q, *rest):
    _, y, z = position()
    *parts_p, block_p, block_q = rest
    piece = parts_p[0].shape[0]
    for other, part in enumerate(parts_p):
        block_p[aligned((z ^ other) * piece, piece), :] = part[...]
    piece = piece_q.shape[0]
    block_q[aligned(y * piece, piece), :] = piece_q[...]
    block_q[aligned((1 - y) * piece, piece), :] = other_q[...]


def fifth_kernel(weight_qkv, gain, bias, block_p, other_p, *rest):
    *parts_q, half, row = rest
    core, y, z = position()
    rows = half.shape[0]
    mine = aligned(core * rows, rows)
    piece = block_p.shape[0]
    half[aligned(y * piece, piece), :CUT] = block_p[...]
    half[aligned((1 - y) * piece, piece), :CUT] = other_p[...]
    piece = parts_q[0].shape[0]
    for other, part in enumerate(parts_q):
        half[aligned((z ^ other) * piece, piece), CUT:] = part[...]
    three = weight_qkv.shape[1]
    wide = half[:, :three].astype(F32)
    gain_half = jnp.sum(wide * weight_qkv[mine, :].astype(F32), axis=1, keepdims=True)
    gain_half = jnp.broadcast_to(gain_half, (rows, GROUP)).T[:8]
    own_gain = jnp.where(core == 0, gain[:, :rows], gain[:, rows:])
    gain_half = gain_half / own_gain
    out = half[:, three:].astype(F32)
    square = jnp.sum(jnp.sum(wide * wide, axis=0, keepdims=True), axis=1, keepdims=True)
    square = square + jnp.sum(jnp.sum(out * out, axis=0, keepdims=True), axis=1, keepdims=True)
    square = square + jnp.sum(gain_half[:1] * gain_half[:1], axis=1, keepdims=True)
    square = square + 0.5 * jnp.sum(bias[:1, :] * bias[:1, :], axis=1, keepdims=True)
    row[:, :rows] = gain_half
    row[:, rows:] = jnp.broadcast_to(square, (8, GROUP))


def last_kernel(
    half, other, row, row_core, row_section, row_both, bias,
    grad_qkv, grad_out, grad_gain, grad_bias,
    qkv_v, out_v, gain_v, bias_v, sems,
    *, entries,
):
    core, _, _ = position()
    rows, three = half.shape[0], grad_qkv.shape[1]
    square = row[:1, rows : rows + 1] + row_core[:1, rows : rows + 1]
    square = square + (row_section[:1, rows : rows + 1] + row_both[:1, rows : rows + 1])
    factor = jnp.minimum(1.0, lax.rsqrt(square / entries + 1e-06))
    sent = []
    piece = 64
    for which, ref in enumerate((half, other)):
        base = core * rows if which == 0 else (1 - core) * rows
        for part in range(rows // piece):
            here = slice(part * piece, (part + 1) * piece)
            at = aligned(base + part * piece, piece)
            slot = slice(which * rows + part * piece, which * rows + (part + 1) * piece)
            qkv_v[slot, :] = ref[here, :three].astype(F32) * factor
            sent.append(started(qkv_v.at[slot, :], grad_qkv.at[at, :], sems, len(sent)))
            out_v[slot, :] = ref[here, three:].astype(F32) * factor
            sent.append(started(out_v.at[slot, :], grad_out.at[at, :], sems, len(sent)))
    mine, its = row[:1, :rows] * factor, row_core[:1, :rows] * factor
    gain_v[:, :rows] = jnp.where(core == 0, mine, its)
    gain_v[:, rows:] = jnp.where(core == 0, its, mine)
    bias_v[...] = bias[:1, : bias_v.shape[1]] * factor
    sent.append(started(gain_v, grad_gain, sems, len(sent)))
    sent.append(started(bias_v, grad_bias, sems, len(sent)))
    for copy in sent:
        copy.wait()


def far_first(pieces, axis):
    others = range(len(pieces), 0, -1)
    return [swapped(piece, axis, other) for other, piece in zip(others, pieces)]


def to_all(piece, axis):
    return [swapped(piece, axis, other) for other in range(1, lax.axis_size(axis))]


def vmem(dims, dtype):
    return pltpu.VMEM(dims, dtype)


def copies(number):
    return pltpu.SemaphoreType.DMA((number,))


def body(inputs, cotangent, land_sea, gains, qkv_weight, out_weight, land_bias):
    weight_qkv, weight_out = qkv_weight[0], out_weight[0]
    levels, lats, cols, width = inputs.shape[1:]
    heads = land_bias.shape[1]
    half = levels * lats * SHIFT
    count = 2 * half
    packed = half * 2 + 16
    lons = lax.axis_size("lon")

    tokens = inputs.transpose(0, 2, 3, 1, 4)
    own_cot = cotangent.transpose(0, 2, 3, 1, 4)

    own, rim = call(
        pack_kernel,
        [shape((packed, width), F32), shape((packed, width), BF16)],
        scratch=[
            vmem(tokens.shape, BF16),
            vmem(tokens.shape, BF16),
            vmem(land_sea.shape, jnp.int32),
            vmem(gains.shape, F32),
            vmem(land_bias.shape, F32),
            vmem((packed, width), F32),
            copies(5),
        ],
        places="hhhhh",
        operands=(tokens, own_cot, land_sea, gains, land_bias),
        limit=60,
    )
    rim = from_behind(rim, "lon", -1)
    qkv_v, qkv_t, out_v = call(
        ready_kernel,
        [
            shape(weight_qkv.shape, BF16),
            shape(weight_qkv.shape[::-1], BF16),
            shape(weight_out.shape, BF16),
        ],
        scratch=[copies(2)],
        places="ahh",
        operands=(own, weight_qkv, weight_out),
        limit=48,
    )
    skip, cot, normed_t, qkv, probs, attended_t, extra, normed = call(
        functools.partial(forward_kernel, heads=heads, lats=lats, cols=cols),
        [
            shape((count, width), BF16),
            shape((count, width), BF16),
            shape((width, count), BF16),
            shape((count, 3 * width), BF16),
            shape((heads * count, count), BF16),
            shape((width, count), BF16),
            shape((count, 2 * GROUP), F32),
            shape((count, width), F32),
        ],
        scratch=[
            vmem((heads * count, count), F32),
            vmem((width, count), BF16),
            vmem((width, count), BF16),
            vmem((width, count), BF16),
            vmem((count, 3 * width), BF16),
        ],
        operands=(own, rim, qkv_v, qkv_t, out_v),
        flops=10**9,
        limit=16,
    )
    skip = passed_along(skip, "section", -1)
    rows, wide = width // 2, 4 * width + GROUP
    total, grad_proj, bias_row, give = call(
        functools.partial(backward_kernel, heads=heads),
        [
            shape((count, width), BF16),
            shape((count, 3 * width), BF16),
            shape((8, GROUP), F32),
            shape((rows, wide), BF16),
        ],
        scratch=[vmem((width, count), BF16)],
        operands=(skip, cot, qkv, probs, out_v, extra, normed_t, attended_t),
        flops=10**9,
    )
    came = swapped(give, "lat", 1)
    keep, own_grad, back = call(
        finish_kernel,
        [
            shape((rows, wide), F32),
            shape((half, width), F32),
            shape((half, width), BF16),
        ],
        operands=(
            total, grad_proj, bias_row, normed_t, attended_t, normed, extra, qkv_t, own,
        ),
        flops=5 * 10**8,
    )
    back = from_behind(back, "lon", 1)
    entries = 2 * (4 * width * width + width + heads)
    if rows // 2 // lons % 16 == 0 and lons & (lons - 1) == 0:
        grads = staged(keep, came, back, qkv_v, gains, lons, heads, entries)
    else:
        grads = plain(keep, came, weight_qkv, gains, heads, entries)
    (final_grad,) = call(
        unpack_kernel,
        [shape(tokens.shape, F32)],
        scratch=[vmem(tokens.shape, F32), copies(1)],
        out_places="h",
        operands=(own_grad, back),
    )
    final_grad = final_grad.transpose(0, 3, 1, 2, 4)
    return (final_grad, *(grad[None] for grad in grads))


def staged(keep, came, after, weight_qkv, gains, lons, heads, entries):
    rows, wide = keep.shape
    width = 2 * rows
    wide_p = CUT + GROUP
    wide_q = wide - wide_p
    some = range(lons - 1)
    several = "v" * len(some)
    give_p, kept_p, kept_q, *give_q = call(
        first_kernel,
        [
            shape((rows // 2, wide_p), BF16),
            shape((rows // 2, wide_p), F32),
            shape((rows // lons, wide_q), F32),
            *(shape((rows // lons, wide_q), BF16) for _ in some),
        ],
        scratch=[vmem((rows, wide), F32)],
        operands=(keep, came),
    )
    came_p = swapped(give_p, "lat", 2)
    came_q = far_first(give_q, "lon")
    piece = rows // 2 // lons
    give_q, left_q, left_p, *give_p = call(
        second_kernel,
        [
            shape((piece, wide_q), BF16),
            shape((piece, wide_q), F32),
            shape((piece, wide_p), F32),
            *(shape((piece, wide_p), BF16) for _ in some),
        ],
        scratch=[vmem((rows // 2, wide_p), F32), vmem((rows // lons, wide_q), F32)],
        places="avvv" + several,
        operands=(after, kept_p, came_p, kept_q, *came_q),
    )
    came_p = far_first(give_p, "lon")
    came_q = swapped(give_q, "lat", 2)
    piece_p, piece_q, bias = call(
        third_kernel,
        [
            shape((piece, CUT), BF16),
            shape((piece, wide_q), BF16),
            shape((8, GROUP), F32),
        ],
        operands=(left_p, left_q, came_q, *came_p),
    )
    others_p = to_all(piece_p, "lon")
    other_q = swapped(piece_q, "lat", 2)
    block_p, block_q = call(
        fourth_kernel,
        [shape((rows // 2, CUT), BF16), shape((rows // lons, wide_q), BF16)],
        operands=(piece_q, other_q, piece_p, *others_p),
    )
    other_p = swapped(block_p, "lat", 2)
    others_q = to_all(block_q, "lon")
    half, row = call(
        fifth_kernel,
        [shape((rows, 4 * width), BF16), shape((8, rows + GROUP), F32)],
        operands=(weight_qkv, gains, bias, block_p, other_p, block_q, *others_q),
    )
    row_section = swapped(row, "section", 1)
    row_both = lax.ppermute(row, ("section", "lat"), across())
    row_core = swapped(row, "lat", 1)
    other = swapped(half, "lat", 1)
    grads = call(
        functools.partial(last_kernel, entries=entries),
        [
            shape((width, 3 * width), F32),
            shape((width, width), F32),
            shape((1, width), F32),
            shape((1, heads), F32),
        ],
        scratch=[
            vmem((width, 3 * width), F32),
            vmem((width, width), F32),
            vmem((1, width), F32),
            vmem((1, heads), F32),
            copies(4 * rows // 64 + 2),
        ],
        out_places="hhhh",
        operands=(half, other, row, row_core, row_section, row_both, bias),
    )
    return grads[0], grads[1], grads[2][0], grads[3][0]


def across():
    sections, lats = lax.axis_size("section"), lax.axis_size("lat")
    return [
        (s * lats + i, (sections - 1 - s) * lats + (i ^ 1))
        for s in range(sections)
        for i in range(lats)
    ]


def split_two(block, axis, bit):
    mine = (lax.axis_index(axis) // bit) % 2
    pair = block.reshape(2, block.shape[0] // 2, -1)
    give = lax.dynamic_index_in_dim(pair, 1 - mine, 0, keepdims=False).astype(BF16)
    return give, lax.dynamic_index_in_dim(pair, mine, 0, keepdims=False)


def doubled(block, axis, bit):
    mine = (lax.axis_index(axis) // bit) % 2
    other = swapped(block, axis, bit)
    low = jnp.where(mine == 0, block, other)
    high = jnp.where(mine == 0, other, block)
    return jnp.concatenate([low, high], axis=0)


def scattered(block, axis):
    count = lax.axis_size(axis)
    mine = lax.axis_index(axis)
    pieces = block.reshape(count, block.shape[0] // count, -1)
    total = lax.dynamic_index_in_dim(pieces, mine, 0, keepdims=False)
    others = []
    for by in range(1, count):
        give = lax.dynamic_index_in_dim(pieces, (mine + by) % count, 0, keepdims=False)
        others.append(from_behind(give.astype(BF16), axis, by))
    for other in others:
        total = total + other.astype(F32)
    return total, others


def gathered(block, axis):
    count = lax.axis_size(axis)
    mine = lax.axis_index(axis)
    whole = jnp.zeros((count,) + block.shape, block.dtype)
    whole = lax.dynamic_update_index_in_dim(whole, block, mine, 0)
    for by in range(1, count):
        whole = lax.dynamic_update_index_in_dim(
            whole, from_behind(block, axis, by), (mine - by) % count, 0
        )
    return whole.reshape(count * block.shape[0], -1)


def sum_squares(block):
    wide = block.astype(F32)
    return jnp.sum(wide * wide)


def plain(keep, came, weight_qkv, gains, heads, entries):
    width = gains.shape[1]
    lat, lon = lax.axis_index("lat"), lax.axis_index("lon")
    part = keep + came.astype(F32)
    give, keep = split_two(part, "lat", 2)
    came = swapped(give, "lat", 2).astype(F32)
    column = lax.broadcasted_iota(jnp.int32, keep.shape, 1)
    is_bias = (column >= CUT) & (column < CUT + GROUP)
    part = jnp.where(is_bias, lax.reduce_precision(keep, 8, 7), keep) + came
    bias_part = lax.reduce_precision(part[:1, CUT : CUT + GROUP], 8, 7)
    part, others = scattered(part, "lon")
    terms = [bias_part] + [other[:1, CUT : CUT + GROUP].astype(F32) for other in others]
    terms = jnp.concatenate(terms[:1] + terms[:0:-1], axis=0)
    bias = jnp.sum(jnp.roll(terms, lon, axis=0), axis=0)[:heads]
    part = jnp.concatenate([part[:, :CUT], part[:, CUT + GROUP :]], axis=1).astype(BF16)
    half = doubled(gathered(part, "lon"), "lat", 2)
    mine = lat % 2
    weight_half = lax.dynamic_slice_in_dim(weight_qkv, mine * (width // 2), width // 2, 0)
    gain_half = lax.dynamic_slice_in_dim(gains[0], mine * (width // 2), width // 2, 0)
    weighed = half[:, : 3 * width].astype(F32) * weight_half.astype(F32)
    gain_half = jnp.sum(weighed, axis=1) / gain_half
    square = sum_squares(half) + sum_squares(gain_half) + 0.5 * sum_squares(bias)
    square = square.reshape(1)
    square = square + swapped(square, "lat", 1)
    square = square + swapped(square, "section", 1)
    factor = jnp.minimum(1.0, lax.rsqrt(square[0] / entries + 1e-06))
    grads = doubled(half, "lat", 1).astype(F32) * factor
    gain = doubled(gain_half.reshape(-1, 1), "lat", 1)[:, 0] * factor
    return grads[:, : 3 * width], grads[:, 3 * width :], gain, bias * factor


def solution(mesh):
    placed = (
        P("section", None, "lat", "lon", None),
        P("section", None, "lat", "lon", None),
        P("lat", "lon"),
        P("section", None),
        P("section", None, None),
        P("section", None, None),
        P("section", None),
    )
    return jax.shard_map(
        body,
        mesh=mesh,
        in_specs=placed,
        out_specs=(
            P("section", None, "lat", "lon", None),
            P("section", None, None),
            P("section", None, None),
            P("section", None),
            P("section", None),
        ),
        check_vma=False,
    )
```

```python
import functools

import jax
import jax.numpy as jnp
from jax import lax
from jax.experimental import pallas as pl
from jax.experimental.pallas import tpu as pltpu
from jax.sharding import PartitionSpec as P

SHIFT = 6
GROUP = 128
CUT = 1408
EPSILON = 1e-05
F32 = jnp.float32
BF16 = jnp.bfloat16


def from_behind(value, axis, by):
    count = lax.axis_size(axis)
    return lax.ppermute(value, axis, [(i, (i + by) % count) for i in range(count)])


def passed_along(block, axis, distance):
    devices = range(lax.axis_size(axis))
    route = [(i - distance, i) for i in devices if i - distance in devices]
    return lax.ppermute(block, axis, route)


def swapped(value, axis, bit):
    count = lax.axis_size(axis)
    return lax.ppermute(value, axis, [(i, i ^ bit) for i in range(count)])


def dot(left, right):
    return jnp.dot(left, right, preferred_element_type=F32)


def dot_last(left, right):
    return lax.dot_general(left, right, (((1,), (1,)), ((), ())), preferred_element_type=F32)


def call(kernel, outs, scratch=(), places="", out_places="", operands=(), flops=10**8, limit=8):
    spaces = {"v": pltpu.VMEM, "s": pltpu.SMEM, "a": pl.ANY, "h": pltpu.HBM}
    places = places or "v" * len(operands)
    out_places = out_places or "v" * len(outs)
    moved = sum(o.size * o.dtype.itemsize for o in list(outs) + list(operands))
    return pl.pallas_call(
        kernel,
        out_shape=list(outs),
        in_specs=[pl.BlockSpec(memory_space=spaces[letter]) for letter in places],
        out_specs=[pl.BlockSpec(memory_space=spaces[letter]) for letter in out_places],
        scratch_shapes=list(scratch),
        compiler_params=pltpu.CompilerParams(vmem_limit_bytes=limit * 2**20),
        cost_estimate=pl.CostEstimate(flops=flops, bytes_accessed=moved, transcendentals=0),
    )(*operands)


def started(source, target, semaphores, index):
    copy = pltpu.make_async_copy(source, target, semaphores.at[index])
    copy.start()
    return copy


def shape(dims, dtype):
    return jax.ShapeDtypeStruct(dims, dtype)


def aligned(start, size):
    return pl.ds(pl.multiple_of(start, size), size)


def position():
    lat, lon = lax.axis_index("lat"), lax.axis_index("lon")
    return lax.rem(lat, 2), lax.div(lat, 2), lon


def pack_kernel(
    tokens, cot, land, gain, bias, own, rim,
    tokens_v, cot_v, land_v, gain_v, bias_v, rim32, sems,
):
    arrays = ((tokens, tokens_v), (cot, cot_v), (land, land_v), (gain, gain_v), (bias, bias_v))
    copies = [started(source, target, sems, i) for i, (source, target) in enumerate(arrays)]
    lats, cols, levels, width = tokens.shape[1:]
    half = levels * lats * SHIFT
    rim32[2 * half :, :] = jnp.zeros((rim32.shape[0] - 2 * half, width), F32)
    own[2 * half :, :] = jnp.zeros((own.shape[0] - 2 * half, width), F32)
    for which, ref in enumerate((tokens_v, cot_v)):
        copies[which].wait()
        for lat in range(lats):
            for col in range(cols):
                row = which * half + (lat * SHIFT + col % SHIFT) * levels
                part = rim32 if col < SHIFT else own
                part[row : row + levels, :] = ref[0, lat, col].astype(F32)
    for copy in copies[2:]:
        copy.wait()
    rim32[2 * half : 2 * half + lats, :cols] = land_v[...].astype(F32)
    own[2 * half : 2 * half + 1, :] = gain_v[...]
    own[2 * half + 1 : 2 * half + 2, : bias.shape[1]] = bias_v[...]
    own[2 * half + 8 : 2 * half + 8 + lats, :cols] = land_v[...].astype(F32)
    rim[...] = rim32[...].astype(BF16)


def unpack_kernel(own, back, grid, grid_v, sems):
    lats, cols, levels, width = grid.shape[1:]
    came = back[...].astype(F32)
    for lat in range(lats):
        for col in range(cols):
            row = (lat * SHIFT + col % SHIFT) * levels
            if col < SHIFT:
                grid_v[0, lat, col] = came[row : row + levels]
            else:
                grid_v[0, lat, col] = own[row : row + levels, :]
    started(grid_v, grid, sems, 0).wait()


def land_column(land, rows, first):
    lats, cols = land.shape
    row = lax.broadcasted_iota(jnp.int32, (rows, lats), 0)
    lat = lax.div(row, rows // lats)
    pick = (lat == lax.broadcasted_iota(jnp.int32, (rows, lats), 1)).astype(F32)
    lines = dot(pick.astype(BF16), land.astype(BF16))
    row = lax.broadcasted_iota(jnp.int32, (rows, cols), 0)
    column = lax.broadcasted_iota(jnp.int32, (rows, cols), 1)
    levels = rows // (lats * SHIFT)
    here = column == lax.rem(lax.div(row, levels), SHIFT) + first
    return jnp.sum(jnp.where(here, lines, 0.0), axis=1, keepdims=True)


def head_masks(dtype, size):
    lane = lax.broadcasted_iota(jnp.int32, (1, GROUP), 1)
    return [
        (lax.div(lane, size) == part).astype(F32).astype(dtype) for part in range(GROUP // size)
    ]


def stacked(block, masks):
    return jnp.concatenate([block * mask for mask in masks], axis=0)


def folded(block, masks):
    rows = block.shape[0] // len(masks)
    return sum(block[i * rows : (i + 1) * rows] * mask for i, mask in enumerate(masks))


def back_through(grad_out, probs, probs_b, qkv, keys_t, weight_out, grad_proj, size, land):
    count, width = grad_out.shape
    per = GROUP // size
    scale = size ** (-0.5)
    masks_b, masks = head_masks(BF16, size), head_masks(F32, size)
    att_t = dot_last(weight_out[...], grad_out)
    grad_att = att_t.T.astype(BF16)
    att_t = att_t.astype(BF16)
    lane = lax.broadcasted_iota(jnp.int32, (1, GROUP), 1)
    bias_row = jnp.zeros((1, GROUP), F32)
    for group in range(width // GROUP):
        at = group * GROUP
        values = qkv[:, 2 * width + at : 2 * width + at + GROUP]
        grad_probs = dot(stacked(values, masks_b), att_t[at : at + GROUP, :])
        scores_b, queries_t = [], []
        for part in range(per):
            head = group * per + part
            weights = probs[head * count : (head + 1) * count, :].astype(F32)
            grad_weights = grad_probs[part * count : (part + 1) * count]
            inner = jnp.sum(weights * grad_weights, axis=0, keepdims=True)
            grad_scores = weights * (grad_weights - inner)
            if land is not None:
                on_land = jnp.sum(grad_scores * land, axis=0, keepdims=True)
                on_land = jnp.sum(on_land, axis=1, keepdims=True)
                bias_row = bias_row + jnp.where(lane == head, on_land, 0.0)
            scaled_b = (grad_scores * scale).astype(BF16)
            scores_b.append(scaled_b)
            queries_t.append(dot(keys_t[head * size : (head + 1) * size, :], scaled_b))
        queries = qkv[:, at : at + GROUP]
        grad_keys = dot(jnp.concatenate(scores_b, axis=0), queries)
        mixed = probs_b[group * per * count : (group + 1) * per * count, :]
        grad_values = dot(mixed, grad_att[:, at : at + GROUP])
        grad_proj[:, at : at + GROUP] = jnp.concatenate(queries_t, axis=0).T.astype(BF16)
        grad_proj[:, width + at : width + at + GROUP] = folded(grad_keys, masks).astype(BF16)
        grad_proj[:, 2 * width + at : 2 * width + at + GROUP] = folded(grad_values, masks).astype(
            BF16
        )
    return bias_row


def through_norm(grad_proj, weight_t, gain, normed, inverse):
    scaled = dot(grad_proj, weight_t[...]) * gain
    mean = jnp.mean(scaled, axis=-1, keepdims=True)
    along = jnp.mean(scaled * normed, axis=-1, keepdims=True)
    return inverse * (scaled - mean - normed * along)


def ready_kernel(after, weight_qkv, weight_out, qkv_v, qkv_t, out_v, sems):
    copies = [
        started(weight_qkv, qkv_v, sems, 0),
        started(weight_out, out_v, sems, 1),
    ]
    copies[0].wait()
    width = weight_qkv.shape[0]
    for part in range(weight_qkv.shape[1] // width):
        rows = slice(part * width, (part + 1) * width)
        qkv_t[rows, :] = qkv_v[:, rows].T
    copies[1].wait()


def forward_kernel(
    own, rim, weight_qkv, weight_t, weight_out,
    skip, cot, normed_t, qkv, probs_b, attended_t, extra, normed_out,
    probs, queries_t, keys_t, values_t, grad_proj,
    *, heads, lats, cols,
):
    width = own.shape[1]
    size = width // heads
    half = cot.shape[0] // 2
    count = 2 * half
    per = GROUP // size
    scale = size ** (-0.5)
    masks_b = head_masks(BF16, size)
    mine = own[: 2 * half, :]
    params = own[2 * half :, :]
    came = rim[...].astype(F32)
    gain = params[0:1, :]
    values = jnp.concatenate([mine[:half], came[:half]], axis=0)
    centred = values - jnp.mean(values, axis=-1, keepdims=True)
    inverse = lax.rsqrt(jnp.mean(centred * centred, axis=-1, keepdims=True) + EPSILON)
    normed = centred * inverse
    normed_out[...] = normed
    normed_b = (normed * gain).astype(BF16)
    normed_t[...] = normed_b.T
    land = jnp.concatenate(
        [
            land_column(params[8 : 8 + lats, :cols], half, SHIFT),
            land_column(came[2 * half : 2 * half + lats, :cols], half, 0),
        ],
        axis=0,
    )
    extra[:, :GROUP] = jnp.broadcast_to(land, (count, GROUP))
    extra[:, GROUP:] = jnp.broadcast_to(inverse, (count, GROUP))
    for part, turned in enumerate((queries_t, keys_t, values_t)):
        columns = slice(part * width, (part + 1) * width)
        qkv[:, columns] = dot(normed_b, weight_qkv[:, columns]).astype(BF16)
        turned[...] = qkv[:, columns].T
    for group in range(width // GROUP):
        at = group * GROUP
        keys = qkv[:, width + at : width + at + GROUP]
        scores = dot(stacked(keys, masks_b), queries_t[at : at + GROUP, :])
        for part in range(per):
            head = group * per + part
            block = scores[part * count : (part + 1) * count] * scale
            block = block + params[1:2, head : head + 1] * land
            block = jnp.exp(block - jnp.max(block, axis=0, keepdims=True))
            weights = block * (1.0 / jnp.sum(block, axis=0, keepdims=True))
            probs[head * count : (head + 1) * count, :] = weights
            weights_b = weights.astype(BF16)
            probs_b[head * count : (head + 1) * count, :] = weights_b
            out = dot(values_t[head * size : (head + 1) * size, :], weights_b)
            attended_t[head * size : (head + 1) * size, :] = out.astype(BF16)
    grad_out = jnp.concatenate([mine[half:], came[half : 2 * half]], axis=0)
    cot[...] = grad_out.astype(BF16)
    back_through(cot[...], probs, probs_b, qkv, keys_t, weight_out, grad_proj, size, None)
    skip[...] = (
        through_norm(grad_proj[...], weight_t, gain, normed, inverse) + grad_out
    ).astype(BF16)


def backward_kernel(
    skip, cot, qkv, probs, weight_out, extra, normed_t, attended_t,
    total_out, grad_proj, bias_out, give,
    keys_t,
    *, heads,
):
    count, width = cot.shape
    core, _, _ = position()
    total_out[...] = (cot[...].astype(F32) + skip[...].astype(F32)).astype(BF16)
    keys_t[...] = qkv[:, width : 2 * width].T
    bias_row = back_through(
        total_out[...], probs, probs, qkv, keys_t, weight_out, grad_proj, width // heads,
        extra[:, :1],
    )
    bias_out[...] = jnp.broadcast_to(bias_row, bias_out.shape)
    half = width // 2
    rows = aligned((1 - core) * half, half)
    weight_rows(rows, normed_t, attended_t, grad_proj, total_out, bias_row, give)


def weight_rows(rows, normed_t, attended_t, grad_proj, total, bias_row, out):
    tokens = normed_t[rows, :]
    three = grad_proj.shape[1]
    out[:, :CUT] = dot(tokens, grad_proj[:, :CUT]).astype(out.dtype)
    out[:, CUT : CUT + GROUP] = jnp.broadcast_to(bias_row, (out.shape[0], GROUP)).astype(out.dtype)
    out[:, CUT + GROUP : three + GROUP] = dot(tokens, grad_proj[:, CUT:]).astype(out.dtype)
    out[:, three + GROUP :] = dot(attended_t[rows, :], total[...]).astype(out.dtype)


def finish_kernel(
    total, grad_proj, bias_row, normed_t, attended_t, normed, extra, weight_t, params,
    keep, own, back,
):
    count, width = total.shape
    half = width // 2
    core, _, _ = position()
    rows = aligned(core * half, half)
    bias_b = bias_row[:1, :].astype(BF16).astype(F32)
    weight_rows(rows, normed_t, attended_t, grad_proj, total, bias_b, keep)
    inverse = extra[:, GROUP : GROUP + 1]
    final = through_norm(grad_proj[...], weight_t, params[count : count + 1, :], normed[...], inverse)
    final = final + total[...].astype(F32)
    own[...] = final[: count // 2]
    back[...] = final[count // 2 :].astype(BF16)


def first_kernel(keep, came, give_p, kept_p, kept_q, *rest):
    _, y, z = position()
    *give_q, total = rest
    wide_p = give_p.shape[1]
    half = keep.shape[0] // 2
    total[...] = keep[...] + came[...].astype(F32)
    give_p[...] = total[aligned((1 - y) * half, half), :wide_p].astype(BF16)
    mine = aligned(y * half, half)
    kept_p[:, :CUT] = total[mine, :CUT]
    kept_p[:, CUT:] = total[mine, CUT:wide_p].astype(BF16).astype(F32)
    piece = kept_q.shape[0]
    kept_q[...] = total[aligned(z * piece, piece), wide_p:]
    for other, ref in zip(range(len(give_q), 0, -1), give_q):
        ref[...] = total[aligned((z ^ other) * piece, piece), wide_p:].astype(BF16)


def second_kernel(after, kept_p, came_p, kept_q, *rest):
    _, y, z = position()
    count = (len(rest) - 5) // 2
    came_q, (give_q, left_q, left_p) = rest[:count], rest[count : count + 3]
    *give_p, total_p, total_q = rest[count + 3 :]
    total_p[...] = kept_p[...] + came_p[...].astype(F32)
    piece = left_p.shape[0]
    mine = aligned(z * piece, piece)
    left_p[:, :CUT] = total_p[mine, :CUT]
    left_p[:, CUT:] = total_p[mine, CUT:].astype(BF16).astype(F32)
    for other, ref in zip(range(len(give_p), 0, -1), give_p):
        ref[...] = total_p[aligned((z ^ other) * piece, piece), :].astype(BF16)
    total = kept_q[...]
    for ref in came_q:
        total = total + ref[...].astype(F32)
    total_q[...] = total
    half = give_q.shape[0]
    give_q[...] = total_q[aligned((1 - y) * half, half), :].astype(BF16)
    left_q[...] = total_q[aligned(y * half, half), :]


def third_kernel(left_p, left_q, came_q, *rest):
    _, _, z = position()
    *came_p, piece_p, piece_q, bias = rest
    total = left_p[:, :CUT]
    for ref in came_p:
        total = total + ref[:, :CUT].astype(F32)
    piece_p[...] = total.astype(BF16)
    piece_q[...] = (left_q[...] + came_q[...].astype(F32)).astype(BF16)
    terms = [left_p[:8, CUT:]] + [ref[...].astype(F32)[:8, CUT:] for ref in came_p[::-1]]
    total = jnp.zeros_like(terms[0])
    for source in range(len(terms)):
        for other, term in enumerate(terms):
            total = total + jnp.where((z ^ other) == source, term, 0.0)
    bias[...] = total


def fourth_kernel(piece_q, other_q, *rest):
    _, y, z = position()
    *parts_p, block_p, block_q = rest
    piece = parts_p[0].shape[0]
    for other, part in enumerate(parts_p):
        block_p[aligned((z ^ other) * piece, piece), :] = part[...]
    piece = piece_q.shape[0]
    block_q[aligned(y * piece, piece), :] = piece_q[...]
    block_q[aligned((1 - y) * piece, piece), :] = other_q[...]


def fifth_kernel(weight_qkv, own, bias, block_p, other_p, *rest):
    *parts_q, half, row = rest
    core, y, z = position()
    rows = half.shape[0]
    mine = aligned(core * rows, rows)
    piece = block_p.shape[0]
    half[aligned(y * piece, piece), :CUT] = block_p[...]
    half[aligned((1 - y) * piece, piece), :CUT] = other_p[...]
    piece = parts_q[0].shape[0]
    for other, part in enumerate(parts_q):
        half[aligned((z ^ other) * piece, piece), CUT:] = part[...]
    three = weight_qkv.shape[1]
    wide = half[:, :three].astype(F32)
    gain_half = jnp.sum(wide * weight_qkv[mine, :].astype(F32), axis=1, keepdims=True)
    gain_half = jnp.broadcast_to(gain_half, (rows, GROUP)).T[:8]
    gain = own[own.shape[0] - 16 : own.shape[0] - 15, :]
    own_gain = jnp.where(core == 0, gain[:, :rows], gain[:, rows:])
    gain_half = gain_half / own_gain
    out = half[:, three:].astype(F32)
    square = jnp.sum(jnp.sum(wide * wide, axis=0, keepdims=True), axis=1, keepdims=True)
    square = square + jnp.sum(jnp.sum(out * out, axis=0, keepdims=True), axis=1, keepdims=True)
    square = square + jnp.sum(gain_half[:1] * gain_half[:1], axis=1, keepdims=True)
    square = square + 0.5 * jnp.sum(bias[:1, :] * bias[:1, :], axis=1, keepdims=True)
    row[:, :rows] = gain_half
    row[:, rows:] = jnp.broadcast_to(square, (8, GROUP))


def last_kernel(
    half, other, row, row_core, row_section, row_both, bias,
    grad_qkv, grad_out, grad_gain, grad_bias,
    qkv_v, out_v, gain_v, bias_v, sems,
    *, entries,
):
    core, _, _ = position()
    rows, three = half.shape[0], grad_qkv.shape[1]
    square = row[:1, rows : rows + 1] + row_core[:1, rows : rows + 1]
    square = square + (row_section[:1, rows : rows + 1] + row_both[:1, rows : rows + 1])
    factor = jnp.minimum(1.0, lax.rsqrt(square / entries + 1e-06))
    sent = []
    piece = 64
    for which, ref in enumerate((half, other)):
        base = core * rows if which == 0 else (1 - core) * rows
        for part in range(rows // piece):
            here = slice(part * piece, (part + 1) * piece)
            at = aligned(base + part * piece, piece)
            slot = slice(which * rows + part * piece, which * rows + (part + 1) * piece)
            qkv_v[slot, :] = ref[here, :three].astype(F32) * factor
            sent.append(started(qkv_v.at[slot, :], grad_qkv.at[at, :], sems, len(sent)))
            out_v[slot, :] = ref[here, three:].astype(F32) * factor
            sent.append(started(out_v.at[slot, :], grad_out.at[at, :], sems, len(sent)))
    mine, its = row[:1, :rows] * factor, row_core[:1, :rows] * factor
    gain_v[:, :rows] = jnp.where(core == 0, mine, its)
    gain_v[:, rows:] = jnp.where(core == 0, its, mine)
    bias_v[...] = bias[:1, : bias_v.shape[1]] * factor
    sent.append(started(gain_v, grad_gain, sems, len(sent)))
    sent.append(started(bias_v, grad_bias, sems, len(sent)))
    for copy in sent:
        copy.wait()


def far_first(pieces, axis):
    others = range(len(pieces), 0, -1)
    return [swapped(piece, axis, other) for other, piece in zip(others, pieces)]


def to_all(piece, axis):
    return [swapped(piece, axis, other) for other in range(1, lax.axis_size(axis))]


def vmem(dims, dtype):
    return pltpu.VMEM(dims, dtype)


def copies(number):
    return pltpu.SemaphoreType.DMA((number,))


def body(inputs, cotangent, land_sea, gains, qkv_weight, out_weight, land_bias):
    weight_qkv, weight_out = qkv_weight[0], out_weight[0]
    levels, lats, cols, width = inputs.shape[1:]
    heads = land_bias.shape[1]
    half = levels * lats * SHIFT
    count = 2 * half
    packed = half * 2 + 16
    lons = lax.axis_size("lon")

    tokens = inputs.transpose(0, 2, 3, 1, 4)
    own_cot = cotangent.transpose(0, 2, 3, 1, 4)

    own, rim = call(
        pack_kernel,
        [shape((packed, width), F32), shape((packed, width), BF16)],
        scratch=[
            vmem(tokens.shape, BF16),
            vmem(tokens.shape, BF16),
            vmem(land_sea.shape, jnp.int32),
            vmem(gains.shape, F32),
            vmem(land_bias.shape, F32),
            vmem((packed, width), F32),
            copies(5),
        ],
        places="hhhhh",
        operands=(tokens, own_cot, land_sea, gains, land_bias),
        limit=60,
    )
    rim = from_behind(rim, "lon", -1)
    qkv_v, qkv_t, out_v = call(
        ready_kernel,
        [
            shape(weight_qkv.shape, BF16),
            shape(weight_qkv.shape[::-1], BF16),
            shape(weight_out.shape, BF16),
        ],
        scratch=[copies(2)],
        places="ahh",
        operands=(own, weight_qkv, weight_out),
        limit=48,
    )
    skip, cot, normed_t, qkv, probs, attended_t, extra, normed = call(
        functools.partial(forward_kernel, heads=heads, lats=lats, cols=cols),
        [
            shape((count, width), BF16),
            shape((count, width), BF16),
            shape((width, count), BF16),
            shape((count, 3 * width), BF16),
            shape((heads * count, count), BF16),
            shape((width, count), BF16),
            shape((count, 2 * GROUP), F32),
            shape((count, width), F32),
        ],
        scratch=[
            vmem((heads * count, count), F32),
            vmem((width, count), BF16),
            vmem((width, count), BF16),
            vmem((width, count), BF16),
            vmem((count, 3 * width), BF16),
        ],
        operands=(own, rim, qkv_v, qkv_t, out_v),
        flops=10**9,
        limit=16,
    )
    skip = passed_along(skip, "section", -1)
    rows, wide = width // 2, 4 * width + GROUP
    total, grad_proj, bias_row, give = call(
        functools.partial(backward_kernel, heads=heads),
        [
            shape((count, width), BF16),
            shape((count, 3 * width), BF16),
            shape((8, GROUP), F32),
            shape((rows, wide), BF16),
        ],
        scratch=[vmem((width, count), BF16)],
        operands=(skip, cot, qkv, probs, out_v, extra, normed_t, attended_t),
        flops=10**9,
    )
    came = swapped(give, "lat", 1)
    keep, own_grad, back = call(
        finish_kernel,
        [
            shape((rows, wide), F32),
            shape((half, width), F32),
            shape((half, width), BF16),
        ],
        operands=(
            total, grad_proj, bias_row, normed_t, attended_t, normed, extra, qkv_t, own,
        ),
        flops=5 * 10**8,
    )
    back = from_behind(back, "lon", 1)
    entries = 2 * (4 * width * width + width + heads)
    if rows // 2 // lons % 16 == 0 and lons & (lons - 1) == 0:
        grads = staged(keep, came, back, qkv_v, own, lons, heads, entries)
    else:
        grads = plain(keep, came, weight_qkv, gains, heads, entries)
    (final_grad,) = call(
        unpack_kernel,
        [shape(tokens.shape, F32)],
        scratch=[vmem(tokens.shape, F32), copies(1)],
        out_places="h",
        operands=(own_grad, back),
    )
    final_grad = final_grad.transpose(0, 3, 1, 2, 4)
    return (final_grad, *(grad[None] for grad in grads))


def staged(keep, came, after, weight_qkv, own, lons, heads, entries):
    rows, wide = keep.shape
    width = 2 * rows
    wide_p = CUT + GROUP
    wide_q = wide - wide_p
    some = range(lons - 1)
    several = "v" * len(some)
    give_p, kept_p, kept_q, *give_q = call(
        first_kernel,
        [
            shape((rows // 2, wide_p), BF16),
            shape((rows // 2, wide_p), F32),
            shape((rows // lons, wide_q), F32),
            *(shape((rows // lons, wide_q), BF16) for _ in some),
        ],
        scratch=[vmem((rows, wide), F32)],
        operands=(keep, came),
    )
    came_p = swapped(give_p, "lat", 2)
    came_q = far_first(give_q, "lon")
    piece = rows // 2 // lons
    give_q, left_q, left_p, *give_p = call(
        second_kernel,
        [
            shape((piece, wide_q), BF16),
            shape((piece, wide_q), F32),
            shape((piece, wide_p), F32),
            *(shape((piece, wide_p), BF16) for _ in some),
        ],
        scratch=[vmem((rows // 2, wide_p), F32), vmem((rows // lons, wide_q), F32)],
        places="avvv" + several,
        operands=(after, kept_p, came_p, kept_q, *came_q),
    )
    came_p = far_first(give_p, "lon")
    came_q = swapped(give_q, "lat", 2)
    piece_p, piece_q, bias = call(
        third_kernel,
        [
            shape((piece, CUT), BF16),
            shape((piece, wide_q), BF16),
            shape((8, GROUP), F32),
        ],
        operands=(left_p, left_q, came_q, *came_p),
    )
    others_p = to_all(piece_p, "lon")
    other_q = swapped(piece_q, "lat", 2)
    block_p, block_q = call(
        fourth_kernel,
        [shape((rows // 2, CUT), BF16), shape((rows // lons, wide_q), BF16)],
        operands=(piece_q, other_q, piece_p, *others_p),
    )
    other_p = swapped(block_p, "lat", 2)
    others_q = to_all(block_q, "lon")
    half, row = call(
        fifth_kernel,
        [shape((rows, 4 * width), BF16), shape((8, rows + GROUP), F32)],
        operands=(weight_qkv, own, bias, block_p, other_p, block_q, *others_q),
    )
    row_section = swapped(row, "section", 1)
    row_both = lax.ppermute(row, ("section", "lat"), across())
    row_core = swapped(row, "lat", 1)
    other = swapped(half, "lat", 1)
    grads = call(
        functools.partial(last_kernel, entries=entries),
        [
            shape((width, 3 * width), F32),
            shape((width, width), F32),
            shape((1, width), F32),
            shape((1, heads), F32),
        ],
        scratch=[
            vmem((width, 3 * width), F32),
            vmem((width, width), F32),
            vmem((1, width), F32),
            vmem((1, heads), F32),
            copies(4 * rows // 64 + 2),
        ],
        out_places="hhhh",
        operands=(half, other, row, row_core, row_section, row_both, bias),
    )
    return grads[0], grads[1], grads[2][0], grads[3][0]


def across():
    sections, lats = lax.axis_size("section"), lax.axis_size("lat")
    return [
        (s * lats + i, (sections - 1 - s) * lats + (i ^ 1))
        for s in range(sections)
        for i in range(lats)
    ]


def split_two(block, axis, bit):
    mine = (lax.axis_index(axis) // bit) % 2
    pair = block.reshape(2, block.shape[0] // 2, -1)
    give = lax.dynamic_index_in_dim(pair, 1 - mine, 0, keepdims=False).astype(BF16)
    return give, lax.dynamic_index_in_dim(pair, mine, 0, keepdims=False)


def doubled(block, axis, bit):
    mine = (lax.axis_index(axis) // bit) % 2
    other = swapped(block, axis, bit)
    low = jnp.where(mine == 0, block, other)
    high = jnp.where(mine == 0, other, block)
    return jnp.concatenate([low, high], axis=0)


def scattered(block, axis):
    count = lax.axis_size(axis)
    mine = lax.axis_index(axis)
    pieces = block.reshape(count, block.shape[0] // count, -1)
    total = lax.dynamic_index_in_dim(pieces, mine, 0, keepdims=False)
    others = []
    for by in range(1, count):
        give = lax.dynamic_index_in_dim(pieces, (mine + by) % count, 0, keepdims=False)
        others.append(from_behind(give.astype(BF16), axis, by))
    for other in others:
        total = total + other.astype(F32)
    return total, others


def gathered(block, axis):
    count = lax.axis_size(axis)
    mine = lax.axis_index(axis)
    whole = jnp.zeros((count,) + block.shape, block.dtype)
    whole = lax.dynamic_update_index_in_dim(whole, block, mine, 0)
    for by in range(1, count):
        whole = lax.dynamic_update_index_in_dim(
            whole, from_behind(block, axis, by), (mine - by) % count, 0
        )
    return whole.reshape(count * block.shape[0], -1)


def sum_squares(block):
    wide = block.astype(F32)
    return jnp.sum(wide * wide)


def plain(keep, came, weight_qkv, gains, heads, entries):
    width = gains.shape[1]
    lat, lon = lax.axis_index("lat"), lax.axis_index("lon")
    part = keep + came.astype(F32)
    give, keep = split_two(part, "lat", 2)
    came = swapped(give, "lat", 2).astype(F32)
    column = lax.broadcasted_iota(jnp.int32, keep.shape, 1)
    is_bias = (column >= CUT) & (column < CUT + GROUP)
    part = jnp.where(is_bias, lax.reduce_precision(keep, 8, 7), keep) + came
    bias_part = lax.reduce_precision(part[:1, CUT : CUT + GROUP], 8, 7)
    part, others = scattered(part, "lon")
    terms = [bias_part] + [other[:1, CUT : CUT + GROUP].astype(F32) for other in others]
    terms = jnp.concatenate(terms[:1] + terms[:0:-1], axis=0)
    bias = jnp.sum(jnp.roll(terms, lon, axis=0), axis=0)[:heads]
    part = jnp.concatenate([part[:, :CUT], part[:, CUT + GROUP :]], axis=1).astype(BF16)
    half = doubled(gathered(part, "lon"), "lat", 2)
    mine = lat % 2
    weight_half = lax.dynamic_slice_in_dim(weight_qkv, mine * (width // 2), width // 2, 0)
    gain_half = lax.dynamic_slice_in_dim(gains[0], mine * (width // 2), width // 2, 0)
    weighed = half[:, : 3 * width].astype(F32) * weight_half.astype(F32)
    gain_half = jnp.sum(weighed, axis=1) / gain_half
    square = sum_squares(half) + sum_squares(gain_half) + 0.5 * sum_squares(bias)
    square = square.reshape(1)
    square = square + swapped(square, "lat", 1)
    square = square + swapped(square, "section", 1)
    factor = jnp.minimum(1.0, lax.rsqrt(square[0] / entries + 1e-06))
    grads = doubled(half, "lat", 1).astype(F32) * factor
    gain = doubled(gain_half.reshape(-1, 1), "lat", 1)[:, 0] * factor
    return grads[:, : 3 * width], grads[:, 3 * width :], gain, bias * factor


def solution(mesh):
    placed = (
        P("section", None, "lat", "lon", None),
        P("section", None, "lat", "lon", None),
        P("lat", "lon"),
        P("section", None),
        P("section", None, None),
        P("section", None, None),
        P("section", None),
    )
    return jax.shard_map(
        body,
        mesh=mesh,
        in_specs=placed,
        out_specs=(
            P("section", None, "lat", "lon", None),
            P("section", None, None),
            P("section", None, None),
            P("section", None),
            P("section", None),
        ),
        check_vma=False,
    )
```

```python
import functools

import jax
import jax.numpy as jnp
from jax import lax
from jax.experimental import pallas as pl
from jax.experimental.pallas import tpu as pltpu
from jax.sharding import PartitionSpec as P

SHIFT = 6
GROUP = 128
CUT = 1408
EPSILON = 1e-05
F32 = jnp.float32
BF16 = jnp.bfloat16


def from_behind(value, axis, by):
    count = lax.axis_size(axis)
    return lax.ppermute(value, axis, [(i, (i + by) % count) for i in range(count)])


def passed_along(block, axis, distance):
    devices = range(lax.axis_size(axis))
    route = [(i - distance, i) for i in devices if i - distance in devices]
    return lax.ppermute(block, axis, route)


def swapped(value, axis, bit):
    count = lax.axis_size(axis)
    return lax.ppermute(value, axis, [(i, i ^ bit) for i in range(count)])


def dot(left, right):
    return jnp.dot(left, right, preferred_element_type=F32)


def dot_last(left, right):
    return lax.dot_general(left, right, (((1,), (1,)), ((), ())), preferred_element_type=F32)


def call(kernel, outs, scratch=(), places="", out_places="", operands=(), flops=10**8, limit=8):
    spaces = {"v": pltpu.VMEM, "s": pltpu.SMEM, "a": pl.ANY, "h": pltpu.HBM}
    places = places or "v" * len(operands)
    out_places = out_places or "v" * len(outs)
    moved = sum(o.size * o.dtype.itemsize for o in list(outs) + list(operands))
    return pl.pallas_call(
        kernel,
        out_shape=list(outs),
        in_specs=[pl.BlockSpec(memory_space=spaces[letter]) for letter in places],
        out_specs=[pl.BlockSpec(memory_space=spaces[letter]) for letter in out_places],
        scratch_shapes=list(scratch),
        compiler_params=pltpu.CompilerParams(vmem_limit_bytes=limit * 2**20),
        cost_estimate=pl.CostEstimate(flops=flops, bytes_accessed=moved, transcendentals=0),
    )(*operands)


def started(source, target, semaphores, index):
    copy = pltpu.make_async_copy(source, target, semaphores.at[index])
    copy.start()
    return copy


def shape(dims, dtype):
    return jax.ShapeDtypeStruct(dims, dtype)


def aligned(start, size):
    return pl.ds(pl.multiple_of(start, size), size)


def position():
    lat, lon = lax.axis_index("lat"), lax.axis_index("lon")
    return lax.rem(lat, 2), lax.div(lat, 2), lon


def pack_kernel(
    tokens, cot, land, gain, bias, own, rim, rim_cot,
    tokens_v, cot_v, land_v, gain_v, bias_v, rim32, rim_cot32, sems,
):
    arrays = ((tokens, tokens_v), (cot, cot_v), (land, land_v), (gain, gain_v), (bias, bias_v))
    copies = [started(source, target, sems, i) for i, (source, target) in enumerate(arrays)]
    lats, cols, levels, width = tokens.shape[1:]
    half = levels * lats * SHIFT
    rim32[half:, :] = jnp.zeros((rim32.shape[0] - half, width), F32)
    rim_cot32[half:, :] = jnp.zeros((rim32.shape[0] - half, width), F32)
    own[2 * half :, :] = jnp.zeros((own.shape[0] - 2 * half, width), F32)
    for which, (ref, part) in enumerate(((tokens_v, rim32), (cot_v, rim_cot32))):
        copies[which].wait()
        for lat in range(lats):
            for col in range(SHIFT):
                row = (lat * SHIFT + col) * levels
                part[row : row + levels, :] = ref[0, lat, col].astype(F32)
                row = row + which * half
                own[row : row + levels, :] = ref[0, lat, SHIFT + col].astype(F32)
    for copy in copies[2:]:
        copy.wait()
    rim32[half : half + lats, :cols] = land_v[...].astype(F32)
    own[2 * half : 2 * half + 1, :] = gain_v[...]
    own[2 * half + 1 : 2 * half + 2, : bias.shape[1]] = bias_v[...]
    own[2 * half + 8 : 2 * half + 8 + lats, :cols] = land_v[...].astype(F32)
    rim[...] = rim32[...].astype(BF16)
    rim_cot[...] = rim_cot32[...].astype(BF16)


def unpack_kernel(own, back, grid, grid_v, sems):
    lats, cols, levels, width = grid.shape[1:]
    came = back[...].astype(F32)
    for lat in range(lats):
        for col in range(cols):
            row = (lat * SHIFT + col % SHIFT) * levels
            if col < SHIFT:
                grid_v[0, lat, col] = came[row : row + levels]
            else:
                grid_v[0, lat, col] = own[row : row + levels, :]
    started(grid_v, grid, sems, 0).wait()


def land_column(land, rows, first):
    lats, cols = land.shape
    row = lax.broadcasted_iota(jnp.int32, (rows, lats), 0)
    lat = lax.div(row, rows // lats)
    pick = (lat == lax.broadcasted_iota(jnp.int32, (rows, lats), 1)).astype(F32)
    lines = dot(pick.astype(BF16), land.astype(BF16))
    row = lax.broadcasted_iota(jnp.int32, (rows, cols), 0)
    column = lax.broadcasted_iota(jnp.int32, (rows, cols), 1)
    levels = rows // (lats * SHIFT)
    here = column == lax.rem(lax.div(row, levels), SHIFT) + first
    return jnp.sum(jnp.where(here, lines, 0.0), axis=1, keepdims=True)


def head_masks(dtype, size):
    lane = lax.broadcasted_iota(jnp.int32, (1, GROUP), 1)
    return [
        (lax.div(lane, size) == part).astype(F32).astype(dtype) for part in range(GROUP // size)
    ]


def stacked(block, masks):
    return jnp.concatenate([block * mask for mask in masks], axis=0)


def folded(block, masks):
    rows = block.shape[0] // len(masks)
    return sum(block[i * rows : (i + 1) * rows] * mask for i, mask in enumerate(masks))


def back_through(grad_out, probs, qkv, keys_t, weight_out, grad_proj, size, land):
    count, width = grad_out.shape
    per = GROUP // size
    scale = size ** (-0.5)
    masks_b, masks = head_masks(BF16, size), head_masks(F32, size)
    att_t = dot_last(weight_out[...], grad_out)
    grad_att = att_t.T.astype(BF16)
    att_t = att_t.astype(BF16)
    lane = lax.broadcasted_iota(jnp.int32, (1, GROUP), 1)
    bias_row = jnp.zeros((1, GROUP), F32)
    for group in range(width // GROUP):
        at = group * GROUP
        values = qkv[:, 2 * width + at : 2 * width + at + GROUP]
        grad_probs = dot(stacked(values, masks_b), att_t[at : at + GROUP, :])
        scores_b, queries_t = [], []
        for part in range(per):
            head = group * per + part
            weights = probs[head * count : (head + 1) * count, :].astype(F32)
            grad_weights = grad_probs[part * count : (part + 1) * count]
            inner = jnp.sum(weights * grad_weights, axis=0, keepdims=True)
            grad_scores = weights * (grad_weights - inner)
            if land is not None:
                on_land = jnp.sum(grad_scores * land, axis=0, keepdims=True)
                on_land = jnp.sum(on_land, axis=1, keepdims=True)
                bias_row = bias_row + jnp.where(lane == head, on_land, 0.0)
            scaled_b = (grad_scores * scale).astype(BF16)
            scores_b.append(scaled_b)
            queries_t.append(dot(keys_t[head * size : (head + 1) * size, :], scaled_b))
        queries = qkv[:, at : at + GROUP]
        grad_keys = dot(jnp.concatenate(scores_b, axis=0), queries)
        mixed = probs[group * per * count : (group + 1) * per * count, :]
        grad_values = dot(mixed, grad_att[:, at : at + GROUP])
        grad_proj[:, at : at + GROUP] = jnp.concatenate(queries_t, axis=0).T.astype(BF16)
        grad_proj[:, width + at : width + at + GROUP] = folded(grad_keys, masks).astype(BF16)
        grad_proj[:, 2 * width + at : 2 * width + at + GROUP] = folded(grad_values, masks).astype(
            BF16
        )
    return bias_row


def through_norm(grad_proj, weight_t, gain, normed, inverse):
    scaled = dot(grad_proj, weight_t[...]) * gain
    mean = jnp.mean(scaled, axis=-1, keepdims=True)
    along = jnp.mean(scaled * normed, axis=-1, keepdims=True)
    return inverse * (scaled - mean - normed * along)


def ready_kernel(after, weight_qkv, weight_out, qkv_v, qkv_t, out_v, sems):
    copies = [
        started(weight_qkv, qkv_v, sems, 0),
        started(weight_out, out_v, sems, 1),
    ]
    copies[0].wait()
    width = weight_qkv.shape[0]
    for part in range(weight_qkv.shape[1] // width):
        rows = slice(part * width, (part + 1) * width)
        qkv_t[rows, :] = qkv_v[:, rows].T
    copies[1].wait()


def forward_kernel(
    own, rim, weight_qkv,
    normed_t, qkv, probs, attended_t, extra, normed_out,
    queries_t, values_t,
    *, heads, lats, cols,
):
    width = own.shape[1]
    size = width // heads
    count = qkv.shape[0]
    half = count // 2
    per = GROUP // size
    scale = size ** (-0.5)
    masks_b = head_masks(BF16, size)
    params = own[count:, :]
    came = rim[...].astype(F32)
    gain = params[0:1, :]
    values = jnp.concatenate([own[:half, :], came[:half]], axis=0)
    centred = values - jnp.mean(values, axis=-1, keepdims=True)
    inverse = lax.rsqrt(jnp.mean(centred * centred, axis=-1, keepdims=True) + EPSILON)
    normed = centred * inverse
    normed_out[...] = normed
    normed_b = (normed * gain).astype(BF16)
    normed_t[...] = normed_b.T
    land = jnp.concatenate(
        [
            land_column(params[8 : 8 + lats, :cols], half, SHIFT),
            land_column(came[half : half + lats, :cols], half, 0),
        ],
        axis=0,
    )
    extra[:, :GROUP] = jnp.broadcast_to(land, (count, GROUP))
    extra[:, GROUP:] = jnp.broadcast_to(inverse, (count, GROUP))
    for part, turned in enumerate((queries_t, None, values_t)):
        columns = slice(part * width, (part + 1) * width)
        qkv[:, columns] = dot(normed_b, weight_qkv[:, columns]).astype(BF16)
        if turned is not None:
            turned[...] = qkv[:, columns].T
    for group in range(width // GROUP):
        at = group * GROUP
        keys = qkv[:, width + at : width + at + GROUP]
        scores = dot(stacked(keys, masks_b), queries_t[at : at + GROUP, :])
        for part in range(per):
            head = group * per + part
            block = scores[part * count : (part + 1) * count] * scale
            block = block + params[1:2, head : head + 1] * land
            block = jnp.exp(block - jnp.max(block, axis=0, keepdims=True))
            weights = block * (1.0 / jnp.sum(block, axis=0, keepdims=True))
            weights_b = weights.astype(BF16)
            probs[head * count : (head + 1) * count, :] = weights_b
            out = dot(values_t[head * size : (head + 1) * size, :], weights_b)
            attended_t[head * size : (head + 1) * size, :] = out.astype(BF16)


def first_backward_kernel(
    own, rim, qkv, probs, weight_out, weight_t, extra, normed,
    skip, cot,
    keys_t, grad_proj,
    *, heads,
):
    count, width = cot.shape
    half = count // 2
    came = rim[...].astype(F32)
    grad_out = jnp.concatenate([own[half:count, :], came[:half]], axis=0)
    cot[...] = grad_out.astype(BF16)
    keys_t[...] = qkv[:, width : 2 * width].T
    back_through(cot[...], probs, qkv, keys_t, weight_out, grad_proj, width // heads, None)
    gain, inverse = own[count : count + 1, :], extra[:, GROUP : GROUP + 1]
    skip[...] = (
        through_norm(grad_proj[...], weight_t, gain, normed[...], inverse) + grad_out
    ).astype(BF16)


def backward_kernel(
    skip, cot, qkv, probs, weight_out, extra, normed_t, attended_t,
    total_out, grad_proj, bias_out, give,
    keys_t,
    *, heads,
):
    count, width = cot.shape
    core, _, _ = position()
    total_out[...] = (cot[...].astype(F32) + skip[...].astype(F32)).astype(BF16)
    keys_t[...] = qkv[:, width : 2 * width].T
    bias_row = back_through(
        total_out[...], probs, qkv, keys_t, weight_out, grad_proj, width // heads,
        extra[:, :1],
    )
    bias_out[...] = jnp.broadcast_to(bias_row, bias_out.shape)
    half = width // 2
    rows = aligned((1 - core) * half, half)
    weight_rows(rows, normed_t, attended_t, grad_proj, total_out, bias_row, give)


def weight_rows(rows, normed_t, attended_t, grad_proj, total, bias_row, out):
    tokens = normed_t[rows, :]
    three = grad_proj.shape[1]
    out[:, :CUT] = dot(tokens, grad_proj[:, :CUT]).astype(out.dtype)
    out[:, CUT : CUT + GROUP] = jnp.broadcast_to(bias_row, (out.shape[0], GROUP)).astype(out.dtype)
    out[:, CUT + GROUP : three + GROUP] = dot(tokens, grad_proj[:, CUT:]).astype(out.dtype)
    out[:, three + GROUP :] = dot(attended_t[rows, :], total[...]).astype(out.dtype)


def finish_kernel(
    total, grad_proj, bias_row, normed_t, attended_t, normed, extra, weight_t, params,
    keep, own, back,
):
    count, width = total.shape
    half = width // 2
    core, _, _ = position()
    rows = aligned(core * half, half)
    bias_b = bias_row[:1, :].astype(BF16).astype(F32)
    weight_rows(rows, normed_t, attended_t, grad_proj, total, bias_b, keep)
    inverse = extra[:, GROUP : GROUP + 1]
    final = through_norm(grad_proj[...], weight_t, params[count : count + 1, :], normed[...], inverse)
    final = final + total[...].astype(F32)
    own[...] = final[: count // 2]
    back[...] = final[count // 2 :].astype(BF16)


def first_kernel(keep, came, give_p, kept_p, kept_q, *rest):
    _, y, z = position()
    *give_q, total = rest
    wide_p = give_p.shape[1]
    half = keep.shape[0] // 2
    total[...] = keep[...] + came[...].astype(F32)
    give_p[...] = total[aligned((1 - y) * half, half), :wide_p].astype(BF16)
    mine = aligned(y * half, half)
    kept_p[:, :CUT] = total[mine, :CUT]
    kept_p[:, CUT:] = total[mine, CUT:wide_p].astype(BF16).astype(F32)
    piece = kept_q.shape[0]
    kept_q[...] = total[aligned(z * piece, piece), wide_p:]
    for other, ref in zip(range(len(give_q), 0, -1), give_q):
        ref[...] = total[aligned((z ^ other) * piece, piece), wide_p:].astype(BF16)


def second_kernel(after, kept_p, came_p, kept_q, *rest):
    _, y, z = position()
    count = (len(rest) - 5) // 2
    came_q, (give_q, left_q, left_p) = rest[:count], rest[count : count + 3]
    *give_p, total_p, total_q = rest[count + 3 :]
    total_p[...] = kept_p[...] + came_p[...].astype(F32)
    piece = left_p.shape[0]
    mine = aligned(z * piece, piece)
    left_p[:, :CUT] = total_p[mine, :CUT]
    left_p[:, CUT:] = total_p[mine, CUT:].astype(BF16).astype(F32)
    for other, ref in zip(range(len(give_p), 0, -1), give_p):
        ref[...] = total_p[aligned((z ^ other) * piece, piece), :].astype(BF16)
    total = kept_q[...]
    for ref in came_q:
        total = total + ref[...].astype(F32)
    total_q[...] = total
    half = give_q.shape[0]
    give_q[...] = total_q[aligned((1 - y) * half, half), :].astype(BF16)
    left_q[...] = total_q[aligned(y * half, half), :]


def third_kernel(left_p, left_q, came_q, *rest):
    _, _, z = position()
    *came_p, piece_p, piece_q, bias = rest
    total = left_p[:, :CUT]
    for ref in came_p:
        total = total + ref[:, :CUT].astype(F32)
    piece_p[...] = total.astype(BF16)
    piece_q[...] = (left_q[...] + came_q[...].astype(F32)).astype(BF16)
    terms = [left_p[:8, CUT:]] + [ref[...].astype(F32)[:8, CUT:] for ref in came_p[::-1]]
    total = jnp.zeros_like(terms[0])
    for source in range(len(terms)):
        for other, term in enumerate(terms):
            total = total + jnp.where((z ^ other) == source, term, 0.0)
    bias[...] = total


def fourth_kernel(piece_q, other_q, *rest):
    _, y, z = position()
    *parts_p, block_p, block_q = rest
    piece = parts_p[0].shape[0]
    for other, part in enumerate(parts_p):
        block_p[aligned((z ^ other) * piece, piece), :] = part[...]
    piece = piece_q.shape[0]
    block_q[aligned(y * piece, piece), :] = piece_q[...]
    block_q[aligned((1 - y) * piece, piece), :] = other_q[...]


def fifth_kernel(weight_qkv, own, bias, block_p, other_p, *rest):
    *parts_q, half, row = rest
    core, y, z = position()
    rows = half.shape[0]
    mine = aligned(core * rows, rows)
    piece = block_p.shape[0]
    half[aligned(y * piece, piece), :CUT] = block_p[...]
    half[aligned((1 - y) * piece, piece), :CUT] = other_p[...]
    piece = parts_q[0].shape[0]
    for other, part in enumerate(parts_q):
        half[aligned((z ^ other) * piece, piece), CUT:] = part[...]
    three = weight_qkv.shape[1]
    wide = half[:, :three].astype(F32)
    gain_half = jnp.sum(wide * weight_qkv[mine, :].astype(F32), axis=1, keepdims=True)
    gain_half = jnp.broadcast_to(gain_half, (rows, GROUP)).T[:8]
    gain = own[own.shape[0] - 16 : own.shape[0] - 15, :]
    own_gain = jnp.where(core == 0, gain[:, :rows], gain[:, rows:])
    gain_half = gain_half / own_gain
    out = half[:, three:].astype(F32)
    square = jnp.sum(jnp.sum(wide * wide, axis=0, keepdims=True), axis=1, keepdims=True)
    square = square + jnp.sum(jnp.sum(out * out, axis=0, keepdims=True), axis=1, keepdims=True)
    square = square + jnp.sum(gain_half[:1] * gain_half[:1], axis=1, keepdims=True)
    square = square + 0.5 * jnp.sum(bias[:1, :] * bias[:1, :], axis=1, keepdims=True)
    row[:, :rows] = gain_half
    row[:, rows:] = jnp.broadcast_to(square, (8, GROUP))


def last_kernel(
    half, other, row, row_core, row_section, row_both, bias,
    grad_qkv, grad_out, grad_gain, grad_bias,
    qkv_v, out_v, gain_v, bias_v, sems,
    *, entries,
):
    core, _, _ = position()
    rows, three = half.shape[0], grad_qkv.shape[1]
    square = row[:1, rows : rows + 1] + row_core[:1, rows : rows + 1]
    square = square + (row_section[:1, rows : rows + 1] + row_both[:1, rows : rows + 1])
    factor = jnp.minimum(1.0, lax.rsqrt(square / entries + 1e-06))
    sent = []
    piece = 64
    for which, ref in enumerate((half, other)):
        base = core * rows if which == 0 else (1 - core) * rows
        for part in range(rows // piece):
            here = slice(part * piece, (part + 1) * piece)
            at = aligned(base + part * piece, piece)
            slot = slice(which * rows + part * piece, which * rows + (part + 1) * piece)
            qkv_v[slot, :] = ref[here, :three].astype(F32) * factor
            sent.append(started(qkv_v.at[slot, :], grad_qkv.at[at, :], sems, len(sent)))
            out_v[slot, :] = ref[here, three:].astype(F32) * factor
            sent.append(started(out_v.at[slot, :], grad_out.at[at, :], sems, len(sent)))
    mine, its = row[:1, :rows] * factor, row_core[:1, :rows] * factor
    gain_v[:, :rows] = jnp.where(core == 0, mine, its)
    gain_v[:, rows:] = jnp.where(core == 0, its, mine)
    bias_v[...] = bias[:1, : bias_v.shape[1]] * factor
    sent.append(started(gain_v, grad_gain, sems, len(sent)))
    sent.append(started(bias_v, grad_bias, sems, len(sent)))
    for copy in sent:
        copy.wait()


def far_first(pieces, axis):
    others = range(len(pieces), 0, -1)
    return [swapped(piece, axis, other) for other, piece in zip(others, pieces)]


def to_all(piece, axis):
    return [swapped(piece, axis, other) for other in range(1, lax.axis_size(axis))]


def vmem(dims, dtype):
    return pltpu.VMEM(dims, dtype)


def copies(number):
    return pltpu.SemaphoreType.DMA((number,))


def body(inputs, cotangent, land_sea, gains, qkv_weight, out_weight, land_bias):
    weight_qkv, weight_out = qkv_weight[0], out_weight[0]
    levels, lats, cols, width = inputs.shape[1:]
    heads = land_bias.shape[1]
    half = levels * lats * SHIFT
    count = 2 * half
    packed = half * 2 + 16
    lons = lax.axis_size("lon")

    tokens = inputs.transpose(0, 2, 3, 1, 4)
    own_cot = cotangent.transpose(0, 2, 3, 1, 4)

    own, rim, rim_cot = call(
        pack_kernel,
        [
            shape((packed, width), F32),
            shape((half + 8, width), BF16),
            shape((half + 8, width), BF16),
        ],
        scratch=[
            vmem(tokens.shape, BF16),
            vmem(tokens.shape, BF16),
            vmem(land_sea.shape, jnp.int32),
            vmem(gains.shape, F32),
            vmem(land_bias.shape, F32),
            vmem((half + 8, width), F32),
            vmem((half + 8, width), F32),
            copies(5),
        ],
        places="hhhhh",
        operands=(tokens, own_cot, land_sea, gains, land_bias),
        limit=60,
    )
    rim = from_behind(rim, "lon", -1)
    rim_cot = from_behind(rim_cot, "lon", -1)
    qkv_v, qkv_t, out_v = call(
        ready_kernel,
        [
            shape(weight_qkv.shape, BF16),
            shape(weight_qkv.shape[::-1], BF16),
            shape(weight_out.shape, BF16),
        ],
        scratch=[copies(2)],
        places="ahh",
        operands=(own, weight_qkv, weight_out),
        limit=48,
    )
    normed_t, qkv, probs, attended_t, extra, normed = call(
        functools.partial(forward_kernel, heads=heads, lats=lats, cols=cols),
        [
            shape((width, count), BF16),
            shape((count, 3 * width), BF16),
            shape((heads * count, count), BF16),
            shape((width, count), BF16),
            shape((count, 2 * GROUP), F32),
            shape((count, width), F32),
        ],
        scratch=[vmem((width, count), BF16), vmem((width, count), BF16)],
        operands=(own, rim, qkv_v),
        flops=10**9,
    )
    skip, cot = call(
        functools.partial(first_backward_kernel, heads=heads),
        [shape((count, width), BF16), shape((count, width), BF16)],
        scratch=[vmem((width, count), BF16), vmem((count, 3 * width), BF16)],
        operands=(own, rim_cot, qkv, probs, out_v, qkv_t, extra, normed),
        flops=10**9,
    )
    skip = passed_along(skip, "section", -1)
    rows, wide = width // 2, 4 * width + GROUP
    total, grad_proj, bias_row, give = call(
        functools.partial(backward_kernel, heads=heads),
        [
            shape((count, width), BF16),
            shape((count, 3 * width), BF16),
            shape((8, GROUP), F32),
            shape((rows, wide), BF16),
        ],
        scratch=[vmem((width, count), BF16)],
        operands=(skip, cot, qkv, probs, out_v, extra, normed_t, attended_t),
        flops=10**9,
    )
    came = swapped(give, "lat", 1)
    keep, own_grad, back = call(
        finish_kernel,
        [
            shape((rows, wide), F32),
            shape((half, width), F32),
            shape((half, width), BF16),
        ],
        operands=(
            total, grad_proj, bias_row, normed_t, attended_t, normed, extra, qkv_t, own,
        ),
        flops=5 * 10**8,
    )
    back = from_behind(back, "lon", 1)
    entries = 2 * (4 * width * width + width + heads)
    if rows // 2 // lons % 16 == 0 and lons & (lons - 1) == 0:
        grads = staged(keep, came, back, qkv_v, own, lons, heads, entries)
    else:
        grads = plain(keep, came, weight_qkv, gains, heads, entries)
    (final_grad,) = call(
        unpack_kernel,
        [shape(tokens.shape, F32)],
        scratch=[vmem(tokens.shape, F32), copies(1)],
        out_places="h",
        operands=(own_grad, back),
    )
    final_grad = final_grad.transpose(0, 3, 1, 2, 4)
    return (final_grad, *(grad[None] for grad in grads))


def staged(keep, came, after, weight_qkv, own, lons, heads, entries):
    rows, wide = keep.shape
    width = 2 * rows
    wide_p = CUT + GROUP
    wide_q = wide - wide_p
    some = range(lons - 1)
    several = "v" * len(some)
    give_p, kept_p, kept_q, *give_q = call(
        first_kernel,
        [
            shape((rows // 2, wide_p), BF16),
            shape((rows // 2, wide_p), F32),
            shape((rows // lons, wide_q), F32),
            *(shape((rows // lons, wide_q), BF16) for _ in some),
        ],
        scratch=[vmem((rows, wide), F32)],
        operands=(keep, came),
    )
    came_p = swapped(give_p, "lat", 2)
    came_q = far_first(give_q, "lon")
    piece = rows // 2 // lons
    give_q, left_q, left_p, *give_p = call(
        second_kernel,
        [
            shape((piece, wide_q), BF16),
            shape((piece, wide_q), F32),
            shape((piece, wide_p), F32),
            *(shape((piece, wide_p), BF16) for _ in some),
        ],
        scratch=[vmem((rows // 2, wide_p), F32), vmem((rows // lons, wide_q), F32)],
        places="avvv" + several,
        operands=(after, kept_p, came_p, kept_q, *came_q),
    )
    came_p = far_first(give_p, "lon")
    came_q = swapped(give_q, "lat", 2)
    piece_p, piece_q, bias = call(
        third_kernel,
        [
            shape((piece, CUT), BF16),
            shape((piece, wide_q), BF16),
            shape((8, GROUP), F32),
        ],
        operands=(left_p, left_q, came_q, *came_p),
    )
    others_p = to_all(piece_p, "lon")
    other_q = swapped(piece_q, "lat", 2)
    block_p, block_q = call(
        fourth_kernel,
        [shape((rows // 2, CUT), BF16), shape((rows // lons, wide_q), BF16)],
        operands=(piece_q, other_q, piece_p, *others_p),
    )
    other_p = swapped(block_p, "lat", 2)
    others_q = to_all(block_q, "lon")
    half, row = call(
        fifth_kernel,
        [shape((rows, 4 * width), BF16), shape((8, rows + GROUP), F32)],
        operands=(weight_qkv, own, bias, block_p, other_p, block_q, *others_q),
    )
    row_section = swapped(row, "section", 1)
    row_both = lax.ppermute(row, ("section", "lat"), across())
    row_core = swapped(row, "lat", 1)
    other = swapped(half, "lat", 1)
    grads = call(
        functools.partial(last_kernel, entries=entries),
        [
            shape((width, 3 * width), F32),
            shape((width, width), F32),
            shape((1, width), F32),
            shape((1, heads), F32),
        ],
        scratch=[
            vmem((width, 3 * width), F32),
            vmem((width, width), F32),
            vmem((1, width), F32),
            vmem((1, heads), F32),
            copies(4 * rows // 64 + 2),
        ],
        out_places="hhhh",
        operands=(half, other, row, row_core, row_section, row_both, bias),
    )
    return grads[0], grads[1], grads[2][0], grads[3][0]


def across():
    sections, lats = lax.axis_size("section"), lax.axis_size("lat")
    return [
        (s * lats + i, (sections - 1 - s) * lats + (i ^ 1))
        for s in range(sections)
        for i in range(lats)
    ]


def split_two(block, axis, bit):
    mine = (lax.axis_index(axis) // bit) % 2
    pair = block.reshape(2, block.shape[0] // 2, -1)
    give = lax.dynamic_index_in_dim(pair, 1 - mine, 0, keepdims=False).astype(BF16)
    return give, lax.dynamic_index_in_dim(pair, mine, 0, keepdims=False)


def doubled(block, axis, bit):
    mine = (lax.axis_index(axis) // bit) % 2
    other = swapped(block, axis, bit)
    low = jnp.where(mine == 0, block, other)
    high = jnp.where(mine == 0, other, block)
    return jnp.concatenate([low, high], axis=0)


def scattered(block, axis):
    count = lax.axis_size(axis)
    mine = lax.axis_index(axis)
    pieces = block.reshape(count, block.shape[0] // count, -1)
    total = lax.dynamic_index_in_dim(pieces, mine, 0, keepdims=False)
    others = []
    for by in range(1, count):
        give = lax.dynamic_index_in_dim(pieces, (mine + by) % count, 0, keepdims=False)
        others.append(from_behind(give.astype(BF16), axis, by))
    for other in others:
        total = total + other.astype(F32)
    return total, others


def gathered(block, axis):
    count = lax.axis_size(axis)
    mine = lax.axis_index(axis)
    whole = jnp.zeros((count,) + block.shape, block.dtype)
    whole = lax.dynamic_update_index_in_dim(whole, block, mine, 0)
    for by in range(1, count):
        whole = lax.dynamic_update_index_in_dim(
            whole, from_behind(block, axis, by), (mine - by) % count, 0
        )
    return whole.reshape(count * block.shape[0], -1)


def sum_squares(block):
    wide = block.astype(F32)
    return jnp.sum(wide * wide)


def plain(keep, came, weight_qkv, gains, heads, entries):
    width = gains.shape[1]
    lat, lon = lax.axis_index("lat"), lax.axis_index("lon")
    part = keep + came.astype(F32)
    give, keep = split_two(part, "lat", 2)
    came = swapped(give, "lat", 2).astype(F32)
    column = lax.broadcasted_iota(jnp.int32, keep.shape, 1)
    is_bias = (column >= CUT) & (column < CUT + GROUP)
    part = jnp.where(is_bias, lax.reduce_precision(keep, 8, 7), keep) + came
    bias_part = lax.reduce_precision(part[:1, CUT : CUT + GROUP], 8, 7)
    part, others = scattered(part, "lon")
    terms = [bias_part] + [other[:1, CUT : CUT + GROUP].astype(F32) for other in others]
    terms = jnp.concatenate(terms[:1] + terms[:0:-1], axis=0)
    bias = jnp.sum(jnp.roll(terms, lon, axis=0), axis=0)[:heads]
    part = jnp.concatenate([part[:, :CUT], part[:, CUT + GROUP :]], axis=1).astype(BF16)
    half = doubled(gathered(part, "lon"), "lat", 2)
    mine = lat % 2
    weight_half = lax.dynamic_slice_in_dim(weight_qkv, mine * (width // 2), width // 2, 0)
    gain_half = lax.dynamic_slice_in_dim(gains[0], mine * (width // 2), width // 2, 0)
    weighed = half[:, : 3 * width].astype(F32) * weight_half.astype(F32)
    gain_half = jnp.sum(weighed, axis=1) / gain_half
    square = sum_squares(half) + sum_squares(gain_half) + 0.5 * sum_squares(bias)
    square = square.reshape(1)
    square = square + swapped(square, "lat", 1)
    square = square + swapped(square, "section", 1)
    factor = jnp.minimum(1.0, lax.rsqrt(square[0] / entries + 1e-06))
    grads = doubled(half, "lat", 1).astype(F32) * factor
    gain = doubled(gain_half.reshape(-1, 1), "lat", 1)[:, 0] * factor
    return grads[:, : 3 * width], grads[:, 3 * width :], gain, bias * factor


def solution(mesh):
    placed = (
        P("section", None, "lat", "lon", None),
        P("section", None, "lat", "lon", None),
        P("lat", "lon"),
        P("section", None),
        P("section", None, None),
        P("section", None, None),
        P("section", None),
    )
    return jax.shard_map(
        body,
        mesh=mesh,
        in_specs=placed,
        out_specs=(
            P("section", None, "lat", "lon", None),
            P("section", None, None),
            P("section", None, None),
            P("section", None),
            P("section", None),
        ),
        check_vma=False,
    )
```

```python
import functools

import jax
import jax.numpy as jnp
from jax import lax
from jax.experimental import pallas as pl
from jax.experimental.pallas import tpu as pltpu
from jax.sharding import PartitionSpec as P

SHIFT = 6
GROUP = 128
CUT = 1408
EPSILON = 1e-05
F32 = jnp.float32
BF16 = jnp.bfloat16


def from_behind(value, axis, by):
    count = lax.axis_size(axis)
    return lax.ppermute(value, axis, [(i, (i + by) % count) for i in range(count)])


def passed_along(block, axis, distance):
    devices = range(lax.axis_size(axis))
    route = [(i - distance, i) for i in devices if i - distance in devices]
    return lax.ppermute(block, axis, route)


def swapped(value, axis, bit):
    count = lax.axis_size(axis)
    return lax.ppermute(value, axis, [(i, i ^ bit) for i in range(count)])


def dot(left, right):
    return jnp.dot(left, right, preferred_element_type=F32)


def dot_last(left, right):
    return lax.dot_general(left, right, (((1,), (1,)), ((), ())), preferred_element_type=F32)


def call(kernel, outs, scratch=(), places="", out_places="", operands=(), flops=10**8, limit=8):
    spaces = {"v": pltpu.VMEM, "s": pltpu.SMEM, "a": pl.ANY, "h": pltpu.HBM}
    places = places or "v" * len(operands)
    out_places = out_places or "v" * len(outs)
    moved = sum(o.size * o.dtype.itemsize for o in list(outs) + list(operands))
    return pl.pallas_call(
        kernel,
        out_shape=list(outs),
        in_specs=[pl.BlockSpec(memory_space=spaces[letter]) for letter in places],
        out_specs=[pl.BlockSpec(memory_space=spaces[letter]) for letter in out_places],
        scratch_shapes=list(scratch),
        compiler_params=pltpu.CompilerParams(vmem_limit_bytes=limit * 2**20),
        cost_estimate=pl.CostEstimate(flops=flops, bytes_accessed=moved, transcendentals=0),
    )(*operands)


def started(source, target, semaphores, index):
    copy = pltpu.make_async_copy(source, target, semaphores.at[index])
    copy.start()
    return copy


def shape(dims, dtype):
    return jax.ShapeDtypeStruct(dims, dtype)


def aligned(start, size):
    return pl.ds(pl.multiple_of(start, size), size)


def position():
    lat, lon = lax.axis_index("lat"), lax.axis_index("lon")
    return lax.rem(lat, 2), lax.div(lat, 2), lon


def pack_kernel(
    tokens, cot, land, gain, bias, own, rim,
    tokens_v, cot_v, land_v, gain_v, bias_v, rim32, sems,
):
    arrays = ((tokens, tokens_v), (cot, cot_v), (land, land_v), (gain, gain_v), (bias, bias_v))
    copies = [started(source, target, sems, i) for i, (source, target) in enumerate(arrays)]
    lats, cols, levels, width = tokens.shape[1:]
    half = levels * lats * SHIFT
    rim32[2 * half :, :] = jnp.zeros((rim32.shape[0] - 2 * half, width), F32)
    own[2 * half :, :] = jnp.zeros((own.shape[0] - 2 * half, width), F32)
    for which, ref in enumerate((tokens_v, cot_v)):
        copies[which].wait()
        for lat in range(lats):
            for col in range(cols):
                row = which * half + (lat * SHIFT + col % SHIFT) * levels
                part = rim32 if col < SHIFT else own
                part[row : row + levels, :] = ref[0, lat, col].astype(F32)
    for copy in copies[2:]:
        copy.wait()
    rim32[2 * half : 2 * half + lats, :cols] = land_v[...].astype(F32)
    own[2 * half : 2 * half + 1, :] = gain_v[...]
    own[2 * half + 1 : 2 * half + 2, : bias.shape[1]] = bias_v[...]
    own[2 * half + 8 : 2 * half + 8 + lats, :cols] = land_v[...].astype(F32)
    rim[...] = rim32[...].astype(BF16)


def unpack_kernel(own, back, grid, grid_v, sems):
    lats, cols, levels, width = grid.shape[1:]
    came = back[...].astype(F32)
    for lat in range(lats):
        for col in range(cols):
            row = (lat * SHIFT + col % SHIFT) * levels
            if col < SHIFT:
                grid_v[0, lat, col] = came[row : row + levels]
            else:
                grid_v[0, lat, col] = own[row : row + levels, :]
    started(grid_v, grid, sems, 0).wait()


def land_column(land, rows, first):
    lats, cols = land.shape
    row = lax.broadcasted_iota(jnp.int32, (rows, lats), 0)
    lat = lax.div(row, rows // lats)
    pick = (lat == lax.broadcasted_iota(jnp.int32, (rows, lats), 1)).astype(F32)
    lines = dot(pick.astype(BF16), land.astype(BF16))
    row = lax.broadcasted_iota(jnp.int32, (rows, cols), 0)
    column = lax.broadcasted_iota(jnp.int32, (rows, cols), 1)
    levels = rows // (lats * SHIFT)
    here = column == lax.rem(lax.div(row, levels), SHIFT) + first
    return jnp.sum(jnp.where(here, lines, 0.0), axis=1, keepdims=True)


def head_masks(dtype, size):
    lane = lax.broadcasted_iota(jnp.int32, (1, GROUP), 1)
    return [
        (lax.div(lane, size) == part).astype(F32).astype(dtype) for part in range(GROUP // size)
    ]


def stacked(block, masks):
    return jnp.concatenate([block * mask for mask in masks], axis=0)


def folded(block, masks):
    rows = block.shape[0] // len(masks)
    return sum(block[i * rows : (i + 1) * rows] * mask for i, mask in enumerate(masks))


def back_through(grad_out, probs, probs_b, qkv, keys_t, weight_out, grad_proj, size, land):
    count, width = grad_out.shape
    per = GROUP // size
    scale = size ** (-0.5)
    masks_b, masks = head_masks(BF16, size), head_masks(F32, size)
    att_t = dot_last(weight_out[...], grad_out)
    grad_att = att_t.T.astype(BF16)
    att_t = att_t.astype(BF16)
    lane = lax.broadcasted_iota(jnp.int32, (1, GROUP), 1)
    bias_row = jnp.zeros((1, GROUP), F32)
    for group in range(width // GROUP):
        at = group * GROUP
        values = qkv[:, 2 * width + at : 2 * width + at + GROUP]
        grad_probs = dot(stacked(values, masks_b), att_t[at : at + GROUP, :])
        scores_b, queries_t = [], []
        for part in range(per):
            head = group * per + part
            weights = probs[head * count : (head + 1) * count, :].astype(F32)
            grad_weights = grad_probs[part * count : (part + 1) * count]
            inner = jnp.sum(weights * grad_weights, axis=0, keepdims=True)
            grad_scores = weights * (grad_weights - inner)
            if land is not None:
                on_land = jnp.sum(grad_scores * land, axis=0, keepdims=True)
                on_land = jnp.sum(on_land, axis=1, keepdims=True)
                bias_row = bias_row + jnp.where(lane == head, on_land, 0.0)
            scaled_b = (grad_scores * scale).astype(BF16)
            scores_b.append(scaled_b)
            queries_t.append(dot(keys_t[head * size : (head + 1) * size, :], scaled_b))
        queries = qkv[:, at : at + GROUP]
        grad_keys = dot(jnp.concatenate(scores_b, axis=0), queries)
        mixed = probs_b[group * per * count : (group + 1) * per * count, :]
        grad_values = dot(mixed, grad_att[:, at : at + GROUP])
        grad_proj[:, at : at + GROUP] = jnp.concatenate(queries_t, axis=0).T.astype(BF16)
        grad_proj[:, width + at : width + at + GROUP] = folded(grad_keys, masks).astype(BF16)
        grad_proj[:, 2 * width + at : 2 * width + at + GROUP] = folded(grad_values, masks).astype(
            BF16
        )
    return bias_row


def through_norm(grad_proj, weight_t, gain, normed, inverse):
    scaled = dot(grad_proj, weight_t[...]) * gain
    mean = jnp.mean(scaled, axis=-1, keepdims=True)
    along = jnp.mean(scaled * normed, axis=-1, keepdims=True)
    return inverse * (scaled - mean - normed * along)


def ready_kernel(after, weight_qkv, weight_out, qkv_v, qkv_t, out_v, sems):
    copies = [
        started(weight_qkv, qkv_v, sems, 0),
        started(weight_out, out_v, sems, 1),
    ]
    copies[0].wait()
    width = weight_qkv.shape[0]
    for part in range(weight_qkv.shape[1] // width):
        rows = slice(part * width, (part + 1) * width)
        qkv_t[rows, :] = qkv_v[:, rows].T
    copies[1].wait()


def forward_kernel(
    own, rim, weight_qkv, weight_t, weight_out,
    skip, cot, normed_t, qkv, probs_b, attended_t, extra, normed_out,
    queries_t, keys_t, values_t, grad_proj,
    *, heads, lats, cols,
):
    width = own.shape[1]
    size = width // heads
    half = cot.shape[0] // 2
    count = 2 * half
    per = GROUP // size
    scale = size ** (-0.5)
    masks_b = head_masks(BF16, size)
    mine = own[: 2 * half, :]
    params = own[2 * half :, :]
    came = rim[...].astype(F32)
    gain = params[0:1, :]
    values = jnp.concatenate([mine[:half], came[:half]], axis=0)
    centred = values - jnp.mean(values, axis=-1, keepdims=True)
    inverse = lax.rsqrt(jnp.mean(centred * centred, axis=-1, keepdims=True) + EPSILON)
    normed = centred * inverse
    normed_out[...] = normed
    normed_b = (normed * gain).astype(BF16)
    normed_t[...] = normed_b.T
    land = jnp.concatenate(
        [
            land_column(params[8 : 8 + lats, :cols], half, SHIFT),
            land_column(came[2 * half : 2 * half + lats, :cols], half, 0),
        ],
        axis=0,
    )
    extra[:, :GROUP] = jnp.broadcast_to(land, (count, GROUP))
    extra[:, GROUP:] = jnp.broadcast_to(inverse, (count, GROUP))
    for part, turned in enumerate((queries_t, keys_t, values_t)):
        columns = slice(part * width, (part + 1) * width)
        qkv[:, columns] = dot(normed_b, weight_qkv[:, columns]).astype(BF16)
        turned[...] = qkv[:, columns].T
    for group in range(width // GROUP):
        at = group * GROUP
        keys = qkv[:, width + at : width + at + GROUP]
        scores = dot(stacked(keys, masks_b), queries_t[at : at + GROUP, :])
        for part in range(per):
            head = group * per + part
            block = scores[part * count : (part + 1) * count] * scale
            block = block + params[1:2, head : head + 1] * land
            block = jnp.exp(block - jnp.max(block, axis=0, keepdims=True))
            weights = block * (1.0 / jnp.sum(block, axis=0, keepdims=True))
            weights_b = weights.astype(BF16)
            probs_b[head * count : (head + 1) * count, :] = weights_b
            out = dot(values_t[head * size : (head + 1) * size, :], weights_b)
            attended_t[head * size : (head + 1) * size, :] = out.astype(BF16)
    grad_out = jnp.concatenate([mine[half:], came[half : 2 * half]], axis=0)
    cot[...] = grad_out.astype(BF16)
    back_through(cot[...], probs_b, probs_b, qkv, keys_t, weight_out, grad_proj, size, None)
    skip[...] = (
        through_norm(grad_proj[...], weight_t, gain, normed, inverse) + grad_out
    ).astype(BF16)


def backward_kernel(
    skip, cot, qkv, probs, weight_out, extra, normed_t, attended_t,
    total_out, grad_proj, bias_out, give,
    keys_t,
    *, heads,
):
    count, width = cot.shape
    core, _, _ = position()
    total_out[...] = (cot[...].astype(F32) + skip[...].astype(F32)).astype(BF16)
    keys_t[...] = qkv[:, width : 2 * width].T
    bias_row = back_through(
        total_out[...], probs, probs, qkv, keys_t, weight_out, grad_proj, width // heads,
        extra[:, :1],
    )
    bias_out[...] = jnp.broadcast_to(bias_row, bias_out.shape)
    half = width // 2
    rows = aligned((1 - core) * half, half)
    weight_rows(rows, normed_t, attended_t, grad_proj, total_out, bias_row, give)


def weight_rows(rows, normed_t, attended_t, grad_proj, total, bias_row, out):
    tokens = normed_t[rows, :]
    three = grad_proj.shape[1]
    out[:, :CUT] = dot(tokens, grad_proj[:, :CUT]).astype(out.dtype)
    out[:, CUT : CUT + GROUP] = jnp.broadcast_to(bias_row, (out.shape[0], GROUP)).astype(out.dtype)
    out[:, CUT + GROUP : three + GROUP] = dot(tokens, grad_proj[:, CUT:]).astype(out.dtype)
    out[:, three + GROUP :] = dot(attended_t[rows, :], total[...]).astype(out.dtype)


def finish_kernel(
    total, grad_proj, bias_row, normed_t, attended_t, normed, extra, weight_t, params,
    keep, own, back,
):
    count, width = total.shape
    half = width // 2
    core, _, _ = position()
    rows = aligned(core * half, half)
    bias_b = bias_row[:1, :].astype(BF16).astype(F32)
    weight_rows(rows, normed_t, attended_t, grad_proj, total, bias_b, keep)
    inverse = extra[:, GROUP : GROUP + 1]
    final = through_norm(grad_proj[...], weight_t, params[count : count + 1, :], normed[...], inverse)
    final = final + total[...].astype(F32)
    own[...] = final[: count // 2]
    back[...] = final[count // 2 :].astype(BF16)


def first_kernel(keep, came, give_p, kept_p, kept_q, *rest):
    _, y, z = position()
    *give_q, total = rest
    wide_p = give_p.shape[1]
    half = keep.shape[0] // 2
    total[...] = keep[...] + came[...].astype(F32)
    give_p[...] = total[aligned((1 - y) * half, half), :wide_p].astype(BF16)
    mine = aligned(y * half, half)
    kept_p[:, :CUT] = total[mine, :CUT]
    kept_p[:, CUT:] = total[mine, CUT:wide_p].astype(BF16).astype(F32)
    piece = kept_q.shape[0]
    kept_q[...] = total[aligned(z * piece, piece), wide_p:]
    for other, ref in zip(range(len(give_q), 0, -1), give_q):
        ref[...] = total[aligned((z ^ other) * piece, piece), wide_p:].astype(BF16)


def second_kernel(after, kept_p, came_p, kept_q, *rest):
    _, y, z = position()
    count = (len(rest) - 5) // 2
    came_q, (give_q, left_q, left_p) = rest[:count], rest[count : count + 3]
    *give_p, total_p, total_q = rest[count + 3 :]
    total_p[...] = kept_p[...] + came_p[...].astype(F32)
    piece = left_p.shape[0]
    mine = aligned(z * piece, piece)
    left_p[:, :CUT] = total_p[mine, :CUT]
    left_p[:, CUT:] = total_p[mine, CUT:].astype(BF16).astype(F32)
    for other, ref in zip(range(len(give_p), 0, -1), give_p):
        ref[...] = total_p[aligned((z ^ other) * piece, piece), :].astype(BF16)
    total = kept_q[...]
    for ref in came_q:
        total = total + ref[...].astype(F32)
    total_q[...] = total
    half = give_q.shape[0]
    give_q[...] = total_q[aligned((1 - y) * half, half), :].astype(BF16)
    left_q[...] = total_q[aligned(y * half, half), :]


def third_kernel(left_p, left_q, came_q, *rest):
    _, _, z = position()
    *came_p, piece_p, piece_q, bias = rest
    total = left_p[:, :CUT]
    for ref in came_p:
        total = total + ref[:, :CUT].astype(F32)
    piece_p[...] = total.astype(BF16)
    piece_q[...] = (left_q[...] + came_q[...].astype(F32)).astype(BF16)
    terms = [left_p[:8, CUT:]] + [ref[...].astype(F32)[:8, CUT:] for ref in came_p[::-1]]
    total = jnp.zeros_like(terms[0])
    for source in range(len(terms)):
        for other, term in enumerate(terms):
            total = total + jnp.where((z ^ other) == source, term, 0.0)
    bias[...] = total


def fourth_kernel(piece_q, other_q, *rest):
    _, y, z = position()
    *parts_p, block_p, block_q = rest
    piece = parts_p[0].shape[0]
    for other, part in enumerate(parts_p):
        block_p[aligned((z ^ other) * piece, piece), :] = part[...]
    piece = piece_q.shape[0]
    block_q[aligned(y * piece, piece), :] = piece_q[...]
    block_q[aligned((1 - y) * piece, piece), :] = other_q[...]


def fifth_kernel(weight_qkv, own, bias, block_p, other_p, *rest):
    *parts_q, half, row = rest
    core, y, z = position()
    rows = half.shape[0]
    mine = aligned(core * rows, rows)
    piece = block_p.shape[0]
    half[aligned(y * piece, piece), :CUT] = block_p[...]
    half[aligned((1 - y) * piece, piece), :CUT] = other_p[...]
    piece = parts_q[0].shape[0]
    for other, part in enumerate(parts_q):
        half[aligned((z ^ other) * piece, piece), CUT:] = part[...]
    three = weight_qkv.shape[1]
    wide = half[:, :three].astype(F32)
    gain_half = jnp.sum(wide * weight_qkv[mine, :].astype(F32), axis=1, keepdims=True)
    gain_half = jnp.broadcast_to(gain_half, (rows, GROUP)).T[:8]
    gain = own[own.shape[0] - 16 : own.shape[0] - 15, :]
    own_gain = jnp.where(core == 0, gain[:, :rows], gain[:, rows:])
    gain_half = gain_half / own_gain
    out = half[:, three:].astype(F32)
    square = jnp.sum(jnp.sum(wide * wide, axis=0, keepdims=True), axis=1, keepdims=True)
    square = square + jnp.sum(jnp.sum(out * out, axis=0, keepdims=True), axis=1, keepdims=True)
    square = square + jnp.sum(gain_half[:1] * gain_half[:1], axis=1, keepdims=True)
    square = square + 0.5 * jnp.sum(bias[:1, :] * bias[:1, :], axis=1, keepdims=True)
    row[:, :rows] = gain_half
    row[:, rows:] = jnp.broadcast_to(square, (8, GROUP))


def last_kernel(
    half, other, row, row_core, row_section, row_both, bias,
    grad_qkv, grad_out, grad_gain, grad_bias,
    qkv_v, out_v, gain_v, bias_v, sems,
    *, entries,
):
    core, _, _ = position()
    rows, three = half.shape[0], grad_qkv.shape[1]
    square = row[:1, rows : rows + 1] + row_core[:1, rows : rows + 1]
    square = square + (row_section[:1, rows : rows + 1] + row_both[:1, rows : rows + 1])
    factor = jnp.minimum(1.0, lax.rsqrt(square / entries + 1e-06))
    sent = []
    piece = 64
    for which, ref in enumerate((half, other)):
        base = core * rows if which == 0 else (1 - core) * rows
        for part in range(rows // piece):
            here = slice(part * piece, (part + 1) * piece)
            at = aligned(base + part * piece, piece)
            slot = slice(which * rows + part * piece, which * rows + (part + 1) * piece)
            qkv_v[slot, :] = ref[here, :three].astype(F32) * factor
            sent.append(started(qkv_v.at[slot, :], grad_qkv.at[at, :], sems, len(sent)))
            out_v[slot, :] = ref[here, three:].astype(F32) * factor
            sent.append(started(out_v.at[slot, :], grad_out.at[at, :], sems, len(sent)))
    mine, its = row[:1, :rows] * factor, row_core[:1, :rows] * factor
    gain_v[:, :rows] = jnp.where(core == 0, mine, its)
    gain_v[:, rows:] = jnp.where(core == 0, its, mine)
    bias_v[...] = bias[:1, : bias_v.shape[1]] * factor
    sent.append(started(gain_v, grad_gain, sems, len(sent)))
    sent.append(started(bias_v, grad_bias, sems, len(sent)))
    for copy in sent:
        copy.wait()


def far_first(pieces, axis):
    others = range(len(pieces), 0, -1)
    return [swapped(piece, axis, other) for other, piece in zip(others, pieces)]


def to_all(piece, axis):
    return [swapped(piece, axis, other) for other in range(1, lax.axis_size(axis))]


def vmem(dims, dtype):
    return pltpu.VMEM(dims, dtype)


def copies(number):
    return pltpu.SemaphoreType.DMA((number,))


def body(inputs, cotangent, land_sea, gains, qkv_weight, out_weight, land_bias):
    weight_qkv, weight_out = qkv_weight[0], out_weight[0]
    levels, lats, cols, width = inputs.shape[1:]
    heads = land_bias.shape[1]
    half = levels * lats * SHIFT
    count = 2 * half
    packed = half * 2 + 16
    lons = lax.axis_size("lon")

    tokens = inputs.transpose(0, 2, 3, 1, 4)
    own_cot = cotangent.transpose(0, 2, 3, 1, 4)

    own, rim = call(
        pack_kernel,
        [shape((packed, width), F32), shape((packed, width), BF16)],
        scratch=[
            vmem(tokens.shape, BF16),
            vmem(tokens.shape, BF16),
            vmem(land_sea.shape, jnp.int32),
            vmem(gains.shape, F32),
            vmem(land_bias.shape, F32),
            vmem((packed, width), F32),
            copies(5),
        ],
        places="hhhhh",
        operands=(tokens, own_cot, land_sea, gains, land_bias),
        limit=60,
    )
    rim = from_behind(rim, "lon", -1)
    qkv_v, qkv_t, out_v = call(
        ready_kernel,
        [
            shape(weight_qkv.shape, BF16),
            shape(weight_qkv.shape[::-1], BF16),
            shape(weight_out.shape, BF16),
        ],
        scratch=[copies(2)],
        places="ahh",
        operands=(own, weight_qkv, weight_out),
        limit=48,
    )
    skip, cot, normed_t, qkv, probs, attended_t, extra, normed = call(
        functools.partial(forward_kernel, heads=heads, lats=lats, cols=cols),
        [
            shape((count, width), BF16),
            shape((count, width), BF16),
            shape((width, count), BF16),
            shape((count, 3 * width), BF16),
            shape((heads * count, count), BF16),
            shape((width, count), BF16),
            shape((count, 2 * GROUP), F32),
            shape((count, width), F32),
        ],
        scratch=[
            vmem((width, count), BF16),
            vmem((width, count), BF16),
            vmem((width, count), BF16),
            vmem((count, 3 * width), BF16),
        ],
        operands=(own, rim, qkv_v, qkv_t, out_v),
        flops=10**9,
        limit=16,
    )
    skip = passed_along(skip, "section", -1)
    rows, wide = width // 2, 4 * width + GROUP
    total, grad_proj, bias_row, give = call(
        functools.partial(backward_kernel, heads=heads),
        [
            shape((count, width), BF16),
            shape((count, 3 * width), BF16),
            shape((8, GROUP), F32),
            shape((rows, wide), BF16),
        ],
        scratch=[vmem((width, count), BF16)],
        operands=(skip, cot, qkv, probs, out_v, extra, normed_t, attended_t),
        flops=10**9,
    )
    came = swapped(give, "lat", 1)
    keep, own_grad, back = call(
        finish_kernel,
        [
            shape((rows, wide), F32),
            shape((half, width), F32),
            shape((half, width), BF16),
        ],
        operands=(
            total, grad_proj, bias_row, normed_t, attended_t, normed, extra, qkv_t, own,
        ),
        flops=5 * 10**8,
    )
    back = from_behind(back, "lon", 1)
    entries = 2 * (4 * width * width + width + heads)
    if rows // 2 // lons % 16 == 0 and lons & (lons - 1) == 0:
        grads = staged(keep, came, back, qkv_v, own, lons, heads, entries)
    else:
        grads = plain(keep, came, weight_qkv, gains, heads, entries)
    (final_grad,) = call(
        unpack_kernel,
        [shape(tokens.shape, F32)],
        scratch=[vmem(tokens.shape, F32), copies(1)],
        out_places="h",
        operands=(own_grad, back),
    )
    final_grad = final_grad.transpose(0, 3, 1, 2, 4)
    return (final_grad, *(grad[None] for grad in grads))


def staged(keep, came, after, weight_qkv, own, lons, heads, entries):
    rows, wide = keep.shape
    width = 2 * rows
    wide_p = CUT + GROUP
    wide_q = wide - wide_p
    some = range(lons - 1)
    several = "v" * len(some)
    give_p, kept_p, kept_q, *give_q = call(
        first_kernel,
        [
            shape((rows // 2, wide_p), BF16),
            shape((rows // 2, wide_p), F32),
            shape((rows // lons, wide_q), F32),
            *(shape((rows // lons, wide_q), BF16) for _ in some),
        ],
        scratch=[vmem((rows, wide), F32)],
        operands=(keep, came),
    )
    came_p = swapped(give_p, "lat", 2)
    came_q = far_first(give_q, "lon")
    piece = rows // 2 // lons
    give_q, left_q, left_p, *give_p = call(
        second_kernel,
        [
            shape((piece, wide_q), BF16),
            shape((piece, wide_q), F32),
            shape((piece, wide_p), F32),
            *(shape((piece, wide_p), BF16) for _ in some),
        ],
        scratch=[vmem((rows // 2, wide_p), F32), vmem((rows // lons, wide_q), F32)],
        places="avvv" + several,
        operands=(after, kept_p, came_p, kept_q, *came_q),
    )
    came_p = far_first(give_p, "lon")
    came_q = swapped(give_q, "lat", 2)
    piece_p, piece_q, bias = call(
        third_kernel,
        [
            shape((piece, CUT), BF16),
            shape((piece, wide_q), BF16),
            shape((8, GROUP), F32),
        ],
        operands=(left_p, left_q, came_q, *came_p),
    )
    others_p = to_all(piece_p, "lon")
    other_q = swapped(piece_q, "lat", 2)
    block_p, block_q = call(
        fourth_kernel,
        [shape((rows // 2, CUT), BF16), shape((rows // lons, wide_q), BF16)],
        operands=(piece_q, other_q, piece_p, *others_p),
    )
    other_p = swapped(block_p, "lat", 2)
    others_q = to_all(block_q, "lon")
    half, row = call(
        fifth_kernel,
        [shape((rows, 4 * width), BF16), shape((8, rows + GROUP), F32)],
        operands=(weight_qkv, own, bias, block_p, other_p, block_q, *others_q),
    )
    row_section = swapped(row, "section", 1)
    row_both = lax.ppermute(row, ("section", "lat"), across())
    row_core = swapped(row, "lat", 1)
    other = swapped(half, "lat", 1)
    grads = call(
        functools.partial(last_kernel, entries=entries),
        [
            shape((width, 3 * width), F32),
            shape((width, width), F32),
            shape((1, width), F32),
            shape((1, heads), F32),
        ],
        scratch=[
            vmem((width, 3 * width), F32),
            vmem((width, width), F32),
            vmem((1, width), F32),
            vmem((1, heads), F32),
            copies(4 * rows // 64 + 2),
        ],
        out_places="hhhh",
        operands=(half, other, row, row_core, row_section, row_both, bias),
    )
    return grads[0], grads[1], grads[2][0], grads[3][0]


def across():
    sections, lats = lax.axis_size("section"), lax.axis_size("lat")
    return [
        (s * lats + i, (sections - 1 - s) * lats + (i ^ 1))
        for s in range(sections)
        for i in range(lats)
    ]


def split_two(block, axis, bit):
    mine = (lax.axis_index(axis) // bit) % 2
    pair = block.reshape(2, block.shape[0] // 2, -1)
    give = lax.dynamic_index_in_dim(pair, 1 - mine, 0, keepdims=False).astype(BF16)
    return give, lax.dynamic_index_in_dim(pair, mine, 0, keepdims=False)


def doubled(block, axis, bit):
    mine = (lax.axis_index(axis) // bit) % 2
    other = swapped(block, axis, bit)
    low = jnp.where(mine == 0, block, other)
    high = jnp.where(mine == 0, other, block)
    return jnp.concatenate([low, high], axis=0)


def scattered(block, axis):
    count = lax.axis_size(axis)
    mine = lax.axis_index(axis)
    pieces = block.reshape(count, block.shape[0] // count, -1)
    total = lax.dynamic_index_in_dim(pieces, mine, 0, keepdims=False)
    others = []
    for by in range(1, count):
        give = lax.dynamic_index_in_dim(pieces, (mine + by) % count, 0, keepdims=False)
        others.append(from_behind(give.astype(BF16), axis, by))
    for other in others:
        total = total + other.astype(F32)
    return total, others


def gathered(block, axis):
    count = lax.axis_size(axis)
    mine = lax.axis_index(axis)
    whole = jnp.zeros((count,) + block.shape, block.dtype)
    whole = lax.dynamic_update_index_in_dim(whole, block, mine, 0)
    for by in range(1, count):
        whole = lax.dynamic_update_index_in_dim(
            whole, from_behind(block, axis, by), (mine - by) % count, 0
        )
    return whole.reshape(count * block.shape[0], -1)


def sum_squares(block):
    wide = block.astype(F32)
    return jnp.sum(wide * wide)


def plain(keep, came, weight_qkv, gains, heads, entries):
    width = gains.shape[1]
    lat, lon = lax.axis_index("lat"), lax.axis_index("lon")
    part = keep + came.astype(F32)
    give, keep = split_two(part, "lat", 2)
    came = swapped(give, "lat", 2).astype(F32)
    column = lax.broadcasted_iota(jnp.int32, keep.shape, 1)
    is_bias = (column >= CUT) & (column < CUT + GROUP)
    part = jnp.where(is_bias, lax.reduce_precision(keep, 8, 7), keep) + came
    bias_part = lax.reduce_precision(part[:1, CUT : CUT + GROUP], 8, 7)
    part, others = scattered(part, "lon")
    terms = [bias_part] + [other[:1, CUT : CUT + GROUP].astype(F32) for other in others]
    terms = jnp.concatenate(terms[:1] + terms[:0:-1], axis=0)
    bias = jnp.sum(jnp.roll(terms, lon, axis=0), axis=0)[:heads]
    part = jnp.concatenate([part[:, :CUT], part[:, CUT + GROUP :]], axis=1).astype(BF16)
    half = doubled(gathered(part, "lon"), "lat", 2)
    mine = lat % 2
    weight_half = lax.dynamic_slice_in_dim(weight_qkv, mine * (width // 2), width // 2, 0)
    gain_half = lax.dynamic_slice_in_dim(gains[0], mine * (width // 2), width // 2, 0)
    weighed = half[:, : 3 * width].astype(F32) * weight_half.astype(F32)
    gain_half = jnp.sum(weighed, axis=1) / gain_half
    square = sum_squares(half) + sum_squares(gain_half) + 0.5 * sum_squares(bias)
    square = square.reshape(1)
    square = square + swapped(square, "lat", 1)
    square = square + swapped(square, "section", 1)
    factor = jnp.minimum(1.0, lax.rsqrt(square[0] / entries + 1e-06))
    grads = doubled(half, "lat", 1).astype(F32) * factor
    gain = doubled(gain_half.reshape(-1, 1), "lat", 1)[:, 0] * factor
    return grads[:, : 3 * width], grads[:, 3 * width :], gain, bias * factor


def solution(mesh):
    placed = (
        P("section", None, "lat", "lon", None),
        P("section", None, "lat", "lon", None),
        P("lat", "lon"),
        P("section", None),
        P("section", None, None),
        P("section", None, None),
        P("section", None),
    )
    return jax.shard_map(
        body,
        mesh=mesh,
        in_specs=placed,
        out_specs=(
            P("section", None, "lat", "lon", None),
            P("section", None, None),
            P("section", None, None),
            P("section", None),
            P("section", None),
        ),
        check_vma=False,
    )
```
